32 devices in a mesh: pipe: 4 (over z), dp: 8 (over y, x, core).
Axes of the slice: x: 2, y: 2, z: 4, core: 2. Of those that a mesh axis runs over, the one named last changes fastest.
Arguments:
- tokens: bfloat16 [4096, 768], P('dp'), may hold values from -6 to 6
- gain_one: float32 [8, 768], P('pipe'), may hold values from 0.25 to 1.75
- qkv_weight: bfloat16 [8, 768, 2304], P('pipe'), may hold values from -0.21875 to 0.21875
- out_weight: bfloat16 [8, 768, 768], P('pipe'), may hold values from -1.25 to 1.25
- gain_two: float32 [8, 768], P('pipe'), may hold values from 0.25 to 1.75
- up_weight: bfloat16 [8, 768, 3072], P('pipe'), may hold values from -0.21875 to 0.21875
- down_weight: bfloat16 [8, 3072, 768], P('pipe'), may hold values from -0.109375 to 0.109375
- cotangent: bfloat16 [4096, 768], P('dp'), may hold values from -6 to 6
- flags: int32 [4096], P('dp'), may hold values from 0 to 1, as said below
- groups: int32 [32], P('dp'), may hold values from 0 to 1, as said below
Outputs:
- final_acts: bfloat16 [4096, 768], P('dp', 'pipe')
- input_grad: float32 [4096, 768], P('dp', 'pipe')
- grad_gain_one: float32 [8, 768], P('pipe', 'dp')
- grad_qkv: float32 [8, 768, 2304], P('pipe', 'dp')
- grad_out: float32 [8, 768, 768], P('pipe', 'dp')
- grad_gain_two: float32 [8, 768], P('pipe', 'dp')
- grad_up: float32 [8, 768, 3072], P('pipe', 'dp')
- grad_down: float32 [8, 3072, 768], P('pipe', 'dp')
The draws below stay inside these ranges and needn't reach their ends.
Inputs may be any that keep to these rules, and one draw needn't show every extreme that they name: `groups`: 0: the micro-batch is one image of 128 slots; 1: it holds four images of 32 slots each. `flags`: the valid slots of each image form a prefix of it covering at least half of its slots.
All inputs are finite; a program needn't handle non-finite values.
Results may differ from the reference program's by a relative error of at most 0.024.
Values may be sent and summed in bfloat16 or wider, within the bound.
A program may use at most 320 MiB of HBM per device.

```python
import math
import jax
import jax.numpy as jnp
from jax import lax

D = 768
HEADS = 16
HEAD_DIM = 48
FF = 3072
SEQ = 128
MB = 4
TOKENS = 4096
LAYERS = 8
N_PIPE = 4
N_DP = 8


def draw_pattern(key):
    return jax.random.randint(key, (N_DP * MB,), 0, 2).astype(jnp.int32)


def draw_groups(key, part):
    shared = draw_pattern(key)
    return shared


def draw_flags(key, part):
    shared = draw_pattern(key)
    key = jax.random.fold_in(key, 7)
    first_key, second_key = jax.random.split(key)
    count = N_DP * MB
    whole_len = jax.random.randint(first_key, (count, 1), SEQ // 2, SEQ + 1)
    quarter_len = jax.random.randint(second_key, (count, 4, 1), SEQ // 8, SEQ // 4 + 1)
    position = jnp.arange(SEQ)
    local = jnp.arange(SEQ // 4)
    whole_valid = position[None, :] < whole_len
    quarter_valid = (local[None, None, :] < quarter_len).reshape(count, SEQ)
    valid = jnp.where(shared[:, None] == 1, quarter_valid, whole_valid)
    return valid.reshape(-1).astype(jnp.int32)


def steps_of(stream_key, extent, cuts, low, largest):
    def one(dim, shards_of):
        steps = jax.random.uniform(jax.random.fold_in(jax.random.fold_in(stream_key, 6), dim), (shards_of,), jnp.float32, low / len(cuts), largest / len(cuts))
        return jnp.repeat(jnp.exp(steps), extent[dim] // shards_of).reshape((-1,) + (1,) * (len(extent) - dim - 1))

    loudness = one(*cuts[0])
    for cut in cuts[1:]:
        loudness = loudness * one(*cut)
    return loudness


def normal_values(rng, extent, width, most, cuts=(), held_as=jnp.bfloat16):
    array = width * jax.random.normal(rng, extent, jnp.float32)
    if cuts:
        array = array * steps_of(rng, extent, cuts, -0.22, 0.18)
    return jnp.clip(array, -most, most).astype(held_as)


def setup_inputs(seed: int = 0) -> dict:
    streams_of = jax.random.split(jax.random.key(seed), 11)
    return {
        "tokens": normal_values(streams_of[0], (TOKENS, D), 1.0, 6.0, ((0, 8),)),
        "gain_one": jnp.clip(1.0 + 0.15 * jax.random.normal(streams_of[1], (LAYERS, D), jnp.float32), 0.25, 1.75),
        "qkv_weight": normal_values(streams_of[2], (LAYERS, D, 3 * D), D ** -0.5, 0.21875, ((0, 4),)),
        "out_weight": normal_values(streams_of[3], (LAYERS, D, D), (D * 4 // SEQ) ** -0.5, 1.25, ((0, 4),)),
        "gain_two": jnp.clip(1.0 + 0.15 * jax.random.normal(streams_of[4], (LAYERS, D), jnp.float32), 0.25, 1.75),
        "up_weight": normal_values(streams_of[5], (LAYERS, D, FF), D ** -0.5, 0.21875, ((0, 4),)),
        "down_weight": normal_values(streams_of[6], (LAYERS, FF, D), FF ** -0.5, 0.109375, ((0, 4),)),
        "cotangent": normal_values(streams_of[7], (TOKENS, D), 1.0, 6.0, ((0, 8),)),
        "flags": draw_flags(jax.random.fold_in(streams_of[10], 71), 0),
        "groups": draw_groups(jax.random.fold_in(streams_of[10], 71), 0),
    }


EPS = 1e-06

@jax.custom_vjp
def low(v):
    return lax.optimization_barrier(v.astype(jnp.bfloat16)).astype(jnp.float32)

@jax.custom_vjp
def low_back(v):
    return v

def low_keep(v):
    return (low(v), None)

def low_pass(kept, grad):
    return (grad,)

def back_keep(v):
    return (v, None)

def back_low(kept, grad):
    return (low(grad),)
low.defvjp(low_keep, low_pass)
low_back.defvjp(back_keep, back_low)

def norm(x, g):
    centre = x - lax.optimization_barrier(jnp.mean(x, axis=-1, keepdims=True))
    spread = lax.optimization_barrier(jnp.mean(centre * centre, axis=-1, keepdims=True))
    return centre * lax.rsqrt(spread + EPS) * g

def gelu_exact(v):
    return jax.nn.gelu(v, approximate=False)

def layer(x, g1, wqkv, wo, g2, w1, w2, mask):
    highest = lax.Precision.HIGHEST
    batch, slots = (x.shape[0], x.shape[1])
    u = low(norm(x, g1))
    qkv = low(low_back(jnp.einsum('bsd,de->bse', u, wqkv, precision=highest)))
    query = qkv[..., :D].reshape(batch, slots, HEADS, HEAD_DIM)
    keys = qkv[..., D:2 * D].reshape(batch, slots, HEADS, HEAD_DIM)
    values = qkv[..., 2 * D:].reshape(batch, slots, HEADS, HEAD_DIM)
    scores = jnp.einsum('bqhd,bkhd->bhqk', query, keys, precision=highest) * HEAD_DIM ** (-0.5)
    scores = low_back(scores)
    scores = jnp.where(mask[:, None], scores, -1e+30)
    probs = low(jax.nn.softmax(scores, axis=-1))
    mixed = jnp.einsum('bhqk,bkhd->bqhd', probs, values, precision=highest).reshape(batch, slots, D)
    mixed = low(low_back(mixed))
    h = x + low_back(jnp.einsum('bsd,de->bse', mixed, wo, precision=highest))
    u_two = low(norm(h, g2))
    inner = low_back(jnp.einsum('bsd,df->bsf', u_two, w1, precision=highest))
    active = low(gelu_exact(inner))
    return h + low_back(jnp.einsum('bsf,fd->bsd', active, w2, precision=highest))

def forward(x, g1s, wqkvs, wos, g2s, w1s, w2s, mask):
    for section in range(N_PIPE):
        for inner in range(2):
            index = 2 * section + inner
            x = layer(x, g1s[index], wqkvs[index], wos[index], g2s[index], w1s[index], w2s[index], mask)
        x = low(x)
        if section < N_PIPE - 1:
            x = low_back(x)
    return x

def reference(tokens, gain_one, qkv_weight, out_weight, gain_two, up_weight, down_weight, cotangent, flags, groups):
    total_seqs = N_DP * MB
    block = math.gcd(total_seqs, max(1, 4096 // SEQ))
    blocks = total_seqs // block
    weights = tuple((w.astype(jnp.float32) for w in (gain_one, qkv_weight, out_weight, gain_two, up_weight, down_weight)))
    position = jnp.arange(SEQ)

    def step(acc, item):
        inputs, grads_in, valid, group = item
        image = jnp.where(group[:, None] == 1, position[None, :] // (SEQ // 4), 0)
        mask = (image[:, :, None] == image[:, None, :]) & (valid[:, None, :] == 1)
        result, back = jax.vjp(lambda xx, *ws: forward(xx, *ws, mask), inputs.astype(jnp.float32), *weights)
        grads = back(grads_in.astype(jnp.float32))
        acc = tuple((a + g for a, g in zip(acc, grads[1:])))
        return (acc, (result.astype(jnp.bfloat16), grads[0]))
    items = (tokens.reshape(blocks, block, SEQ, D), cotangent.reshape(blocks, block, SEQ, D), flags.reshape(blocks, block, SEQ), groups.reshape(blocks, block))
    start = tuple((jnp.zeros(w.shape, jnp.float32) for w in weights))
    acc, (finals, igrads) = lax.scan(step, start, items)
    return (finals.reshape(-1, D), igrads.reshape(-1, D), acc[0], acc[1], acc[2], acc[3], acc[4], acc[5])
```

```python
import functools

import jax
import jax.numpy as jnp
from jax import lax
from jax.experimental import pallas as pl
from jax.experimental.pallas import tpu as pltpu
from jax.sharding import PartitionSpec as P

D = 768
HEADS = 16
HEAD_DIM = 48
FF = 3072
SEQ = 128
EPS = 1e-06
MESH = pl.DeviceIdType.MESH
F32 = jnp.float32
BF16 = jnp.bfloat16
LOG2E = 1.4426950408889634
SCALE = HEAD_DIM ** (-0.5)
MIB = 2**20
CHUNK = 768

PAIRS = ((0, 1, 0), (0, 2, 96), (1, 2, 64), (2, 1, 32))
GROUP = 384


def nn(a, b):
    return jnp.dot(a, b, preferred_element_type=F32)


def nt(a, b):
    return lax.dot_general(a, b, (((1,), (1,)), ((), ())), preferred_element_type=F32)


def tn(a, b):
    return lax.dot_general(a, b, (((0,), (0,)), ((), ())), preferred_element_type=F32)


def lanes_of_head(first, width):
    lane = lax.broadcasted_iota(jnp.int32, (SEQ, width), 1)
    return ((lane >= first) & (lane < first + HEAD_DIM)).astype(F32).astype(BF16)


def two_heads(window, first):
    width = window.shape[1]
    return jnp.concatenate(
        [window * lanes_of_head(first, width), window * lanes_of_head(first + HEAD_DIM, width)], axis=0
    )


def add_window(tiles, first, part):
    for i in range(part.shape[1] // 128):
        piece = part[:, i * 128 : (i + 1) * 128]
        tiles[first + i] = piece if tiles[first + i] is None else tiles[first + i] + piece


def norm_parts(x):
    centre = x - jnp.mean(x, axis=-1, keepdims=True)
    spread = jnp.mean(centre * centre, axis=-1, keepdims=True)
    inverse = lax.rsqrt(spread + EPS)
    return centre * inverse, inverse


def gelu_parts(z):
    phi = 0.5 * (1.0 + lax.erf(z * 0.7071067811865476))
    density = jnp.exp2(z * z * (-0.5 * LOG2E)) * 0.3989422804014327
    return z * phi, phi + z * density


def relay_kernel(
    sections,
    micros,
    tokens,
    cotangent,
    flags,
    groups,
    gain_one,
    gain_two,
    wqkv_hbm,
    wout_hbm,
    wup_hbm,
    wdown_hbm,
    fin_out,
    inp_out,
    gains_out,
    u_out,
    dqkv_out,
    o_out,
    da_out,
    u2_out,
    dz_out,
    act_out,
    dm_out,
    wqkv,
    wout,
    wup,
    wdown,
    fwd_in,
    fwd_out,
    bwd_in,
    bwd_out,
    fin_stage,
    inp_stage,
    u_s,
    qkv_s,
    p_s,
    u2_s,
    gp_s,
    stat_s,
    o_s,
    act_s,
    dm_s,
    da_s,
    state,
    acc,
    bias,
    w_sem,
    in_sem,
    fwd_send,
    fwd_recv,
    bwd_send,
    bwd_recv,
    fin_send,
    fin_recv,
    inp_send,
    inp_recv,
    out_sem,
):
    me = lax.axis_index("pipe")
    last = sections - 1
    width = D // sections

    barrier = pltpu.get_barrier_semaphore()
    for j in range(sections):

        @pl.when(me != j)
        def _():
            pl.semaphore_signal(barrier, inc=1, device_id={"pipe": j}, device_id_type=MESH)

    def weight_copy(l, k):
        src = (wqkv_hbm, wout_hbm, wup_hbm, wdown_hbm)[k]
        dst = (wqkv, wout, wup, wdown)[k]
        return pltpu.make_async_copy(src.at[l], dst.at[l], w_sem.at[l, k])

    def token_copy(m):
        return pltpu.make_async_copy(tokens.at[pl.ds(m * SEQ, SEQ)], fwd_in.at[m], in_sem.at[0, m])

    def cotangent_copy(m):
        return pltpu.make_async_copy(cotangent.at[pl.ds(m * SEQ, SEQ)], bwd_in.at[m], in_sem.at[1, m])

    @pl.when(me == 0)
    def _():
        for m in range(micros):
            token_copy(m).start()

    for l in range(2):
        for k in range(4):
            weight_copy(l, k).start()

    @pl.when(me == last)
    def _():
        for m in range(micros):
            cotangent_copy(m).start()

    def forward_copy(m):
        return pltpu.make_async_remote_copy(
            src_ref=fwd_out.at[m],
            dst_ref=fwd_in.at[m],
            send_sem=fwd_send.at[m],
            recv_sem=fwd_recv.at[m],
            device_id={"pipe": lax.rem(me + 1, sections)},
            device_id_type=MESH,
        )

    def backward_copy(m):
        return pltpu.make_async_remote_copy(
            src_ref=bwd_out.at[m],
            dst_ref=bwd_in.at[m],
            send_sem=bwd_send.at[m],
            recv_sem=bwd_recv.at[m],
            device_id={"pipe": lax.rem(me + sections - 1, sections)},
            device_id_type=MESH,
        )

    def piece_copy(stage, out, send, recv, m, j):
        return pltpu.make_async_remote_copy(
            src_ref=stage.at[m, j],
            dst_ref=out.at[pl.ds(m * SEQ, SEQ)],
            send_sem=send.at[m, j],
            recv_sem=recv.at[m],
            device_id={"pipe": j},
            device_id_type=MESH,
        )

    def own_piece(stage, out, send, m, j):
        return pltpu.make_async_copy(stage.at[m, j], out.at[pl.ds(m * SEQ, SEQ)], send.at[m, j])

    def spread(stage, out, send, recv, m, source):
        for j in range(sections):
            stage[m, j] = state[:, j * width : (j + 1) * width].astype(BF16)
            if j == source:
                own_piece(stage, out, send, m, j).start()
            else:
                piece_copy(stage, out, send, recv, m, j).start()

    outs = (u_out, dqkv_out, o_out, da_out, u2_out, dz_out, act_out, dm_out)

    def out_copy(kind, l, m):
        slot = lax.rem(2 * m + l, 2)
        src = (
            u_s.at[l, m],
            qkv_s.at[l, m],
            o_s.at[slot],
            da_s.at[slot],
            u2_s.at[l, m],
            gp_s.at[l, m],
            act_s.at[slot],
            dm_s.at[slot],
        )[kind]
        return pltpu.make_async_copy(src, outs[kind].at[l, pl.ds(m * SEQ, SEQ)], out_sem.at[kind, l, m])

    def free_slot(kind, l, m):
        @pl.when(m > 0)
        def _():
            out_copy(kind, l, m - 1).wait()

    row = lax.broadcasted_iota(jnp.int32, (SEQ, SEQ), 0) // (SEQ // 4)
    column = lax.broadcasted_iota(jnp.int32, (SEQ, SEQ), 1) // (SEQ // 4)
    same = (row == column).astype(F32)
    for m in range(micros):
        parted = (jnp.full((1, SEQ), groups[m], jnp.int32) == 1).astype(F32)
        valid = (flags[pl.ds(m, 1), :] == 1).astype(F32)
        keep = jnp.maximum(same, 1.0 - parted) * valid
        bias[m] = (keep - 1.0) * 1e30

    pl.semaphore_wait(barrier, sections - 1)

    def forward_layer(l, m):
        first = m == 0

        def weight_wait(k):
            @pl.when(first)
            def _():
                weight_copy(l, k).wait()

        x = state[...]
        xhat, inverse = norm_parts(x)
        stat_s[l, m, :, 0:1] = inverse
        u = (xhat * gain_one[pl.ds(l, 1), :]).astype(BF16)
        u_s[l, m] = u
        out_copy(0, l, m).start()
        weight_wait(0)
        for c in range(0, 3 * D, CHUNK):
            qkv_s[l, m, :, c : c + CHUNK] = nn(u_s[l, m], wqkv[l, :, c : c + CHUNK]).astype(BF16)
        free_slot(2, l, m)
        slot = lax.rem(2 * m + l, 2)
        added = bias[m]
        for g in range(2):
            tiles = [None] * 3
            for j, (tile, count, inside) in enumerate(PAIRS):
                lo = g * GROUP + tile * 128
                hi = lo + count * 128
                q = qkv_s[l, m, :, lo:hi]
                k = two_heads(qkv_s[l, m, :, D + lo : D + hi], inside)
                v = two_heads(qkv_s[l, m, :, 2 * D + lo : 2 * D + hi], inside)
                s = nt(q, k) * (SCALE * LOG2E)
                halves = []
                for h in range(2):
                    sh = s[:, h * SEQ : (h + 1) * SEQ] + added
                    e = jnp.exp2(sh - jnp.max(sh, axis=-1, keepdims=True))
                    halves.append(e * (1.0 / jnp.sum(e, axis=-1, keepdims=True)))
                p = jnp.concatenate(halves, axis=1).astype(BF16)
                at = (g * 4 + j) * 2 * SEQ
                p_s[l, m, :, at : at + 2 * SEQ] = p
                add_window(tiles, tile, nn(p, v))
            for i in range(3):
                at = g * GROUP + i * 128
                o_s[slot, :, at : at + 128] = tiles[i].astype(BF16)
        out_copy(2, l, m).start()
        weight_wait(1)
        h = state[...] + nn(o_s[slot], wout[l])
        state[...] = h
        hhat, inverse = norm_parts(h)
        stat_s[l, m, :, 1:2] = inverse
        u2_s[l, m] = (hhat * gain_two[pl.ds(l, 1), :]).astype(BF16)
        out_copy(4, l, m).start()
        weight_wait(2)
        free_slot(6, l, m)
        weight_wait(3)
        total = state[...]
        for c in range(0, FF, CHUNK):
            z = nn(u2_s[l, m], wup[l, :, c : c + CHUNK])
            act, slope = gelu_parts(z)
            act = act.astype(BF16)
            act_s[slot, :, c : c + CHUNK] = act
            gp_s[l, m, :, c : c + CHUNK] = slope.astype(BF16)
            total = total + nn(act, wdown[l, c : c + CHUNK, :])
        state[...] = total
        out_copy(6, l, m).start()

    def norm_back(du, hat_scaled, gain, inverse):
        t = du * gain
        hat = hat_scaled * (1.0 / gain)
        weighted = du * hat_scaled
        return inverse * (
            t - jnp.mean(t, axis=-1, keepdims=True) - hat * jnp.mean(weighted, axis=-1, keepdims=True)
        ), weighted

    def add_rows(at, weighted):
        part = weighted[0:8]
        for r in range(8, SEQ, 8):
            part = part + weighted[r : r + 8]
        acc[at] = acc[at] + part

    def backward_layer(l, m):
        slot = lax.rem(2 * m + l, 2)
        dy = state[...]
        free_slot(7, l, m)
        dm_s[slot] = dy.astype(BF16)
        out_copy(7, l, m).start()
        total = None
        for c in range(0, FF, CHUNK):
            da = nt(dm_s[slot], wdown[l, c : c + CHUNK, :])
            dz = (gp_s[l, m, :, c : c + CHUNK].astype(F32) * da).astype(BF16)
            gp_s[l, m, :, c : c + CHUNK] = dz
            part = nt(dz, wup[l, :, c : c + CHUNK])
            total = part if total is None else total + part
        out_copy(5, l, m).start()
        dh, weighted = norm_back(
            total, u2_s[l, m].astype(F32), gain_two[pl.ds(l, 1), :], stat_s[l, m, :, 1:2]
        )
        add_rows(2 + l, weighted)
        dh = state[...] + dh
        state[...] = dh
        free_slot(3, l, m)
        da_s[slot] = dh.astype(BF16)
        out_copy(3, l, m).start()
        do = nt(da_s[slot], wout[l]).astype(BF16)
        for g in range(2):
            q_tiles, k_tiles, v_tiles = [None] * 3, [None] * 3, [None] * 3
            for j, (tile, count, inside) in enumerate(PAIRS):
                lo = g * GROUP + tile * 128
                hi = lo + count * 128
                q2 = two_heads(qkv_s[l, m, :, lo:hi], inside)
                k2 = two_heads(qkv_s[l, m, :, D + lo : D + hi], inside)
                v2 = two_heads(qkv_s[l, m, :, 2 * D + lo : 2 * D + hi], inside)
                d2 = two_heads(do[:, lo:hi], inside)
                at = (g * 4 + j) * 2 * SEQ
                p = p_s[l, m, :, at : at + 2 * SEQ]
                dp = nt(do[:, lo:hi], v2)
                halves = []
                for h in range(2):
                    ph = p[:, h * SEQ : (h + 1) * SEQ].astype(F32)
                    dph = dp[:, h * SEQ : (h + 1) * SEQ]
                    inner = jnp.sum(ph * dph, axis=-1, keepdims=True)
                    halves.append((ph * (dph - inner)).astype(BF16))
                add_window(q_tiles, tile, nn(jnp.concatenate(halves, axis=1), k2))
                add_window(k_tiles, tile, tn(jnp.concatenate(halves, axis=0), q2))
                stacked = jnp.concatenate([p[:, :SEQ], p[:, SEQ:]], axis=0)
                add_window(v_tiles, tile, tn(stacked, d2))
            for i in range(3):
                at = g * GROUP + i * 128
                qkv_s[l, m, :, at : at + 128] = (q_tiles[i] * SCALE).astype(BF16)
                qkv_s[l, m, :, D + at : D + at + 128] = (k_tiles[i] * SCALE).astype(BF16)
                qkv_s[l, m, :, 2 * D + at : 2 * D + at + 128] = v_tiles[i].astype(BF16)
        out_copy(1, l, m).start()
        du = nt(qkv_s[l, m], wqkv[l])
        dx, weighted = norm_back(
            du, u_s[l, m].astype(F32), gain_one[pl.ds(l, 1), :], stat_s[l, m, :, 0:1]
        )
        add_rows(l, weighted)
        state[...] = state[...] + dx

    def forward_micro(m, carry):
        @pl.when(me == 0)
        def _():
            token_copy(m).wait()

        @pl.when(me > 0)
        def _():
            forward_copy(m).wait_recv()

        state[...] = fwd_in[m].astype(F32)

        def one(l, c):
            forward_layer(l, m)
            return c

        lax.fori_loop(0, 2, one, 0)

        @pl.when(me < last)
        def _():
            fwd_out[m] = state[...].astype(BF16)
            forward_copy(m).start()

        @pl.when(me == last)
        def _():
            spread(fin_stage, fin_out, fin_send, fin_recv, m, last)

        return carry

    lax.fori_loop(0, micros, forward_micro, 0)

    acc[...] = jnp.zeros_like(acc)

    def backward_micro(m, carry):
        @pl.when(me == last)
        def _():
            cotangent_copy(m).wait()

        @pl.when(me < last)
        def _():
            backward_copy(m).wait_recv()

        state[...] = bwd_in[m].astype(F32)

        def one(i, c):
            backward_layer(1 - i, m)
            return c

        lax.fori_loop(0, 2, one, 0)

        @pl.when(me > 0)
        def _():
            bwd_out[m] = state[...].astype(BF16)
            backward_copy(m).start()

        @pl.when(me == 0)
        def _():
            spread(inp_stage, inp_out, inp_send, inp_recv, m, 0)

        return carry

    lax.fori_loop(0, micros, backward_micro, 0)
    for l in range(2):
        gains_out[l : l + 1, :] = jnp.sum(acc[l], axis=0, keepdims=True) / gain_one[l : l + 1, :]
        gains_out[2 + l : 3 + l, :] = jnp.sum(acc[2 + l], axis=0, keepdims=True) / gain_two[l : l + 1, :]

    for l in range(2):
        for kind in (2, 3, 6, 7):
            out_copy(kind, l, micros - 1).wait()
        for m in range(micros):
            for kind in (0, 1, 4, 5):
                out_copy(kind, l, m).wait()
    for m in range(micros):

        @pl.when(me < last)
        def _():
            forward_copy(m).wait_send()

        @pl.when(me > 0)
        def _():
            backward_copy(m).wait_send()

        for source, stage, out, send, recv in (
            (last, fin_stage, fin_out, fin_send, fin_recv),
            (0, inp_stage, inp_out, inp_send, inp_recv),
        ):

            @pl.when(me == source)
            def _():
                for j in range(sections):
                    if j == source:
                        own_piece(stage, out, send, m, j).wait()
                    else:
                        piece_copy(stage, out, send, recv, m, j).wait_send()

            @pl.when(me != source)
            def _():
                piece_copy(stage, out, send, recv, m, source).wait_recv()


def relay(tokens, cotangent, flags, groups, gain_one, gain_two, wqkv, wout, wup, wdown):
    sections = lax.axis_size("pipe")
    rows = tokens.shape[0]
    micros = rows // SEQ
    width = D // sections
    anywhere = pl.BlockSpec(memory_space=pl.ANY)
    vmem = pl.BlockSpec(memory_space=pltpu.VMEM)
    smem = pl.BlockSpec(memory_space=pltpu.SMEM)
    dma = pltpu.SemaphoreType.DMA

    def factor(columns):
        return jax.ShapeDtypeStruct((2, rows, columns), BF16)

    def saved(columns):
        return pltpu.VMEM((2, micros, SEQ, columns), BF16)

    def two(columns):
        return pltpu.VMEM((2, SEQ, columns), BF16)

    def per_micro(columns):
        return pltpu.VMEM((micros, SEQ, columns), BF16)

    return pl.pallas_call(
        functools.partial(relay_kernel, sections, micros),
        out_shape=(
            jax.ShapeDtypeStruct((rows, width), BF16),
            jax.ShapeDtypeStruct((rows, width), BF16),
            jax.ShapeDtypeStruct((4, D), F32),
            factor(D),
            factor(3 * D),
            factor(D),
            factor(D),
            factor(D),
            factor(FF),
            factor(FF),
            factor(D),
        ),
        in_specs=[anywhere, anywhere, vmem, smem, vmem, vmem] + [anywhere] * 4,
        out_specs=(anywhere, anywhere, vmem) + (anywhere,) * 8,
        scratch_shapes=[
            pltpu.VMEM((2, D, 3 * D), BF16),
            pltpu.VMEM((2, D, D), BF16),
            pltpu.VMEM((2, D, FF), BF16),
            pltpu.VMEM((2, FF, D), BF16),
            per_micro(D),
            per_micro(D),
            per_micro(D),
            per_micro(D),
            pltpu.VMEM((micros, sections, SEQ, width), BF16),
            pltpu.VMEM((micros, sections, SEQ, width), BF16),
            saved(D),
            saved(3 * D),
            saved(HEADS * SEQ),
            saved(D),
            saved(FF),
            pltpu.VMEM((2, micros, SEQ, 128), F32),
            two(D),
            two(FF),
            two(D),
            two(D),
            pltpu.VMEM((SEQ, D), F32),
            pltpu.VMEM((4, 8, D), F32),
            pltpu.VMEM((micros, SEQ, SEQ), F32),
            dma((2, 4)),
            dma((2, micros)),
            dma((micros,)),
            dma((micros,)),
            dma((micros,)),
            dma((micros,)),
            dma((micros, sections)),
            dma((micros,)),
            dma((micros, sections)),
            dma((micros,)),
            dma((8, 2, micros)),
        ],
        compiler_params=pltpu.CompilerParams(
            collective_id=0, has_side_effects=True, vmem_limit_bytes=60 * MIB
        ),
        name="relay",
    )(tokens, cotangent, flags, groups, gain_one, gain_two, wqkv, wout, wup, wdown)


def body(
    tokens,
    gain_one,
    qkv_weight,
    out_weight,
    gain_two,
    up_weight,
    down_weight,
    cotangent,
    flags,
    groups,
):
    micros = tokens.shape[0] // SEQ
    fin, inp, gains, u, dqkv, o, da, u2, dz, act, dm = relay(
        tokens,
        cotangent,
        flags.reshape(micros, SEQ),
        groups,
        gain_one,
        gain_two,
        qkv_weight,
        out_weight,
        up_weight,
        down_weight,
    )

    def grad(a, g):
        return jnp.einsum("lsa,lsb->lab", a, g, preferred_element_type=F32).astype(BF16)

    def scattered(total):
        return lax.psum_scatter(total, "dp", scatter_dimension=1, tiled=True).astype(F32)

    return (
        fin,
        inp.astype(F32),
        scattered(gains[0:2].astype(BF16)),
        scattered(grad(u, dqkv)),
        scattered(grad(o, da)),
        scattered(gains[2:4].astype(BF16)),
        scattered(grad(u2, dz)),
        scattered(grad(act, dm)),
    )


def solution(mesh):
    return jax.shard_map(
        body,
        mesh=mesh,
        in_specs=(
            P("dp", None),
            P("pipe", None),
            P("pipe", None, None),
            P("pipe", None, None),
            P("pipe", None),
            P("pipe", None, None),
            P("pipe", None, None),
            P("dp", None),
            P("dp"),
            P("dp"),
        ),
        out_specs=(
            P("dp", "pipe"),
            P("dp", "pipe"),
            P("pipe", "dp"),
            P("pipe", "dp", None),
            P("pipe", "dp", None),
            P("pipe", "dp"),
            P("pipe", "dp", None),
            P("pipe", "dp", None),
        ),
        check_vma=False,
    )
```

```python
import functools

import jax
import jax.numpy as jnp
from jax import lax
from jax.experimental import pallas as pl
from jax.experimental.pallas import tpu as pltpu
from jax.sharding import PartitionSpec as P

D = 768
HEADS = 16
HEAD_DIM = 48
FF = 3072
SEQ = 128
EPS = 1e-06
MESH = pl.DeviceIdType.MESH
F32 = jnp.float32
BF16 = jnp.bfloat16
LOG2E = 1.4426950408889634
SCALE = HEAD_DIM ** (-0.5)
MIB = 2**20
CHUNK = 768

PAIRS = ((0, 1, 0), (0, 2, 96), (1, 2, 64), (2, 1, 32))
GROUP = 384


def nn(a, b):
    return jnp.dot(a, b, preferred_element_type=F32)


def nt(a, b):
    return lax.dot_general(a, b, (((1,), (1,)), ((), ())), preferred_element_type=F32)


def tn(a, b):
    return lax.dot_general(a, b, (((0,), (0,)), ((), ())), preferred_element_type=F32)


def lanes_of_head(first, width):
    lane = lax.broadcasted_iota(jnp.int32, (SEQ, width), 1)
    return ((lane >= first) & (lane < first + HEAD_DIM)).astype(F32).astype(BF16)


def two_heads(window, first):
    width = window.shape[1]
    return jnp.concatenate(
        [window * lanes_of_head(first, width), window * lanes_of_head(first + HEAD_DIM, width)], axis=0
    )


def add_window(tiles, first, part):
    for i in range(part.shape[1] // 128):
        piece = part[:, i * 128 : (i + 1) * 128]
        tiles[first + i] = piece if tiles[first + i] is None else tiles[first + i] + piece


def norm_parts(x):
    centre = x - jnp.mean(x, axis=-1, keepdims=True)
    spread = jnp.mean(centre * centre, axis=-1, keepdims=True)
    inverse = lax.rsqrt(spread + EPS)
    return centre * inverse, inverse


def gelu_parts(z):
    phi = 0.5 * (1.0 + lax.erf(z * 0.7071067811865476))
    density = jnp.exp2(z * z * (-0.5 * LOG2E)) * 0.3989422804014327
    return z * phi, phi + z * density


def relay_kernel(
    sections,
    replicas,
    micros,
    tokens,
    cotangent,
    flags,
    groups,
    gain_one,
    gain_two,
    wqkv_hbm,
    wout_hbm,
    wup_hbm,
    wdown_hbm,
    fin_out,
    inp_out,
    gains_out,
    u_out,
    dqkv_out,
    o_out,
    da_out,
    u2_out,
    dz_out,
    act_out,
    dm_out,
    wqkv,
    wout,
    wup,
    wdown,
    fwd_in,
    fwd_out,
    bwd_in,
    bwd_out,
    fin_stage,
    inp_stage,
    u_s,
    qkv_s,
    p_s,
    u2_s,
    gp_s,
    stat_s,
    o_s,
    act_s,
    dm_s,
    da_s,
    state,
    acc,
    bias,
    w_sem,
    in_sem,
    fwd_send,
    fwd_recv,
    bwd_send,
    bwd_recv,
    fin_send,
    fin_recv,
    inp_send,
    inp_recv,
    out_sem,
):
    me = lax.axis_index("pipe")
    last = sections - 1
    width = D // sections

    barrier = pltpu.get_barrier_semaphore()
    for j in range(sections):

        @pl.when(me != j)
        def _():
            pl.semaphore_signal(barrier, inc=1, device_id={"pipe": j}, device_id_type=MESH)

    def weight_copy(l, k):
        src = (wqkv_hbm, wout_hbm, wup_hbm, wdown_hbm)[k]
        dst = (wqkv, wout, wup, wdown)[k]
        return pltpu.make_async_copy(src.at[l], dst.at[l], w_sem.at[l, k])

    def token_copy(m):
        return pltpu.make_async_copy(tokens.at[pl.ds(m * SEQ, SEQ)], fwd_in.at[m], in_sem.at[0, m])

    def cotangent_copy(m):
        return pltpu.make_async_copy(cotangent.at[pl.ds(m * SEQ, SEQ)], bwd_in.at[m], in_sem.at[1, m])

    @pl.when(me == 0)
    def _():
        for m in range(micros):
            token_copy(m).start()

    for l in range(2):
        for k in range(4):
            weight_copy(l, k).start()

    @pl.when(me == last)
    def _():
        for m in range(micros):
            cotangent_copy(m).start()

    def forward_copy(m):
        return pltpu.make_async_remote_copy(
            src_ref=fwd_out.at[m],
            dst_ref=fwd_in.at[m],
            send_sem=fwd_send.at[m],
            recv_sem=fwd_recv.at[m],
            device_id={"pipe": lax.rem(me + 1, sections)},
            device_id_type=MESH,
        )

    def backward_copy(m):
        return pltpu.make_async_remote_copy(
            src_ref=bwd_out.at[m],
            dst_ref=bwd_in.at[m],
            send_sem=bwd_send.at[m],
            recv_sem=bwd_recv.at[m],
            device_id={"pipe": lax.rem(me + sections - 1, sections)},
            device_id_type=MESH,
        )

    def piece_copy(stage, out, send, recv, m, j):
        return pltpu.make_async_remote_copy(
            src_ref=stage.at[m, j],
            dst_ref=out.at[pl.ds(m * SEQ, SEQ)],
            send_sem=send.at[m, j],
            recv_sem=recv.at[m],
            device_id={"pipe": j},
            device_id_type=MESH,
        )

    def own_piece(stage, out, send, m, j):
        return pltpu.make_async_copy(stage.at[m, j], out.at[pl.ds(m * SEQ, SEQ)], send.at[m, j])

    def spread(stage, out, send, recv, m, source):
        for j in range(sections):
            stage[m, j] = state[:, j * width : (j + 1) * width].astype(BF16)
            if j == source:
                own_piece(stage, out, send, m, j).start()
            else:
                piece_copy(stage, out, send, recv, m, j).start()

    outs = (u_out, dqkv_out, o_out, da_out, u2_out, dz_out, act_out, dm_out)

    def out_copy(kind, l, m):
        slot = lax.rem(2 * m + l, 2)
        src = (
            u_s.at[l, m],
            qkv_s.at[l, m],
            o_s.at[slot],
            da_s.at[slot],
            u2_s.at[l, m],
            gp_s.at[l, m],
            act_s.at[slot],
            dm_s.at[slot],
        )[kind]
        return pltpu.make_async_copy(src, outs[kind].at[l, pl.ds(m * SEQ, SEQ)], out_sem.at[kind, l, m])

    def free_slot(kind, l, m):
        @pl.when(m > 0)
        def _():
            out_copy(kind, l, m - 1).wait()

    row = lax.broadcasted_iota(jnp.int32, (SEQ, SEQ), 0) // (SEQ // 4)
    column = lax.broadcasted_iota(jnp.int32, (SEQ, SEQ), 1) // (SEQ // 4)
    same = (row == column).astype(F32)
    for m in range(micros):
        parted = (jnp.full((1, SEQ), groups[m], jnp.int32) == 1).astype(F32)
        valid = (flags[pl.ds(m, 1), :] == 1).astype(F32)
        keep = jnp.maximum(same, 1.0 - parted) * valid
        bias[m] = (keep - 1.0) * 1e30

    pl.semaphore_wait(barrier, sections - 1)

    def forward_layer(l, m):
        first = m == 0

        def weight_wait(k):
            @pl.when(first)
            def _():
                weight_copy(l, k).wait()

        x = state[...]
        xhat, inverse = norm_parts(x)
        stat_s[l, m, :, 0:1] = inverse
        u = (xhat * gain_one[pl.ds(l, 1), :]).astype(BF16)
        u_s[l, m] = u
        out_copy(0, l, m).start()
        weight_wait(0)
        for c in range(0, 3 * D, CHUNK):
            qkv_s[l, m, :, c : c + CHUNK] = nn(u_s[l, m], wqkv[l, :, c : c + CHUNK]).astype(BF16)
        free_slot(2, l, m)
        slot = lax.rem(2 * m + l, 2)
        added = bias[m]
        for g in range(2):
            tiles = [None] * 3
            for j, (tile, count, inside) in enumerate(PAIRS):
                lo = g * GROUP + tile * 128
                hi = lo + count * 128
                q = qkv_s[l, m, :, lo:hi]
                k = two_heads(qkv_s[l, m, :, D + lo : D + hi], inside)
                v = two_heads(qkv_s[l, m, :, 2 * D + lo : 2 * D + hi], inside)
                s = nt(q, k) * (SCALE * LOG2E)
                halves = []
                for h in range(2):
                    sh = s[:, h * SEQ : (h + 1) * SEQ] + added
                    e = jnp.exp2(sh - jnp.max(sh, axis=-1, keepdims=True))
                    halves.append(e * (1.0 / jnp.sum(e, axis=-1, keepdims=True)))
                p = jnp.concatenate(halves, axis=1).astype(BF16)
                at = (g * 4 + j) * 2 * SEQ
                p_s[l, m, :, at : at + 2 * SEQ] = p
                add_window(tiles, tile, nn(p, v))
            for i in range(3):
                at = g * GROUP + i * 128
                o_s[slot, :, at : at + 128] = tiles[i].astype(BF16)
        out_copy(2, l, m).start()
        weight_wait(1)
        h = state[...] + nn(o_s[slot], wout[l])
        state[...] = h
        hhat, inverse = norm_parts(h)
        stat_s[l, m, :, 1:2] = inverse
        u2_s[l, m] = (hhat * gain_two[pl.ds(l, 1), :]).astype(BF16)
        out_copy(4, l, m).start()
        weight_wait(2)
        free_slot(6, l, m)
        weight_wait(3)
        total = state[...]
        for c in range(0, FF, CHUNK):
            z = nn(u2_s[l, m], wup[l, :, c : c + CHUNK])
            act, slope = gelu_parts(z)
            act = act.astype(BF16)
            act_s[slot, :, c : c + CHUNK] = act
            gp_s[l, m, :, c : c + CHUNK] = slope.astype(BF16)
            total = total + nn(act, wdown[l, c : c + CHUNK, :])
        state[...] = total
        out_copy(6, l, m).start()

    def norm_back(du, hat_scaled, gain, inverse):
        t = du * gain
        hat = hat_scaled * (1.0 / gain)
        weighted = du * hat_scaled
        return inverse * (
            t - jnp.mean(t, axis=-1, keepdims=True) - hat * jnp.mean(weighted, axis=-1, keepdims=True)
        ), weighted

    def add_rows(at, weighted):
        part = weighted[0:8]
        for r in range(8, SEQ, 8):
            part = part + weighted[r : r + 8]
        acc[at] = acc[at] + part

    def backward_layer(l, m):
        slot = lax.rem(2 * m + l, 2)
        dy = state[...]
        free_slot(7, l, m)
        dm_s[slot] = dy.astype(BF16)
        out_copy(7, l, m).start()
        total = None
        for c in range(0, FF, CHUNK):
            da = nt(dm_s[slot], wdown[l, c : c + CHUNK, :])
            dz = (gp_s[l, m, :, c : c + CHUNK].astype(F32) * da).astype(BF16)
            gp_s[l, m, :, c : c + CHUNK] = dz
            part = nt(dz, wup[l, :, c : c + CHUNK])
            total = part if total is None else total + part
        out_copy(5, l, m).start()
        dh, weighted = norm_back(
            total, u2_s[l, m].astype(F32), gain_two[pl.ds(l, 1), :], stat_s[l, m, :, 1:2]
        )
        add_rows(2 + l, weighted)
        dh = state[...] + dh
        state[...] = dh
        free_slot(3, l, m)
        da_s[slot] = dh.astype(BF16)
        out_copy(3, l, m).start()
        do = nt(da_s[slot], wout[l]).astype(BF16)
        for g in range(2):
            q_tiles, k_tiles, v_tiles = [None] * 3, [None] * 3, [None] * 3
            for j, (tile, count, inside) in enumerate(PAIRS):
                lo = g * GROUP + tile * 128
                hi = lo + count * 128
                q2 = two_heads(qkv_s[l, m, :, lo:hi], inside)
                k2 = two_heads(qkv_s[l, m, :, D + lo : D + hi], inside)
                v2 = two_heads(qkv_s[l, m, :, 2 * D + lo : 2 * D + hi], inside)
                d2 = two_heads(do[:, lo:hi], inside)
                at = (g * 4 + j) * 2 * SEQ
                p = p_s[l, m, :, at : at + 2 * SEQ]
                dp = nt(do[:, lo:hi], v2)
                halves = []
                for h in range(2):
                    ph = p[:, h * SEQ : (h + 1) * SEQ].astype(F32)
                    dph = dp[:, h * SEQ : (h + 1) * SEQ]
                    inner = jnp.sum(ph * dph, axis=-1, keepdims=True)
                    halves.append((ph * (dph - inner)).astype(BF16))
                add_window(q_tiles, tile, nn(jnp.concatenate(halves, axis=1), k2))
                add_window(k_tiles, tile, tn(jnp.concatenate(halves, axis=0), q2))
                stacked = jnp.concatenate([p[:, :SEQ], p[:, SEQ:]], axis=0)
                add_window(v_tiles, tile, tn(stacked, d2))
            for i in range(3):
                at = g * GROUP + i * 128
                qkv_s[l, m, :, at : at + 128] = (q_tiles[i] * SCALE).astype(BF16)
                qkv_s[l, m, :, D + at : D + at + 128] = (k_tiles[i] * SCALE).astype(BF16)
                qkv_s[l, m, :, 2 * D + at : 2 * D + at + 128] = v_tiles[i].astype(BF16)
        out_copy(1, l, m).start()
        du = nt(qkv_s[l, m], wqkv[l])
        dx, weighted = norm_back(
            du, u_s[l, m].astype(F32), gain_one[pl.ds(l, 1), :], stat_s[l, m, :, 0:1]
        )
        add_rows(l, weighted)
        state[...] = state[...] + dx

    def forward_micro(m, carry):
        @pl.when(me == 0)
        def _():
            token_copy(m).wait()

        @pl.when(me > 0)
        def _():
            forward_copy(m).wait_recv()

        state[...] = fwd_in[m].astype(F32)

        def one(l, c):
            forward_layer(l, m)
            return c

        lax.fori_loop(0, 2, one, 0)

        @pl.when(me < last)
        def _():
            fwd_out[m] = state[...].astype(BF16)
            forward_copy(m).start()

        @pl.when(me == last)
        def _():
            spread(fin_stage, fin_out, fin_send, fin_recv, m, last)

        return carry

    lax.fori_loop(0, micros, forward_micro, 0)

    acc[...] = jnp.zeros_like(acc)

    def backward_micro(m, carry):
        @pl.when(me == last)
        def _():
            cotangent_copy(m).wait()

        @pl.when(me < last)
        def _():
            backward_copy(m).wait_recv()

        state[...] = bwd_in[m].astype(F32)

        def one(i, c):
            backward_layer(1 - i, m)
            return c

        lax.fori_loop(0, 2, one, 0)

        @pl.when(me > 0)
        def _():
            bwd_out[m] = state[...].astype(BF16)
            backward_copy(m).start()

        @pl.when(me == 0)
        def _():
            spread(inp_stage, inp_out, inp_send, inp_recv, m, 0)

        return carry

    lax.fori_loop(0, micros, backward_micro, 0)
    share = D // replicas
    for k in range(4):
        gain = (gain_one, gain_two)[k // 2][k % 2 : k % 2 + 1, :]
        total = jnp.sum(acc[k], axis=0, keepdims=True) / gain
        for r in range(replicas):
            gains_out[r, k : k + 1, 0:share] = total[:, r * share : (r + 1) * share]

    for l in range(2):
        for kind in (2, 3, 6, 7):
            out_copy(kind, l, micros - 1).wait()
        for m in range(micros):
            for kind in (0, 1, 4, 5):
                out_copy(kind, l, m).wait()
    for m in range(micros):

        @pl.when(me < last)
        def _():
            forward_copy(m).wait_send()

        @pl.when(me > 0)
        def _():
            backward_copy(m).wait_send()

        for source, stage, out, send, recv in (
            (last, fin_stage, fin_out, fin_send, fin_recv),
            (0, inp_stage, inp_out, inp_send, inp_recv),
        ):

            @pl.when(me == source)
            def _():
                for j in range(sections):
                    if j == source:
                        own_piece(stage, out, send, m, j).wait()
                    else:
                        piece_copy(stage, out, send, recv, m, j).wait_send()

            @pl.when(me != source)
            def _():
                piece_copy(stage, out, send, recv, m, source).wait_recv()


def relay(tokens, cotangent, flags, groups, gain_one, gain_two, wqkv, wout, wup, wdown):
    sections = lax.axis_size("pipe")
    replicas = lax.axis_size("dp")
    rows = tokens.shape[0]
    micros = rows // SEQ
    width = D // sections
    anywhere = pl.BlockSpec(memory_space=pl.ANY)
    vmem = pl.BlockSpec(memory_space=pltpu.VMEM)
    smem = pl.BlockSpec(memory_space=pltpu.SMEM)
    dma = pltpu.SemaphoreType.DMA

    def factor(columns):
        return jax.ShapeDtypeStruct((2, rows, columns), BF16)

    def saved(columns):
        return pltpu.VMEM((2, micros, SEQ, columns), BF16)

    def two(columns):
        return pltpu.VMEM((2, SEQ, columns), BF16)

    def per_micro(columns):
        return pltpu.VMEM((micros, SEQ, columns), BF16)

    return pl.pallas_call(
        functools.partial(relay_kernel, sections, replicas, micros),
        out_shape=(
            jax.ShapeDtypeStruct((rows, width), BF16),
            jax.ShapeDtypeStruct((rows, width), BF16),
            jax.ShapeDtypeStruct((replicas, 8, 128), F32),
            factor(D),
            factor(3 * D),
            factor(D),
            factor(D),
            factor(D),
            factor(FF),
            factor(FF),
            factor(D),
        ),
        in_specs=[anywhere, anywhere, vmem, smem, vmem, vmem] + [anywhere] * 4,
        out_specs=(anywhere, anywhere, vmem) + (anywhere,) * 8,
        scratch_shapes=[
            pltpu.VMEM((2, D, 3 * D), BF16),
            pltpu.VMEM((2, D, D), BF16),
            pltpu.VMEM((2, D, FF), BF16),
            pltpu.VMEM((2, FF, D), BF16),
            per_micro(D),
            per_micro(D),
            per_micro(D),
            per_micro(D),
            pltpu.VMEM((micros, sections, SEQ, width), BF16),
            pltpu.VMEM((micros, sections, SEQ, width), BF16),
            saved(D),
            saved(3 * D),
            saved(HEADS * SEQ),
            saved(D),
            saved(FF),
            pltpu.VMEM((2, micros, SEQ, 128), F32),
            two(D),
            two(FF),
            two(D),
            two(D),
            pltpu.VMEM((SEQ, D), F32),
            pltpu.VMEM((4, 8, D), F32),
            pltpu.VMEM((micros, SEQ, SEQ), F32),
            dma((2, 4)),
            dma((2, micros)),
            dma((micros,)),
            dma((micros,)),
            dma((micros,)),
            dma((micros,)),
            dma((micros, sections)),
            dma((micros,)),
            dma((micros, sections)),
            dma((micros,)),
            dma((8, 2, micros)),
        ],
        compiler_params=pltpu.CompilerParams(
            collective_id=0, has_side_effects=True, vmem_limit_bytes=60 * MIB
        ),
        name="relay",
    )(tokens, cotangent, flags, groups, gain_one, gain_two, wqkv, wout, wup, wdown)


SHARDS = 8
ROWS = 96
CHUNKS = 12


def sum_kernel(
    gains_in,
    u_in,
    dqkv_in,
    o_in,
    da_in,
    u2_in,
    dz_in,
    act_in,
    dm_in,
    gains_out,
    qkv_out,
    out_out,
    up_out,
    down_out,
    u_v,
    dqkv_v,
    o_v,
    da_v,
    u2_v,
    dz_v,
    act_v,
    dm_v,
    own,
    first,
    second,
    third,
    gains_v,
    load_sem,
    gain_send,
    gain_recv,
    send,
    recv,
    out_sem,
):
    me = lax.axis_index("dp")
    core = lax.rem(me, 2)
    x = lax.rem(me // 2, 2)
    y = me // 4
    other_core = me + 1 - 2 * core
    other_x = me + 2 - 4 * x
    other_y = me + 4 - 8 * y

    barrier = pltpu.get_barrier_semaphore()
    for j in range(SHARDS):

        @pl.when(me != j)
        def _():
            pl.semaphore_signal(barrier, inc=1, device_id={"dp": j}, device_id_type=MESH)

    sources = (u_in, dqkv_in, o_in, da_in, u2_in, dz_in, act_in, dm_in)
    held = (u_v, dqkv_v, o_v, da_v, u2_v, dz_v, act_v, dm_v)

    def load(k, l):
        return pltpu.make_async_copy(sources[k].at[l], held[k], load_sem.at[k])

    for k in range(8):
        load(k, 1).start()

    pl.semaphore_wait(barrier, SHARDS - 1)

    def gain_copy(j, source):
        return pltpu.make_async_remote_copy(
            src_ref=gains_in.at[j],
            dst_ref=gains_v.at[source],
            send_sem=gain_send.at[j],
            recv_sem=gain_recv.at[source],
            device_id={"dp": j},
            device_id_type=MESH,
        )

    for j in range(SHARDS):

        @pl.when(me != j)
        def _():
            gain_copy(j, me).start()

    def remote(src, dst, step, n, to):
        return pltpu.make_async_remote_copy(
            src_ref=src,
            dst_ref=dst,
            send_sem=send.at[step, n],
            recv_sem=recv.at[step, n],
            device_id={"dp": to},
            device_id_type=MESH,
        )

    def give_copy(n, i):
        return remote(own.at[i, 1 - core], first.at[n], 0, n, other_core)

    def first_copy(n, i):
        if i % 2 == 0:
            return remote(first.at[n, :, 1 - x], second.at[n], 1, n, other_x)
        return remote(first.at[n, 1 - y], second.at[n], 1, n, other_y)

    def second_copy(n, i):
        if i % 2 == 0:
            return remote(second.at[n, 1 - y], third.at[n], 2, n, other_y)
        return remote(second.at[n, 1 - x], third.at[n], 2, n, other_x)

    def result_copy(n, l, i):
        if i < 3:
            dst = qkv_out.at[l, :, pl.ds(i * CHUNK, CHUNK)]
        elif i < 4:
            dst = out_out.at[l]
        elif i < 8:
            dst = up_out.at[l, :, pl.ds((i - 4) * CHUNK, CHUNK)]
        else:
            dst = down_out.at[l, pl.ds((i - 8) * ROWS, ROWS)]
        return pltpu.make_async_copy(third.at[n], dst, out_sem.at[n])

    def add_core(n, i):
        give_copy(n, i).wait_recv()
        first[n] = first[n] + own[i, core]
        first_copy(n, i).start()

    def layer_products(step, carry):
        l = 1 - step
        base = step * CHUNKS

        def free(i):
            @pl.when(step > 0)
            def _():
                give_copy(i, i).wait_send()

        def products(k, a, g, slots):
            load(k, l).wait()
            load(k + 1, l).wait()
            for i, columns in slots:
                free(i)
                part = tn(a[...], g[:, columns * CHUNK : (columns + 1) * CHUNK]).astype(BF16)
                for r in range(SHARDS):
                    own[i, r % 2, r // 4, (r // 2) % 2] = part[r * ROWS : (r + 1) * ROWS]
                give_copy(base + i, i).start()
                if i > 0:
                    add_core(base + i - 1, i - 1)

        def reload(k):
            @pl.when(step == 0)
            def _():
                load(k, 0).start()
                load(k + 1, 0).start()

        products(0, u_v, dqkv_v, ((0, 0), (1, 1), (2, 2)))
        reload(0)
        products(2, o_v, da_v, ((3, 0),))
        reload(2)
        products(4, u2_v, dz_v, ((4, 0), (5, 1), (6, 2), (7, 3)))
        reload(4)
        load(6, l).wait()
        load(7, l).wait()
        for i in range(8, CHUNKS):
            free(i)
        for b in range(4):
            part = tn(act_v[:, b * CHUNK : (b + 1) * CHUNK], dm_v[...]).astype(BF16)
            for r in range(8):
                own[8 + r % 4, r // 4, b // 2, b % 2] = part[r * ROWS : (r + 1) * ROWS]
        reload(6)
        for i in range(8, CHUNKS):
            give_copy(base + i, i).start()
        for i in range(7, CHUNKS):
            add_core(base + i, i)
        return carry

    lax.fori_loop(0, 2, layer_products, 0)

    def second_sums(step, carry):
        for i in range(CHUNKS):
            n = step * CHUNKS + i
            first_copy(n, i).wait_recv()
            kept = first[n, :, x] if i % 2 == 0 else first[n, y]
            second[n] = second[n] + kept
            second_copy(n, i).start()
        return carry

    lax.fori_loop(0, 2, second_sums, 0)

    gains_v[me] = gains_in[me]
    for j in range(SHARDS):

        @pl.when(me != j)
        def _():
            gain_copy(j, j).wait_recv()

    total = gains_v[0]
    for j in range(1, SHARDS):
        total = total + gains_v[j]
    gains_out[...] = total

    def last_sums(step, carry):
        for i in range(CHUNKS):
            n = step * CHUNKS + i
            second_copy(n, i).wait_recv()
            third[n] = third[n] + second[n, y if i % 2 == 0 else x]
            result_copy(n, 1 - step, i).start()
        return carry

    lax.fori_loop(0, 2, last_sums, 0)

    def finish(step, carry):
        for i in range(CHUNKS):
            n = step * CHUNKS + i
            first_copy(n, i).wait_send()
            second_copy(n, i).wait_send()
            result_copy(n, 1 - step, i).wait()
        return carry

    lax.fori_loop(0, 2, finish, 0)
    for i in range(CHUNKS):
        give_copy(CHUNKS + i, i).wait_send()
    for j in range(SHARDS):

        @pl.when(me != j)
        def _():
            gain_copy(j, me).wait_send()


def summed(gains, *factors):
    rows = factors[0].shape[1]
    anywhere = pl.BlockSpec(memory_space=pl.ANY)
    vmem = pl.BlockSpec(memory_space=pltpu.VMEM)
    dma = pltpu.SemaphoreType.DMA
    total = 2 * CHUNKS

    def shard(height, columns):
        return jax.ShapeDtypeStruct((2, height, columns), BF16)

    return pl.pallas_call(
        sum_kernel,
        out_shape=(
            jax.ShapeDtypeStruct((8, 128), F32),
            shard(ROWS, 3 * D),
            shard(ROWS, D),
            shard(ROWS, FF),
            shard(4 * ROWS, D),
        ),
        in_specs=[vmem] + [anywhere] * 8,
        out_specs=(vmem,) + (anywhere,) * 4,
        scratch_shapes=[pltpu.VMEM((rows, f.shape[2]), BF16) for f in factors]
        + [
            pltpu.VMEM((CHUNKS, 2, 2, 2, ROWS, CHUNK), BF16),
            pltpu.VMEM((total, 2, 2, ROWS, CHUNK), BF16),
            pltpu.VMEM((total, 2, ROWS, CHUNK), BF16),
            pltpu.VMEM((total, ROWS, CHUNK), BF16),
            pltpu.VMEM((SHARDS, 8, 128), F32),
            dma((8,)),
            dma((SHARDS,)),
            dma((SHARDS,)),
            dma((3, total)),
            dma((3, total)),
            dma((total,)),
        ],
        compiler_params=pltpu.CompilerParams(
            collective_id=1, has_side_effects=True, vmem_limit_bytes=60 * MIB
        ),
        name="sum",
    )(gains, *factors)


def body(
    tokens,
    gain_one,
    qkv_weight,
    out_weight,
    gain_two,
    up_weight,
    down_weight,
    cotangent,
    flags,
    groups,
):
    micros = tokens.shape[0] // SEQ
    fin, inp, gains, u, dqkv, o, da, u2, dz, act, dm = relay(
        tokens,
        cotangent,
        flags.reshape(micros, SEQ),
        groups,
        gain_one,
        gain_two,
        qkv_weight,
        out_weight,
        up_weight,
        down_weight,
    )

    replicas = lax.axis_size("dp")
    share = D // replicas
    if replicas == SHARDS and share == ROWS:
        gains, g_qkv, g_out, g_up, g_down = summed(gains, u, dqkv, o, da, u2, dz, act, dm)
        gains = gains[0:4, 0:share]
    else:

        def grad(a, g):
            total = jnp.einsum("lsa,lsb->lab", a, g, preferred_element_type=F32).astype(BF16)
            return lax.psum_scatter(total, "dp", scatter_dimension=1, tiled=True)

        gains = lax.psum_scatter(gains[:, 0:4, 0:share], "dp", scatter_dimension=0)
        g_qkv, g_out, g_up, g_down = grad(u, dqkv), grad(o, da), grad(u2, dz), grad(act, dm)
    return (
        fin,
        inp.astype(F32),
        gains[0:2],
        g_qkv.astype(F32),
        g_out.astype(F32),
        gains[2:4],
        g_up.astype(F32),
        g_down.astype(F32),
    )


def solution(mesh):
    return jax.shard_map(
        body,
        mesh=mesh,
        in_specs=(
            P("dp", None),
            P("pipe", None),
            P("pipe", None, None),
            P("pipe", None, None),
            P("pipe", None),
            P("pipe", None, None),
            P("pipe", None, None),
            P("dp", None),
            P("dp"),
            P("dp"),
        ),
        out_specs=(
            P("dp", "pipe"),
            P("dp", "pipe"),
            P("pipe", "dp"),
            P("pipe", "dp", None),
            P("pipe", "dp", None),
            P("pipe", "dp"),
            P("pipe", "dp", None),
            P("pipe", "dp", None),
        ),
        check_vma=False,
    )
```

```python
import functools

import jax
import jax.numpy as jnp
from jax import lax
from jax.experimental import pallas as pl
from jax.experimental.pallas import tpu as pltpu
from jax.sharding import PartitionSpec as P

D = 768
HEADS = 16
HEAD_DIM = 48
FF = 3072
SEQ = 128
EPS = 1e-06
MESH = pl.DeviceIdType.MESH
F32 = jnp.float32
BF16 = jnp.bfloat16
LOG2E = 1.4426950408889634
SCALE = HEAD_DIM ** (-0.5)
MIB = 2**20
CHUNK = 768

WINDOWS = tuple(
    (96 * j // 128, -(-(96 * j % 128 + 96) // 128), 96 * j % 128) for j in range(HEADS // 2)
)


def nn(a, b):
    return jnp.dot(a, b, preferred_element_type=F32)


def nt(a, b):
    return lax.dot_general(a, b, (((1,), (1,)), ((), ())), preferred_element_type=F32)


def tn(a, b):
    return lax.dot_general(a, b, (((0,), (0,)), ((), ())), preferred_element_type=F32)


def lanes_of_head(first, width):
    lane = lax.broadcasted_iota(jnp.int32, (SEQ, width), 1)
    return ((lane >= first) & (lane < first + HEAD_DIM)).astype(F32).astype(BF16)


def two_heads(window, first):
    width = window.shape[1]
    return jnp.concatenate(
        [window * lanes_of_head(first, width), window * lanes_of_head(first + HEAD_DIM, width)], axis=0
    )


def add_window(tiles, first, part):
    for i in range(part.shape[1] // 128):
        piece = part[:, i * 128 : (i + 1) * 128]
        tiles[first + i] = piece if tiles[first + i] is None else tiles[first + i] + piece


def norm_parts(x):
    centre = x - jnp.mean(x, axis=-1, keepdims=True)
    spread = jnp.mean(centre * centre, axis=-1, keepdims=True)
    inverse = lax.rsqrt(spread + EPS)
    return centre * inverse, inverse


def gelu_parts(z):
    phi = 0.5 * (1.0 + lax.erf(z * 0.7071067811865476))
    density = jnp.exp2(z * z * (-0.5 * LOG2E)) * 0.3989422804014327
    return z * phi, phi + z * density


def relay_kernel(
    sections,
    replicas,
    micros,
    tokens,
    cotangent,
    flags,
    groups,
    gain_one,
    gain_two,
    wqkv_hbm,
    wout_hbm,
    wup_hbm,
    wdown_hbm,
    fin_out,
    inp_out,
    gains_out,
    u_out,
    dqkv_out,
    o_out,
    da_out,
    u2_out,
    dz_out,
    act_out,
    dm_out,
    wqkv,
    wout,
    wup,
    wdown,
    fwd_in,
    fwd_out,
    bwd_in,
    bwd_out,
    fin_stage,
    inp_stage,
    u_s,
    qkv_s,
    p_s,
    u2_s,
    gp_s,
    stat_s,
    o_s,
    act_s,
    dm_s,
    da_s,
    state,
    acc,
    bias,
    w_sem,
    in_sem,
    fwd_send,
    fwd_recv,
    bwd_send,
    bwd_recv,
    fin_send,
    fin_recv,
    inp_send,
    inp_recv,
    out_sem,
):
    me = lax.axis_index("pipe")
    last = sections - 1
    width = D // sections

    barrier = pltpu.get_barrier_semaphore()
    for j in range(sections):

        @pl.when(me != j)
        def _():
            pl.semaphore_signal(barrier, inc=1, device_id={"pipe": j}, device_id_type=MESH)

    def weight_copy(l, k):
        src = (wqkv_hbm, wout_hbm, wup_hbm, wdown_hbm)[k]
        dst = (wqkv, wout, wup, wdown)[k]
        return pltpu.make_async_copy(src.at[l], dst.at[l], w_sem.at[l, k])

    def token_copy(m):
        return pltpu.make_async_copy(tokens.at[pl.ds(m * SEQ, SEQ)], fwd_in.at[m], in_sem.at[0, m])

    def cotangent_copy(m):
        return pltpu.make_async_copy(cotangent.at[pl.ds(m * SEQ, SEQ)], bwd_in.at[m], in_sem.at[1, m])

    @pl.when(me == 0)
    def _():
        for m in range(micros):
            token_copy(m).start()

    for l in range(2):
        for k in range(4):
            weight_copy(l, k).start()

    @pl.when(me == last)
    def _():
        for m in range(micros):
            cotangent_copy(m).start()

    def forward_copy(m):
        return pltpu.make_async_remote_copy(
            src_ref=fwd_out.at[m],
            dst_ref=fwd_in.at[m],
            send_sem=fwd_send.at[m],
            recv_sem=fwd_recv.at[m],
            device_id={"pipe": lax.rem(me + 1, sections)},
            device_id_type=MESH,
        )

    def backward_copy(m):
        return pltpu.make_async_remote_copy(
            src_ref=bwd_out.at[m],
            dst_ref=bwd_in.at[m],
            send_sem=bwd_send.at[m],
            recv_sem=bwd_recv.at[m],
            device_id={"pipe": lax.rem(me + sections - 1, sections)},
            device_id_type=MESH,
        )

    def piece_copy(stage, out, send, recv, m, j):
        return pltpu.make_async_remote_copy(
            src_ref=stage.at[m, j],
            dst_ref=out.at[pl.ds(m * SEQ, SEQ)],
            send_sem=send.at[m, j],
            recv_sem=recv.at[m],
            device_id={"pipe": j},
            device_id_type=MESH,
        )

    def own_piece(stage, out, send, m, j):
        return pltpu.make_async_copy(stage.at[m, j], out.at[pl.ds(m * SEQ, SEQ)], send.at[m, j])

    def spread(stage, out, send, recv, m, source):
        for j in range(sections):
            stage[m, j] = state[:, j * width : (j + 1) * width].astype(BF16)
            if j == source:
                own_piece(stage, out, send, m, j).start()
            else:
                piece_copy(stage, out, send, recv, m, j).start()

    outs = (u_out, dqkv_out, o_out, da_out, u2_out, dz_out, act_out, dm_out)

    def out_copy(kind, l, m):
        slot = l
        src = (
            u_s.at[l, m],
            qkv_s.at[l, m],
            o_s.at[slot],
            da_s.at[slot],
            u2_s.at[l, m],
            gp_s.at[l, m],
            act_s.at[slot],
            dm_s.at[slot],
        )[kind]
        return pltpu.make_async_copy(src, outs[kind].at[l, pl.ds(m * SEQ, SEQ)], out_sem.at[kind, l, m])

    def free_slot(kind, l, m):
        @pl.when(m > 0)
        def _():
            out_copy(kind, l, m - 1).wait()

    row = lax.broadcasted_iota(jnp.int32, (SEQ, SEQ), 0) // (SEQ // 4)
    column = lax.broadcasted_iota(jnp.int32, (SEQ, SEQ), 1) // (SEQ // 4)
    same = (row == column).astype(F32)
    for m in range(micros):
        parted = (jnp.full((1, SEQ), groups[m], jnp.int32) == 1).astype(F32)
        valid = (flags[:, m : m + 1] == 1).astype(F32)
        keep = jnp.maximum(same, 1.0 - parted) * valid
        bias[m] = (keep - 1.0) * 1e30

    pl.semaphore_wait(barrier, sections - 1)

    def forward_layer(l, m):
        first = m == 0

        def weight_wait(k):
            @pl.when(first)
            def _():
                weight_copy(l, k).wait()

        x = state[...]
        xhat, inverse = norm_parts(x)
        stat_s[l, m, :, 0:1] = inverse
        u = (xhat * gain_one[pl.ds(l, 1), :]).astype(BF16)
        u_s[l, m] = u
        out_copy(0, l, m).start()
        weight_wait(0)
        for c in range(0, 3 * D, CHUNK):
            qkv_s[l, m, :, c : c + CHUNK] = nn(u_s[l, m], wqkv[l, :, c : c + CHUNK]).astype(BF16)
        free_slot(2, l, m)
        slot = l
        added = bias[m]
        scores, tiles = [], [None] * 6
        for tile, count, inside in WINDOWS:
            lo, hi = tile * 128, (tile + count) * 128
            keys = two_heads(qkv_s[l, m, :, D + lo : D + hi], inside)
            scores.append(nt(keys, qkv_s[l, m, :, lo:hi]) * (SCALE * LOG2E))
        for j in range(len(WINDOWS)):
            for h in range(2):
                s = scores[j][h * SEQ : (h + 1) * SEQ] + added
                e = jnp.exp2(s - jnp.max(s, axis=0, keepdims=True))
                p = e * (1.0 / jnp.sum(e, axis=0, keepdims=True))
                p_s[l, m, 2 * j + h] = p.astype(BF16)
        for j, (tile, count, inside) in enumerate(WINDOWS):
            lo, hi = tile * 128, (tile + count) * 128
            values = two_heads(qkv_s[l, m, :, 2 * D + lo : 2 * D + hi], inside)
            p = jnp.concatenate([p_s[l, m, 2 * j], p_s[l, m, 2 * j + 1]], axis=0)
            add_window(tiles, tile, tn(p, values))
        for i in range(6):
            o_s[slot, :, i * 128 : (i + 1) * 128] = tiles[i].astype(BF16)
        out_copy(2, l, m).start()
        weight_wait(1)
        h = state[...] + nn(o_s[slot], wout[l])
        state[...] = h
        hhat, inverse = norm_parts(h)
        stat_s[l, m, :, 1:2] = inverse
        u2_s[l, m] = (hhat * gain_two[pl.ds(l, 1), :]).astype(BF16)
        out_copy(4, l, m).start()
        weight_wait(2)
        free_slot(6, l, m)
        weight_wait(3)
        for c in range(0, FF, CHUNK):
            act, slope = gelu_parts(nn(u2_s[l, m], wup[l, :, c : c + CHUNK]))
            act_s[slot, :, c : c + CHUNK] = act.astype(BF16)
            gp_s[l, m, :, c : c + CHUNK] = slope.astype(BF16)
        state[...] = state[...] + nn(act_s[slot], wdown[l])
        out_copy(6, l, m).start()

    def norm_back(du, hat_scaled, gain, inverse):
        t = du * gain
        hat = hat_scaled * (1.0 / gain)
        weighted = du * hat_scaled
        return inverse * (
            t - jnp.mean(t, axis=-1, keepdims=True) - hat * jnp.mean(weighted, axis=-1, keepdims=True)
        ), weighted

    def add_rows(at, weighted):
        part = weighted[0:8]
        for r in range(8, SEQ, 8):
            part = part + weighted[r : r + 8]
        acc[at] = acc[at] + part

    def backward_layer(l, m):
        slot = l
        dy = state[...]
        free_slot(7, l, m)
        dm_s[slot] = dy.astype(BF16)
        out_copy(7, l, m).start()
        for c in range(0, FF, CHUNK):
            da = nt(dm_s[slot], wdown[l, c : c + CHUNK, :])
            dz = gp_s[l, m, :, c : c + CHUNK].astype(F32) * da
            gp_s[l, m, :, c : c + CHUNK] = dz.astype(BF16)
        out_copy(5, l, m).start()
        dh, weighted = norm_back(
            nt(gp_s[l, m], wup[l]), u2_s[l, m].astype(F32), gain_two[pl.ds(l, 1), :], stat_s[l, m, :, 1:2]
        )
        add_rows(2 + l, weighted)
        dh = state[...] + dh
        state[...] = dh
        free_slot(3, l, m)
        da_s[slot] = dh.astype(BF16)
        out_copy(3, l, m).start()
        do = nt(da_s[slot], wout[l]).astype(BF16)
        slopes, products = [], []
        q_tiles, k_tiles, v_tiles = [None] * 6, [None] * 6, [None] * 6
        for tile, count, inside in WINDOWS:
            lo, hi = tile * 128, (tile + count) * 128
            values = two_heads(qkv_s[l, m, :, 2 * D + lo : 2 * D + hi], inside)
            products.append(nt(values, do[:, lo:hi]))
        for j in range(len(WINDOWS)):
            for h in range(2):
                p = p_s[l, m, 2 * j + h].astype(F32)
                dp = products[j][h * SEQ : (h + 1) * SEQ]
                slopes.append((p * (dp - jnp.sum(p * dp, axis=0, keepdims=True))).astype(BF16))
        for j, (tile, count, inside) in enumerate(WINDOWS):
            lo, hi = tile * 128, (tile + count) * 128
            pair = slopes[2 * j : 2 * j + 2]
            keys = two_heads(qkv_s[l, m, :, D + lo : D + hi], inside)
            query = two_heads(qkv_s[l, m, :, lo:hi], inside)
            add_window(q_tiles, tile, tn(jnp.concatenate(pair, axis=0), keys))
            add_window(k_tiles, tile, nn(jnp.concatenate(pair, axis=1), query))
        for j, (tile, count, inside) in enumerate(WINDOWS):
            given = two_heads(do[:, tile * 128 : (tile + count) * 128], inside)
            p = jnp.concatenate([p_s[l, m, 2 * j], p_s[l, m, 2 * j + 1]], axis=1)
            add_window(v_tiles, tile, nn(p, given))
        for i in range(6):
            at = i * 128
            qkv_s[l, m, :, at : at + 128] = (q_tiles[i] * SCALE).astype(BF16)
            qkv_s[l, m, :, D + at : D + at + 128] = (k_tiles[i] * SCALE).astype(BF16)
            qkv_s[l, m, :, 2 * D + at : 2 * D + at + 128] = v_tiles[i].astype(BF16)
        out_copy(1, l, m).start()
        du = nt(qkv_s[l, m], wqkv[l])
        dx, weighted = norm_back(
            du, u_s[l, m].astype(F32), gain_one[pl.ds(l, 1), :], stat_s[l, m, :, 0:1]
        )
        add_rows(l, weighted)
        state[...] = state[...] + dx

    def forward_micro(m, carry):
        @pl.when(me == 0)
        def _():
            token_copy(m).wait()

        @pl.when(me > 0)
        def _():
            forward_copy(m).wait_recv()

        state[...] = fwd_in[m].astype(F32)

        def one(l, c):
            forward_layer(l, m)
            return c

        lax.fori_loop(0, 2, one, 0)

        @pl.when(me < last)
        def _():
            fwd_out[m] = state[...].astype(BF16)
            forward_copy(m).start()

        @pl.when(me == last)
        def _():
            spread(fin_stage, fin_out, fin_send, fin_recv, m, last)

        return carry

    lax.fori_loop(0, micros, forward_micro, 0)

    acc[...] = jnp.zeros_like(acc)

    def backward_micro(m, carry):
        @pl.when(me == last)
        def _():
            cotangent_copy(m).wait()

        @pl.when(me < last)
        def _():
            backward_copy(m).wait_recv()

        state[...] = bwd_in[m].astype(F32)

        def one(i, c):
            backward_layer(1 - i, m)
            return c

        lax.fori_loop(0, 2, one, 0)

        @pl.when(me > 0)
        def _():
            bwd_out[m] = state[...].astype(BF16)
            backward_copy(m).start()

        @pl.when(me == 0)
        def _():
            spread(inp_stage, inp_out, inp_send, inp_recv, m, 0)

        return carry

    lax.fori_loop(0, micros, backward_micro, 0)
    share = D // replicas
    for k in range(4):
        gain = (gain_one, gain_two)[k // 2][k % 2 : k % 2 + 1, :]
        total = jnp.sum(acc[k], axis=0, keepdims=True) / gain
        for r in range(replicas):
            gains_out[r, k : k + 1, 0:share] = total[:, r * share : (r + 1) * share]

    for l in range(2):
        for kind in (2, 3, 6, 7):
            out_copy(kind, l, micros - 1).wait()
        for m in range(micros):
            for kind in (0, 1, 4, 5):
                out_copy(kind, l, m).wait()
    for m in range(micros):

        @pl.when(me < last)
        def _():
            forward_copy(m).wait_send()

        @pl.when(me > 0)
        def _():
            backward_copy(m).wait_send()

        for source, stage, out, send, recv in (
            (last, fin_stage, fin_out, fin_send, fin_recv),
            (0, inp_stage, inp_out, inp_send, inp_recv),
        ):

            @pl.when(me == source)
            def _():
                for j in range(sections):
                    if j == source:
                        own_piece(stage, out, send, m, j).wait()
                    else:
                        piece_copy(stage, out, send, recv, m, j).wait_send()

            @pl.when(me != source)
            def _():
                piece_copy(stage, out, send, recv, m, source).wait_recv()


def relay(tokens, cotangent, flags, groups, gain_one, gain_two, wqkv, wout, wup, wdown):
    sections = lax.axis_size("pipe")
    replicas = lax.axis_size("dp")
    rows = tokens.shape[0]
    micros = rows // SEQ
    width = D // sections
    anywhere = pl.BlockSpec(memory_space=pl.ANY)
    vmem = pl.BlockSpec(memory_space=pltpu.VMEM)
    smem = pl.BlockSpec(memory_space=pltpu.SMEM)
    dma = pltpu.SemaphoreType.DMA

    def factor(columns):
        return jax.ShapeDtypeStruct((2, rows, columns), BF16)

    def saved(columns):
        return pltpu.VMEM((2, micros, SEQ, columns), BF16)

    def two(columns):
        return pltpu.VMEM((2, SEQ, columns), BF16)

    def per_micro(columns):
        return pltpu.VMEM((micros, SEQ, columns), BF16)

    return pl.pallas_call(
        functools.partial(relay_kernel, sections, replicas, micros),
        out_shape=(
            jax.ShapeDtypeStruct((rows, width), BF16),
            jax.ShapeDtypeStruct((rows, width), BF16),
            jax.ShapeDtypeStruct((replicas, 8, 128), F32),
            factor(D),
            factor(3 * D),
            factor(D),
            factor(D),
            factor(D),
            factor(FF),
            factor(FF),
            factor(D),
        ),
        in_specs=[anywhere, anywhere, vmem, smem, vmem, vmem] + [anywhere] * 4,
        out_specs=(anywhere, anywhere, vmem) + (anywhere,) * 8,
        scratch_shapes=[
            pltpu.VMEM((2, D, 3 * D), BF16),
            pltpu.VMEM((2, D, D), BF16),
            pltpu.VMEM((2, D, FF), BF16),
            pltpu.VMEM((2, FF, D), BF16),
            per_micro(D),
            per_micro(D),
            per_micro(D),
            per_micro(D),
            pltpu.VMEM((micros, sections, SEQ, width), BF16),
            pltpu.VMEM((micros, sections, SEQ, width), BF16),
            saved(D),
            saved(3 * D),
            pltpu.VMEM((2, micros, HEADS, SEQ, SEQ), BF16),
            saved(D),
            saved(FF),
            pltpu.VMEM((2, micros, SEQ, 128), F32),
            two(D),
            two(FF),
            two(D),
            two(D),
            pltpu.VMEM((SEQ, D), F32),
            pltpu.VMEM((4, 8, D), F32),
            pltpu.VMEM((micros, SEQ, SEQ), F32),
            dma((2, 4)),
            dma((2, micros)),
            dma((micros,)),
            dma((micros,)),
            dma((micros,)),
            dma((micros,)),
            dma((micros, sections)),
            dma((micros,)),
            dma((micros, sections)),
            dma((micros,)),
            dma((8, 2, micros)),
        ],
        compiler_params=pltpu.CompilerParams(
            collective_id=0, has_side_effects=True, vmem_limit_bytes=60 * MIB
        ),
        name="relay",
    )(tokens, cotangent, flags, groups, gain_one, gain_two, wqkv, wout, wup, wdown)


SHARDS = 8
ROWS = 96
CHUNKS = 12


def sum_kernel(
    gains_in,
    u_in,
    dqkv_in,
    o_in,
    da_in,
    u2_in,
    dz_in,
    act_in,
    dm_in,
    gains_out,
    qkv_out,
    out_out,
    up_out,
    down_out,
    u_v,
    dqkv_v,
    o_v,
    da_v,
    u2_v,
    dz_v,
    act_v,
    dm_v,
    own,
    first,
    second,
    third,
    gains_v,
    load_sem,
    gain_send,
    gain_recv,
    send,
    recv,
    out_sem,
):
    me = lax.axis_index("dp")
    core = lax.rem(me, 2)
    x = lax.rem(me // 2, 2)
    y = me // 4
    other_core = me + 1 - 2 * core
    other_x = me + 2 - 4 * x
    other_y = me + 4 - 8 * y

    barrier = pltpu.get_barrier_semaphore()
    for j in range(SHARDS):

        @pl.when(me != j)
        def _():
            pl.semaphore_signal(barrier, inc=1, device_id={"dp": j}, device_id_type=MESH)

    sources = (u_in, dqkv_in, o_in, da_in, u2_in, dz_in, act_in, dm_in)
    held = (u_v, dqkv_v, o_v, da_v, u2_v, dz_v, act_v, dm_v)

    def load(k, l):
        return pltpu.make_async_copy(sources[k].at[l], held[k], load_sem.at[k])

    for k in range(8):
        load(k, 1).start()

    pl.semaphore_wait(barrier, SHARDS - 1)

    def gain_copy(j, source):
        return pltpu.make_async_remote_copy(
            src_ref=gains_in.at[j],
            dst_ref=gains_v.at[source],
            send_sem=gain_send.at[j],
            recv_sem=gain_recv.at[source],
            device_id={"dp": j},
            device_id_type=MESH,
        )

    for j in range(SHARDS):

        @pl.when(me != j)
        def _():
            gain_copy(j, me).start()

    def remote(src, dst, step, n, to):
        return pltpu.make_async_remote_copy(
            src_ref=src,
            dst_ref=dst,
            send_sem=send.at[step, n],
            recv_sem=recv.at[step, n],
            device_id={"dp": to},
            device_id_type=MESH,
        )

    def give_copy(n, i):
        return remote(own.at[i, 1 - core], first.at[n], 0, n, other_core)

    def first_copy(n, i):
        if i % 2 == 0:
            return remote(first.at[n, :, 1 - x], second.at[n], 1, n, other_x)
        return remote(first.at[n, 1 - y], second.at[n], 1, n, other_y)

    def second_copy(n, i):
        if i % 2 == 0:
            return remote(second.at[n, 1 - y], third.at[n], 2, n, other_y)
        return remote(second.at[n, 1 - x], third.at[n], 2, n, other_x)

    def result_copy(n, l, i):
        if i < 3:
            dst = qkv_out.at[l, :, pl.ds(i * CHUNK, CHUNK)]
        elif i < 4:
            dst = out_out.at[l]
        elif i < 8:
            dst = up_out.at[l, :, pl.ds((i - 4) * CHUNK, CHUNK)]
        else:
            dst = down_out.at[l, pl.ds((i - 8) * ROWS, ROWS)]
        return pltpu.make_async_copy(third.at[n], dst, out_sem.at[n])

    def add_core(n, i):
        give_copy(n, i).wait_recv()
        first[n] = first[n] + own[i, core]
        first_copy(n, i).start()

    def layer_products(step, carry):
        l = 1 - step
        base = step * CHUNKS

        def free(i):
            @pl.when(step > 0)
            def _():
                give_copy(i, i).wait_send()

        def products(k, a, g, slots):
            load(k, l).wait()
            load(k + 1, l).wait()
            for i, columns in slots:
                free(i)
                part = tn(a[...], g[:, columns * CHUNK : (columns + 1) * CHUNK]).astype(BF16)
                for r in range(SHARDS):
                    own[i, r % 2, r // 4, (r // 2) % 2] = part[r * ROWS : (r + 1) * ROWS]
                give_copy(base + i, i).start()
                if i > 0:
                    add_core(base + i - 1, i - 1)

        def reload(k):
            @pl.when(step == 0)
            def _():
                load(k, 0).start()
                load(k + 1, 0).start()

        products(0, u_v, dqkv_v, ((0, 0), (1, 1), (2, 2)))
        reload(0)
        products(2, o_v, da_v, ((3, 0),))
        reload(2)
        products(4, u2_v, dz_v, ((4, 0), (5, 1), (6, 2), (7, 3)))
        reload(4)
        load(6, l).wait()
        load(7, l).wait()
        for i in range(8, CHUNKS):
            free(i)
        for b in range(4):
            part = tn(act_v[:, b * CHUNK : (b + 1) * CHUNK], dm_v[...]).astype(BF16)
            for r in range(8):
                own[8 + r % 4, r // 4, b // 2, b % 2] = part[r * ROWS : (r + 1) * ROWS]
        reload(6)
        for i in range(8, CHUNKS):
            give_copy(base + i, i).start()
        for i in range(7, CHUNKS):
            add_core(base + i, i)
        return carry

    lax.fori_loop(0, 2, layer_products, 0)

    def second_sums(step, carry):
        for i in range(CHUNKS):
            n = step * CHUNKS + i
            first_copy(n, i).wait_recv()
            kept = first[n, :, x] if i % 2 == 0 else first[n, y]
            second[n] = second[n] + kept
            second_copy(n, i).start()
        return carry

    lax.fori_loop(0, 2, second_sums, 0)

    gains_v[me] = gains_in[me]
    for j in range(SHARDS):

        @pl.when(me != j)
        def _():
            gain_copy(j, j).wait_recv()

    total = gains_v[0]
    for j in range(1, SHARDS):
        total = total + gains_v[j]
    gains_out[...] = total

    def last_sums(step, carry):
        for i in range(CHUNKS):
            n = step * CHUNKS + i
            second_copy(n, i).wait_recv()
            third[n] = third[n] + second[n, y if i % 2 == 0 else x]
            result_copy(n, 1 - step, i).start()
        return carry

    lax.fori_loop(0, 2, last_sums, 0)

    def finish(step, carry):
        for i in range(CHUNKS):
            n = step * CHUNKS + i
            first_copy(n, i).wait_send()
            second_copy(n, i).wait_send()
            result_copy(n, 1 - step, i).wait()
        return carry

    lax.fori_loop(0, 2, finish, 0)
    for i in range(CHUNKS):
        give_copy(CHUNKS + i, i).wait_send()
    for j in range(SHARDS):

        @pl.when(me != j)
        def _():
            gain_copy(j, me).wait_send()


def summed(gains, *factors):
    rows = factors[0].shape[1]
    anywhere = pl.BlockSpec(memory_space=pl.ANY)
    vmem = pl.BlockSpec(memory_space=pltpu.VMEM)
    dma = pltpu.SemaphoreType.DMA
    total = 2 * CHUNKS

    def shard(height, columns):
        return jax.ShapeDtypeStruct((2, height, columns), BF16)

    return pl.pallas_call(
        sum_kernel,
        out_shape=(
            jax.ShapeDtypeStruct((8, 128), F32),
            shard(ROWS, 3 * D),
            shard(ROWS, D),
            shard(ROWS, FF),
            shard(4 * ROWS, D),
        ),
        in_specs=[vmem] + [anywhere] * 8,
        out_specs=(vmem,) + (anywhere,) * 4,
        scratch_shapes=[pltpu.VMEM((rows, f.shape[2]), BF16) for f in factors]
        + [
            pltpu.VMEM((CHUNKS, 2, 2, 2, ROWS, CHUNK), BF16),
            pltpu.VMEM((total, 2, 2, ROWS, CHUNK), BF16),
            pltpu.VMEM((total, 2, ROWS, CHUNK), BF16),
            pltpu.VMEM((total, ROWS, CHUNK), BF16),
            pltpu.VMEM((SHARDS, 8, 128), F32),
            dma((8,)),
            dma((SHARDS,)),
            dma((SHARDS,)),
            dma((3, total)),
            dma((3, total)),
            dma((total,)),
        ],
        compiler_params=pltpu.CompilerParams(
            collective_id=1, has_side_effects=True, vmem_limit_bytes=60 * MIB
        ),
        name="sum",
    )(gains, *factors)


def body(
    tokens,
    gain_one,
    qkv_weight,
    out_weight,
    gain_two,
    up_weight,
    down_weight,
    cotangent,
    flags,
    groups,
):
    micros = tokens.shape[0] // SEQ
    fin, inp, gains, u, dqkv, o, da, u2, dz, act, dm = relay(
        tokens,
        cotangent,
        flags.reshape(micros, SEQ).T,
        groups,
        gain_one,
        gain_two,
        qkv_weight,
        out_weight,
        up_weight,
        down_weight,
    )

    replicas = lax.axis_size("dp")
    share = D // replicas
    if replicas == SHARDS and share == ROWS:
        gains, g_qkv, g_out, g_up, g_down = summed(gains, u, dqkv, o, da, u2, dz, act, dm)
        gains = gains[0:4, 0:share]
    else:

        def grad(a, g):
            total = jnp.einsum("lsa,lsb->lab", a, g, preferred_element_type=F32).astype(BF16)
            return lax.psum_scatter(total, "dp", scatter_dimension=1, tiled=True)

        gains = lax.psum_scatter(gains[:, 0:4, 0:share], "dp", scatter_dimension=0)
        g_qkv, g_out, g_up, g_down = grad(u, dqkv), grad(o, da), grad(u2, dz), grad(act, dm)
    return (
        fin,
        inp.astype(F32),
        gains[0:2],
        g_qkv.astype(F32),
        g_out.astype(F32),
        gains[2:4],
        g_up.astype(F32),
        g_down.astype(F32),
    )


def solution(mesh):
    return jax.shard_map(
        body,
        mesh=mesh,
        in_specs=(
            P("dp", None),
            P("pipe", None),
            P("pipe", None, None),
            P("pipe", None, None),
            P("pipe", None),
            P("pipe", None, None),
            P("pipe", None, None),
            P("dp", None),
            P("dp"),
            P("dp"),
        ),
        out_specs=(
            P("dp", "pipe"),
            P("dp", "pipe"),
            P("pipe", "dp"),
            P("pipe", "dp", None),
            P("pipe", "dp", None),
            P("pipe", "dp"),
            P("pipe", "dp", None),
            P("pipe", "dp", None),
        ),
        check_vma=False,
    )
```

```python
import functools

import jax
import jax.numpy as jnp
from jax import lax
from jax.experimental import pallas as pl
from jax.experimental.pallas import tpu as pltpu
from jax.sharding import PartitionSpec as P

D = 768
HEADS = 16
HEAD_DIM = 48
FF = 3072
SEQ = 128
EPS = 1e-06
MESH = pl.DeviceIdType.MESH
F32 = jnp.float32
BF16 = jnp.bfloat16
LOG2E = 1.4426950408889634
SCALE = HEAD_DIM ** (-0.5)
MIB = 2**20
CHUNK = 768
TILE = 256

KINDS = ((0, 3), (3, 1), (4, 4), (8, 4))
BLOCKS = 12

WINDOWS = tuple(
    (96 * j // 128, -(-(96 * j % 128 + 96) // 128), 96 * j % 128) for j in range(HEADS // 2)
)


def nn(a, b):
    return jnp.dot(a, b, preferred_element_type=F32)


def nt(a, b):
    return lax.dot_general(a, b, (((1,), (1,)), ((), ())), preferred_element_type=F32)


def tn(a, b):
    return lax.dot_general(a, b, (((0,), (0,)), ((), ())), preferred_element_type=F32)


def lanes_of_head(first, width):
    lane = lax.broadcasted_iota(jnp.int32, (SEQ, width), 1)
    return ((lane >= first) & (lane < first + HEAD_DIM)).astype(F32).astype(BF16)


def two_heads(window, first):
    width = window.shape[1]
    return jnp.concatenate(
        [window * lanes_of_head(first, width), window * lanes_of_head(first + HEAD_DIM, width)], axis=0
    )


def add_window(tiles, first, part):
    for i in range(part.shape[1] // 128):
        piece = part[:, i * 128 : (i + 1) * 128]
        tiles[first + i] = piece if tiles[first + i] is None else tiles[first + i] + piece


def norm_parts(x):
    centre = x - jnp.mean(x, axis=-1, keepdims=True)
    spread = jnp.mean(centre * centre, axis=-1, keepdims=True)
    inverse = lax.rsqrt(spread + EPS)
    return centre * inverse, inverse


def gelu_parts(z):
    phi = 0.5 * (1.0 + lax.erf(z * 0.7071067811865476))
    density = jnp.exp2(z * z * (-0.5 * LOG2E)) * 0.3989422804014327
    return z * phi, phi + z * density


def relay_kernel(
    sections,
    replicas,
    micros,
    tokens,
    cotangent,
    flags,
    groups,
    gain_one,
    gain_two,
    wqkv_hbm,
    wout_hbm,
    wup_hbm,
    wdown_hbm,
    fin_out,
    inp_out,
    gains_out,
    u_out,
    dqkv_out,
    o_out,
    da_out,
    u2_out,
    dz_out,
    act_out,
    dm_out,
    turned_hbm,
    weights,
    fwd_in,
    fwd_out,
    bwd_in,
    bwd_out,
    fin_stage,
    inp_stage,
    u_s,
    qkv_s,
    p_s,
    u2_s,
    gp_s,
    stat_s,
    o_s,
    act_s,
    dm_s,
    da_s,
    state,
    acc,
    bias,
    w_sem,
    turn_sem,
    swap_sem,
    in_sem,
    fwd_send,
    fwd_recv,
    bwd_send,
    bwd_recv,
    fin_send,
    fin_recv,
    inp_send,
    inp_recv,
    out_sem,
):
    me = lax.axis_index("pipe")
    last = sections - 1
    width = D // sections

    barrier = pltpu.get_barrier_semaphore()
    for j in range(sections):

        @pl.when(me != j)
        def _():
            pl.semaphore_signal(barrier, inc=1, device_id={"pipe": j}, device_id_type=MESH)

    def block_rows(b, count=1):
        start = b * D
        return pl.ds(start if isinstance(b, int) else pl.multiple_of(start, D), count * D)

    def weight_copy(l, k, j):
        first, _ = KINDS[k]
        if k == 1:
            src = wout_hbm.at[l]
        elif k == 3:
            src = wdown_hbm.at[l, block_rows(j)]
        else:
            src = (wqkv_hbm, None, wup_hbm)[k].at[l, :, block_rows(j)]
        return pltpu.make_async_copy(src, weights.at[l, block_rows(first + j)], w_sem.at[l, first + j])

    def turned_copy(l, b):
        return pltpu.make_async_copy(
            weights.at[l, block_rows(b)], turned_hbm.at[l, block_rows(b)], turn_sem.at[l, b]
        )

    def swap_copy(l, k):
        rows = block_rows(*KINDS[k])
        return pltpu.make_async_copy(turned_hbm.at[l, rows], weights.at[1 - l, rows], swap_sem.at[l, k])

    def turn(l, b):
        def tile(r, c):
            return l, pl.ds(pl.multiple_of(b * D + r * TILE, TILE), TILE), pl.ds(c * TILE, TILE)

        for r in range(D // TILE):
            weights[tile(r, r)] = weights[tile(r, r)].T
            for c in range(r):
                lower = weights[tile(r, c)].T
                upper = weights[tile(c, r)].T
                weights[tile(c, r)] = lower
                weights[tile(r, c)] = upper

    def each_block(l, action):
        for k, (_, count) in enumerate(KINDS):

            def one(j, c):
                action(l, k, j)
                return c

            lax.fori_loop(0, count, one, 0)

    def token_copy(m):
        return pltpu.make_async_copy(tokens.at[pl.ds(m * SEQ, SEQ)], fwd_in.at[m], in_sem.at[0, m])

    def cotangent_copy(m):
        return pltpu.make_async_copy(cotangent.at[pl.ds(m * SEQ, SEQ)], bwd_in.at[m], in_sem.at[1, m])

    @pl.when(me == 0)
    def _():
        for m in range(micros):
            token_copy(m).start()

    for l in range(2):
        for k, (_, count) in enumerate(KINDS):
            for j in range(count):
                weight_copy(l, k, j).start()

    @pl.when(me == last)
    def _():
        for m in range(micros):
            cotangent_copy(m).start()

    def forward_copy(m):
        return pltpu.make_async_remote_copy(
            src_ref=fwd_out.at[m],
            dst_ref=fwd_in.at[m],
            send_sem=fwd_send.at[m],
            recv_sem=fwd_recv.at[m],
            device_id={"pipe": lax.rem(me + 1, sections)},
            device_id_type=MESH,
        )

    def backward_copy(m):
        return pltpu.make_async_remote_copy(
            src_ref=bwd_out.at[m],
            dst_ref=bwd_in.at[m],
            send_sem=bwd_send.at[m],
            recv_sem=bwd_recv.at[m],
            device_id={"pipe": lax.rem(me + sections - 1, sections)},
            device_id_type=MESH,
        )

    def piece_copy(stage, out, send, recv, m, j):
        return pltpu.make_async_remote_copy(
            src_ref=stage.at[m, j],
            dst_ref=out.at[pl.ds(m * SEQ, SEQ)],
            send_sem=send.at[m, j],
            recv_sem=recv.at[m],
            device_id={"pipe": j},
            device_id_type=MESH,
        )

    def own_piece(stage, out, send, m, j):
        return pltpu.make_async_copy(stage.at[m, j], out.at[pl.ds(m * SEQ, SEQ)], send.at[m, j])

    def spread(stage, out, send, recv, m, source):
        for j in range(sections):
            stage[m, j] = state[:, j * width : (j + 1) * width].astype(BF16)
            if j == source:
                own_piece(stage, out, send, m, j).start()
            else:
                piece_copy(stage, out, send, recv, m, j).start()

    outs = (u_out, dqkv_out, o_out, da_out, u2_out, dz_out, act_out, dm_out)

    def out_copy(kind, l, m):
        slot = l
        src = (
            u_s.at[l, m],
            qkv_s.at[l, m],
            o_s.at[slot],
            da_s.at[slot],
            u2_s.at[l, m],
            gp_s.at[l, m],
            act_s.at[slot],
            dm_s.at[slot],
        )[kind]
        return pltpu.make_async_copy(src, outs[kind].at[l, pl.ds(m * SEQ, SEQ)], out_sem.at[kind, l, m])

    def free_slot(kind, l, m):
        @pl.when(m > 0)
        def _():
            out_copy(kind, l, m - 1).wait()

    row = lax.broadcasted_iota(jnp.int32, (SEQ, SEQ), 0) // (SEQ // 4)
    column = lax.broadcasted_iota(jnp.int32, (SEQ, SEQ), 1) // (SEQ // 4)
    same = (row == column).astype(F32)
    for m in range(micros):
        parted = (jnp.full((1, SEQ), groups[m], jnp.int32) == 1).astype(F32)
        valid = jnp.broadcast_to((flags[m : m + 1, :] == 1).astype(F32), (SEQ, SEQ)).T
        keep = jnp.maximum(same, 1.0 - parted) * valid
        bias[m] = (keep - 1.0) * 1e30

    pl.semaphore_wait(barrier, sections - 1)

    def forward_layer(l, m):
        def weight_wait(k):
            @pl.when((m == 0) & (me < last))
            def _():
                for j in range(KINDS[k][1]):
                    weight_copy(l, k, j).wait()

        x = state[...]
        xhat, inverse = norm_parts(x)
        stat_s[l, m, :, 0:1] = inverse
        u = (xhat * gain_one[pl.ds(l, 1), :]).astype(BF16)
        u_s[l, m] = u
        out_copy(0, l, m).start()
        weight_wait(0)
        for j in range(3):
            qkv_s[l, m, :, j * D : (j + 1) * D] = nn(u_s[l, m], weights[l, block_rows(j)]).astype(BF16)
        free_slot(2, l, m)
        slot = l
        added = bias[m]
        scores, tiles = [], [None] * 6
        for tile, count, inside in WINDOWS:
            lo, hi = tile * 128, (tile + count) * 128
            keys = two_heads(qkv_s[l, m, :, D + lo : D + hi], inside)
            scores.append(nt(keys, qkv_s[l, m, :, lo:hi]) * (SCALE * LOG2E))
        for j in range(len(WINDOWS)):
            for h in range(2):
                s = scores[j][h * SEQ : (h + 1) * SEQ] + added
                e = jnp.exp2(s - jnp.max(s, axis=0, keepdims=True))
                p = e * (1.0 / jnp.sum(e, axis=0, keepdims=True))
                p_s[l, m, 2 * j + h] = p.astype(BF16)
        for j, (tile, count, inside) in enumerate(WINDOWS):
            lo, hi = tile * 128, (tile + count) * 128
            values = two_heads(qkv_s[l, m, :, 2 * D + lo : 2 * D + hi], inside)
            p = jnp.concatenate([p_s[l, m, 2 * j], p_s[l, m, 2 * j + 1]], axis=0)
            add_window(tiles, tile, tn(p, values))
        for i in range(6):
            o_s[slot, :, i * 128 : (i + 1) * 128] = tiles[i].astype(BF16)
        out_copy(2, l, m).start()
        weight_wait(1)
        h = state[...] + nn(o_s[slot], weights[l, block_rows(3)])
        state[...] = h
        hhat, inverse = norm_parts(h)
        stat_s[l, m, :, 1:2] = inverse
        u2_s[l, m] = (hhat * gain_two[pl.ds(l, 1), :]).astype(BF16)
        out_copy(4, l, m).start()
        weight_wait(2)
        free_slot(6, l, m)
        weight_wait(3)
        for j in range(4):
            act, slope = gelu_parts(nn(u2_s[l, m], weights[l, block_rows(4 + j)]))
            act_s[slot, :, j * D : (j + 1) * D] = act.astype(BF16)
            gp_s[l, m, :, j * D : (j + 1) * D] = slope.astype(BF16)
        state[...] = state[...] + nn(act_s[slot], weights[l, block_rows(8, 4)])
        out_copy(6, l, m).start()

    def norm_back(du, hat_scaled, gain, inverse):
        t = du * gain
        hat = hat_scaled * (1.0 / gain)
        weighted = du * hat_scaled
        return inverse * (
            t - jnp.mean(t, axis=-1, keepdims=True) - hat * jnp.mean(weighted, axis=-1, keepdims=True)
        ), weighted

    def add_rows(at, weighted):
        part = weighted[0:8]
        for r in range(8, SEQ, 8):
            part = part + weighted[r : r + 8]
        acc[at] = acc[at] + part

    def backward_layer(l, m):
        slot = l
        held = lax.select(me == last, 1 - l, l)

        def turned_wait(k):
            @pl.when((m == 0) & (me == last))
            def _():
                swap_copy(l, k).wait()

        dy = state[...]
        free_slot(7, l, m)
        turned_wait(3)
        turned_wait(2)
        dm_s[slot] = dy.astype(BF16)
        out_copy(7, l, m).start()
        for j in range(4):
            da = nn(dm_s[slot], weights[held, block_rows(8 + j)])
            dz = gp_s[l, m, :, j * D : (j + 1) * D].astype(F32) * da
            gp_s[l, m, :, j * D : (j + 1) * D] = dz.astype(BF16)
        out_copy(5, l, m).start()
        dh, weighted = norm_back(
            nn(gp_s[l, m], weights[held, block_rows(4, 4)]), u2_s[l, m].astype(F32), gain_two[pl.ds(l, 1), :], stat_s[l, m, :, 1:2]
        )
        add_rows(2 + l, weighted)
        dh = state[...] + dh
        state[...] = dh
        free_slot(3, l, m)
        da_s[slot] = dh.astype(BF16)
        out_copy(3, l, m).start()
        turned_wait(1)
        turned_wait(0)
        do = nn(da_s[slot], weights[held, block_rows(3)]).astype(BF16)
        slopes, products = [], []
        q_tiles, k_tiles, v_tiles = [None] * 6, [None] * 6, [None] * 6
        for tile, count, inside in WINDOWS:
            lo, hi = tile * 128, (tile + count) * 128
            values = two_heads(qkv_s[l, m, :, 2 * D + lo : 2 * D + hi], inside)
            products.append(nt(values, do[:, lo:hi]))
        for j in range(len(WINDOWS)):
            for h in range(2):
                p = p_s[l, m, 2 * j + h].astype(F32)
                dp = products[j][h * SEQ : (h + 1) * SEQ]
                slopes.append((p * (dp - jnp.sum(p * dp, axis=0, keepdims=True))).astype(BF16))
        for j, (tile, count, inside) in enumerate(WINDOWS):
            lo, hi = tile * 128, (tile + count) * 128
            pair = slopes[2 * j : 2 * j + 2]
            keys = two_heads(qkv_s[l, m, :, D + lo : D + hi], inside)
            query = two_heads(qkv_s[l, m, :, lo:hi], inside)
            add_window(q_tiles, tile, tn(jnp.concatenate(pair, axis=0), keys))
            add_window(k_tiles, tile, nn(jnp.concatenate(pair, axis=1), query))
        for j, (tile, count, inside) in enumerate(WINDOWS):
            given = two_heads(do[:, tile * 128 : (tile + count) * 128], inside)
            p = jnp.concatenate([p_s[l, m, 2 * j], p_s[l, m, 2 * j + 1]], axis=1)
            add_window(v_tiles, tile, nn(p, given))
        for i in range(6):
            at = i * 128
            qkv_s[l, m, :, at : at + 128] = (q_tiles[i] * SCALE).astype(BF16)
            qkv_s[l, m, :, D + at : D + at + 128] = (k_tiles[i] * SCALE).astype(BF16)
            qkv_s[l, m, :, 2 * D + at : 2 * D + at + 128] = v_tiles[i].astype(BF16)
        out_copy(1, l, m).start()
        du = nn(qkv_s[l, m], weights[held, block_rows(0, 3)])
        dx, weighted = norm_back(
            du, u_s[l, m].astype(F32), gain_one[pl.ds(l, 1), :], stat_s[l, m, :, 0:1]
        )
        add_rows(l, weighted)
        state[...] = state[...] + dx

    @pl.when(me == last)
    def _():
        def make(l, k, j):
            b = KINDS[k][0] + j
            weight_copy(l, k, j).wait()
            turn(l, b)
            turned_copy(l, b).start()

        def again(l, k, j):
            turned_copy(l, KINDS[k][0] + j).wait()
            weight_copy(l, k, j).start()

        def ready(l, k, j):
            weight_copy(l, k, j).wait()

        for action in (make, again, ready):

            def one(l, c):
                each_block(l, action)
                return c

            lax.fori_loop(0, 2, one, 0)

    def forward_micro(m, carry):
        @pl.when(me == 0)
        def _():
            token_copy(m).wait()

        @pl.when(me > 0)
        def _():
            forward_copy(m).wait_recv()

        state[...] = fwd_in[m].astype(F32)

        def one(l, c):
            forward_layer(l, m)

            @pl.when((m == micros - 1) & (me == last))
            def _():
                for k in (3, 2, 1, 0):
                    swap_copy(1 - l, k).start()

            return c

        lax.fori_loop(0, 2, one, 0)

        @pl.when(me < last)
        def _():
            fwd_out[m] = state[...].astype(BF16)
            forward_copy(m).start()

        @pl.when(me == last)
        def _():
            spread(fin_stage, fin_out, fin_send, fin_recv, m, last)

        return carry

    lax.fori_loop(0, micros, forward_micro, 0)

    @pl.when(me < last)
    def _():
        def one(i, c):
            turn(1 - i // BLOCKS, lax.rem(i, BLOCKS))
            return c

        lax.fori_loop(0, 2 * BLOCKS, one, 0)

    acc[...] = jnp.zeros_like(acc)

    def backward_micro(m, carry):
        @pl.when(me == last)
        def _():
            cotangent_copy(m).wait()

        @pl.when(me < last)
        def _():
            backward_copy(m).wait_recv()

        state[...] = bwd_in[m].astype(F32)

        def one(i, c):
            backward_layer(1 - i, m)
            return c

        lax.fori_loop(0, 2, one, 0)

        @pl.when(me > 0)
        def _():
            bwd_out[m] = state[...].astype(BF16)
            backward_copy(m).start()

        @pl.when(me == 0)
        def _():
            spread(inp_stage, inp_out, inp_send, inp_recv, m, 0)

        return carry

    lax.fori_loop(0, micros, backward_micro, 0)
    share = D // replicas
    for k in range(4):
        gain = (gain_one, gain_two)[k // 2][k % 2 : k % 2 + 1, :]
        total = jnp.sum(acc[k], axis=0, keepdims=True) / gain
        for r in range(replicas):
            gains_out[r, k : k + 1, 0:share] = total[:, r * share : (r + 1) * share]

    for l in range(2):
        for kind in (2, 3, 6, 7):
            out_copy(kind, l, micros - 1).wait()
        for m in range(micros):
            for kind in (0, 1, 4, 5):
                out_copy(kind, l, m).wait()
    for m in range(micros):

        @pl.when(me < last)
        def _():
            forward_copy(m).wait_send()

        @pl.when(me > 0)
        def _():
            backward_copy(m).wait_send()

        for source, stage, out, send, recv in (
            (last, fin_stage, fin_out, fin_send, fin_recv),
            (0, inp_stage, inp_out, inp_send, inp_recv),
        ):

            @pl.when(me == source)
            def _():
                for j in range(sections):
                    if j == source:
                        own_piece(stage, out, send, m, j).wait()
                    else:
                        piece_copy(stage, out, send, recv, m, j).wait_send()

            @pl.when(me != source)
            def _():
                piece_copy(stage, out, send, recv, m, source).wait_recv()


def relay(tokens, cotangent, flags, groups, gain_one, gain_two, wqkv, wout, wup, wdown):
    sections = lax.axis_size("pipe")
    replicas = lax.axis_size("dp")
    rows = tokens.shape[0]
    micros = rows // SEQ
    width = D // sections
    anywhere = pl.BlockSpec(memory_space=pl.ANY)
    vmem = pl.BlockSpec(memory_space=pltpu.VMEM)
    smem = pl.BlockSpec(memory_space=pltpu.SMEM)
    dma = pltpu.SemaphoreType.DMA

    def factor(columns):
        return jax.ShapeDtypeStruct((2, rows, columns), BF16)

    def saved(columns):
        return pltpu.VMEM((2, micros, SEQ, columns), BF16)

    def two(columns):
        return pltpu.VMEM((2, SEQ, columns), BF16)

    def per_micro(columns):
        return pltpu.VMEM((micros, SEQ, columns), BF16)

    return pl.pallas_call(
        functools.partial(relay_kernel, sections, replicas, micros),
        out_shape=(
            jax.ShapeDtypeStruct((rows, width), BF16),
            jax.ShapeDtypeStruct((rows, width), BF16),
            jax.ShapeDtypeStruct((replicas, 8, 128), F32),
            factor(D),
            factor(3 * D),
            factor(D),
            factor(D),
            factor(D),
            factor(FF),
            factor(FF),
            factor(D),
            jax.ShapeDtypeStruct((2, BLOCKS * D, D), BF16),
        ),
        in_specs=[anywhere, anywhere, vmem, smem, vmem, vmem] + [anywhere] * 4,
        out_specs=(anywhere, anywhere, vmem) + (anywhere,) * 9,
        scratch_shapes=[
            pltpu.VMEM((2, BLOCKS * D, D), BF16),
            per_micro(D),
            per_micro(D),
            per_micro(D),
            per_micro(D),
            pltpu.VMEM((micros, sections, SEQ, width), BF16),
            pltpu.VMEM((micros, sections, SEQ, width), BF16),
            saved(D),
            saved(3 * D),
            pltpu.VMEM((2, micros, HEADS, SEQ, SEQ), BF16),
            saved(D),
            saved(FF),
            pltpu.VMEM((2, micros, SEQ, 128), F32),
            two(D),
            two(FF),
            two(D),
            two(D),
            pltpu.VMEM((SEQ, D), F32),
            pltpu.VMEM((4, 8, D), F32),
            pltpu.VMEM((micros, SEQ, SEQ), F32),
            dma((2, BLOCKS)),
            dma((2, BLOCKS)),
            dma((2, len(KINDS))),
            dma((2, micros)),
            dma((micros,)),
            dma((micros,)),
            dma((micros,)),
            dma((micros,)),
            dma((micros, sections)),
            dma((micros,)),
            dma((micros, sections)),
            dma((micros,)),
            dma((8, 2, micros)),
        ],
        compiler_params=pltpu.CompilerParams(
            collective_id=0, has_side_effects=True, vmem_limit_bytes=60 * MIB
        ),
        name="relay",
    )(tokens, cotangent, flags, groups, gain_one, gain_two, wqkv, wout, wup, wdown)


SHARDS = 8
ROWS = 96
CHUNKS = 12


def sum_kernel(
    gains_in,
    u_in,
    dqkv_in,
    o_in,
    da_in,
    u2_in,
    dz_in,
    act_in,
    dm_in,
    gains_out,
    qkv_out,
    out_out,
    up_out,
    down_out,
    u_v,
    dqkv_v,
    o_v,
    da_v,
    u2_v,
    dz_v,
    act_v,
    dm_v,
    own,
    first,
    second,
    third,
    gains_v,
    load_sem,
    gain_send,
    gain_recv,
    send,
    recv,
    out_sem,
):
    me = lax.axis_index("dp")
    core = lax.rem(me, 2)
    x = lax.rem(me // 2, 2)
    y = me // 4
    other_core = me + 1 - 2 * core
    other_x = me + 2 - 4 * x
    other_y = me + 4 - 8 * y

    barrier = pltpu.get_barrier_semaphore()
    for j in range(SHARDS):

        @pl.when(me != j)
        def _():
            pl.semaphore_signal(barrier, inc=1, device_id={"dp": j}, device_id_type=MESH)

    sources = (u_in, dqkv_in, o_in, da_in, u2_in, dz_in, act_in, dm_in)
    held = (u_v, dqkv_v, o_v, da_v, u2_v, dz_v, act_v, dm_v)

    def load(k, l):
        return pltpu.make_async_copy(sources[k].at[l], held[k], load_sem.at[k])

    for k in range(8):
        load(k, 1).start()

    pl.semaphore_wait(barrier, SHARDS - 1)

    def gain_copy(j, source):
        return pltpu.make_async_remote_copy(
            src_ref=gains_in.at[j],
            dst_ref=gains_v.at[source],
            send_sem=gain_send.at[j],
            recv_sem=gain_recv.at[source],
            device_id={"dp": j},
            device_id_type=MESH,
        )

    for j in range(SHARDS):

        @pl.when(me != j)
        def _():
            gain_copy(j, me).start()

    def remote(src, dst, step, n, to):
        return pltpu.make_async_remote_copy(
            src_ref=src,
            dst_ref=dst,
            send_sem=send.at[step, n],
            recv_sem=recv.at[step, n],
            device_id={"dp": to},
            device_id_type=MESH,
        )

    def give_copy(n, i):
        return remote(own.at[i, 1 - core], first.at[n], 0, n, other_core)

    def first_copy(n, i):
        if i % 2 == 0:
            return remote(first.at[n, :, 1 - x], second.at[n], 1, n, other_x)
        return remote(first.at[n, 1 - y], second.at[n], 1, n, other_y)

    def second_copy(n, i):
        if i % 2 == 0:
            return remote(second.at[n, 1 - y], third.at[n], 2, n, other_y)
        return remote(second.at[n, 1 - x], third.at[n], 2, n, other_x)

    def result_copy(n, l, i):
        if i < 3:
            dst = qkv_out.at[l, :, pl.ds(i * CHUNK, CHUNK)]
        elif i < 4:
            dst = out_out.at[l]
        elif i < 8:
            dst = up_out.at[l, :, pl.ds((i - 4) * CHUNK, CHUNK)]
        else:
            dst = down_out.at[l, pl.ds((i - 8) * ROWS, ROWS)]
        return pltpu.make_async_copy(third.at[n], dst, out_sem.at[n])

    def add_core(n, i):
        give_copy(n, i).wait_recv()
        first[n] = first[n] + own[i, core]
        first_copy(n, i).start()

    def layer_products(step, carry):
        l = 1 - step
        base = step * CHUNKS

        def free(i):
            @pl.when(step > 0)
            def _():
                give_copy(i, i).wait_send()

        def products(k, a, g, slots):
            load(k, l).wait()
            load(k + 1, l).wait()
            for i, columns in slots:
                free(i)
                part = tn(a[...], g[:, columns * CHUNK : (columns + 1) * CHUNK]).astype(BF16)
                for r in range(SHARDS):
                    own[i, r % 2, r // 4, (r // 2) % 2] = part[r * ROWS : (r + 1) * ROWS]
                give_copy(base + i, i).start()
                if i > 0:
                    add_core(base + i - 1, i - 1)

        def reload(k):
            @pl.when(step == 0)
            def _():
                load(k, 0).start()
                load(k + 1, 0).start()

        products(0, u_v, dqkv_v, ((0, 0), (1, 1), (2, 2)))
        reload(0)
        products(2, o_v, da_v, ((3, 0),))
        reload(2)
        products(4, u2_v, dz_v, ((4, 0), (5, 1), (6, 2), (7, 3)))
        reload(4)
        load(6, l).wait()
        load(7, l).wait()
        for i in range(8, CHUNKS):
            free(i)
        for b in range(4):
            part = tn(act_v[:, b * CHUNK : (b + 1) * CHUNK], dm_v[...]).astype(BF16)
            for r in range(8):
                own[8 + r % 4, r // 4, b // 2, b % 2] = part[r * ROWS : (r + 1) * ROWS]
        reload(6)
        for i in range(8, CHUNKS):
            give_copy(base + i, i).start()
        for i in range(7, CHUNKS):
            add_core(base + i, i)
        return carry

    lax.fori_loop(0, 2, layer_products, 0)

    def second_sums(step, carry):
        for i in range(CHUNKS):
            n = step * CHUNKS + i
            first_copy(n, i).wait_recv()
            kept = first[n, :, x] if i % 2 == 0 else first[n, y]
            second[n] = second[n] + kept
            second_copy(n, i).start()
        return carry

    lax.fori_loop(0, 2, second_sums, 0)

    gains_v[me] = gains_in[me]
    for j in range(SHARDS):

        @pl.when(me != j)
        def _():
            gain_copy(j, j).wait_recv()

    total = gains_v[0]
    for j in range(1, SHARDS):
        total = total + gains_v[j]
    gains_out[...] = total

    def last_sums(step, carry):
        for i in range(CHUNKS):
            n = step * CHUNKS + i
            second_copy(n, i).wait_recv()
            third[n] = third[n] + second[n, y if i % 2 == 0 else x]
            result_copy(n, 1 - step, i).start()
        return carry

    lax.fori_loop(0, 2, last_sums, 0)

    def finish(step, carry):
        for i in range(CHUNKS):
            n = step * CHUNKS + i
            first_copy(n, i).wait_send()
            second_copy(n, i).wait_send()
            result_copy(n, 1 - step, i).wait()
        return carry

    lax.fori_loop(0, 2, finish, 0)
    for i in range(CHUNKS):
        give_copy(CHUNKS + i, i).wait_send()
    for j in range(SHARDS):

        @pl.when(me != j)
        def _():
            gain_copy(j, me).wait_send()


def summed(gains, *factors):
    rows = factors[0].shape[1]
    anywhere = pl.BlockSpec(memory_space=pl.ANY)
    vmem = pl.BlockSpec(memory_space=pltpu.VMEM)
    dma = pltpu.SemaphoreType.DMA
    total = 2 * CHUNKS

    def shard(height, columns):
        return jax.ShapeDtypeStruct((2, height, columns), BF16)

    return pl.pallas_call(
        sum_kernel,
        out_shape=(
            jax.ShapeDtypeStruct((8, 128), F32),
            shard(ROWS, 3 * D),
            shard(ROWS, D),
            shard(ROWS, FF),
            shard(4 * ROWS, D),
        ),
        in_specs=[vmem] + [anywhere] * 8,
        out_specs=(vmem,) + (anywhere,) * 4,
        scratch_shapes=[pltpu.VMEM((rows, f.shape[2]), BF16) for f in factors]
        + [
            pltpu.VMEM((CHUNKS, 2, 2, 2, ROWS, CHUNK), BF16),
            pltpu.VMEM((total, 2, 2, ROWS, CHUNK), BF16),
            pltpu.VMEM((total, 2, ROWS, CHUNK), BF16),
            pltpu.VMEM((total, ROWS, CHUNK), BF16),
            pltpu.VMEM((SHARDS, 8, 128), F32),
            dma((8,)),
            dma((SHARDS,)),
            dma((SHARDS,)),
            dma((3, total)),
            dma((3, total)),
            dma((total,)),
        ],
        compiler_params=pltpu.CompilerParams(
            collective_id=1, has_side_effects=True, vmem_limit_bytes=60 * MIB
        ),
        name="sum",
    )(gains, *factors)


def body(
    tokens,
    gain_one,
    qkv_weight,
    out_weight,
    gain_two,
    up_weight,
    down_weight,
    cotangent,
    flags,
    groups,
):
    micros = tokens.shape[0] // SEQ
    fin, inp, gains, u, dqkv, o, da, u2, dz, act, dm, _ = relay(
        tokens,
        cotangent,
        flags.reshape(micros, SEQ),
        groups,
        gain_one,
        gain_two,
        qkv_weight,
        out_weight,
        up_weight,
        down_weight,
    )

    replicas = lax.axis_size("dp")
    share = D // replicas
    if replicas == SHARDS and share == ROWS:
        gains, g_qkv, g_out, g_up, g_down = summed(gains, u, dqkv, o, da, u2, dz, act, dm)
        gains = gains[0:4, 0:share]
    else:

        def grad(a, g):
            total = jnp.einsum("lsa,lsb->lab", a, g, preferred_element_type=F32).astype(BF16)
            return lax.psum_scatter(total, "dp", scatter_dimension=1, tiled=True)

        gains = lax.psum_scatter(gains[:, 0:4, 0:share], "dp", scatter_dimension=0)
        g_qkv, g_out, g_up, g_down = grad(u, dqkv), grad(o, da), grad(u2, dz), grad(act, dm)
    return (
        fin,
        inp.astype(F32),
        gains[0:2],
        g_qkv.astype(F32),
        g_out.astype(F32),
        gains[2:4],
        g_up.astype(F32),
        g_down.astype(F32),
    )


def solution(mesh):
    return jax.shard_map(
        body,
        mesh=mesh,
        in_specs=(
            P("dp", None),
            P("pipe", None),
            P("pipe", None, None),
            P("pipe", None, None),
            P("pipe", None),
            P("pipe", None, None),
            P("pipe", None, None),
            P("dp", None),
            P("dp"),
            P("dp"),
        ),
        out_specs=(
            P("dp", "pipe"),
            P("dp", "pipe"),
            P("pipe", "dp"),
            P("pipe", "dp", None),
            P("pipe", "dp", None),
            P("pipe", "dp"),
            P("pipe", "dp", None),
            P("pipe", "dp", None),
        ),
        check_vma=False,
    )
```

```python
import functools

import jax
import jax.numpy as jnp
from jax import lax
from jax.experimental import pallas as pl
from jax.experimental.pallas import tpu as pltpu
from jax.sharding import PartitionSpec as P

D = 768
HEADS = 16
HEAD_DIM = 48
FF = 3072
SEQ = 128
EPS = 1e-06
MESH = pl.DeviceIdType.MESH
F32 = jnp.float32
BF16 = jnp.bfloat16
LOG2E = 1.4426950408889634
SCALE = HEAD_DIM ** (-0.5)
MIB = 2**20
CHUNK = 768
TILE = 256

KINDS = ((0, 3), (3, 1), (4, 4), (8, 4))
BLOCKS = 12

WINDOWS = tuple(
    (96 * j // 128, -(-(96 * j % 128 + 96) // 128), 96 * j % 128) for j in range(HEADS // 2)
)


def nn(a, b):
    return jnp.dot(a, b, preferred_element_type=F32)


def nt(a, b):
    return lax.dot_general(a, b, (((1,), (1,)), ((), ())), preferred_element_type=F32)


def tn(a, b):
    return lax.dot_general(a, b, (((0,), (0,)), ((), ())), preferred_element_type=F32)


def lanes_of_head(first, width):
    lane = lax.broadcasted_iota(jnp.int32, (SEQ, width), 1)
    return ((lane >= first) & (lane < first + HEAD_DIM)).astype(F32).astype(BF16)


def two_heads(window, first):
    width = window.shape[1]
    return jnp.concatenate(
        [window * lanes_of_head(first, width), window * lanes_of_head(first + HEAD_DIM, width)], axis=0
    )


def add_window(tiles, first, part):
    for i in range(part.shape[1] // 128):
        piece = part[:, i * 128 : (i + 1) * 128]
        tiles[first + i] = piece if tiles[first + i] is None else tiles[first + i] + piece


def norm_parts(x):
    centre = x - jnp.mean(x, axis=-1, keepdims=True)
    spread = jnp.mean(centre * centre, axis=-1, keepdims=True)
    inverse = lax.rsqrt(spread + EPS)
    return centre * inverse, inverse


def gelu_parts(z):
    phi = 0.5 * (1.0 + lax.erf(z * 0.7071067811865476))
    density = jnp.exp2(z * z * (-0.5 * LOG2E)) * 0.3989422804014327
    return z * phi, phi + z * density


def relay_kernel(
    sections,
    replicas,
    micros,
    tokens,
    cotangent,
    flags,
    groups,
    gain_one,
    gain_two,
    wqkv_hbm,
    wout_hbm,
    wup_hbm,
    wdown_hbm,
    fin_out,
    inp_out,
    gains_out,
    u_out,
    dqkv_out,
    o_out,
    da_out,
    u2_out,
    dz_out,
    act_out,
    dm_out,
    turned_hbm,
    weights,
    fwd_in,
    fwd_out,
    bwd_in,
    bwd_out,
    fin_stage,
    inp_stage,
    u_s,
    qkv_s,
    p_s,
    u2_s,
    gp_s,
    stat_s,
    o_s,
    act_s,
    dm_s,
    da_s,
    state,
    acc,
    bias,
    w_sem,
    turn_sem,
    swap_sem,
    in_sem,
    fwd_send,
    fwd_recv,
    bwd_send,
    bwd_recv,
    fin_send,
    fin_recv,
    inp_send,
    out_sem,
):
    me = lax.axis_index("pipe")
    last = sections - 1
    width = D // sections

    barrier = pltpu.get_barrier_semaphore()
    for j in range(sections):

        @pl.when(me != j)
        def _():
            pl.semaphore_signal(barrier, inc=1, device_id={"pipe": j}, device_id_type=MESH)

    def block_rows(b, count=1):
        start = b * D
        return pl.ds(start if isinstance(b, int) else pl.multiple_of(start, D), count * D)

    def weight_copy(l, k, j):
        first, _ = KINDS[k]
        if k == 1:
            src = wout_hbm.at[l]
        elif k == 3:
            src = wdown_hbm.at[l, block_rows(j)]
        else:
            src = (wqkv_hbm, None, wup_hbm)[k].at[l, :, block_rows(j)]
        return pltpu.make_async_copy(src, weights.at[l, block_rows(first + j)], w_sem.at[l, first + j])

    def turned_copy(l, b):
        return pltpu.make_async_copy(
            weights.at[l, block_rows(b)], turned_hbm.at[l, block_rows(b)], turn_sem.at[l, b]
        )

    def swap_copy(l, k):
        rows = block_rows(*KINDS[k])
        return pltpu.make_async_copy(turned_hbm.at[l, rows], weights.at[1 - l, rows], swap_sem.at[l, k])

    def turn(l, b):
        def tile(r, c):
            return l, pl.ds(pl.multiple_of(b * D + r * TILE, TILE), TILE), pl.ds(c * TILE, TILE)

        for r in range(D // TILE):
            weights[tile(r, r)] = weights[tile(r, r)].T
            for c in range(r):
                lower = weights[tile(r, c)].T
                upper = weights[tile(c, r)].T
                weights[tile(c, r)] = lower
                weights[tile(r, c)] = upper

    def each_block(l, action):
        for k, (_, count) in enumerate(KINDS):

            def one(j, c):
                action(l, k, j)
                return c

            lax.fori_loop(0, count, one, 0)

    def token_copy(m):
        return pltpu.make_async_copy(tokens.at[pl.ds(m * SEQ, SEQ)], fwd_in.at[m], in_sem.at[0, m])

    def cotangent_copy(m):
        return pltpu.make_async_copy(cotangent.at[pl.ds(m * SEQ, SEQ)], bwd_in.at[m], in_sem.at[1, m])

    @pl.when(me == 0)
    def _():
        for m in range(micros):
            token_copy(m).start()

    for l in range(2):
        for k, (_, count) in enumerate(KINDS):
            for j in range(count):
                weight_copy(l, k, j).start()

    @pl.when(me == last)
    def _():
        for m in range(micros):
            cotangent_copy(m).start()

    def forward_copy(m):
        return pltpu.make_async_remote_copy(
            src_ref=fwd_out.at[m],
            dst_ref=fwd_in.at[m],
            send_sem=fwd_send.at[m],
            recv_sem=fwd_recv.at[m],
            device_id={"pipe": lax.rem(me + 1, sections)},
            device_id_type=MESH,
        )

    def backward_copy(m):
        return pltpu.make_async_remote_copy(
            src_ref=bwd_out.at[m],
            dst_ref=bwd_in.at[m],
            send_sem=bwd_send.at[m],
            recv_sem=bwd_recv.at[m],
            device_id={"pipe": lax.rem(me + sections - 1, sections)},
            device_id_type=MESH,
        )

    def slots_of(m):
        return pl.ds(pl.multiple_of(m * SEQ, SEQ), SEQ)

    def fin_copy(m, j):
        return pltpu.make_async_remote_copy(
            src_ref=fin_stage.at[m, j],
            dst_ref=fin_out.at[:, slots_of(m)],
            send_sem=fin_send.at[m, j],
            recv_sem=fin_recv.at[m],
            device_id={"pipe": j},
            device_id_type=MESH,
        )

    def own_fin_copy(m):
        return pltpu.make_async_copy(fin_stage.at[m, last], fin_out.at[:, slots_of(m)], fin_send.at[m, last])

    def inp_copy(m, j):
        return pltpu.make_async_copy(inp_stage.at[m, j], inp_out.at[j, :, slots_of(m)], inp_send.at[m, j])

    def piece(j):
        return state[:, j * width : (j + 1) * width].T.astype(BF16)

    outs = (u_out, dqkv_out, o_out, da_out, u2_out, dz_out, act_out, dm_out)

    def out_copy(kind, l, m):
        slot = l
        src = (
            u_s.at[l, m],
            qkv_s.at[l, m],
            o_s.at[slot],
            da_s.at[slot],
            u2_s.at[l, m],
            gp_s.at[l, m],
            act_s.at[slot],
            dm_s.at[slot],
        )[kind]
        return pltpu.make_async_copy(src, outs[kind].at[l, pl.ds(m * SEQ, SEQ)], out_sem.at[kind, l, m])

    def free_slot(kind, l, m):
        @pl.when(m > 0)
        def _():
            out_copy(kind, l, m - 1).wait()

    row = lax.broadcasted_iota(jnp.int32, (SEQ, SEQ), 0) // (SEQ // 4)
    column = lax.broadcasted_iota(jnp.int32, (SEQ, SEQ), 1) // (SEQ // 4)
    same = (row == column).astype(F32)
    for m in range(micros):
        parted = (jnp.full((1, SEQ), groups[m], jnp.int32) == 1).astype(F32)
        valid = jnp.broadcast_to((flags[m : m + 1, :] == 1).astype(F32), (SEQ, SEQ)).T
        keep = jnp.maximum(same, 1.0 - parted) * valid
        bias[m] = (keep - 1.0) * 1e30

    pl.semaphore_wait(barrier, sections - 1)

    def forward_layer(l, m):
        def weight_wait(k):
            @pl.when((m == 0) & (me < last))
            def _():
                for j in range(KINDS[k][1]):
                    weight_copy(l, k, j).wait()

        x = state[...]
        xhat, inverse = norm_parts(x)
        stat_s[l, m, :, 0:1] = inverse
        u = (xhat * gain_one[pl.ds(l, 1), :]).astype(BF16)
        u_s[l, m] = u
        out_copy(0, l, m).start()
        weight_wait(0)
        for j in range(3):
            qkv_s[l, m, :, j * D : (j + 1) * D] = nn(u_s[l, m], weights[l, block_rows(j)]).astype(BF16)
        free_slot(2, l, m)
        slot = l
        added = bias[m]
        scores, tiles = [], [None] * 6
        for tile, count, inside in WINDOWS:
            lo, hi = tile * 128, (tile + count) * 128
            keys = two_heads(qkv_s[l, m, :, D + lo : D + hi], inside)
            scores.append(nt(keys, qkv_s[l, m, :, lo:hi]) * (SCALE * LOG2E))
        for j in range(len(WINDOWS)):
            for h in range(2):
                s = scores[j][h * SEQ : (h + 1) * SEQ] + added
                e = jnp.exp2(s - jnp.max(s, axis=0, keepdims=True))
                p = e * (1.0 / jnp.sum(e, axis=0, keepdims=True))
                p_s[l, m, 2 * j + h] = p.astype(BF16)
        for j, (tile, count, inside) in enumerate(WINDOWS):
            lo, hi = tile * 128, (tile + count) * 128
            values = two_heads(qkv_s[l, m, :, 2 * D + lo : 2 * D + hi], inside)
            p = jnp.concatenate([p_s[l, m, 2 * j], p_s[l, m, 2 * j + 1]], axis=0)
            add_window(tiles, tile, tn(p, values))
        for i in range(6):
            o_s[slot, :, i * 128 : (i + 1) * 128] = tiles[i].astype(BF16)
        out_copy(2, l, m).start()
        weight_wait(1)
        h = state[...] + nn(o_s[slot], weights[l, block_rows(3)])
        state[...] = h
        hhat, inverse = norm_parts(h)
        stat_s[l, m, :, 1:2] = inverse
        u2_s[l, m] = (hhat * gain_two[pl.ds(l, 1), :]).astype(BF16)
        out_copy(4, l, m).start()
        weight_wait(2)
        free_slot(6, l, m)
        weight_wait(3)
        for j in range(4):
            act, slope = gelu_parts(nn(u2_s[l, m], weights[l, block_rows(4 + j)]))
            act_s[slot, :, j * D : (j + 1) * D] = act.astype(BF16)
            gp_s[l, m, :, j * D : (j + 1) * D] = slope.astype(BF16)
        state[...] = state[...] + nn(act_s[slot], weights[l, block_rows(8, 4)])
        out_copy(6, l, m).start()

    def norm_back(du, hat_scaled, gain, inverse):
        t = du * gain
        hat = hat_scaled * (1.0 / gain)
        weighted = du * hat_scaled
        return inverse * (
            t - jnp.mean(t, axis=-1, keepdims=True) - hat * jnp.mean(weighted, axis=-1, keepdims=True)
        ), weighted

    def add_rows(at, weighted):
        part = weighted[0:8]
        for r in range(8, SEQ, 8):
            part = part + weighted[r : r + 8]
        acc[at] = acc[at] + part

    def backward_layer(l, m):
        slot = l
        held = lax.select(me == last, 1 - l, l)

        def turned_wait(k):
            @pl.when((m == 0) & (me == last))
            def _():
                swap_copy(l, k).wait()

        dy = state[...]
        free_slot(7, l, m)
        turned_wait(3)
        turned_wait(2)
        dm_s[slot] = dy.astype(BF16)
        out_copy(7, l, m).start()
        for j in range(4):
            da = nn(dm_s[slot], weights[held, block_rows(8 + j)])
            dz = gp_s[l, m, :, j * D : (j + 1) * D].astype(F32) * da
            gp_s[l, m, :, j * D : (j + 1) * D] = dz.astype(BF16)
        out_copy(5, l, m).start()
        dh, weighted = norm_back(
            nn(gp_s[l, m], weights[held, block_rows(4, 4)]), u2_s[l, m].astype(F32), gain_two[pl.ds(l, 1), :], stat_s[l, m, :, 1:2]
        )
        add_rows(2 + l, weighted)
        dh = state[...] + dh
        state[...] = dh
        free_slot(3, l, m)
        da_s[slot] = dh.astype(BF16)
        out_copy(3, l, m).start()
        turned_wait(1)
        turned_wait(0)
        do = nn(da_s[slot], weights[held, block_rows(3)]).astype(BF16)
        slopes, products = [], []
        q_tiles, k_tiles, v_tiles = [None] * 6, [None] * 6, [None] * 6
        for tile, count, inside in WINDOWS:
            lo, hi = tile * 128, (tile + count) * 128
            values = two_heads(qkv_s[l, m, :, 2 * D + lo : 2 * D + hi], inside)
            products.append(nt(values, do[:, lo:hi]))
        for j in range(len(WINDOWS)):
            for h in range(2):
                p = p_s[l, m, 2 * j + h].astype(F32)
                dp = products[j][h * SEQ : (h + 1) * SEQ]
                slopes.append((p * (dp - jnp.sum(p * dp, axis=0, keepdims=True))).astype(BF16))
        for j, (tile, count, inside) in enumerate(WINDOWS):
            lo, hi = tile * 128, (tile + count) * 128
            pair = slopes[2 * j : 2 * j + 2]
            keys = two_heads(qkv_s[l, m, :, D + lo : D + hi], inside)
            query = two_heads(qkv_s[l, m, :, lo:hi], inside)
            add_window(q_tiles, tile, tn(jnp.concatenate(pair, axis=0), keys))
            add_window(k_tiles, tile, nn(jnp.concatenate(pair, axis=1), query))
        for j, (tile, count, inside) in enumerate(WINDOWS):
            given = two_heads(do[:, tile * 128 : (tile + count) * 128], inside)
            p = jnp.concatenate([p_s[l, m, 2 * j], p_s[l, m, 2 * j + 1]], axis=1)
            add_window(v_tiles, tile, nn(p, given))
        for i in range(6):
            at = i * 128
            qkv_s[l, m, :, at : at + 128] = (q_tiles[i] * SCALE).astype(BF16)
            qkv_s[l, m, :, D + at : D + at + 128] = (k_tiles[i] * SCALE).astype(BF16)
            qkv_s[l, m, :, 2 * D + at : 2 * D + at + 128] = v_tiles[i].astype(BF16)
        out_copy(1, l, m).start()
        du = nn(qkv_s[l, m], weights[held, block_rows(0, 3)])
        dx, weighted = norm_back(
            du, u_s[l, m].astype(F32), gain_one[pl.ds(l, 1), :], stat_s[l, m, :, 0:1]
        )
        add_rows(l, weighted)
        state[...] = state[...] + dx

    @pl.when(me == last)
    def _():
        def make(l, k, j):
            b = KINDS[k][0] + j
            weight_copy(l, k, j).wait()
            turn(l, b)
            turned_copy(l, b).start()

        def again(l, k, j):
            turned_copy(l, KINDS[k][0] + j).wait()
            weight_copy(l, k, j).start()

        def ready(l, k, j):
            weight_copy(l, k, j).wait()

        for action in (make, again, ready):

            def one(l, c):
                each_block(l, action)
                return c

            lax.fori_loop(0, 2, one, 0)

    def forward_micro(m, carry):
        @pl.when(me == 0)
        def _():
            token_copy(m).wait()

        @pl.when(me > 0)
        def _():
            forward_copy(m).wait_recv()

        state[...] = fwd_in[m].astype(F32)

        def one(l, c):
            forward_layer(l, m)

            @pl.when((m == micros - 1) & (me == last))
            def _():
                for k in (3, 2, 1, 0):
                    swap_copy(1 - l, k).start()

            return c

        lax.fori_loop(0, 2, one, 0)

        @pl.when(me < last)
        def _():
            fwd_out[m] = state[...].astype(BF16)
            forward_copy(m).start()

        @pl.when(me == last)
        def _():
            for j in range(sections):
                fin_stage[m, j] = piece(j)
                if j == last:
                    own_fin_copy(m).start()
                else:
                    fin_copy(m, j).start()

        return carry

    lax.fori_loop(0, micros, forward_micro, 0)

    @pl.when(me < last)
    def _():
        def one(i, c):
            turn(1 - i // BLOCKS, lax.rem(i, BLOCKS))
            return c

        lax.fori_loop(0, 2 * BLOCKS, one, 0)

    acc[...] = jnp.zeros_like(acc)

    def backward_micro(m, carry):
        @pl.when(me == last)
        def _():
            cotangent_copy(m).wait()

        @pl.when(me < last)
        def _():
            backward_copy(m).wait_recv()

        state[...] = bwd_in[m].astype(F32)

        def one(i, c):
            backward_layer(1 - i, m)
            return c

        lax.fori_loop(0, 2, one, 0)

        @pl.when(me > 0)
        def _():
            bwd_out[m] = state[...].astype(BF16)
            backward_copy(m).start()

        @pl.when(me == 0)
        def _():
            for j in range(sections):
                inp_stage[m, j] = piece(j)
                inp_copy(m, j).start()

        return carry

    lax.fori_loop(0, micros, backward_micro, 0)
    share = D // replicas
    for k in range(4):
        gain = (gain_one, gain_two)[k // 2][k % 2 : k % 2 + 1, :]
        total = jnp.sum(acc[k], axis=0, keepdims=True) / gain
        for r in range(replicas):
            gains_out[r, k : k + 1, 0:share] = total[:, r * share : (r + 1) * share]

    for l in range(2):
        for kind in (2, 3, 6, 7):
            out_copy(kind, l, micros - 1).wait()
        for m in range(micros):
            for kind in (0, 1, 4, 5):
                out_copy(kind, l, m).wait()
    for m in range(micros):

        @pl.when(me < last)
        def _():
            forward_copy(m).wait_send()

        @pl.when(me > 0)
        def _():
            backward_copy(m).wait_send()

        @pl.when(me == last)
        def _():
            for j in range(last):
                fin_copy(m, j).wait_send()
            own_fin_copy(m).wait()

        @pl.when(me < last)
        def _():
            fin_copy(m, last).wait_recv()

        @pl.when(me == 0)
        def _():
            for j in range(sections):
                inp_copy(m, j).wait()


def relay(tokens, cotangent, flags, groups, gain_one, gain_two, wqkv, wout, wup, wdown):
    sections = lax.axis_size("pipe")
    replicas = lax.axis_size("dp")
    rows = tokens.shape[0]
    micros = rows // SEQ
    width = D // sections
    anywhere = pl.BlockSpec(memory_space=pl.ANY)
    vmem = pl.BlockSpec(memory_space=pltpu.VMEM)
    smem = pl.BlockSpec(memory_space=pltpu.SMEM)
    dma = pltpu.SemaphoreType.DMA

    def factor(columns):
        return jax.ShapeDtypeStruct((2, rows, columns), BF16)

    def saved(columns):
        return pltpu.VMEM((2, micros, SEQ, columns), BF16)

    def two(columns):
        return pltpu.VMEM((2, SEQ, columns), BF16)

    def per_micro(columns):
        return pltpu.VMEM((micros, SEQ, columns), BF16)

    return pl.pallas_call(
        functools.partial(relay_kernel, sections, replicas, micros),
        out_shape=(
            jax.ShapeDtypeStruct((width, rows), BF16),
            jax.ShapeDtypeStruct((sections, width, rows), BF16),
            jax.ShapeDtypeStruct((replicas, 8, 128), F32),
            factor(D),
            factor(3 * D),
            factor(D),
            factor(D),
            factor(D),
            factor(FF),
            factor(FF),
            factor(D),
            jax.ShapeDtypeStruct((2, BLOCKS * D, D), BF16),
        ),
        in_specs=[anywhere, anywhere, vmem, smem, vmem, vmem] + [anywhere] * 4,
        out_specs=(anywhere, anywhere, vmem) + (anywhere,) * 9,
        scratch_shapes=[
            pltpu.VMEM((2, BLOCKS * D, D), BF16),
            per_micro(D),
            per_micro(D),
            per_micro(D),
            per_micro(D),
            pltpu.VMEM((micros, sections, width, SEQ), BF16),
            pltpu.VMEM((micros, sections, width, SEQ), BF16),
            saved(D),
            saved(3 * D),
            pltpu.VMEM((2, micros, HEADS, SEQ, SEQ), BF16),
            saved(D),
            saved(FF),
            pltpu.VMEM((2, micros, SEQ, 128), F32),
            two(D),
            two(FF),
            two(D),
            two(D),
            pltpu.VMEM((SEQ, D), F32),
            pltpu.VMEM((4, 8, D), F32),
            pltpu.VMEM((micros, SEQ, SEQ), F32),
            dma((2, BLOCKS)),
            dma((2, BLOCKS)),
            dma((2, len(KINDS))),
            dma((2, micros)),
            dma((micros,)),
            dma((micros,)),
            dma((micros,)),
            dma((micros,)),
            dma((micros, sections)),
            dma((micros,)),
            dma((micros, sections)),
            dma((8, 2, micros)),
        ],
        compiler_params=pltpu.CompilerParams(
            collective_id=0, has_side_effects=True, vmem_limit_bytes=60 * MIB
        ),
        name="relay",
    )(tokens, cotangent, flags, groups, gain_one, gain_two, wqkv, wout, wup, wdown)


SHARDS = 8
ROWS = 96
CHUNKS = 12


def sum_kernel(
    sections,
    gains_in,
    inp_in,
    u_in,
    dqkv_in,
    o_in,
    da_in,
    u2_in,
    dz_in,
    act_in,
    dm_in,
    gains_out,
    inp_out,
    qkv_out,
    out_out,
    up_out,
    down_out,
    u_v,
    dqkv_v,
    o_v,
    da_v,
    u2_v,
    dz_v,
    act_v,
    dm_v,
    own,
    first,
    second,
    third,
    gains_v,
    load_sem,
    gain_send,
    gain_recv,
    inp_send,
    inp_recv,
    send,
    recv,
    out_sem,
):
    me = lax.axis_index("dp")
    section = lax.axis_index("pipe")
    core = lax.rem(me, 2)
    x = lax.rem(me // 2, 2)
    y = me // 4
    other_core = me + 1 - 2 * core
    other_x = me + 2 - 4 * x
    other_y = me + 4 - 8 * y

    barrier = pltpu.get_barrier_semaphore()
    for j in range(SHARDS):

        @pl.when(me != j)
        def _():
            pl.semaphore_signal(barrier, inc=1, device_id={"dp": j}, device_id_type=MESH)

    @pl.when(section > 0)
    def _():
        pl.semaphore_signal(barrier, inc=1, device_id={"pipe": 0}, device_id_type=MESH)

    sources = (u_in, dqkv_in, o_in, da_in, u2_in, dz_in, act_in, dm_in)
    held = (u_v, dqkv_v, o_v, da_v, u2_v, dz_v, act_v, dm_v)

    def load(k, l):
        return pltpu.make_async_copy(sources[k].at[l], held[k], load_sem.at[k])

    for k in range(8):
        load(k, 1).start()

    def gain_copy(j, source):
        return pltpu.make_async_remote_copy(
            src_ref=gains_in.at[j],
            dst_ref=gains_v.at[source],
            send_sem=gain_send.at[j],
            recv_sem=gain_recv.at[source],
            device_id={"dp": j},
            device_id_type=MESH,
        )

    def inp_copy(j):
        return pltpu.make_async_remote_copy(
            src_ref=inp_in.at[j],
            dst_ref=inp_out,
            send_sem=inp_send.at[j],
            recv_sem=inp_recv,
            device_id={"pipe": j},
            device_id_type=MESH,
        )

    def own_inp_copy():
        return pltpu.make_async_copy(inp_in.at[0], inp_out, inp_send.at[0])

    def meet():
        pl.semaphore_wait(barrier, SHARDS - 1 + lax.select(section == 0, sections - 1, 0))
        for j in range(SHARDS):

            @pl.when(me != j)
            def _():
                gain_copy(j, me).start()

        @pl.when(section == 0)
        def _():
            own_inp_copy().start()
            for j in range(1, sections):
                inp_copy(j).start()

    def remote(src, dst, step, n, to):
        return pltpu.make_async_remote_copy(
            src_ref=src,
            dst_ref=dst,
            send_sem=send.at[step, n],
            recv_sem=recv.at[step, n],
            device_id={"dp": to},
            device_id_type=MESH,
        )

    def give_copy(n, i):
        return remote(own.at[i, 1 - core], first.at[n], 0, n, other_core)

    def first_copy(n, i):
        if i % 2 == 0:
            return remote(first.at[n, :, 1 - x], second.at[n], 1, n, other_x)
        return remote(first.at[n, 1 - y], second.at[n], 1, n, other_y)

    def second_copy(n, i):
        if i % 2 == 0:
            return remote(second.at[n, 1 - y], third.at[n], 2, n, other_y)
        return remote(second.at[n, 1 - x], third.at[n], 2, n, other_x)

    def result_copy(n, l, i):
        if i < 3:
            dst = qkv_out.at[l, :, pl.ds(i * CHUNK, CHUNK)]
        elif i < 4:
            dst = out_out.at[l]
        elif i < 8:
            dst = up_out.at[l, :, pl.ds((i - 4) * CHUNK, CHUNK)]
        else:
            dst = down_out.at[l, pl.ds((i - 8) * ROWS, ROWS)]
        return pltpu.make_async_copy(third.at[n], dst, out_sem.at[n])

    def add_core(n, i):
        give_copy(n, i).wait_recv()
        first[n] = first[n] + own[i, core]
        first_copy(n, i).start()

    def layer_products(step, carry):
        l = 1 - step
        base = step * CHUNKS

        def free(i):
            @pl.when(step > 0)
            def _():
                give_copy(i, i).wait_send()

        def products(k, a, g, slots):
            load(k, l).wait()
            load(k + 1, l).wait()
            for i, columns in slots:
                free(i)
                part = tn(a[...], g[:, columns * CHUNK : (columns + 1) * CHUNK]).astype(BF16)
                for r in range(SHARDS):
                    own[i, r % 2, r // 4, (r // 2) % 2] = part[r * ROWS : (r + 1) * ROWS]
                if i == 0:
                    pl.when(step == 0)(meet)
                give_copy(base + i, i).start()
                if i > 0:
                    add_core(base + i - 1, i - 1)

        def reload(k):
            @pl.when(step == 0)
            def _():
                load(k, 0).start()
                load(k + 1, 0).start()

        products(0, u_v, dqkv_v, ((0, 0), (1, 1), (2, 2)))
        reload(0)
        products(2, o_v, da_v, ((3, 0),))
        reload(2)
        products(4, u2_v, dz_v, ((4, 0), (5, 1), (6, 2), (7, 3)))
        reload(4)
        load(6, l).wait()
        load(7, l).wait()
        for i in range(8, CHUNKS):
            free(i)
        for b in range(4):
            part = tn(act_v[:, b * CHUNK : (b + 1) * CHUNK], dm_v[...]).astype(BF16)
            for r in range(8):
                own[8 + r % 4, r // 4, b // 2, b % 2] = part[r * ROWS : (r + 1) * ROWS]
        reload(6)
        for i in range(8, CHUNKS):
            give_copy(base + i, i).start()
        for i in range(7, CHUNKS):
            add_core(base + i, i)
        return carry

    lax.fori_loop(0, 2, layer_products, 0)

    def second_sums(step, carry):
        for i in range(CHUNKS):
            n = step * CHUNKS + i
            first_copy(n, i).wait_recv()
            kept = first[n, :, x] if i % 2 == 0 else first[n, y]
            second[n] = second[n] + kept
            second_copy(n, i).start()
        return carry

    lax.fori_loop(0, 2, second_sums, 0)

    gains_v[me] = gains_in[me]
    for j in range(SHARDS):

        @pl.when(me != j)
        def _():
            gain_copy(j, j).wait_recv()

    total = gains_v[0]
    for j in range(1, SHARDS):
        total = total + gains_v[j]
    gains_out[...] = total

    def last_sums(step, carry):
        for i in range(CHUNKS):
            n = step * CHUNKS + i
            second_copy(n, i).wait_recv()
            third[n] = third[n] + second[n, y if i % 2 == 0 else x]
            result_copy(n, 1 - step, i).start()
        return carry

    lax.fori_loop(0, 2, last_sums, 0)

    def finish(step, carry):
        for i in range(CHUNKS):
            n = step * CHUNKS + i
            first_copy(n, i).wait_send()
            second_copy(n, i).wait_send()
            result_copy(n, 1 - step, i).wait()
        return carry

    lax.fori_loop(0, 2, finish, 0)
    for i in range(CHUNKS):
        give_copy(CHUNKS + i, i).wait_send()
    for j in range(SHARDS):

        @pl.when(me != j)
        def _():
            gain_copy(j, me).wait_send()

    @pl.when(section == 0)
    def _():
        own_inp_copy().wait()
        for j in range(1, sections):
            inp_copy(j).wait_send()

    @pl.when(section > 0)
    def _():
        inp_copy(0).wait_recv()


def summed(gains, inp, *factors):
    sections, width, rows = inp.shape
    anywhere = pl.BlockSpec(memory_space=pl.ANY)
    vmem = pl.BlockSpec(memory_space=pltpu.VMEM)
    dma = pltpu.SemaphoreType.DMA
    total = 2 * CHUNKS

    def shard(height, columns):
        return jax.ShapeDtypeStruct((2, height, columns), BF16)

    return pl.pallas_call(
        functools.partial(sum_kernel, sections),
        out_shape=(
            jax.ShapeDtypeStruct((8, 128), F32),
            jax.ShapeDtypeStruct((width, rows), BF16),
            shard(ROWS, 3 * D),
            shard(ROWS, D),
            shard(ROWS, FF),
            shard(4 * ROWS, D),
        ),
        in_specs=[vmem] + [anywhere] * 9,
        out_specs=(vmem,) + (anywhere,) * 5,
        scratch_shapes=[pltpu.VMEM((rows, f.shape[2]), BF16) for f in factors]
        + [
            pltpu.VMEM((CHUNKS, 2, 2, 2, ROWS, CHUNK), BF16),
            pltpu.VMEM((total, 2, 2, ROWS, CHUNK), BF16),
            pltpu.VMEM((total, 2, ROWS, CHUNK), BF16),
            pltpu.VMEM((total, ROWS, CHUNK), BF16),
            pltpu.VMEM((SHARDS, 8, 128), F32),
            dma((8,)),
            dma((SHARDS,)),
            dma((SHARDS,)),
            dma((sections,)),
            dma(()),
            dma((3, total)),
            dma((3, total)),
            dma((total,)),
        ],
        compiler_params=pltpu.CompilerParams(
            collective_id=1, has_side_effects=True, vmem_limit_bytes=60 * MIB
        ),
        name="sum",
    )(gains, inp, *factors)


def write_kernel(count, share, gains, *refs):
    gain_one, gain_two = refs[count], refs[count + 1]
    gain_one[...] = gains[0:2, 0:share]
    gain_two[...] = gains[2:4, 0:share]
    sources, results, held, wide = (
        refs[:count],
        refs[count + 2 : 2 * count + 2],
        refs[2 * count + 2 : 3 * count + 2],
        refs[3 * count + 2 : 4 * count + 2],
    )
    load_sem, store_sem = refs[4 * count + 2 :]
    loads = [pltpu.make_async_copy(sources[k], held[k], load_sem.at[k]) for k in range(count)]
    stores = [pltpu.make_async_copy(wide[k], results[k], store_sem.at[k]) for k in range(count)]
    for load in loads:
        load.start()
    for k in range(count):
        loads[k].wait()
        wide[k][...] = held[k][...].astype(wide[k].dtype)
        stores[k].start()
    for store in stores:
        store.wait()


def written(gains, share, arrays, types):
    count = len(arrays)
    anywhere = pl.BlockSpec(memory_space=pl.ANY)
    vmem = pl.BlockSpec(memory_space=pltpu.VMEM)
    return pl.pallas_call(
        functools.partial(write_kernel, count, share),
        out_shape=(jax.ShapeDtypeStruct((2, share), F32),) * 2
        + tuple(jax.ShapeDtypeStruct(a.shape, t) for a, t in zip(arrays, types)),
        in_specs=[vmem] + [anywhere] * count,
        out_specs=(vmem, vmem) + (anywhere,) * count,
        scratch_shapes=[pltpu.VMEM(a.shape, a.dtype) for a in arrays]
        + [pltpu.VMEM(a.shape, t) for a, t in zip(arrays, types)]
        + [pltpu.SemaphoreType.DMA((count,)), pltpu.SemaphoreType.DMA((count,))],
        compiler_params=pltpu.CompilerParams(vmem_limit_bytes=60 * MIB),
        name="write",
    )(gains, *arrays)


def body(
    tokens,
    gain_one,
    qkv_weight,
    out_weight,
    gain_two,
    up_weight,
    down_weight,
    cotangent,
    flags,
    groups,
):
    micros = tokens.shape[0] // SEQ
    fin, inp, gains, u, dqkv, o, da, u2, dz, act, dm, _ = relay(
        tokens,
        cotangent,
        flags.reshape(micros, SEQ),
        groups,
        gain_one,
        gain_two,
        qkv_weight,
        out_weight,
        up_weight,
        down_weight,
    )

    replicas = lax.axis_size("dp")
    share = D // replicas
    if replicas == SHARDS and share == ROWS:
        gains, inp, g_qkv, g_out, g_up, g_down = summed(gains, inp, u, dqkv, o, da, u2, dz, act, dm)
    else:

        def grad(a, g):
            total = jnp.einsum("lsa,lsb->lab", a, g, preferred_element_type=F32).astype(BF16)
            return lax.psum_scatter(total, "dp", scatter_dimension=1, tiled=True)

        gains = lax.psum_scatter(gains, "dp", scatter_dimension=0)
        inp = jnp.where(lax.axis_index("pipe") == 0, inp, jnp.zeros_like(inp))
        inp = lax.psum_scatter(inp, "pipe", scatter_dimension=0)
        g_qkv, g_out, g_up, g_down = grad(u, dqkv), grad(o, da), grad(u2, dz), grad(act, dm)
    gain_one_grad, gain_two_grad, fin, inp, g_qkv, g_out, g_up, g_down = written(
        gains, share, (fin, inp, g_qkv, g_out, g_up, g_down), (BF16,) + (F32,) * 5
    )
    return (fin.T, inp.T, gain_one_grad, g_qkv, g_out, gain_two_grad, g_up, g_down)


def solution(mesh):
    return jax.shard_map(
        body,
        mesh=mesh,
        in_specs=(
            P("dp", None),
            P("pipe", None),
            P("pipe", None, None),
            P("pipe", None, None),
            P("pipe", None),
            P("pipe", None, None),
            P("pipe", None, None),
            P("dp", None),
            P("dp"),
            P("dp"),
        ),
        out_specs=(
            P("dp", "pipe"),
            P("dp", "pipe"),
            P("pipe", "dp"),
            P("pipe", "dp", None),
            P("pipe", "dp", None),
            P("pipe", "dp"),
            P("pipe", "dp", None),
            P("pipe", "dp", None),
        ),
        check_vma=False,
    )
```

```python
import functools

import jax
import jax.numpy as jnp
from jax import lax
from jax.experimental import pallas as pl
from jax.experimental.pallas import tpu as pltpu
from jax.sharding import PartitionSpec as P

D = 768
HEADS = 16
HEAD_DIM = 48
FF = 3072
SEQ = 128
EPS = 1e-06
MESH = pl.DeviceIdType.MESH
F32 = jnp.float32
BF16 = jnp.bfloat16
LOG2E = 1.4426950408889634
SCALE = HEAD_DIM ** (-0.5)
MIB = 2**20
CHUNK = 768
TILE = 256

KINDS = ((0, 3), (3, 1), (4, 4), (8, 4))
BLOCKS = 12
SHARDS = 8

WINDOWS = tuple(
    (96 * j // 128, -(-(96 * j % 128 + 96) // 128), 96 * j % 128) for j in range(HEADS // 2)
)


def nn(a, b):
    return jnp.dot(a, b, preferred_element_type=F32)


def nt(a, b):
    return lax.dot_general(a, b, (((1,), (1,)), ((), ())), preferred_element_type=F32)


def tn(a, b):
    return lax.dot_general(a, b, (((0,), (0,)), ((), ())), preferred_element_type=F32)


def lanes_of_head(first, width):
    lane = lax.broadcasted_iota(jnp.int32, (SEQ, width), 1)
    return ((lane >= first) & (lane < first + HEAD_DIM)).astype(F32).astype(BF16)


def two_heads(window, first):
    width = window.shape[1]
    return jnp.concatenate(
        [window * lanes_of_head(first, width), window * lanes_of_head(first + HEAD_DIM, width)], axis=0
    )


def add_window(tiles, first, part):
    for i in range(part.shape[1] // 128):
        piece = part[:, i * 128 : (i + 1) * 128]
        tiles[first + i] = piece if tiles[first + i] is None else tiles[first + i] + piece


def norm_parts(x):
    centre = x - jnp.mean(x, axis=-1, keepdims=True)
    spread = jnp.mean(centre * centre, axis=-1, keepdims=True)
    inverse = lax.rsqrt(spread + EPS)
    return centre * inverse, inverse


def gelu_parts(z):
    phi = 0.5 * (1.0 + lax.erf(z * 0.7071067811865476))
    density = jnp.exp2(z * z * (-0.5 * LOG2E)) * 0.3989422804014327
    return z * phi, phi + z * density


def relay_kernel(
    sections,
    replicas,
    micros,
    paired,
    tokens,
    cotangent,
    flags,
    groups,
    gain_one,
    gain_two,
    wqkv_hbm,
    wout_hbm,
    wup_hbm,
    wdown_hbm,
    fin_out,
    inp_out,
    gains_out,
    u_out,
    dqkv_out,
    o_out,
    da_out,
    u2_out,
    dz_out,
    act_out,
    dm_out,
    act_other,
    dm_other,
    turned_hbm,
    weights,
    fwd_in,
    fwd_out,
    bwd_in,
    bwd_out,
    fin_stage,
    inp_stage,
    u_s,
    qkv_s,
    p_s,
    u2_s,
    gp_s,
    stat_s,
    o_s,
    act_s,
    dm_s,
    da_s,
    state,
    acc,
    bias,
    w_sem,
    turn_sem,
    swap_sem,
    in_sem,
    fwd_send,
    fwd_recv,
    bwd_send,
    bwd_recv,
    fin_send,
    fin_recv,
    inp_send,
    out_sem,
    act_send,
    act_recv,
    dm_send,
    dm_recv,
):
    me = lax.axis_index("pipe")
    last = sections - 1
    width = D // sections

    barrier = pltpu.get_barrier_semaphore()
    for j in range(sections):

        @pl.when(me != j)
        def _():
            pl.semaphore_signal(barrier, inc=1, device_id={"pipe": j}, device_id_type=MESH)

    replica = lax.axis_index("dp")
    x, y = lax.rem(replica // 2, 2), replica // 4
    if paired:
        for j in (replica + 2 - 4 * x, replica + 4 - 8 * y):
            pl.semaphore_signal(barrier, inc=1, device_id={"dp": j}, device_id_type=MESH)

    def block_rows(b, count=1):
        start = b * D
        return pl.ds(start if isinstance(b, int) else pl.multiple_of(start, D), count * D)

    def weight_copy(l, k, j):
        first, _ = KINDS[k]
        if k == 1:
            src = wout_hbm.at[l]
        elif k == 3:
            src = wdown_hbm.at[l, block_rows(j)]
        else:
            src = (wqkv_hbm, None, wup_hbm)[k].at[l, :, block_rows(j)]
        return pltpu.make_async_copy(src, weights.at[l, block_rows(first + j)], w_sem.at[l, first + j])

    def turned_copy(l, b):
        return pltpu.make_async_copy(
            weights.at[l, block_rows(b)], turned_hbm.at[l, block_rows(b)], turn_sem.at[l, b]
        )

    def swap_copy(l, k):
        rows = block_rows(*KINDS[k])
        return pltpu.make_async_copy(turned_hbm.at[l, rows], weights.at[1 - l, rows], swap_sem.at[l, k])

    def turn(l, b):
        def tile(r, c):
            return l, pl.ds(pl.multiple_of(b * D + r * TILE, TILE), TILE), pl.ds(c * TILE, TILE)

        for r in range(D // TILE):
            weights[tile(r, r)] = weights[tile(r, r)].T
            for c in range(r):
                lower = weights[tile(r, c)].T
                upper = weights[tile(c, r)].T
                weights[tile(c, r)] = lower
                weights[tile(r, c)] = upper

    def each_block(l, action):
        for k, (_, count) in enumerate(KINDS):

            def one(j, c):
                action(l, k, j)
                return c

            lax.fori_loop(0, count, one, 0)

    def token_copy(m):
        return pltpu.make_async_copy(tokens.at[pl.ds(m * SEQ, SEQ)], fwd_in.at[m], in_sem.at[0, m])

    def cotangent_copy(m):
        return pltpu.make_async_copy(cotangent.at[pl.ds(m * SEQ, SEQ)], bwd_in.at[m], in_sem.at[1, m])

    @pl.when(me == 0)
    def _():
        for m in range(micros):
            token_copy(m).start()

    for l in range(2):
        for k, (_, count) in enumerate(KINDS):
            for j in range(count):
                weight_copy(l, k, j).start()

    @pl.when(me == last)
    def _():
        for m in range(micros):
            cotangent_copy(m).start()

    def forward_copy(m):
        return pltpu.make_async_remote_copy(
            src_ref=fwd_out.at[m],
            dst_ref=fwd_in.at[m],
            send_sem=fwd_send.at[m],
            recv_sem=fwd_recv.at[m],
            device_id={"pipe": lax.rem(me + 1, sections)},
            device_id_type=MESH,
        )

    def backward_copy(m):
        return pltpu.make_async_remote_copy(
            src_ref=bwd_out.at[m],
            dst_ref=bwd_in.at[m],
            send_sem=bwd_send.at[m],
            recv_sem=bwd_recv.at[m],
            device_id={"pipe": lax.rem(me + sections - 1, sections)},
            device_id_type=MESH,
        )

    def slots_of(m):
        return pl.ds(pl.multiple_of(m * SEQ, SEQ), SEQ)

    def fin_copy(m, j):
        return pltpu.make_async_remote_copy(
            src_ref=fin_stage.at[m, j],
            dst_ref=fin_out.at[:, slots_of(m)],
            send_sem=fin_send.at[m, j],
            recv_sem=fin_recv.at[m],
            device_id={"pipe": j},
            device_id_type=MESH,
        )

    def own_fin_copy(m):
        return pltpu.make_async_copy(fin_stage.at[m, last], fin_out.at[:, slots_of(m)], fin_send.at[m, last])

    def inp_copy(m, j):
        return pltpu.make_async_copy(inp_stage.at[m, j], inp_out.at[j, :, slots_of(m)], inp_send.at[m, j])

    def piece(j):
        return state[:, j * width : (j + 1) * width].T.astype(BF16)

    outs = (u_out, dqkv_out, o_out, da_out, u2_out, dz_out, act_out, dm_out)

    def out_copy(kind, l, m):
        slot = l
        src = (
            u_s.at[l, m],
            qkv_s.at[l, m],
            o_s.at[slot],
            da_s.at[slot],
            u2_s.at[l, m],
            gp_s.at[l, m],
            act_s.at[slot],
            dm_s.at[l, m],
        )[kind]
        return pltpu.make_async_copy(src, outs[kind].at[l, pl.ds(m * SEQ, SEQ)], out_sem.at[kind, l, m])

    def partner(l):
        return {"dp": lax.select(l == 1, replica + 2 - 4 * x, replica + 4 - 8 * y)}

    def act_copy(l, m, b):
        block = l * (2 * b + 1 - x) + (1 - l) * (2 * (1 - y) + b)
        return pltpu.make_async_remote_copy(
            src_ref=act_out.at[l, slots_of(m), block_rows(block)],
            dst_ref=act_other.at[l, slots_of(m), pl.ds(b * D, D)],
            send_sem=act_send.at[l, m, b],
            recv_sem=act_recv.at[l, m, b],
            device_id=partner(l),
            device_id_type=MESH,
        )

    def act_start(l, m):
        if paired:
            for b in range(2):
                act_copy(l, m, b).start()

    def dm_copy(l, m):
        return pltpu.make_async_remote_copy(
            src_ref=dm_s.at[l, m],
            dst_ref=dm_other.at[l, slots_of(m)],
            send_sem=dm_send.at[l, m],
            recv_sem=dm_recv.at[l, m],
            device_id=partner(l),
            device_id_type=MESH,
        )

    def free_slot(kind, l, m):
        @pl.when(m > 0)
        def _():
            out_copy(kind, l, m - 1).wait()
            if kind == 6:
                act_start(l, m - 1)

    row = lax.broadcasted_iota(jnp.int32, (SEQ, SEQ), 0) // (SEQ // 4)
    column = lax.broadcasted_iota(jnp.int32, (SEQ, SEQ), 1) // (SEQ // 4)
    same = (row == column).astype(F32)
    for m in range(micros):
        parted = (jnp.full((1, SEQ), groups[m], jnp.int32) == 1).astype(F32)
        valid = jnp.broadcast_to((flags[m : m + 1, :] == 1).astype(F32), (SEQ, SEQ)).T
        keep = jnp.maximum(same, 1.0 - parted) * valid
        bias[m] = (keep - 1.0) * 1e30

    pl.semaphore_wait(barrier, sections - 1 + 2 * paired)

    def forward_layer(l, m):
        def weight_wait(k):
            @pl.when((m == 0) & (me < last))
            def _():
                for j in range(KINDS[k][1]):
                    weight_copy(l, k, j).wait()

        x = state[...]
        xhat, inverse = norm_parts(x)
        stat_s[l, m, :, 0:1] = inverse
        u = (xhat * gain_one[pl.ds(l, 1), :]).astype(BF16)
        u_s[l, m] = u
        out_copy(0, l, m).start()
        weight_wait(0)
        for j in range(3):
            qkv_s[l, m, :, j * D : (j + 1) * D] = nn(u_s[l, m], weights[l, block_rows(j)]).astype(BF16)
        free_slot(2, l, m)
        slot = l
        added = bias[m]
        scores, tiles = [], [None] * 6
        for tile, count, inside in WINDOWS:
            lo, hi = tile * 128, (tile + count) * 128
            keys = two_heads(qkv_s[l, m, :, D + lo : D + hi], inside)
            scores.append(nt(keys, qkv_s[l, m, :, lo:hi]) * (SCALE * LOG2E))
        for j in range(len(WINDOWS)):
            for h in range(2):
                s = scores[j][h * SEQ : (h + 1) * SEQ] + added
                e = jnp.exp2(s - jnp.max(s, axis=0, keepdims=True))
                p = e * (1.0 / jnp.sum(e, axis=0, keepdims=True))
                p_s[l, m, 2 * j + h] = p.astype(BF16)
        for j, (tile, count, inside) in enumerate(WINDOWS):
            lo, hi = tile * 128, (tile + count) * 128
            values = two_heads(qkv_s[l, m, :, 2 * D + lo : 2 * D + hi], inside)
            p = jnp.concatenate([p_s[l, m, 2 * j], p_s[l, m, 2 * j + 1]], axis=0)
            add_window(tiles, tile, tn(p, values))
        for i in range(6):
            o_s[slot, :, i * 128 : (i + 1) * 128] = tiles[i].astype(BF16)
        out_copy(2, l, m).start()
        weight_wait(1)
        h = state[...] + nn(o_s[slot], weights[l, block_rows(3)])
        state[...] = h
        hhat, inverse = norm_parts(h)
        stat_s[l, m, :, 1:2] = inverse
        u2_s[l, m] = (hhat * gain_two[pl.ds(l, 1), :]).astype(BF16)
        out_copy(4, l, m).start()
        weight_wait(2)
        free_slot(6, l, m)
        weight_wait(3)
        for j in range(4):
            act, slope = gelu_parts(nn(u2_s[l, m], weights[l, block_rows(4 + j)]))
            act_s[slot, :, j * D : (j + 1) * D] = act.astype(BF16)
            gp_s[l, m, :, j * D : (j + 1) * D] = slope.astype(BF16)
        state[...] = state[...] + nn(act_s[slot], weights[l, block_rows(8, 4)])
        out_copy(6, l, m).start()

    def norm_back(du, hat_scaled, gain, inverse):
        t = du * gain
        hat = hat_scaled * (1.0 / gain)
        weighted = du * hat_scaled
        return inverse * (
            t - jnp.mean(t, axis=-1, keepdims=True) - hat * jnp.mean(weighted, axis=-1, keepdims=True)
        ), weighted

    def add_rows(at, weighted):
        part = weighted[0:8]
        for r in range(8, SEQ, 8):
            part = part + weighted[r : r + 8]
        acc[at] = acc[at] + part

    def backward_layer(l, m):
        slot = l
        held = lax.select(me == last, 1 - l, l)

        def turned_wait(k):
            @pl.when((m == 0) & (me == last))
            def _():
                swap_copy(l, k).wait()

        dy = state[...]
        turned_wait(3)
        turned_wait(2)
        dm_s[l, m] = dy.astype(BF16)
        out_copy(7, l, m).start()
        if paired:
            dm_copy(l, m).start()
        for j in range(4):
            da = nn(dm_s[l, m], weights[held, block_rows(8 + j)])
            dz = gp_s[l, m, :, j * D : (j + 1) * D].astype(F32) * da
            gp_s[l, m, :, j * D : (j + 1) * D] = dz.astype(BF16)
        out_copy(5, l, m).start()
        dh, weighted = norm_back(
            nn(gp_s[l, m], weights[held, block_rows(4, 4)]), u2_s[l, m].astype(F32), gain_two[pl.ds(l, 1), :], stat_s[l, m, :, 1:2]
        )
        add_rows(2 + l, weighted)
        dh = state[...] + dh
        state[...] = dh
        free_slot(3, l, m)
        da_s[slot] = dh.astype(BF16)
        out_copy(3, l, m).start()
        turned_wait(1)
        turned_wait(0)
        do = nn(da_s[slot], weights[held, block_rows(3)]).astype(BF16)
        slopes, products = [], []
        q_tiles, k_tiles, v_tiles = [None] * 6, [None] * 6, [None] * 6
        for tile, count, inside in WINDOWS:
            lo, hi = tile * 128, (tile + count) * 128
            values = two_heads(qkv_s[l, m, :, 2 * D + lo : 2 * D + hi], inside)
            products.append(nt(values, do[:, lo:hi]))
        for j in range(len(WINDOWS)):
            for h in range(2):
                p = p_s[l, m, 2 * j + h].astype(F32)
                dp = products[j][h * SEQ : (h + 1) * SEQ]
                slopes.append((p * (dp - jnp.sum(p * dp, axis=0, keepdims=True))).astype(BF16))
        for j, (tile, count, inside) in enumerate(WINDOWS):
            lo, hi = tile * 128, (tile + count) * 128
            pair = slopes[2 * j : 2 * j + 2]
            keys = two_heads(qkv_s[l, m, :, D + lo : D + hi], inside)
            query = two_heads(qkv_s[l, m, :, lo:hi], inside)
            add_window(q_tiles, tile, tn(jnp.concatenate(pair, axis=0), keys))
            add_window(k_tiles, tile, nn(jnp.concatenate(pair, axis=1), query))
        for j, (tile, count, inside) in enumerate(WINDOWS):
            given = two_heads(do[:, tile * 128 : (tile + count) * 128], inside)
            p = jnp.concatenate([p_s[l, m, 2 * j], p_s[l, m, 2 * j + 1]], axis=1)
            add_window(v_tiles, tile, nn(p, given))
        for i in range(6):
            at = i * 128
            qkv_s[l, m, :, at : at + 128] = (q_tiles[i] * SCALE).astype(BF16)
            qkv_s[l, m, :, D + at : D + at + 128] = (k_tiles[i] * SCALE).astype(BF16)
            qkv_s[l, m, :, 2 * D + at : 2 * D + at + 128] = v_tiles[i].astype(BF16)
        out_copy(1, l, m).start()
        du = nn(qkv_s[l, m], weights[held, block_rows(0, 3)])
        dx, weighted = norm_back(
            du, u_s[l, m].astype(F32), gain_one[pl.ds(l, 1), :], stat_s[l, m, :, 0:1]
        )
        add_rows(l, weighted)
        state[...] = state[...] + dx

    @pl.when(me == last)
    def _():
        def make(l, k, j):
            b = KINDS[k][0] + j
            weight_copy(l, k, j).wait()
            turn(l, b)
            turned_copy(l, b).start()

        def again(l, k, j):
            turned_copy(l, KINDS[k][0] + j).wait()
            weight_copy(l, k, j).start()

        def ready(l, k, j):
            weight_copy(l, k, j).wait()

        for action in (make, again, ready):

            def one(l, c):
                each_block(l, action)
                return c

            lax.fori_loop(0, 2, one, 0)

    def forward_micro(m, carry):
        @pl.when(me == 0)
        def _():
            token_copy(m).wait()

        @pl.when(me > 0)
        def _():
            forward_copy(m).wait_recv()

        state[...] = fwd_in[m].astype(F32)

        def one(l, c):
            forward_layer(l, m)

            @pl.when((m == micros - 1) & (me == last))
            def _():
                for k in (3, 2, 1, 0):
                    swap_copy(1 - l, k).start()

            return c

        lax.fori_loop(0, 2, one, 0)

        @pl.when(me < last)
        def _():
            fwd_out[m] = state[...].astype(BF16)
            forward_copy(m).start()

        @pl.when(me == last)
        def _():
            for j in range(sections):
                fin_stage[m, j] = piece(j)
                if j == last:
                    own_fin_copy(m).start()
                else:
                    fin_copy(m, j).start()

        return carry

    lax.fori_loop(0, micros, forward_micro, 0)
    for l in range(2):
        out_copy(6, l, micros - 1).wait()
        act_start(l, micros - 1)

    @pl.when(me < last)
    def _():
        def one(i, c):
            turn(1 - i // BLOCKS, lax.rem(i, BLOCKS))
            return c

        lax.fori_loop(0, 2 * BLOCKS, one, 0)

    acc[...] = jnp.zeros_like(acc)

    def backward_micro(m, carry):
        @pl.when(me == last)
        def _():
            cotangent_copy(m).wait()

        @pl.when(me < last)
        def _():
            backward_copy(m).wait_recv()

        state[...] = bwd_in[m].astype(F32)

        def one(i, c):
            backward_layer(1 - i, m)
            return c

        lax.fori_loop(0, 2, one, 0)

        @pl.when(me > 0)
        def _():
            bwd_out[m] = state[...].astype(BF16)
            backward_copy(m).start()

        @pl.when(me == 0)
        def _():
            for j in range(sections):
                inp_stage[m, j] = piece(j)
                inp_copy(m, j).start()

        return carry

    lax.fori_loop(0, micros, backward_micro, 0)
    share = D // replicas
    for k in range(4):
        gain = (gain_one, gain_two)[k // 2][k % 2 : k % 2 + 1, :]
        total = jnp.sum(acc[k], axis=0, keepdims=True) / gain
        for r in range(replicas):
            gains_out[r, k : k + 1, 0:share] = total[:, r * share : (r + 1) * share]

    for l in range(2):
        for kind in (2, 3):
            out_copy(kind, l, micros - 1).wait()
        for m in range(micros):
            for kind in (0, 1, 4, 5, 7):
                out_copy(kind, l, m).wait()
            if paired:
                for b in range(2):
                    act_copy(l, m, b).wait()
                dm_copy(l, m).wait()
    for m in range(micros):

        @pl.when(me < last)
        def _():
            forward_copy(m).wait_send()

        @pl.when(me > 0)
        def _():
            backward_copy(m).wait_send()

        @pl.when(me == last)
        def _():
            for j in range(last):
                fin_copy(m, j).wait_send()
            own_fin_copy(m).wait()

        @pl.when(me < last)
        def _():
            fin_copy(m, last).wait_recv()

        @pl.when(me == 0)
        def _():
            for j in range(sections):
                inp_copy(m, j).wait()


def relay(tokens, cotangent, flags, groups, gain_one, gain_two, wqkv, wout, wup, wdown):
    sections = lax.axis_size("pipe")
    replicas = lax.axis_size("dp")
    rows = tokens.shape[0]
    micros = rows // SEQ
    width = D // sections
    paired = replicas == SHARDS
    anywhere = pl.BlockSpec(memory_space=pl.ANY)
    vmem = pl.BlockSpec(memory_space=pltpu.VMEM)
    smem = pl.BlockSpec(memory_space=pltpu.SMEM)
    dma = pltpu.SemaphoreType.DMA

    def factor(columns):
        return jax.ShapeDtypeStruct((2, rows, columns), BF16)

    def saved(columns):
        return pltpu.VMEM((2, micros, SEQ, columns), BF16)

    def two(columns):
        return pltpu.VMEM((2, SEQ, columns), BF16)

    def per_micro(columns):
        return pltpu.VMEM((micros, SEQ, columns), BF16)

    return pl.pallas_call(
        functools.partial(relay_kernel, sections, replicas, micros, paired),
        out_shape=(
            jax.ShapeDtypeStruct((width, rows), BF16),
            jax.ShapeDtypeStruct((sections, width, rows), BF16),
            jax.ShapeDtypeStruct((replicas, 8, 128), F32),
            factor(D),
            factor(3 * D),
            factor(D),
            factor(D),
            factor(D),
            factor(FF),
            factor(FF),
            factor(D),
            factor(2 * D),
            factor(D),
            jax.ShapeDtypeStruct((2, BLOCKS * D, D), BF16),
        ),
        in_specs=[anywhere, anywhere, vmem, smem, vmem, vmem] + [anywhere] * 4,
        out_specs=(anywhere, anywhere, vmem) + (anywhere,) * 11,
        scratch_shapes=[
            pltpu.VMEM((2, BLOCKS * D, D), BF16),
            per_micro(D),
            per_micro(D),
            per_micro(D),
            per_micro(D),
            pltpu.VMEM((micros, sections, width, SEQ), BF16),
            pltpu.VMEM((micros, sections, width, SEQ), BF16),
            saved(D),
            saved(3 * D),
            pltpu.VMEM((2, micros, HEADS, SEQ, SEQ), BF16),
            saved(D),
            saved(FF),
            pltpu.VMEM((2, micros, SEQ, 128), F32),
            two(D),
            two(FF),
            saved(D),
            two(D),
            pltpu.VMEM((SEQ, D), F32),
            pltpu.VMEM((4, 8, D), F32),
            pltpu.VMEM((micros, SEQ, SEQ), F32),
            dma((2, BLOCKS)),
            dma((2, BLOCKS)),
            dma((2, len(KINDS))),
            dma((2, micros)),
            dma((micros,)),
            dma((micros,)),
            dma((micros,)),
            dma((micros,)),
            dma((micros, sections)),
            dma((micros,)),
            dma((micros, sections)),
            dma((8, 2, micros)),
            dma((2, micros, 2)),
            dma((2, micros, 2)),
            dma((2, micros)),
            dma((2, micros)),
        ],
        compiler_params=pltpu.CompilerParams(
            collective_id=0, has_side_effects=True, vmem_limit_bytes=60 * MIB
        ),
        name="relay",
    )(tokens, cotangent, flags, groups, gain_one, gain_two, wqkv, wout, wup, wdown)


ROWS = 96
CHUNKS = 12


def sum_kernel(
    sections,
    gains_in,
    inp_in,
    u_in,
    dqkv_in,
    o_in,
    da_in,
    u2_in,
    dz_in,
    act_in,
    dm_in,
    act_other,
    dm_other,
    gains_out,
    inp_out,
    qkv_out,
    out_out,
    up_out,
    down_out,
    u_v,
    dqkv_v,
    o_v,
    da_v,
    u2_v,
    dz_v,
    act_v,
    dm_v,
    own,
    first,
    second,
    third,
    gains_v,
    load_sem,
    gain_send,
    gain_recv,
    inp_send,
    inp_recv,
    send,
    recv,
    out_sem,
):
    me = lax.axis_index("dp")
    section = lax.axis_index("pipe")
    core = lax.rem(me, 2)
    x = lax.rem(me // 2, 2)
    y = me // 4
    other_core = me + 1 - 2 * core
    other_x = me + 2 - 4 * x
    other_y = me + 4 - 8 * y

    barrier = pltpu.get_barrier_semaphore()
    for j in range(SHARDS):

        @pl.when(me != j)
        def _():
            pl.semaphore_signal(barrier, inc=1, device_id={"dp": j}, device_id_type=MESH)

    @pl.when(section > 0)
    def _():
        pl.semaphore_signal(barrier, inc=1, device_id={"pipe": 0}, device_id_type=MESH)

    sources = (u_in, dqkv_in, o_in, da_in, u2_in, dz_in)
    held = (u_v, dqkv_v, o_v, da_v, u2_v, dz_v)
    rows = dm_in.shape[1]

    def load(k, l):
        return pltpu.make_async_copy(sources[k].at[l], held[k], load_sem.at[k])

    def down_loads(l):
        copies = [(dm_in.at[l], dm_v.at[0:rows]), (dm_other.at[l], dm_v.at[rows : 2 * rows])]
        for b in range(2):
            block = l * (2 * b + x) + (1 - l) * (2 * y + b)
            columns = pl.ds(pl.multiple_of(block * CHUNK, CHUNK), CHUNK)
            copies.append((act_in.at[l, :, columns], act_v.at[b, 0:rows]))
            copies.append((act_other.at[l, :, pl.ds(b * CHUNK, CHUNK)], act_v.at[b, rows : 2 * rows]))
        return [pltpu.make_async_copy(src, dst, load_sem.at[6 + k]) for k, (src, dst) in enumerate(copies)]

    for k in range(6):
        load(k, 1).start()
    for copy in down_loads(1):
        copy.start()

    def gain_copy(j, source):
        return pltpu.make_async_remote_copy(
            src_ref=gains_in.at[j],
            dst_ref=gains_v.at[source],
            send_sem=gain_send.at[j],
            recv_sem=gain_recv.at[source],
            device_id={"dp": j},
            device_id_type=MESH,
        )

    def inp_copy(j):
        return pltpu.make_async_remote_copy(
            src_ref=inp_in.at[j],
            dst_ref=inp_out,
            send_sem=inp_send.at[j],
            recv_sem=inp_recv,
            device_id={"pipe": j},
            device_id_type=MESH,
        )

    def own_inp_copy():
        return pltpu.make_async_copy(inp_in.at[0], inp_out, inp_send.at[0])

    def meet():
        pl.semaphore_wait(barrier, SHARDS - 1 + lax.select(section == 0, sections - 1, 0))
        for j in range(SHARDS):

            @pl.when(me != j)
            def _():
                gain_copy(j, me).start()

        @pl.when(section == 0)
        def _():
            own_inp_copy().start()
            for j in range(1, sections):
                inp_copy(j).start()

    def remote(src, dst, step, n, to):
        return pltpu.make_async_remote_copy(
            src_ref=src,
            dst_ref=dst,
            send_sem=send.at[step, n],
            recv_sem=recv.at[step, n],
            device_id={"dp": to},
            device_id_type=MESH,
        )

    def give_copy(n, i):
        if i >= 8:
            return remote(own.at[i, 1 - core, 0], first.at[n, 0], 0, n, other_core)
        return remote(own.at[i, 1 - core], first.at[n], 0, n, other_core)

    def down_copy(n, l):
        mine, to = lax.select(l == 1, y, x), lax.select(l == 1, other_y, other_x)
        return remote(first.at[n, 0, 1 - mine], third.at[n], 2, n, to)

    def first_copy(n, i):
        if i % 2 == 0:
            return remote(first.at[n, :, 1 - x], second.at[n], 1, n, other_x)
        return remote(first.at[n, 1 - y], second.at[n], 1, n, other_y)

    def second_copy(n, i):
        if i % 2 == 0:
            return remote(second.at[n, 1 - y], third.at[n], 2, n, other_y)
        return remote(second.at[n, 1 - x], third.at[n], 2, n, other_x)

    def result_copy(n, l, i):
        if i < 3:
            dst = qkv_out.at[l, :, pl.ds(i * CHUNK, CHUNK)]
        elif i < 4:
            dst = out_out.at[l]
        elif i < 8:
            dst = up_out.at[l, :, pl.ds((i - 4) * CHUNK, CHUNK)]
        else:
            dst = down_out.at[l, pl.ds((i - 8) * ROWS, ROWS)]
        return pltpu.make_async_copy(third.at[n], dst, out_sem.at[n])

    def add_core(n, l, i):
        give_copy(n, i).wait_recv()
        if i >= 8:
            first[n, 0] = first[n, 0] + own[i, core, 0]
            down_copy(n, l).start()
        else:
            first[n] = first[n] + own[i, core]
            first_copy(n, i).start()

    def layer_products(step, carry):
        l = 1 - step
        base = step * CHUNKS

        def free(i):
            @pl.when(step > 0)
            def _():
                give_copy(i, i).wait_send()

        def products(k, a, g, slots):
            load(k, l).wait()
            load(k + 1, l).wait()
            for i, columns in slots:
                free(i)
                part = tn(a[...], g[:, columns * CHUNK : (columns + 1) * CHUNK]).astype(BF16)
                for r in range(SHARDS):
                    own[i, r % 2, r // 4, (r // 2) % 2] = part[r * ROWS : (r + 1) * ROWS]
                if i == 0:
                    pl.when(step == 0)(meet)
                give_copy(base + i, i).start()
                if i > 0:
                    add_core(base + i - 1, l, i - 1)

        def reload(k):
            @pl.when(step == 0)
            def _():
                load(k, 0).start()
                load(k + 1, 0).start()

        products(0, u_v, dqkv_v, ((0, 0), (1, 1), (2, 2)))
        reload(0)
        products(2, o_v, da_v, ((3, 0),))
        reload(2)
        products(4, u2_v, dz_v, ((4, 0), (5, 1), (6, 2), (7, 3)))
        reload(4)
        for copy in down_loads(l):
            copy.wait()
        for i in range(8, CHUNKS):
            free(i)
        for b in range(2):
            part = tn(act_v[b], dm_v[...]).astype(BF16)
            for r in range(8):
                own[8 + r % 4, r // 4, 0, b] = part[r * ROWS : (r + 1) * ROWS]

        @pl.when(step == 0)
        def _():
            for copy in down_loads(0):
                copy.start()

        for i in range(8, CHUNKS):
            give_copy(base + i, i).start()
        for i in range(7, CHUNKS):
            add_core(base + i, l, i)
        return carry

    lax.fori_loop(0, 2, layer_products, 0)

    def second_sums(step, carry):
        for i in range(8):
            n = step * CHUNKS + i
            first_copy(n, i).wait_recv()
            kept = first[n, :, x] if i % 2 == 0 else first[n, y]
            second[n] = second[n] + kept
            second_copy(n, i).start()
        return carry

    lax.fori_loop(0, 2, second_sums, 0)

    gains_v[me] = gains_in[me]
    for j in range(SHARDS):

        @pl.when(me != j)
        def _():
            gain_copy(j, j).wait_recv()

    total = gains_v[0]
    for j in range(1, SHARDS):
        total = total + gains_v[j]
    gains_out[...] = total

    def last_sums(step, carry):
        for i in range(CHUNKS):
            n = step * CHUNKS + i
            if i >= 8:
                down_copy(n, 1 - step).wait_recv()
                third[n] = third[n] + first[n, 0, lax.select(step == 0, y, x)]
            else:
                second_copy(n, i).wait_recv()
                third[n] = third[n] + second[n, y if i % 2 == 0 else x]
            result_copy(n, 1 - step, i).start()
        return carry

    lax.fori_loop(0, 2, last_sums, 0)

    def finish(step, carry):
        for i in range(CHUNKS):
            n = step * CHUNKS + i
            if i >= 8:
                down_copy(n, 1 - step).wait_send()
            else:
                first_copy(n, i).wait_send()
                second_copy(n, i).wait_send()
            result_copy(n, 1 - step, i).wait()
        return carry

    lax.fori_loop(0, 2, finish, 0)
    for i in range(CHUNKS):
        give_copy(CHUNKS + i, i).wait_send()
    for j in range(SHARDS):

        @pl.when(me != j)
        def _():
            gain_copy(j, me).wait_send()

    @pl.when(section == 0)
    def _():
        own_inp_copy().wait()
        for j in range(1, sections):
            inp_copy(j).wait_send()

    @pl.when(section > 0)
    def _():
        inp_copy(0).wait_recv()


def summed(gains, inp, *factors):
    sections, width, rows = inp.shape
    anywhere = pl.BlockSpec(memory_space=pl.ANY)
    vmem = pl.BlockSpec(memory_space=pltpu.VMEM)
    dma = pltpu.SemaphoreType.DMA
    total = 2 * CHUNKS

    def shard(height, columns):
        return jax.ShapeDtypeStruct((2, height, columns), BF16)

    return pl.pallas_call(
        functools.partial(sum_kernel, sections),
        out_shape=(
            jax.ShapeDtypeStruct((8, 128), F32),
            jax.ShapeDtypeStruct((width, rows), BF16),
            shard(ROWS, 3 * D),
            shard(ROWS, D),
            shard(ROWS, FF),
            shard(4 * ROWS, D),
        ),
        in_specs=[vmem] + [anywhere] * 11,
        out_specs=(vmem,) + (anywhere,) * 5,
        scratch_shapes=[pltpu.VMEM((rows, f.shape[2]), BF16) for f in factors[:6]]
        + [
            pltpu.VMEM((2, 2 * rows, CHUNK), BF16),
            pltpu.VMEM((2 * rows, D), BF16),
            pltpu.VMEM((CHUNKS, 2, 2, 2, ROWS, CHUNK), BF16),
            pltpu.VMEM((total, 2, 2, ROWS, CHUNK), BF16),
            pltpu.VMEM((total, 2, ROWS, CHUNK), BF16),
            pltpu.VMEM((total, ROWS, CHUNK), BF16),
            pltpu.VMEM((SHARDS, 8, 128), F32),
            dma((12,)),
            dma((SHARDS,)),
            dma((SHARDS,)),
            dma((sections,)),
            dma(()),
            dma((3, total)),
            dma((3, total)),
            dma((total,)),
        ],
        compiler_params=pltpu.CompilerParams(
            collective_id=1, has_side_effects=True, vmem_limit_bytes=60 * MIB
        ),
        name="sum",
    )(gains, inp, *factors)


def write_kernel(count, share, gains, *refs):
    gain_one, gain_two = refs[count], refs[count + 1]
    gain_one[...] = gains[0:2, 0:share]
    gain_two[...] = gains[2:4, 0:share]
    sources, results, held, wide = (
        refs[:count],
        refs[count + 2 : 2 * count + 2],
        refs[2 * count + 2 : 3 * count + 2],
        refs[3 * count + 2 : 4 * count + 2],
    )
    load_sem, store_sem = refs[4 * count + 2 :]
    loads = [pltpu.make_async_copy(sources[k], held[k], load_sem.at[k]) for k in range(count)]
    stores = [pltpu.make_async_copy(wide[k], results[k], store_sem.at[k]) for k in range(count)]
    for load in loads:
        load.start()
    for k in range(count):
        loads[k].wait()
        wide[k][...] = held[k][...].astype(wide[k].dtype)
        stores[k].start()
    for store in stores:
        store.wait()


def written(gains, share, arrays, types):
    count = len(arrays)
    anywhere = pl.BlockSpec(memory_space=pl.ANY)
    vmem = pl.BlockSpec(memory_space=pltpu.VMEM)
    return pl.pallas_call(
        functools.partial(write_kernel, count, share),
        out_shape=(jax.ShapeDtypeStruct((2, share), F32),) * 2
        + tuple(jax.ShapeDtypeStruct(a.shape, t) for a, t in zip(arrays, types)),
        in_specs=[vmem] + [anywhere] * count,
        out_specs=(vmem, vmem) + (anywhere,) * count,
        scratch_shapes=[pltpu.VMEM(a.shape, a.dtype) for a in arrays]
        + [pltpu.VMEM(a.shape, t) for a, t in zip(arrays, types)]
        + [pltpu.SemaphoreType.DMA((count,)), pltpu.SemaphoreType.DMA((count,))],
        compiler_params=pltpu.CompilerParams(vmem_limit_bytes=60 * MIB),
        name="write",
    )(gains, *arrays)


def body(
    tokens,
    gain_one,
    qkv_weight,
    out_weight,
    gain_two,
    up_weight,
    down_weight,
    cotangent,
    flags,
    groups,
):
    micros = tokens.shape[0] // SEQ
    fin, inp, gains, u, dqkv, o, da, u2, dz, act, dm, act_other, dm_other, _ = relay(
        tokens,
        cotangent,
        flags.reshape(micros, SEQ),
        groups,
        gain_one,
        gain_two,
        qkv_weight,
        out_weight,
        up_weight,
        down_weight,
    )

    replicas = lax.axis_size("dp")
    share = D // replicas
    if replicas == SHARDS and share == ROWS:
        gains, inp, g_qkv, g_out, g_up, g_down = summed(
            gains, inp, u, dqkv, o, da, u2, dz, act, dm, act_other, dm_other
        )
    else:

        def grad(a, g):
            total = jnp.einsum("lsa,lsb->lab", a, g, preferred_element_type=F32).astype(BF16)
            return lax.psum_scatter(total, "dp", scatter_dimension=1, tiled=True)

        gains = lax.psum_scatter(gains, "dp", scatter_dimension=0)
        inp = jnp.where(lax.axis_index("pipe") == 0, inp, jnp.zeros_like(inp))
        inp = lax.psum_scatter(inp, "pipe", scatter_dimension=0)
        g_qkv, g_out, g_up, g_down = grad(u, dqkv), grad(o, da), grad(u2, dz), grad(act, dm)
    gain_one_grad, gain_two_grad, fin, inp, g_qkv, g_out, g_up, g_down = written(
        gains, share, (fin, inp, g_qkv, g_out, g_up, g_down), (BF16,) + (F32,) * 5
    )
    return (fin.T, inp.T, gain_one_grad, g_qkv, g_out, gain_two_grad, g_up, g_down)


def solution(mesh):
    return jax.shard_map(
        body,
        mesh=mesh,
        in_specs=(
            P("dp", None),
            P("pipe", None),
            P("pipe", None, None),
            P("pipe", None, None),
            P("pipe", None),
            P("pipe", None, None),
            P("pipe", None, None),
            P("dp", None),
            P("dp"),
            P("dp"),
        ),
        out_specs=(
            P("dp", "pipe"),
            P("dp", "pipe"),
            P("pipe", "dp"),
            P("pipe", "dp", None),
            P("pipe", "dp", None),
            P("pipe", "dp"),
            P("pipe", "dp", None),
            P("pipe", "dp", None),
        ),
        check_vma=False,
    )
```

```python
import functools

import jax
import jax.numpy as jnp
from jax import lax
from jax.experimental import pallas as pl
from jax.experimental.pallas import tpu as pltpu
from jax.sharding import PartitionSpec as P

D = 768
HEADS = 16
HEAD_DIM = 48
FF = 3072
SEQ = 128
EPS = 1e-06
MESH = pl.DeviceIdType.MESH
F32 = jnp.float32
BF16 = jnp.bfloat16
LOG2E = 1.4426950408889634
SCALE = HEAD_DIM ** (-0.5)
MIB = 2**20
CHUNK = 768
TILE = 256

KINDS = ((0, 3), (3, 1), (4, 4), (8, 4))
BLOCKS = 12

FIN_WINDOW = 256


def window_start(section, width):
    return min(section * width // 128 * 128, D - FIN_WINDOW)


SHARDS = 8

WINDOWS = tuple(
    (96 * j // 128, -(-(96 * j % 128 + 96) // 128), 96 * j % 128) for j in range(HEADS // 2)
)


def nn(a, b):
    return jnp.dot(a, b, preferred_element_type=F32)


def nt(a, b):
    return lax.dot_general(a, b, (((1,), (1,)), ((), ())), preferred_element_type=F32)


def tn(a, b):
    return lax.dot_general(a, b, (((0,), (0,)), ((), ())), preferred_element_type=F32)


def lanes_of_head(first, width):
    lane = lax.broadcasted_iota(jnp.int32, (SEQ, width), 1)
    return ((lane >= first) & (lane < first + HEAD_DIM)).astype(F32).astype(BF16)


def two_heads(window, first):
    width = window.shape[1]
    return jnp.concatenate(
        [window * lanes_of_head(first, width), window * lanes_of_head(first + HEAD_DIM, width)], axis=0
    )


def add_window(tiles, first, part):
    for i in range(part.shape[1] // 128):
        piece = part[:, i * 128 : (i + 1) * 128]
        tiles[first + i] = piece if tiles[first + i] is None else tiles[first + i] + piece


def norm_parts(x):
    centre = x - jnp.mean(x, axis=-1, keepdims=True)
    spread = jnp.mean(centre * centre, axis=-1, keepdims=True)
    inverse = lax.rsqrt(spread + EPS)
    return centre * inverse, inverse


def gelu_parts(z):
    phi = 0.5 * (1.0 + lax.erf(z * 0.7071067811865476))
    density = jnp.exp2(z * z * (-0.5 * LOG2E)) * 0.3989422804014327
    return z * phi, phi + z * density


def relay_kernel(
    sections,
    replicas,
    micros,
    paired,
    tokens,
    cotangent,
    flags,
    groups,
    gain_one,
    gain_two,
    wqkv_hbm,
    wout_hbm,
    wup_hbm,
    wdown_hbm,
    fin_out,
    inp_out,
    gains_out,
    u_out,
    dqkv_out,
    o_out,
    da_out,
    u2_out,
    dz_out,
    act_out,
    dm_out,
    act_other,
    dm_other,
    turned_hbm,
    weights,
    fwd_in,
    fwd_out,
    bwd_in,
    bwd_out,
    u_s,
    qkv_s,
    p_s,
    u2_s,
    gp_s,
    stat_s,
    o_s,
    act_s,
    dm_s,
    da_s,
    state,
    acc,
    bias,
    w_sem,
    turn_sem,
    swap_sem,
    in_sem,
    fwd_send,
    fwd_recv,
    bwd_send,
    bwd_recv,
    fin_send,
    fin_recv,
    inp_send,
    out_sem,
    act_send,
    act_recv,
    dm_send,
    dm_recv,
):
    me = lax.axis_index("pipe")
    last = sections - 1
    width = D // sections

    barrier = pltpu.get_barrier_semaphore()
    for j in range(sections):

        @pl.when(me != j)
        def _():
            pl.semaphore_signal(barrier, inc=1, device_id={"pipe": j}, device_id_type=MESH)

    replica = lax.axis_index("dp")
    x, y = lax.rem(replica // 2, 2), replica // 4
    if paired:
        for j in (replica + 2 - 4 * x, replica + 4 - 8 * y):
            pl.semaphore_signal(barrier, inc=1, device_id={"dp": j}, device_id_type=MESH)

    def block_rows(b, count=1):
        start = b * D
        return pl.ds(start if isinstance(b, int) else pl.multiple_of(start, D), count * D)

    def weight_copy(l, k, j):
        first, _ = KINDS[k]
        if k == 1:
            src = wout_hbm.at[l]
        elif k == 3:
            src = wdown_hbm.at[l, block_rows(j)]
        else:
            src = (wqkv_hbm, None, wup_hbm)[k].at[l, :, block_rows(j)]
        return pltpu.make_async_copy(src, weights.at[l, block_rows(first + j)], w_sem.at[l, first + j])

    def turned_copy(l, b):
        return pltpu.make_async_copy(
            weights.at[l, block_rows(b)], turned_hbm.at[l, block_rows(b)], turn_sem.at[l, b]
        )

    def swap_copy(l, k):
        rows = block_rows(*KINDS[k])
        return pltpu.make_async_copy(turned_hbm.at[l, rows], weights.at[1 - l, rows], swap_sem.at[l, k])

    def turn(l, b):
        def tile(r, c):
            return l, pl.ds(pl.multiple_of(b * D + r * TILE, TILE), TILE), pl.ds(c * TILE, TILE)

        for r in range(D // TILE):
            weights[tile(r, r)] = weights[tile(r, r)].T
            for c in range(r):
                lower = weights[tile(r, c)].T
                upper = weights[tile(c, r)].T
                weights[tile(c, r)] = lower
                weights[tile(r, c)] = upper

    def each_block(l, action):
        for k, (_, count) in enumerate(KINDS):

            def one(j, c):
                action(l, k, j)
                return c

            lax.fori_loop(0, count, one, 0)

    def token_copy(m):
        return pltpu.make_async_copy(tokens.at[pl.ds(m * SEQ, SEQ)], fwd_in.at[m], in_sem.at[0, m])

    def cotangent_copy(m):
        return pltpu.make_async_copy(cotangent.at[pl.ds(m * SEQ, SEQ)], bwd_in.at[m], in_sem.at[1, m])

    @pl.when(me == 0)
    def _():
        for m in range(micros):
            token_copy(m).start()

    def weights_start(l):
        for k, (_, count) in enumerate(KINDS):
            for j in range(count):
                weight_copy(l, k, j).start()

    weights_start(0)

    @pl.when(me > 0)
    def _():
        weights_start(1)


    @pl.when(me == last)
    def _():
        for m in range(micros):
            cotangent_copy(m).start()

    def forward_copy(m):
        return pltpu.make_async_remote_copy(
            src_ref=fwd_out.at[m],
            dst_ref=fwd_in.at[m],
            send_sem=fwd_send.at[m],
            recv_sem=fwd_recv.at[m],
            device_id={"pipe": lax.rem(me + 1, sections)},
            device_id_type=MESH,
        )

    def backward_copy(m):
        return pltpu.make_async_remote_copy(
            src_ref=bwd_out.at[m],
            dst_ref=bwd_in.at[m],
            send_sem=bwd_send.at[m],
            recv_sem=bwd_recv.at[m],
            device_id={"pipe": lax.rem(me + sections - 1, sections)},
            device_id_type=MESH,
        )

    def slots_of(m):
        return pl.ds(pl.multiple_of(m * SEQ, SEQ), SEQ)

    def fin_source(m, j):
        return fwd_out.at[m, :, pl.ds(window_start(j, width), FIN_WINDOW)]

    def fin_copy(m, j):
        return pltpu.make_async_remote_copy(
            src_ref=fin_source(m, j),
            dst_ref=fin_out.at[slots_of(m)],
            send_sem=fin_send.at[m, j],
            recv_sem=fin_recv.at[m],
            device_id={"pipe": j},
            device_id_type=MESH,
        )

    def own_fin_copy(m):
        return pltpu.make_async_copy(fin_source(m, last), fin_out.at[slots_of(m)], fin_send.at[m, last])

    def inp_copy(m):
        return pltpu.make_async_copy(bwd_out.at[m], inp_out.at[slots_of(m)], inp_send.at[m])


    outs = (u_out, dqkv_out, o_out, da_out, u2_out, dz_out, act_out, dm_out)

    def out_copy(kind, l, m):
        slot = l
        src = (
            u_s.at[l, m],
            qkv_s.at[l, m],
            o_s.at[slot],
            da_s.at[slot],
            u2_s.at[l, m],
            gp_s.at[l, m],
            act_s.at[slot],
            dm_s.at[l, m],
        )[kind]
        return pltpu.make_async_copy(src, outs[kind].at[l, pl.ds(m * SEQ, SEQ)], out_sem.at[kind, l, m])

    def partner(l):
        return {"dp": lax.select(l == 1, replica + 2 - 4 * x, replica + 4 - 8 * y)}

    def act_copy(l, m, b):
        block = l * (2 * b + 1 - x) + (1 - l) * (2 * (1 - y) + b)
        return pltpu.make_async_remote_copy(
            src_ref=act_out.at[l, slots_of(m), block_rows(block)],
            dst_ref=act_other.at[l, slots_of(m), pl.ds(b * D, D)],
            send_sem=act_send.at[l, m, b],
            recv_sem=act_recv.at[l, m, b],
            device_id=partner(l),
            device_id_type=MESH,
        )

    def act_start(l, m):
        if paired:
            for b in range(2):
                act_copy(l, m, b).start()

    def dm_copy(l, m):
        return pltpu.make_async_remote_copy(
            src_ref=dm_s.at[l, m],
            dst_ref=dm_other.at[l, slots_of(m)],
            send_sem=dm_send.at[l, m],
            recv_sem=dm_recv.at[l, m],
            device_id=partner(l),
            device_id_type=MESH,
        )

    def free_slot(kind, l, m):
        @pl.when(m > 0)
        def _():
            out_copy(kind, l, m - 1).wait()
            if kind == 6:
                act_start(l, m - 1)

    row = lax.broadcasted_iota(jnp.int32, (SEQ, SEQ), 0) // (SEQ // 4)
    column = lax.broadcasted_iota(jnp.int32, (SEQ, SEQ), 1) // (SEQ // 4)
    same = (row == column).astype(F32)
    for m in range(micros):
        parted = (jnp.full((1, SEQ), groups[m], jnp.int32) == 1).astype(F32)
        valid = jnp.broadcast_to((flags[m : m + 1, :] == 1).astype(F32), (SEQ, SEQ)).T
        keep = jnp.maximum(same, 1.0 - parted) * valid
        bias[m] = (keep - 1.0) * 1e30

    def forward_layer(l, m):
        def weight_wait(k):
            @pl.when((m == 0) & (me < last))
            def _():
                for j in range(KINDS[k][1]):
                    weight_copy(l, k, j).wait()

        x = state[...]
        xhat, inverse = norm_parts(x)
        stat_s[l, m, :, 0:1] = inverse
        u = (xhat * gain_one[pl.ds(l, 1), :]).astype(BF16)
        u_s[l, m] = u
        out_copy(0, l, m).start()
        weight_wait(0)
        for j in range(3):
            qkv_s[l, m, :, j * D : (j + 1) * D] = nn(u_s[l, m], weights[l, block_rows(j)]).astype(BF16)
        free_slot(2, l, m)
        slot = l
        added = bias[m]
        scores, tiles = [], [None] * 6
        for tile, count, inside in WINDOWS:
            lo, hi = tile * 128, (tile + count) * 128
            keys = two_heads(qkv_s[l, m, :, D + lo : D + hi], inside)
            scores.append(nt(keys, qkv_s[l, m, :, lo:hi]) * (SCALE * LOG2E))
        for j in range(len(WINDOWS)):
            for h in range(2):
                s = scores[j][h * SEQ : (h + 1) * SEQ] + added
                e = jnp.exp2(s - jnp.max(s, axis=0, keepdims=True))
                p = e * (1.0 / jnp.sum(e, axis=0, keepdims=True))
                p_s[l, m, 2 * j + h] = p.astype(BF16)
        for j, (tile, count, inside) in enumerate(WINDOWS):
            lo, hi = tile * 128, (tile + count) * 128
            values = two_heads(qkv_s[l, m, :, 2 * D + lo : 2 * D + hi], inside)
            p = jnp.concatenate([p_s[l, m, 2 * j], p_s[l, m, 2 * j + 1]], axis=0)
            add_window(tiles, tile, tn(p, values))
        for i in range(6):
            o_s[slot, :, i * 128 : (i + 1) * 128] = tiles[i].astype(BF16)
        out_copy(2, l, m).start()
        weight_wait(1)

        @pl.when((m == 0) & (me == 0) & (l == 0))
        def _():
            weights_start(1)

        h = state[...] + nn(o_s[slot], weights[l, block_rows(3)])
        state[...] = h
        hhat, inverse = norm_parts(h)
        stat_s[l, m, :, 1:2] = inverse
        u2_s[l, m] = (hhat * gain_two[pl.ds(l, 1), :]).astype(BF16)
        out_copy(4, l, m).start()
        weight_wait(2)

        @pl.when((m == 0) & (l == 0))
        def _():
            pl.semaphore_wait(barrier, sections - 1 + 2 * paired)

        free_slot(6, l, m)
        weight_wait(3)
        for j in range(4):
            act, slope = gelu_parts(nn(u2_s[l, m], weights[l, block_rows(4 + j)]))
            act_s[slot, :, j * D : (j + 1) * D] = act.astype(BF16)
            gp_s[l, m, :, j * D : (j + 1) * D] = slope.astype(BF16)
        state[...] = state[...] + nn(act_s[slot], weights[l, block_rows(8, 4)])
        out_copy(6, l, m).start()

    def norm_back(du, hat_scaled, gain, inverse):
        t = du * gain
        hat = hat_scaled * (1.0 / gain)
        weighted = du * hat_scaled
        return inverse * (
            t - jnp.mean(t, axis=-1, keepdims=True) - hat * jnp.mean(weighted, axis=-1, keepdims=True)
        ), weighted

    def add_rows(at, weighted):
        part = weighted[0:8]
        for r in range(8, SEQ, 8):
            part = part + weighted[r : r + 8]
        acc[at] = acc[at] + part

    def backward_layer(l, m):
        slot = l
        held = lax.select(me == last, 1 - l, l)

        def turned_wait(k):
            @pl.when((m == 0) & (me == last))
            def _():
                swap_copy(l, k).wait()

        dy = state[...]
        turned_wait(3)
        turned_wait(2)
        dm_s[l, m] = dy.astype(BF16)
        out_copy(7, l, m).start()
        if paired:
            dm_copy(l, m).start()
        for j in range(4):
            da = nn(dm_s[l, m], weights[held, block_rows(8 + j)])
            dz = gp_s[l, m, :, j * D : (j + 1) * D].astype(F32) * da
            gp_s[l, m, :, j * D : (j + 1) * D] = dz.astype(BF16)
        out_copy(5, l, m).start()
        dh, weighted = norm_back(
            nn(gp_s[l, m], weights[held, block_rows(4, 4)]), u2_s[l, m].astype(F32), gain_two[pl.ds(l, 1), :], stat_s[l, m, :, 1:2]
        )
        add_rows(2 + l, weighted)
        dh = state[...] + dh
        state[...] = dh
        free_slot(3, l, m)
        da_s[slot] = dh.astype(BF16)
        out_copy(3, l, m).start()
        turned_wait(1)
        turned_wait(0)
        do = nn(da_s[slot], weights[held, block_rows(3)]).astype(BF16)
        slopes, products = [], []
        q_tiles, k_tiles, v_tiles = [None] * 6, [None] * 6, [None] * 6
        for tile, count, inside in WINDOWS:
            lo, hi = tile * 128, (tile + count) * 128
            values = two_heads(qkv_s[l, m, :, 2 * D + lo : 2 * D + hi], inside)
            products.append(nt(values, do[:, lo:hi]))
        for j in range(len(WINDOWS)):
            for h in range(2):
                p = p_s[l, m, 2 * j + h].astype(F32)
                dp = products[j][h * SEQ : (h + 1) * SEQ]
                slopes.append((p * (dp - jnp.sum(p * dp, axis=0, keepdims=True))).astype(BF16))
        for j, (tile, count, inside) in enumerate(WINDOWS):
            lo, hi = tile * 128, (tile + count) * 128
            pair = slopes[2 * j : 2 * j + 2]
            keys = two_heads(qkv_s[l, m, :, D + lo : D + hi], inside)
            query = two_heads(qkv_s[l, m, :, lo:hi], inside)
            add_window(q_tiles, tile, tn(jnp.concatenate(pair, axis=0), keys))
            add_window(k_tiles, tile, nn(jnp.concatenate(pair, axis=1), query))
        for j, (tile, count, inside) in enumerate(WINDOWS):
            given = two_heads(do[:, tile * 128 : (tile + count) * 128], inside)
            p = jnp.concatenate([p_s[l, m, 2 * j], p_s[l, m, 2 * j + 1]], axis=1)
            add_window(v_tiles, tile, nn(p, given))
        for i in range(6):
            at = i * 128
            qkv_s[l, m, :, at : at + 128] = (q_tiles[i] * SCALE).astype(BF16)
            qkv_s[l, m, :, D + at : D + at + 128] = (k_tiles[i] * SCALE).astype(BF16)
            qkv_s[l, m, :, 2 * D + at : 2 * D + at + 128] = v_tiles[i].astype(BF16)
        out_copy(1, l, m).start()
        du = nn(qkv_s[l, m], weights[held, block_rows(0, 3)])
        dx, weighted = norm_back(
            du, u_s[l, m].astype(F32), gain_one[pl.ds(l, 1), :], stat_s[l, m, :, 0:1]
        )
        add_rows(l, weighted)
        state[...] = state[...] + dx

    @pl.when(me == last)
    def _():
        def make(l, k, j):
            b = KINDS[k][0] + j
            weight_copy(l, k, j).wait()
            turn(l, b)
            turned_copy(l, b).start()

        def again(l, k, j):
            turned_copy(l, KINDS[k][0] + j).wait()
            weight_copy(l, k, j).start()

        def ready(l, k, j):
            weight_copy(l, k, j).wait()

        for action in (make, again, ready):

            def one(l, c):
                each_block(l, action)
                return c

            lax.fori_loop(0, 2, one, 0)

    def forward_micro(m, carry):
        @pl.when(me == 0)
        def _():
            token_copy(m).wait()

        @pl.when(me > 0)
        def _():
            forward_copy(m).wait_recv()

        state[...] = fwd_in[m].astype(F32)

        def one(l, c):
            forward_layer(l, m)

            @pl.when((m == micros - 1) & (me == last))
            def _():
                for k in (3, 2, 1, 0):
                    swap_copy(1 - l, k).start()

            return c

        lax.fori_loop(0, 2, one, 0)

        fwd_out[m] = state[...].astype(BF16)

        @pl.when(me < last)
        def _():
            forward_copy(m).start()

        @pl.when(me == last)
        def _():
            own_fin_copy(m).start()
            for j in range(last):
                fin_copy(m, j).start()

        return carry

    lax.fori_loop(0, micros, forward_micro, 0)
    for l in range(2):
        out_copy(6, l, micros - 1).wait()
        act_start(l, micros - 1)

    @pl.when(me < last)
    def _():
        def one(i, c):
            turn(1 - i // BLOCKS, lax.rem(i, BLOCKS))
            return c

        lax.fori_loop(0, 2 * BLOCKS, one, 0)

    acc[...] = jnp.zeros_like(acc)

    def backward_micro(m, carry):
        @pl.when(me == last)
        def _():
            cotangent_copy(m).wait()

        @pl.when(me < last)
        def _():
            backward_copy(m).wait_recv()

        state[...] = bwd_in[m].astype(F32)

        def one(i, c):
            backward_layer(1 - i, m)
            return c

        lax.fori_loop(0, 2, one, 0)

        bwd_out[m] = state[...].astype(BF16)

        @pl.when(me > 0)
        def _():
            backward_copy(m).start()

        @pl.when(me == 0)
        def _():
            inp_copy(m).start()

        return carry

    lax.fori_loop(0, micros, backward_micro, 0)

    share = D // replicas
    for k in range(4):
        gain = (gain_one, gain_two)[k // 2][k % 2 : k % 2 + 1, :]
        total = jnp.sum(acc[k], axis=0, keepdims=True) / gain
        for r in range(replicas):
            gains_out[r, k : k + 1, 0:share] = total[:, r * share : (r + 1) * share]

    for l in range(2):
        for kind in (2, 3):
            out_copy(kind, l, micros - 1).wait()
        for m in range(micros):
            for kind in (0, 1, 4, 5, 7):
                out_copy(kind, l, m).wait()
            if paired:
                for b in range(2):
                    act_copy(l, m, b).wait()
                dm_copy(l, m).wait()
    for m in range(micros):

        @pl.when(me < last)
        def _():
            forward_copy(m).wait_send()

        @pl.when(me > 0)
        def _():
            backward_copy(m).wait_send()

        @pl.when(me == last)
        def _():
            for j in range(last):
                fin_copy(m, j).wait_send()
            own_fin_copy(m).wait()

        @pl.when(me < last)
        def _():
            fin_copy(m, last).wait_recv()

        @pl.when(me == 0)
        def _():
            inp_copy(m).wait()


def relay(tokens, cotangent, flags, groups, gain_one, gain_two, wqkv, wout, wup, wdown):
    sections = lax.axis_size("pipe")
    replicas = lax.axis_size("dp")
    rows = tokens.shape[0]
    micros = rows // SEQ
    width = D // sections
    paired = replicas == SHARDS
    anywhere = pl.BlockSpec(memory_space=pl.ANY)
    vmem = pl.BlockSpec(memory_space=pltpu.VMEM)
    smem = pl.BlockSpec(memory_space=pltpu.SMEM)
    dma = pltpu.SemaphoreType.DMA

    def factor(columns):
        return jax.ShapeDtypeStruct((2, rows, columns), BF16)

    def saved(columns):
        return pltpu.VMEM((2, micros, SEQ, columns), BF16)

    def two(columns):
        return pltpu.VMEM((2, SEQ, columns), BF16)

    def per_micro(columns):
        return pltpu.VMEM((micros, SEQ, columns), BF16)

    return pl.pallas_call(
        functools.partial(relay_kernel, sections, replicas, micros, paired),
        out_shape=(
            jax.ShapeDtypeStruct((rows, FIN_WINDOW), BF16),
            jax.ShapeDtypeStruct((rows, D), BF16),
            jax.ShapeDtypeStruct((replicas, 8, 128), F32),
            factor(D),
            factor(3 * D),
            factor(D),
            factor(D),
            factor(D),
            factor(FF),
            factor(FF),
            factor(D),
            factor(2 * D),
            factor(D),
            jax.ShapeDtypeStruct((2, BLOCKS * D, D), BF16),
        ),
        in_specs=[anywhere, anywhere, vmem, smem, vmem, vmem] + [anywhere] * 4,
        out_specs=(anywhere, anywhere, vmem) + (anywhere,) * 11,
        scratch_shapes=[
            pltpu.VMEM((2, BLOCKS * D, D), BF16),
            per_micro(D),
            per_micro(D),
            per_micro(D),
            per_micro(D),
            saved(D),
            saved(3 * D),
            pltpu.VMEM((2, micros, HEADS, SEQ, SEQ), BF16),
            saved(D),
            saved(FF),
            pltpu.VMEM((2, micros, SEQ, 128), F32),
            two(D),
            two(FF),
            saved(D),
            two(D),
            pltpu.VMEM((SEQ, D), F32),
            pltpu.VMEM((4, 8, D), F32),
            pltpu.VMEM((micros, SEQ, SEQ), F32),
            dma((2, BLOCKS)),
            dma((2, BLOCKS)),
            dma((2, len(KINDS))),
            dma((2, micros)),
            dma((micros,)),
            dma((micros,)),
            dma((micros,)),
            dma((micros,)),
            dma((micros, sections)),
            dma((micros,)),
            dma((micros,)),
            dma((8, 2, micros)),
            dma((2, micros, 2)),
            dma((2, micros, 2)),
            dma((2, micros)),
            dma((2, micros)),
        ],
        compiler_params=pltpu.CompilerParams(
            collective_id=0, has_side_effects=True, vmem_limit_bytes=60 * MIB
        ),
        name="relay",
    )(tokens, cotangent, flags, groups, gain_one, gain_two, wqkv, wout, wup, wdown)


ROWS = 96
CHUNKS = 12
ORDER = (3, 0, 1, 2) + tuple(range(4, CHUNKS))

GUESTS = (1, 2)


def sum_kernel(
    sections,
    gains_in,
    fin_in,
    inp_in,
    u_in,
    dqkv_in,
    o_in,
    da_in,
    u2_in,
    dz_in,
    act_in,
    dm_in,
    act_other,
    dm_other,
    gains_out,
    fin_out,
    inp_out,
    qkv_out,
    out_out,
    up_out,
    down_out,
    u_v,
    dqkv_v,
    o_v,
    da_v,
    u2_v,
    dz_v,
    act_v,
    dm_v,
    own,
    first,
    second,
    third,
    gains_v,
    fin_v,
    fin_t,
    inp_v,
    inp_stage,
    load_sem,
    gain_send,
    gain_recv,
    fin_sem,
    inp_send,
    inp_recv,
    lend_send,
    lend_recv,
    back_send,
    back_recv,
    send,
    recv,
    out_sem,
):
    me = lax.axis_index("dp")
    section = lax.axis_index("pipe")
    core = lax.rem(me, 2)
    x = lax.rem(me // 2, 2)
    y = me // 4
    other_core = me + 1 - 2 * core
    other_x = me + 2 - 4 * x
    other_y = me + 4 - 8 * y

    barrier = pltpu.get_barrier_semaphore()
    for j in range(SHARDS):

        @pl.when(me != j)
        def _():
            pl.semaphore_signal(barrier, inc=1, device_id={"dp": j}, device_id_type=MESH)

    @pl.when(section > 0)
    def _():
        pl.semaphore_signal(barrier, inc=1, device_id={"pipe": 0}, device_id_type=MESH)

    sources = (u_in, dqkv_in, o_in, da_in, u2_in, dz_in)
    held = (u_v, dqkv_v, o_v, da_v, u2_v, dz_v)
    rows = dm_in.shape[1]

    def load(k, l):
        return pltpu.make_async_copy(sources[k].at[l], held[k], load_sem.at[k])

    def down_loads(l):
        copies = [(dm_in.at[l], dm_v.at[0:rows]), (dm_other.at[l], dm_v.at[rows : 2 * rows])]
        for b in range(2):
            block = l * (2 * b + x) + (1 - l) * (2 * y + b)
            columns = pl.ds(pl.multiple_of(block * CHUNK, CHUNK), CHUNK)
            copies.append((act_in.at[l, :, columns], act_v.at[b, 0:rows]))
            copies.append((act_other.at[l, :, pl.ds(b * CHUNK, CHUNK)], act_v.at[b, rows : 2 * rows]))
        return [pltpu.make_async_copy(src, dst, load_sem.at[6 + k]) for k, (src, dst) in enumerate(copies)]

    for k in (2, 3, 0, 1, 4, 5):
        load(k, 1).start()
    for copy in down_loads(1):
        copy.start()

    def gain_copy(j, source):
        return pltpu.make_async_remote_copy(
            src_ref=gains_in.at[j],
            dst_ref=gains_v.at[source],
            send_sem=gain_send.at[j],
            recv_sem=gain_recv.at[source],
            device_id={"dp": j},
            device_id_type=MESH,
        )

    def inp_copy(j):
        return pltpu.make_async_remote_copy(
            src_ref=inp_stage.at[j],
            dst_ref=inp_out,
            send_sem=inp_send.at[j],
            recv_sem=inp_recv,
            device_id={"pipe": j},
            device_id_type=MESH,
        )

    def own_inp_copy():
        return pltpu.make_async_copy(inp_stage.at[0], inp_out, inp_send.at[0])

    def inp_load():
        return pltpu.make_async_copy(inp_in, inp_v, inp_send.at[0])

    def meet():
        pl.semaphore_wait(barrier, SHARDS - 1 + lax.select(section == 0, sections - 1, 0))
        for j in range(SHARDS):

            @pl.when(me != j)
            def _():
                gain_copy(j, me).start()


    def remote(src, dst, step, n, to):
        return pltpu.make_async_remote_copy(
            src_ref=src,
            dst_ref=dst,
            send_sem=send.at[step, n],
            recv_sem=recv.at[step, n],
            device_id={"dp": to},
            device_id_type=MESH,
        )

    def give_copy(n, i):
        if i >= 8:
            return remote(own.at[i, 1 - core, 0], first.at[n, 0], 0, n, other_core)
        return remote(own.at[i, 1 - core], first.at[n], 0, n, other_core)

    def down_copy(n, l):
        mine, to = lax.select(l == 1, y, x), lax.select(l == 1, other_y, other_x)
        return remote(first.at[n, 0, 1 - mine], third.at[n], 2, n, to)

    def first_copy(n, i):
        if i % 2 == 0:
            return remote(first.at[n, :, 1 - x], second.at[n], 1, n, other_x)
        return remote(first.at[n, 1 - y], second.at[n], 1, n, other_y)

    def second_copy(n, i):
        if i % 2 == 0:
            return remote(second.at[n, 1 - y], third.at[n], 2, n, other_y)
        return remote(second.at[n, 1 - x], third.at[n], 2, n, other_x)

    host = sections - 1
    guests = GUESTS if sections > 2 else ()

    def lend_copy(g):
        return pltpu.make_async_remote_copy(
            src_ref=first.at[guests[g]],
            dst_ref=first.at[2 * CHUNKS + g],
            send_sem=lend_send.at[g],
            recv_sem=lend_recv.at[g],
            device_id={"pipe": host},
            device_id_type=MESH,
        )

    def back_copy(g):
        return pltpu.make_async_remote_copy(
            src_ref=third.at[2 * CHUNKS + g],
            dst_ref=third.at[guests[g]],
            send_sem=back_send.at[g],
            recv_sem=back_recv.at[g],
            device_id={"pipe": 0},
            device_id_type=MESH,
        )

    def lent_or(step, i, lent, kept):
        if i not in guests:
            kept()
            return
        away = (step == 0) & (section == 0)
        pl.when(away)(functools.partial(lent, guests.index(i)))
        pl.when(jnp.logical_not(away))(kept)

    def result_copy(n, l, i):
        if i < 3:
            dst = qkv_out.at[l, :, pl.ds(i * CHUNK, CHUNK)]
        elif i < 4:
            dst = out_out.at[l]
        elif i < 8:
            dst = up_out.at[l, :, pl.ds((i - 4) * CHUNK, CHUNK)]
        else:
            dst = down_out.at[l, pl.ds((i - 8) * ROWS, ROWS)]
        return pltpu.make_async_copy(third.at[n], dst, out_sem.at[n])

    def add_core(n, l, i):
        give_copy(n, i).wait_recv()
        if i >= 8:
            first[n, 0] = first[n, 0] + own[i, core, 0]
            down_copy(n, l).start()
        else:
            first[n] = first[n] + own[i, core]
            lent_or(1 - l, i, lambda g: lend_copy(g).start(), lambda: first_copy(n, i).start())

    def layer_products(step, carry):
        l = 1 - step
        base = step * CHUNKS

        def free(i):
            @pl.when(step > 0)
            def _():
                give_copy(i, i).wait_send()

        def products(k, a, g, slots):
            load(k, l).wait()
            load(k + 1, l).wait()
            for i, columns in slots:
                free(i)
                part = tn(a[...], g[:, columns * CHUNK : (columns + 1) * CHUNK]).astype(BF16)
                for r in range(SHARDS):
                    own[i, r % 2, r // 4, (r // 2) % 2] = part[r * ROWS : (r + 1) * ROWS]
                if i == ORDER[0]:
                    pl.when(step == 0)(meet)
                give_copy(base + i, i).start()
                if i != ORDER[0]:
                    before = ORDER[ORDER.index(i) - 1]
                    add_core(base + before, l, before)

        def reload(k):
            @pl.when(step == 0)
            def _():
                load(k, 0).start()
                load(k + 1, 0).start()

        products(2, o_v, da_v, ((3, 0),))
        reload(2)
        products(0, u_v, dqkv_v, ((0, 0), (1, 1), (2, 2)))
        reload(0)
        products(4, u2_v, dz_v, ((4, 0), (5, 1), (6, 2), (7, 3)))
        reload(4)
        for copy in down_loads(l):
            copy.wait()
        for i in range(8, CHUNKS):
            free(i)
        for b in range(2):
            part = tn(act_v[b], dm_v[...]).astype(BF16)
            for r in range(8):
                own[8 + r % 4, r // 4, 0, b] = part[r * ROWS : (r + 1) * ROWS]

        @pl.when(step == 0)
        def _():
            for copy in down_loads(0):
                copy.start()

        for i in range(8, CHUNKS):
            give_copy(base + i, i).start()
        for i in ORDER[7:]:
            add_core(base + i, l, i)
        return carry

    lax.fori_loop(0, 2, layer_products, 0)

    fin_load = pltpu.make_async_copy(fin_in, fin_v, fin_sem)
    fin_load.start()
    fin_load.wait()
    width = D // sections
    for j in range(sections):
        first_lane = j * width - window_start(j, width)

        @pl.when(section == j)
        def _():
            for r in range(0, rows, SEQ):
                part = fin_v[r : r + SEQ, :].astype(F32)[:, first_lane : first_lane + width]
                fin_t[:, r : r + SEQ] = part.T.astype(BF16)

    fin_store = pltpu.make_async_copy(fin_t, fin_out, fin_sem)
    fin_store.start()

    @pl.when(section == 0)
    def _():
        inp_load().start()
        inp_load().wait()
        for j in range(sections):
            for r in range(0, rows, SEQ):
                part = inp_v[r : r + SEQ, :].astype(F32)[:, j * width : (j + 1) * width]
                inp_stage[j, :, r : r + SEQ] = part.T.astype(BF16)
        own_inp_copy().start()
        for j in range(1, sections):
            inp_copy(j).start()

    for g, i in enumerate(guests):

        @pl.when(section == host)
        def _():
            lend_copy(g).wait_recv()
            first_copy(2 * CHUNKS + g, i).start()

    def second_sum(n, i):
        first_copy(n, i).wait_recv()
        kept = first[n, :, x] if i % 2 == 0 else first[n, y]
        second[n] = second[n] + kept
        second_copy(n, i).start()

    def second_sums(step, carry):
        for i in ORDER[:8]:
            n = step * CHUNKS + i
            lent_or(step, i, lambda g: None, functools.partial(second_sum, n, i))
        return carry

    lax.fori_loop(0, 2, second_sums, 0)
    for g, i in enumerate(guests):
        pl.when(section == host)(functools.partial(second_sum, 2 * CHUNKS + g, i))

    gains_v[me] = gains_in[me]
    for j in range(SHARDS):

        @pl.when(me != j)
        def _():
            gain_copy(j, j).wait_recv()

    total = gains_v[0]
    for j in range(1, SHARDS):
        total = total + gains_v[j]
    gains_out[...] = total

    def last_sum(n, i):
        second_copy(n, i).wait_recv()
        third[n] = third[n] + second[n, y if i % 2 == 0 else x]

    def last_sums(step, carry):
        for i in ORDER:
            n = step * CHUNKS + i
            if i >= 8:
                down_copy(n, 1 - step).wait_recv()
                third[n] = third[n] + first[n, 0, lax.select(step == 0, y, x)]
            else:
                lent_or(step, i, lambda g: None, functools.partial(last_sum, n, i))
            if i not in guests:
                result_copy(n, 1 - step, i).start()
        return carry

    lax.fori_loop(0, 2, last_sums, 0)

    for g, i in enumerate(guests):

        @pl.when(section == host)
        def _():
            last_sum(2 * CHUNKS + g, i)
            back_copy(g).start()

        @pl.when(section == 0)
        def _():
            back_copy(g).wait_recv()

        for step in range(2):
            result_copy(step * CHUNKS + i, 1 - step, i).start()

    def finish(step, carry):
        for i in range(CHUNKS):
            n = step * CHUNKS + i
            if i >= 8:
                down_copy(n, 1 - step).wait_send()
            else:

                def sent():
                    first_copy(n, i).wait_send()
                    second_copy(n, i).wait_send()

                lent_or(step, i, lambda g: lend_copy(g).wait_send(), sent)
            result_copy(n, 1 - step, i).wait()
        return carry

    lax.fori_loop(0, 2, finish, 0)
    for g, i in enumerate(guests):

        @pl.when(section == host)
        def _():
            first_copy(2 * CHUNKS + g, i).wait_send()
            second_copy(2 * CHUNKS + g, i).wait_send()
            back_copy(g).wait_send()

    for i in range(CHUNKS):
        give_copy(CHUNKS + i, i).wait_send()
    for j in range(SHARDS):

        @pl.when(me != j)
        def _():
            gain_copy(j, me).wait_send()

    fin_store.wait()

    @pl.when(section == 0)
    def _():
        own_inp_copy().wait()
        for j in range(1, sections):
            inp_copy(j).wait_send()

    @pl.when(section > 0)
    def _():
        inp_copy(0).wait_recv()


def summed(gains, fin, inp, *factors):
    sections = lax.axis_size("pipe")
    rows, width = inp.shape[0], D // sections
    anywhere = pl.BlockSpec(memory_space=pl.ANY)
    vmem = pl.BlockSpec(memory_space=pltpu.VMEM)
    dma = pltpu.SemaphoreType.DMA
    total = 2 * CHUNKS
    slots = total + len(GUESTS)

    def shard(height, columns):
        return jax.ShapeDtypeStruct((2, height, columns), BF16)

    return pl.pallas_call(
        functools.partial(sum_kernel, sections),
        out_shape=(
            jax.ShapeDtypeStruct((8, 128), F32),
            jax.ShapeDtypeStruct((width, rows), BF16),
            jax.ShapeDtypeStruct((width, rows), BF16),
            shard(ROWS, 3 * D),
            shard(ROWS, D),
            shard(ROWS, FF),
            shard(4 * ROWS, D),
        ),
        in_specs=[vmem] + [anywhere] * 12,
        out_specs=(vmem,) + (anywhere,) * 6,
        scratch_shapes=[pltpu.VMEM((rows, f.shape[2]), BF16) for f in factors[:6]]
        + [
            pltpu.VMEM((2, 2 * rows, CHUNK), BF16),
            pltpu.VMEM((2 * rows, D), BF16),
            pltpu.VMEM((CHUNKS, 2, 2, 2, ROWS, CHUNK), BF16),
            pltpu.VMEM((slots, 2, 2, ROWS, CHUNK), BF16),
            pltpu.VMEM((slots, 2, ROWS, CHUNK), BF16),
            pltpu.VMEM((slots, ROWS, CHUNK), BF16),
            pltpu.VMEM((SHARDS, 8, 128), F32),
            pltpu.VMEM((rows, FIN_WINDOW), BF16),
            pltpu.VMEM((width, rows), BF16),
            pltpu.VMEM((rows, D), BF16),
            pltpu.VMEM((sections, width, rows), BF16),
            dma((12,)),
            dma((SHARDS,)),
            dma((SHARDS,)),
            dma(()),
            dma((sections,)),
            dma(()),
            dma((len(GUESTS),)),
            dma((len(GUESTS),)),
            dma((len(GUESTS),)),
            dma((len(GUESTS),)),
            dma((3, slots)),
            dma((3, slots)),
            dma((total,)),
        ],
        compiler_params=pltpu.CompilerParams(
            collective_id=1, has_side_effects=True, vmem_limit_bytes=60 * MIB
        ),
        name="sum",
    )(gains, fin, inp, *factors)


def write_kernel(count, share, gains, *refs):
    gain_one, gain_two = refs[count], refs[count + 1]
    gain_one[...] = gains[0:2, 0:share]
    gain_two[...] = gains[2:4, 0:share]
    sources, results, held, wide = (
        refs[:count],
        refs[count + 2 : 2 * count + 2],
        refs[2 * count + 2 : 3 * count + 2],
        refs[3 * count + 2 : 4 * count + 2],
    )
    load_sem, store_sem = refs[4 * count + 2 :]
    loads = [pltpu.make_async_copy(sources[k], held[k], load_sem.at[k]) for k in range(count)]
    stores = [pltpu.make_async_copy(wide[k], results[k], store_sem.at[k]) for k in range(count)]
    for load in loads:
        load.start()
    for k in range(count):
        loads[k].wait()
        wide[k][...] = held[k][...].astype(wide[k].dtype)
        stores[k].start()
    for store in stores:
        store.wait()


def written(gains, share, arrays, types):
    count = len(arrays)
    anywhere = pl.BlockSpec(memory_space=pl.ANY)
    vmem = pl.BlockSpec(memory_space=pltpu.VMEM)
    return pl.pallas_call(
        functools.partial(write_kernel, count, share),
        out_shape=(jax.ShapeDtypeStruct((2, share), F32),) * 2
        + tuple(jax.ShapeDtypeStruct(a.shape, t) for a, t in zip(arrays, types)),
        in_specs=[vmem] + [anywhere] * count,
        out_specs=(vmem, vmem) + (anywhere,) * count,
        scratch_shapes=[pltpu.VMEM(a.shape, a.dtype) for a in arrays]
        + [pltpu.VMEM(a.shape, t) for a, t in zip(arrays, types)]
        + [pltpu.SemaphoreType.DMA((count,)), pltpu.SemaphoreType.DMA((count,))],
        compiler_params=pltpu.CompilerParams(vmem_limit_bytes=60 * MIB),
        name="write",
    )(gains, *arrays)


def body(
    tokens,
    gain_one,
    qkv_weight,
    out_weight,
    gain_two,
    up_weight,
    down_weight,
    cotangent,
    flags,
    groups,
):
    micros = tokens.shape[0] // SEQ
    fin, inp, gains, u, dqkv, o, da, u2, dz, act, dm, act_other, dm_other, _ = relay(
        tokens,
        cotangent,
        flags.reshape(micros, SEQ),
        groups,
        gain_one,
        gain_two,
        qkv_weight,
        out_weight,
        up_weight,
        down_weight,
    )

    replicas = lax.axis_size("dp")
    share = D // replicas
    if replicas == SHARDS and share == ROWS:
        gains, fin, inp, g_qkv, g_out, g_up, g_down = summed(
            gains, fin, inp, u, dqkv, o, da, u2, dz, act, dm, act_other, dm_other
        )
    else:

        def grad(a, g):
            total = jnp.einsum("lsa,lsb->lab", a, g, preferred_element_type=F32).astype(BF16)
            return lax.psum_scatter(total, "dp", scatter_dimension=1, tiled=True)

        gains = lax.psum_scatter(gains, "dp", scatter_dimension=0)
        sections = lax.axis_size("pipe")
        width = D // sections
        first_lanes = jnp.array([j * width - window_start(j, width) for j in range(sections)])
        fin = lax.dynamic_slice_in_dim(fin, first_lanes[lax.axis_index("pipe")], width, 1).T
        inp = jnp.where(lax.axis_index("pipe") == 0, inp.T, jnp.zeros_like(inp.T))
        inp = lax.psum_scatter(inp, "pipe", scatter_dimension=0, tiled=True)
        g_qkv, g_out, g_up, g_down = grad(u, dqkv), grad(o, da), grad(u2, dz), grad(act, dm)
    gain_one_grad, gain_two_grad, fin, inp, g_qkv, g_out, g_up, g_down = written(
        gains, share, (fin, inp, g_qkv, g_out, g_up, g_down), (BF16,) + (F32,) * 5
    )
    return (fin.T, inp.T, gain_one_grad, g_qkv, g_out, gain_two_grad, g_up, g_down)


def solution(mesh):
    return jax.shard_map(
        body,
        mesh=mesh,
        in_specs=(
            P("dp", None),
            P("pipe", None),
            P("pipe", None, None),
            P("pipe", None, None),
            P("pipe", None),
            P("pipe", None, None),
            P("pipe", None, None),
            P("dp", None),
            P("dp"),
            P("dp"),
        ),
        out_specs=(
            P("dp", "pipe"),
            P("dp", "pipe"),
            P("pipe", "dp"),
            P("pipe", "dp", None),
            P("pipe", "dp", None),
            P("pipe", "dp"),
            P("pipe", "dp", None),
            P("pipe", "dp", None),
        ),
        check_vma=False,
    )
```

```python
import functools

import jax
import jax.numpy as jnp
from jax import lax
from jax.experimental import pallas as pl
from jax.experimental.pallas import tpu as pltpu
from jax.sharding import PartitionSpec as P

D = 768
HEADS = 16
HEAD_DIM = 48
FF = 3072
SEQ = 128
EPS = 1e-06
MESH = pl.DeviceIdType.MESH
F32 = jnp.float32
BF16 = jnp.bfloat16
LOG2E = 1.4426950408889634
SCALE = HEAD_DIM ** (-0.5)
MIB = 2**20
CHUNK = 768
TILE = 256

KINDS = ((0, 3), (3, 1), (4, 4), (8, 4))
BLOCKS = 12

FIN_WINDOW = 256


def window_start(section, width):
    return min(section * width // 128 * 128, D - FIN_WINDOW)


SHARDS = 8

WINDOWS = tuple(
    (96 * j // 128, -(-(96 * j % 128 + 96) // 128), 96 * j % 128) for j in range(HEADS // 2)
)


def nn(a, b):
    return jnp.dot(a, b, preferred_element_type=F32)


def nt(a, b):
    return lax.dot_general(a, b, (((1,), (1,)), ((), ())), preferred_element_type=F32)


def tn(a, b):
    return lax.dot_general(a, b, (((0,), (0,)), ((), ())), preferred_element_type=F32)


def lanes_of_head(first, width):
    lane = lax.broadcasted_iota(jnp.int32, (SEQ, width), 1)
    return ((lane >= first) & (lane < first + HEAD_DIM)).astype(F32).astype(BF16)


def two_heads(window, first):
    width = window.shape[1]
    return jnp.concatenate(
        [window * lanes_of_head(first, width), window * lanes_of_head(first + HEAD_DIM, width)], axis=0
    )


def add_window(tiles, first, part):
    for i in range(part.shape[1] // 128):
        piece = part[:, i * 128 : (i + 1) * 128]
        tiles[first + i] = piece if tiles[first + i] is None else tiles[first + i] + piece


def norm_parts(x):
    centre = x - jnp.mean(x, axis=-1, keepdims=True)
    spread = jnp.mean(centre * centre, axis=-1, keepdims=True)
    inverse = lax.rsqrt(spread + EPS)
    return centre * inverse, inverse


def gelu_parts(z):
    phi = 0.5 * (1.0 + lax.erf(z * 0.7071067811865476))
    density = jnp.exp2(z * z * (-0.5 * LOG2E)) * 0.3989422804014327
    return z * phi, phi + z * density


def relay_kernel(
    sections,
    replicas,
    micros,
    paired,
    tokens,
    cotangent,
    flags,
    groups,
    gain_one,
    gain_two,
    wqkv_hbm,
    wout_hbm,
    wup_hbm,
    wdown_hbm,
    fin_out,
    inp_out,
    gains_out,
    u_out,
    dqkv_out,
    o_out,
    da_out,
    u2_out,
    dz_out,
    act_out,
    dm_out,
    u2_other,
    dm_other,
    turned_hbm,
    weights,
    fwd_in,
    fwd_out,
    bwd_in,
    bwd_out,
    u_s,
    qkv_s,
    p_s,
    u2_s,
    gp_s,
    stat_s,
    o_s,
    act_s,
    dm_s,
    da_s,
    state,
    acc,
    bias,
    w_sem,
    turn_sem,
    swap_sem,
    in_sem,
    fwd_send,
    fwd_recv,
    bwd_send,
    bwd_recv,
    fin_send,
    fin_recv,
    inp_send,
    out_sem,
    u2_send,
    u2_recv,
    dm_send,
    dm_recv,
):
    me = lax.axis_index("pipe")
    last = sections - 1
    width = D // sections

    barrier = pltpu.get_barrier_semaphore()
    for j in range(sections):

        @pl.when(me != j)
        def _():
            pl.semaphore_signal(barrier, inc=1, device_id={"pipe": j}, device_id_type=MESH)

    replica = lax.axis_index("dp")
    x, y = lax.rem(replica // 2, 2), replica // 4
    if paired:
        for j in (replica + 2 - 4 * x, replica + 4 - 8 * y):
            pl.semaphore_signal(barrier, inc=1, device_id={"dp": j}, device_id_type=MESH)

    def block_rows(b, count=1):
        start = b * D
        return pl.ds(start if isinstance(b, int) else pl.multiple_of(start, D), count * D)

    def weight_copy(l, k, j):
        first, _ = KINDS[k]
        if k == 1:
            src = wout_hbm.at[l]
        elif k == 3:
            src = wdown_hbm.at[l, block_rows(j)]
        else:
            src = (wqkv_hbm, None, wup_hbm)[k].at[l, :, block_rows(j)]
        return pltpu.make_async_copy(src, weights.at[l, block_rows(first + j)], w_sem.at[l, first + j])

    def turned_copy(l, b):
        return pltpu.make_async_copy(
            weights.at[l, block_rows(b)], turned_hbm.at[l, block_rows(b)], turn_sem.at[l, b]
        )

    def swap_copy(l, k):
        rows = block_rows(*KINDS[k])
        return pltpu.make_async_copy(turned_hbm.at[l, rows], weights.at[1 - l, rows], swap_sem.at[l, k])

    def turn(l, b):
        def tile(r, c):
            return l, pl.ds(pl.multiple_of(b * D + r * TILE, TILE), TILE), pl.ds(c * TILE, TILE)

        for r in range(D // TILE):
            weights[tile(r, r)] = weights[tile(r, r)].T
            for c in range(r):
                lower = weights[tile(r, c)].T
                upper = weights[tile(c, r)].T
                weights[tile(c, r)] = lower
                weights[tile(r, c)] = upper

    def each_block(l, action):
        for k, (_, count) in enumerate(KINDS):

            def one(j, c):
                action(l, k, j)
                return c

            lax.fori_loop(0, count, one, 0)

    def token_copy(m):
        return pltpu.make_async_copy(tokens.at[pl.ds(m * SEQ, SEQ)], fwd_in.at[m], in_sem.at[0, m])

    def cotangent_copy(m):
        return pltpu.make_async_copy(cotangent.at[pl.ds(m * SEQ, SEQ)], bwd_in.at[m], in_sem.at[1, m])

    @pl.when(me == 0)
    def _():
        for m in range(micros):
            token_copy(m).start()

    def weights_start(l):
        for k, (_, count) in enumerate(KINDS):
            for j in range(count):
                weight_copy(l, k, j).start()

    weights_start(0)

    @pl.when(me > 0)
    def _():
        weights_start(1)


    @pl.when(me == last)
    def _():
        for m in range(micros):
            cotangent_copy(m).start()

    def forward_copy(m):
        return pltpu.make_async_remote_copy(
            src_ref=fwd_out.at[m],
            dst_ref=fwd_in.at[m],
            send_sem=fwd_send.at[m],
            recv_sem=fwd_recv.at[m],
            device_id={"pipe": lax.rem(me + 1, sections)},
            device_id_type=MESH,
        )

    def backward_copy(m):
        return pltpu.make_async_remote_copy(
            src_ref=bwd_out.at[m],
            dst_ref=bwd_in.at[m],
            send_sem=bwd_send.at[m],
            recv_sem=bwd_recv.at[m],
            device_id={"pipe": lax.rem(me + sections - 1, sections)},
            device_id_type=MESH,
        )

    def slots_of(m):
        return pl.ds(pl.multiple_of(m * SEQ, SEQ), SEQ)

    def fin_source(m, j):
        return fwd_out.at[m, :, pl.ds(window_start(j, width), FIN_WINDOW)]

    def fin_copy(m, j):
        return pltpu.make_async_remote_copy(
            src_ref=fin_source(m, j),
            dst_ref=fin_out.at[slots_of(m)],
            send_sem=fin_send.at[m, j],
            recv_sem=fin_recv.at[m],
            device_id={"pipe": j},
            device_id_type=MESH,
        )

    def own_fin_copy(m):
        return pltpu.make_async_copy(fin_source(m, last), fin_out.at[slots_of(m)], fin_send.at[m, last])

    def inp_copy(m):
        return pltpu.make_async_copy(bwd_out.at[m], inp_out.at[slots_of(m)], inp_send.at[m])


    outs = (u_out, dqkv_out, o_out, da_out, u2_out, dz_out, act_out, dm_out)

    def out_copy(kind, l, m):
        slot = l
        src = (
            u_s.at[l, m],
            qkv_s.at[l, m],
            o_s.at[slot],
            da_s.at[slot],
            u2_s.at[l, m],
            gp_s.at[l, m],
            act_s.at[slot],
            dm_s.at[l, m],
        )[kind]
        return pltpu.make_async_copy(src, outs[kind].at[l, pl.ds(m * SEQ, SEQ)], out_sem.at[kind, l, m])

    def partner(l):
        return {"dp": lax.select(l == 1, replica + 2 - 4 * x, replica + 4 - 8 * y)}

    def u2_copy(l, m):
        return pltpu.make_async_remote_copy(
            src_ref=u2_s.at[l, m],
            dst_ref=u2_other.at[l, slots_of(m)],
            send_sem=u2_send.at[l, m],
            recv_sem=u2_recv.at[l, m],
            device_id=partner(l),
            device_id_type=MESH,
        )

    def dm_copy(l, m):
        return pltpu.make_async_remote_copy(
            src_ref=dm_s.at[l, m],
            dst_ref=dm_other.at[l, slots_of(m)],
            send_sem=dm_send.at[l, m],
            recv_sem=dm_recv.at[l, m],
            device_id=partner(l),
            device_id_type=MESH,
        )

    def free_slot(kind, l, m):
        @pl.when(m > 0)
        def _():
            out_copy(kind, l, m - 1).wait()

    row = lax.broadcasted_iota(jnp.int32, (SEQ, SEQ), 0) // (SEQ // 4)
    column = lax.broadcasted_iota(jnp.int32, (SEQ, SEQ), 1) // (SEQ // 4)
    same = (row == column).astype(F32)
    for m in range(micros):
        parted = (jnp.full((1, SEQ), groups[m], jnp.int32) == 1).astype(F32)
        valid = jnp.broadcast_to((flags[m : m + 1, :] == 1).astype(F32), (SEQ, SEQ)).T
        keep = jnp.maximum(same, 1.0 - parted) * valid
        bias[m] = (keep - 1.0) * 1e30

    def forward_layer(l, m):
        def weight_wait(k):
            @pl.when((m == 0) & (me < last))
            def _():
                for j in range(KINDS[k][1]):
                    weight_copy(l, k, j).wait()

        x = state[...]
        xhat, inverse = norm_parts(x)
        stat_s[l, m, :, 0:1] = inverse
        u = (xhat * gain_one[pl.ds(l, 1), :]).astype(BF16)
        u_s[l, m] = u
        out_copy(0, l, m).start()
        weight_wait(0)
        for j in range(3):
            qkv_s[l, m, :, j * D : (j + 1) * D] = nn(u_s[l, m], weights[l, block_rows(j)]).astype(BF16)
        free_slot(2, l, m)
        slot = l
        added = bias[m]
        scores, tiles = [], [None] * 6
        for tile, count, inside in WINDOWS:
            lo, hi = tile * 128, (tile + count) * 128
            keys = two_heads(qkv_s[l, m, :, D + lo : D + hi], inside)
            scores.append(nt(keys, qkv_s[l, m, :, lo:hi]) * (SCALE * LOG2E))
        for j in range(len(WINDOWS)):
            for h in range(2):
                s = scores[j][h * SEQ : (h + 1) * SEQ] + added
                e = jnp.exp2(s - jnp.max(s, axis=0, keepdims=True))
                p = e * (1.0 / jnp.sum(e, axis=0, keepdims=True))
                p_s[l, m, 2 * j + h] = p.astype(BF16)
        for j, (tile, count, inside) in enumerate(WINDOWS):
            lo, hi = tile * 128, (tile + count) * 128
            values = two_heads(qkv_s[l, m, :, 2 * D + lo : 2 * D + hi], inside)
            p = jnp.concatenate([p_s[l, m, 2 * j], p_s[l, m, 2 * j + 1]], axis=0)
            add_window(tiles, tile, tn(p, values))
        for i in range(6):
            o_s[slot, :, i * 128 : (i + 1) * 128] = tiles[i].astype(BF16)
        out_copy(2, l, m).start()
        weight_wait(1)

        @pl.when((m == 0) & (me == 0) & (l == 0))
        def _():
            weights_start(1)

        h = state[...] + nn(o_s[slot], weights[l, block_rows(3)])
        state[...] = h
        hhat, inverse = norm_parts(h)
        stat_s[l, m, :, 1:2] = inverse
        u2_s[l, m] = (hhat * gain_two[pl.ds(l, 1), :]).astype(BF16)
        out_copy(4, l, m).start()

        @pl.when((m == 0) & (l == 0))
        def _():
            pl.semaphore_wait(barrier, sections - 1 + 2 * paired)

        if paired:
            u2_copy(l, m).start()
        weight_wait(2)
        free_slot(6, l, m)
        weight_wait(3)
        for j in range(4):
            act, slope = gelu_parts(nn(u2_s[l, m], weights[l, block_rows(4 + j)]))
            act_s[slot, :, j * D : (j + 1) * D] = act.astype(BF16)
            gp_s[l, m, :, j * D : (j + 1) * D] = slope.astype(BF16)
        state[...] = state[...] + nn(act_s[slot], weights[l, block_rows(8, 4)])
        out_copy(6, l, m).start()

    def norm_back(du, hat_scaled, gain, inverse):
        t = du * gain
        hat = hat_scaled * (1.0 / gain)
        weighted = du * hat_scaled
        return inverse * (
            t - jnp.mean(t, axis=-1, keepdims=True) - hat * jnp.mean(weighted, axis=-1, keepdims=True)
        ), weighted

    def add_rows(at, weighted):
        part = weighted[0:8]
        for r in range(8, SEQ, 8):
            part = part + weighted[r : r + 8]
        acc[at] = acc[at] + part

    def backward_layer(l, m):
        slot = l
        held = lax.select(me == last, 1 - l, l)

        def turned_wait(k):
            @pl.when((m == 0) & (me == last))
            def _():
                swap_copy(l, k).wait()

        dy = state[...]
        turned_wait(3)
        turned_wait(2)
        dm_s[l, m] = dy.astype(BF16)
        out_copy(7, l, m).start()
        if paired:
            dm_copy(l, m).start()
        for j in range(4):
            da = nn(dm_s[l, m], weights[held, block_rows(8 + j)])
            dz = gp_s[l, m, :, j * D : (j + 1) * D].astype(F32) * da
            gp_s[l, m, :, j * D : (j + 1) * D] = dz.astype(BF16)
        out_copy(5, l, m).start()
        dh, weighted = norm_back(
            nn(gp_s[l, m], weights[held, block_rows(4, 4)]), u2_s[l, m].astype(F32), gain_two[pl.ds(l, 1), :], stat_s[l, m, :, 1:2]
        )
        add_rows(2 + l, weighted)
        dh = state[...] + dh
        state[...] = dh
        free_slot(3, l, m)
        da_s[slot] = dh.astype(BF16)
        out_copy(3, l, m).start()
        turned_wait(1)
        turned_wait(0)
        do = nn(da_s[slot], weights[held, block_rows(3)]).astype(BF16)
        slopes, products = [], []
        q_tiles, k_tiles, v_tiles = [None] * 6, [None] * 6, [None] * 6
        for tile, count, inside in WINDOWS:
            lo, hi = tile * 128, (tile + count) * 128
            values = two_heads(qkv_s[l, m, :, 2 * D + lo : 2 * D + hi], inside)
            products.append(nt(values, do[:, lo:hi]))
        for j in range(len(WINDOWS)):
            for h in range(2):
                p = p_s[l, m, 2 * j + h].astype(F32)
                dp = products[j][h * SEQ : (h + 1) * SEQ]
                slopes.append((p * (dp - jnp.sum(p * dp, axis=0, keepdims=True))).astype(BF16))
        for j, (tile, count, inside) in enumerate(WINDOWS):
            lo, hi = tile * 128, (tile + count) * 128
            pair = slopes[2 * j : 2 * j + 2]
            keys = two_heads(qkv_s[l, m, :, D + lo : D + hi], inside)
            query = two_heads(qkv_s[l, m, :, lo:hi], inside)
            add_window(q_tiles, tile, tn(jnp.concatenate(pair, axis=0), keys))
            add_window(k_tiles, tile, nn(jnp.concatenate(pair, axis=1), query))
        for j, (tile, count, inside) in enumerate(WINDOWS):
            given = two_heads(do[:, tile * 128 : (tile + count) * 128], inside)
            p = jnp.concatenate([p_s[l, m, 2 * j], p_s[l, m, 2 * j + 1]], axis=1)
            add_window(v_tiles, tile, nn(p, given))
        for i in range(6):
            at = i * 128
            qkv_s[l, m, :, at : at + 128] = (q_tiles[i] * SCALE).astype(BF16)
            qkv_s[l, m, :, D + at : D + at + 128] = (k_tiles[i] * SCALE).astype(BF16)
            qkv_s[l, m, :, 2 * D + at : 2 * D + at + 128] = v_tiles[i].astype(BF16)
        out_copy(1, l, m).start()
        du = nn(qkv_s[l, m], weights[held, block_rows(0, 3)])
        dx, weighted = norm_back(
            du, u_s[l, m].astype(F32), gain_one[pl.ds(l, 1), :], stat_s[l, m, :, 0:1]
        )
        add_rows(l, weighted)
        state[...] = state[...] + dx

    @pl.when(me == last)
    def _():
        def make(l, k, j):
            b = KINDS[k][0] + j
            weight_copy(l, k, j).wait()
            turn(l, b)
            turned_copy(l, b).start()

        def again(l, k, j):
            turned_copy(l, KINDS[k][0] + j).wait()
            weight_copy(l, k, j).start()

        def ready(l, k, j):
            weight_copy(l, k, j).wait()

        for action in (make, again, ready):

            def one(l, c):
                each_block(l, action)
                return c

            lax.fori_loop(0, 2, one, 0)

    def forward_micro(m, carry):
        @pl.when(me == 0)
        def _():
            token_copy(m).wait()

        @pl.when(me > 0)
        def _():
            forward_copy(m).wait_recv()

        state[...] = fwd_in[m].astype(F32)

        def one(l, c):
            forward_layer(l, m)

            @pl.when((m == micros - 1) & (me == last))
            def _():
                for k in (3, 2, 1, 0):
                    swap_copy(1 - l, k).start()

            return c

        lax.fori_loop(0, 2, one, 0)

        fwd_out[m] = state[...].astype(BF16)

        @pl.when(me < last)
        def _():
            forward_copy(m).start()

        @pl.when(me == last)
        def _():
            own_fin_copy(m).start()
            for j in range(last):
                fin_copy(m, j).start()

        return carry

    lax.fori_loop(0, micros, forward_micro, 0)
    @pl.when(me < last)
    def _():
        def one(i, c):
            turn(1 - i // BLOCKS, lax.rem(i, BLOCKS))
            return c

        lax.fori_loop(0, 2 * BLOCKS, one, 0)

    acc[...] = jnp.zeros_like(acc)

    def backward_micro(m, carry):
        @pl.when(me == last)
        def _():
            cotangent_copy(m).wait()

        @pl.when(me < last)
        def _():
            backward_copy(m).wait_recv()

        state[...] = bwd_in[m].astype(F32)

        def one(i, c):
            backward_layer(1 - i, m)
            return c

        lax.fori_loop(0, 2, one, 0)

        bwd_out[m] = state[...].astype(BF16)

        @pl.when(me > 0)
        def _():
            backward_copy(m).start()

        @pl.when(me == 0)
        def _():
            inp_copy(m).start()

        return carry

    lax.fori_loop(0, micros, backward_micro, 0)

    share = D // replicas
    for k in range(4):
        gain = (gain_one, gain_two)[k // 2][k % 2 : k % 2 + 1, :]
        total = jnp.sum(acc[k], axis=0, keepdims=True) / gain
        for r in range(replicas):
            gains_out[r, k : k + 1, 0:share] = total[:, r * share : (r + 1) * share]

    for l in range(2):
        for kind in (2, 3, 6):
            out_copy(kind, l, micros - 1).wait()
        for m in range(micros):
            for kind in (0, 1, 4, 5, 7):
                out_copy(kind, l, m).wait()
            if paired:
                u2_copy(l, m).wait()
                dm_copy(l, m).wait()
    for m in range(micros):

        @pl.when(me < last)
        def _():
            forward_copy(m).wait_send()

        @pl.when(me > 0)
        def _():
            backward_copy(m).wait_send()

        @pl.when(me == last)
        def _():
            for j in range(last):
                fin_copy(m, j).wait_send()
            own_fin_copy(m).wait()

        @pl.when(me < last)
        def _():
            fin_copy(m, last).wait_recv()

        @pl.when(me == 0)
        def _():
            inp_copy(m).wait()


def relay(tokens, cotangent, flags, groups, gain_one, gain_two, wqkv, wout, wup, wdown):
    sections = lax.axis_size("pipe")
    replicas = lax.axis_size("dp")
    rows = tokens.shape[0]
    micros = rows // SEQ
    width = D // sections
    paired = replicas == SHARDS
    anywhere = pl.BlockSpec(memory_space=pl.ANY)
    vmem = pl.BlockSpec(memory_space=pltpu.VMEM)
    smem = pl.BlockSpec(memory_space=pltpu.SMEM)
    dma = pltpu.SemaphoreType.DMA

    def factor(columns):
        return jax.ShapeDtypeStruct((2, rows, columns), BF16)

    def saved(columns):
        return pltpu.VMEM((2, micros, SEQ, columns), BF16)

    def two(columns):
        return pltpu.VMEM((2, SEQ, columns), BF16)

    def per_micro(columns):
        return pltpu.VMEM((micros, SEQ, columns), BF16)

    return pl.pallas_call(
        functools.partial(relay_kernel, sections, replicas, micros, paired),
        out_shape=(
            jax.ShapeDtypeStruct((rows, FIN_WINDOW), BF16),
            jax.ShapeDtypeStruct((rows, D), BF16),
            jax.ShapeDtypeStruct((replicas, 8, 128), F32),
            factor(D),
            factor(3 * D),
            factor(D),
            factor(D),
            factor(D),
            factor(FF),
            factor(FF),
            factor(D),
            factor(D),
            factor(D),
            jax.ShapeDtypeStruct((2, BLOCKS * D, D), BF16),
        ),
        in_specs=[anywhere, anywhere, vmem, smem, vmem, vmem] + [anywhere] * 4,
        out_specs=(anywhere, anywhere, vmem) + (anywhere,) * 11,
        scratch_shapes=[
            pltpu.VMEM((2, BLOCKS * D, D), BF16),
            per_micro(D),
            per_micro(D),
            per_micro(D),
            per_micro(D),
            saved(D),
            saved(3 * D),
            pltpu.VMEM((2, micros, HEADS, SEQ, SEQ), BF16),
            saved(D),
            saved(FF),
            pltpu.VMEM((2, micros, SEQ, 128), F32),
            two(D),
            two(FF),
            saved(D),
            two(D),
            pltpu.VMEM((SEQ, D), F32),
            pltpu.VMEM((4, 8, D), F32),
            pltpu.VMEM((micros, SEQ, SEQ), F32),
            dma((2, BLOCKS)),
            dma((2, BLOCKS)),
            dma((2, len(KINDS))),
            dma((2, micros)),
            dma((micros,)),
            dma((micros,)),
            dma((micros,)),
            dma((micros,)),
            dma((micros, sections)),
            dma((micros,)),
            dma((micros,)),
            dma((8, 2, micros)),
            dma((2, micros)),
            dma((2, micros)),
            dma((2, micros)),
            dma((2, micros)),
        ],
        compiler_params=pltpu.CompilerParams(
            collective_id=0, has_side_effects=True, vmem_limit_bytes=60 * MIB
        ),
        name="relay",
    )(tokens, cotangent, flags, groups, gain_one, gain_two, wqkv, wout, wup, wdown)


ROWS = 96
CHUNKS = 10
UP, DOWN = 4, 6
AGAIN = 256
ORDER = (3, 0, 1, 2) + tuple(range(4, CHUNKS))

LOANS = ((0, 1, 1, 0), (0, 1, 2, 1))
GUESTS = 2


def sum_kernel(
    sections,
    gains_in,
    fin_in,
    inp_in,
    u_in,
    dqkv_in,
    o_in,
    da_in,
    u2_in,
    dz_in,
    act_in,
    dm_in,
    u2_other,
    dm_other,
    wup_hbm,
    wdown_hbm,
    gains_out,
    fin_out,
    inp_out,
    qkv_out,
    out_out,
    up_out,
    down_out,
    u_v,
    dqkv_v,
    o_v,
    da_v,
    u2_v,
    dz_v,
    act_v,
    dm_v,
    wup_v,
    wdown_v,
    own,
    first,
    second,
    third,
    gains_v,
    fin_v,
    fin_t,
    inp_v,
    inp_stage,
    load_sem,
    gain_send,
    gain_recv,
    fin_sem,
    inp_send,
    inp_recv,
    lend_send,
    lend_recv,
    back_send,
    back_recv,
    send,
    recv,
    up_sem,
    out_sem,
):
    me = lax.axis_index("dp")
    section = lax.axis_index("pipe")
    core = lax.rem(me, 2)
    x = lax.rem(me // 2, 2)
    y = me // 4
    other_core = me + 1 - 2 * core
    other_x = me + 2 - 4 * x
    other_y = me + 4 - 8 * y

    barrier = pltpu.get_barrier_semaphore()
    for j in range(SHARDS):

        @pl.when(me != j)
        def _():
            pl.semaphore_signal(barrier, inc=1, device_id={"dp": j}, device_id_type=MESH)

    loans = LOANS if sections > 3 else ()
    for j in range(1, sections):
        for to in sorted({0} | {lender for lender, k, _, _ in loans if sections - k == j}):

            @pl.when(section == j)
            def _():
                pl.semaphore_signal(barrier, inc=1, device_id={"pipe": to}, device_id_type=MESH)

    sources = (u_in, dqkv_in, o_in, da_in)
    held = (u_v, dqkv_v, o_v, da_v)
    rows = dm_in.shape[1]

    def load(k, l):
        return pltpu.make_async_copy(sources[k].at[l], held[k], load_sem.at[k])

    def hidden(l, b, other=False):
        px, py = (1 - x, 1 - y) if other else (x, y)
        block = l * (2 * b + px) + (1 - l) * (2 * py + b)
        return pl.ds(pl.multiple_of(block * CHUNK, CHUNK), CHUNK)

    def mlp_loads(l):
        own_rows, other_rows = pl.ds(0, rows), pl.ds(rows, rows)
        copies = [
            (u2_other.at[l], u2_v.at[other_rows]),
            (dm_other.at[l], dm_v.at[other_rows]),
            (u2_in.at[l], u2_v.at[own_rows]),
            (dm_in.at[l], dm_v.at[own_rows]),
        ]
        for b in range(2):
            units = hidden(l, b)
            copies.append((wup_hbm.at[l, :, units], wup_v.at[b]))
            copies.append((wdown_hbm.at[l, units], wdown_v.at[b]))
            copies.append((dz_in.at[l, :, units], dz_v.at[b, own_rows]))
            copies.append((act_in.at[l, :, units], act_v.at[b, own_rows]))
        return [pltpu.make_async_copy(src, dst, load_sem.at[4 + k]) for k, (src, dst) in enumerate(copies)]

    for k in (2, 3, 0, 1):
        load(k, 1).start()
    for copy in mlp_loads(1):
        copy.start()

    def gain_copy(j, source):
        return pltpu.make_async_remote_copy(
            src_ref=gains_in.at[j],
            dst_ref=gains_v.at[source],
            send_sem=gain_send.at[j],
            recv_sem=gain_recv.at[source],
            device_id={"dp": j},
            device_id_type=MESH,
        )

    def inp_copy(j):
        return pltpu.make_async_remote_copy(
            src_ref=inp_stage.at[j],
            dst_ref=inp_out,
            send_sem=inp_send.at[j],
            recv_sem=inp_recv,
            device_id={"pipe": j},
            device_id_type=MESH,
        )

    def own_inp_copy():
        return pltpu.make_async_copy(inp_stage.at[0], inp_out, inp_send.at[0])

    def inp_load():
        return pltpu.make_async_copy(inp_in, inp_v, inp_send.at[0])

    def meet():
        others = lax.select(section == 0, sections - 1, 0)
        for lender in {lender for lender, _, _, _ in loans} - {0}:
            hosts = {k for other, k, _, _ in loans if other == lender}
            others = others + lax.select(section == lender, len(hosts), 0)
        pl.semaphore_wait(barrier, SHARDS - 1 + others)
        for j in range(SHARDS):

            @pl.when(me != j)
            def _():
                gain_copy(j, me).start()


    def remote(src, dst, step, n, to):
        return pltpu.make_async_remote_copy(
            src_ref=src,
            dst_ref=dst,
            send_sem=send.at[step, n],
            recv_sem=recv.at[step, n],
            device_id={"dp": to},
            device_id_type=MESH,
        )

    def give_copy(n, i):
        if i >= DOWN:
            return remote(own.at[i, 1 - core, 0], first.at[n, 0], 0, n, other_core)
        return remote(own.at[i, 1 - core], first.at[n], 0, n, other_core)

    def down_copy(n, l):
        mine, to = lax.select(l == 1, y, x), lax.select(l == 1, other_y, other_x)
        return remote(first.at[n, 0, 1 - mine], third.at[n], 2, n, to)

    def first_copy(n, i, l=None):
        if i >= UP:
            mine = lax.select(l == 1, y, x)
            to = lax.select(l == 1, other_y, other_x)
            return remote(first.at[n, 1 - mine], second.at[n], 1, n, to)
        if i % 2 == 0:
            return remote(first.at[n, :, 1 - x], second.at[n], 1, n, other_x)
        return remote(first.at[n, 1 - y], second.at[n], 1, n, other_y)

    def second_copy(n, i, l=None):
        if i >= UP:
            mine = lax.select(l == 1, x, y)
            to = lax.select(l == 1, other_x, other_y)
            return remote(second.at[n, 1 - mine], third.at[n], 2, n, to)
        if i % 2 == 0:
            return remote(second.at[n, 1 - y], third.at[n], 2, n, other_y)
        return remote(second.at[n, 1 - x], third.at[n], 2, n, other_x)

    def lend_copy(g):
        lender, k, i, slot = loans[g]
        return pltpu.make_async_remote_copy(
            src_ref=first.at[i],
            dst_ref=first.at[2 * CHUNKS + slot],
            send_sem=lend_send.at[g],
            recv_sem=lend_recv.at[g],
            device_id={"pipe": sections - k},
            device_id_type=MESH,
        )

    def back_copy(g):
        lender, k, i, slot = loans[g]
        return pltpu.make_async_remote_copy(
            src_ref=third.at[2 * CHUNKS + slot],
            dst_ref=third.at[i],
            send_sem=back_send.at[g],
            recv_sem=back_recv.at[g],
            device_id={"pipe": lender},
            device_id_type=MESH,
        )

    def lent_or(step, i, lent, kept):
        away = None
        for g, (lender, _, chunk, _) in enumerate(loans):
            if chunk == i:
                here = (step == 0) & (section == lender)
                pl.when(here)(functools.partial(lent, g))
                away = here if away is None else away | here
        if away is None:
            kept()
        else:
            pl.when(jnp.logical_not(away))(kept)

    def as_host(action):
        for g, (_, k, i, slot) in enumerate(loans):
            pl.when(section == sections - k)(functools.partial(action, g, 2 * CHUNKS + slot, i))

    lent_chunks = sorted({i for _, _, i, _ in loans})

    def result_copy(n, l, i):
        if i < 3:
            dst = qkv_out.at[l, :, pl.ds(i * CHUNK, CHUNK)]
        elif i < 4:
            dst = out_out.at[l]
        elif i < DOWN:
            dst = up_out.at[l, :, hidden(l, i - UP, other=True)]
        else:
            dst = down_out.at[l, pl.ds((i - DOWN) * ROWS, ROWS)]
        return pltpu.make_async_copy(third.at[n], dst, out_sem.at[n])

    def own_up_copy(n, l, i):
        mine = lax.select(l == 1, x, y)
        return pltpu.make_async_copy(second.at[n, mine], up_out.at[l, :, hidden(l, i - UP)], up_sem.at[n])

    def add_core(n, l, i):
        give_copy(n, i).wait_recv()
        if i >= DOWN:
            first[n, 0] = first[n, 0] + own[i, core, 0]
            down_copy(n, l).start()
        else:
            first[n] = first[n] + own[i, core]
            lent_or(1 - l, i, lambda g: lend_copy(g).start(), lambda: first_copy(n, i, l).start())

    def free(step, i):
        @pl.when(step > 0)
        def _():
            give_copy(i, i).wait_send()

    def second_sum(n, i, l=None):
        first_copy(n, i, l).wait_recv()
        if i >= UP:
            kept = first[n, lax.select(l == 1, y, x)]
        else:
            kept = first[n, :, x] if i % 2 == 0 else first[n, y]
        second[n] = second[n] + kept
        second_copy(n, i, l).start()
        if i >= UP:
            own_up_copy(n, l, i).start()

    def plain_products(step, carry):
        l = 1 - step
        base = step * CHUNKS

        def products(k, a, g, slots):
            load(k, l).wait()
            load(k + 1, l).wait()
            for i, columns in slots:
                free(step, i)
                part = tn(a[...], g[:, columns * CHUNK : (columns + 1) * CHUNK]).astype(BF16)
                for r in range(SHARDS):
                    own[i, r % 2, r // 4, (r // 2) % 2] = part[r * ROWS : (r + 1) * ROWS]
                if i == ORDER[0]:
                    pl.when(step == 0)(meet)
                give_copy(base + i, i).start()
                if i != ORDER[0]:
                    before = ORDER[ORDER.index(i) - 1]
                    add_core(base + before, l, before)
                else:

                    @pl.when(step > 0)
                    def _():
                        add_core(base - CHUNKS + ORDER[UP - 1], l + 1, ORDER[UP - 1])

        def reload(k):
            @pl.when(step == 0)
            def _():
                load(k, 0).start()
                load(k + 1, 0).start()

        products(2, o_v, da_v, ((3, 0),))
        reload(2)
        products(0, u_v, dqkv_v, ((0, 0), (1, 1), (2, 2)))
        reload(0)
        return carry

    lax.fori_loop(0, 2, plain_products, 0)
    add_core(CHUNKS + ORDER[UP - 1], 0, ORDER[UP - 1])

    def mlp_products(step, carry):
        l = 1 - step
        base = step * CHUNKS
        copies = mlp_loads(l)

        def next_loads(*which):
            @pl.when(step == 0)
            def _():
                later = mlp_loads(0)
                for k in which:
                    later[k].start()

        for k in (0, 1, 4, 5, 8, 9):
            copies[k].wait()

        def again(k, c):
            at = pl.ds(pl.multiple_of(rows + k * AGAIN, AGAIN), AGAIN)
            for b in range(2):
                act, slope = gelu_parts(nn(u2_v[at], wup_v[b]))
                act_v[b, at] = act.astype(BF16)
                dz_v[b, at] = (slope * nt(dm_v[at], wdown_v[b])).astype(BF16)
            return c

        lax.fori_loop(0, rows // AGAIN, again, 0)
        next_loads(4, 5, 8, 9)
        for i in ORDER[:UP]:
            lent_or(step, i, lambda g: None, functools.partial(second_sum, base + i, i, l))
        for k in (2, 3, 6, 7, 10, 11):
            copies[k].wait()
        for b in range(2):
            i = UP + b
            free(step, i)
            part = tn(u2_v[...], dz_v[b]).astype(BF16)
            for r in range(SHARDS):
                ry, rx = r // 4, (r // 2) % 2
                across, along = l * ry + (1 - l) * rx, l * rx + (1 - l) * ry
                own[i, r % 2, across, along] = part[r * ROWS : (r + 1) * ROWS]
            give_copy(base + i, i).start()
            if b == 1:
                add_core(base + UP, l, UP)
        next_loads(0, 2, 6, 10)
        for i in range(DOWN, CHUNKS):
            free(step, i)
        for b in range(2):
            part = tn(act_v[b], dm_v[...]).astype(BF16)
            for r in range(8):
                own[DOWN + r % 4, r // 4, 0, b] = part[r * ROWS : (r + 1) * ROWS]
        next_loads(1, 3, 7, 11)
        for i in range(DOWN, CHUNKS):
            give_copy(base + i, i).start()
        for i in range(UP + 1, CHUNKS):
            add_core(base + i, l, i)
        return carry

    lax.fori_loop(0, 2, mlp_products, 0)

    def up_sums(step, carry):
        for i in range(UP, DOWN):
            second_sum(step * CHUNKS + i, i, 1 - step)
        return carry

    lax.fori_loop(0, 2, up_sums, 0)

    def take_in(g, n, i):
        lend_copy(g).wait_recv()
        first_copy(n, i).start()

    as_host(take_in)
    as_host(lambda g, n, i: second_sum(n, i))

    fin_load = pltpu.make_async_copy(fin_in, fin_v, fin_sem)
    fin_load.start()
    fin_load.wait()
    width = D // sections
    for j in range(sections):
        first_lane = j * width - window_start(j, width)

        @pl.when(section == j)
        def _():
            for r in range(0, rows, SEQ):
                part = fin_v[r : r + SEQ, :].astype(F32)[:, first_lane : first_lane + width]
                fin_t[:, r : r + SEQ] = part.T.astype(BF16)

    fin_store = pltpu.make_async_copy(fin_t, fin_out, fin_sem)
    fin_store.start()

    @pl.when(section == 0)
    def _():
        inp_load().start()
        inp_load().wait()
        for j in range(sections):
            for r in range(0, rows, SEQ):
                part = inp_v[r : r + SEQ, :].astype(F32)[:, j * width : (j + 1) * width]
                inp_stage[j, :, r : r + SEQ] = part.T.astype(BF16)
        own_inp_copy().start()
        for j in range(1, sections):
            inp_copy(j).start()

    def take_in(g, n, i):
        lend_copy(g).wait_recv()
        first_copy(n, i).start()

    gains_v[me] = gains_in[me]
    for j in range(SHARDS):

        @pl.when(me != j)
        def _():
            gain_copy(j, j).wait_recv()

    total = gains_v[0]
    for j in range(1, SHARDS):
        total = total + gains_v[j]
    gains_out[...] = total

    def last_sum(n, i):
        second_copy(n, i).wait_recv()
        third[n] = third[n] + second[n, y if i % 2 == 0 else x]

    def last_sums(step, carry):
        for i in ORDER:
            n = step * CHUNKS + i
            if i >= DOWN:
                down_copy(n, 1 - step).wait_recv()
                third[n] = third[n] + first[n, 0, lax.select(step == 0, y, x)]
            elif i >= UP:
                second_copy(n, i, 1 - step).wait_recv()
            else:
                lent_or(step, i, lambda g: None, functools.partial(last_sum, n, i))
            if i not in lent_chunks:
                result_copy(n, 1 - step, i).start()
        return carry

    lax.fori_loop(0, 2, last_sums, 0)

    def give_back(g, n, i):
        last_sum(n, i)
        back_copy(g).start()

    as_host(give_back)
    for g, (lender, _, _, _) in enumerate(loans):

        @pl.when(section == lender)
        def _():
            back_copy(g).wait_recv()

    for i in lent_chunks:
        for step in range(2):
            result_copy(step * CHUNKS + i, 1 - step, i).start()

    def finish(step, carry):
        for i in range(CHUNKS):
            n = step * CHUNKS + i
            if i >= DOWN:
                down_copy(n, 1 - step).wait_send()
            else:

                def sent():
                    first_copy(n, i, 1 - step).wait_send()
                    second_copy(n, i, 1 - step).wait_send()
                    if i >= UP:
                        own_up_copy(n, 1 - step, i).wait()

                lent_or(step, i, lambda g: lend_copy(g).wait_send(), sent)
            result_copy(n, 1 - step, i).wait()
        return carry

    lax.fori_loop(0, 2, finish, 0)
    def guest_sent(g, n, i):
        first_copy(n, i).wait_send()
        second_copy(n, i).wait_send()
        back_copy(g).wait_send()

    as_host(guest_sent)

    for i in range(CHUNKS):
        give_copy(CHUNKS + i, i).wait_send()
    for j in range(SHARDS):

        @pl.when(me != j)
        def _():
            gain_copy(j, me).wait_send()

    fin_store.wait()

    @pl.when(section == 0)
    def _():
        own_inp_copy().wait()
        for j in range(1, sections):
            inp_copy(j).wait_send()

    @pl.when(section > 0)
    def _():
        inp_copy(0).wait_recv()


def summed(gains, fin, inp, *factors):
    sections = lax.axis_size("pipe")
    rows, width = inp.shape[0], D // sections
    anywhere = pl.BlockSpec(memory_space=pl.ANY)
    vmem = pl.BlockSpec(memory_space=pltpu.VMEM)
    dma = pltpu.SemaphoreType.DMA
    total = 2 * CHUNKS
    slots = total + GUESTS

    def shard(height, columns):
        return jax.ShapeDtypeStruct((2, height, columns), BF16)

    return pl.pallas_call(
        functools.partial(sum_kernel, sections),
        out_shape=(
            jax.ShapeDtypeStruct((8, 128), F32),
            jax.ShapeDtypeStruct((width, rows), BF16),
            jax.ShapeDtypeStruct((width, rows), BF16),
            shard(ROWS, 3 * D),
            shard(ROWS, D),
            shard(ROWS, FF),
            shard(4 * ROWS, D),
        ),
        in_specs=[vmem] + [anywhere] * 14,
        out_specs=(vmem,) + (anywhere,) * 6,
        scratch_shapes=[pltpu.VMEM((rows, f.shape[2]), BF16) for f in factors[:4]]
        + [
            pltpu.VMEM((2 * rows, D), BF16),
            pltpu.VMEM((2, 2 * rows, CHUNK), BF16),
            pltpu.VMEM((2, 2 * rows, CHUNK), BF16),
            pltpu.VMEM((2 * rows, D), BF16),
            pltpu.VMEM((2, D, CHUNK), BF16),
            pltpu.VMEM((2, CHUNK, D), BF16),
            pltpu.VMEM((CHUNKS, 2, 2, 2, ROWS, CHUNK), BF16),
            pltpu.VMEM((slots, 2, 2, ROWS, CHUNK), BF16),
            pltpu.VMEM((slots, 2, ROWS, CHUNK), BF16),
            pltpu.VMEM((slots, ROWS, CHUNK), BF16),
            pltpu.VMEM((SHARDS, 8, 128), F32),
            pltpu.VMEM((rows, FIN_WINDOW), BF16),
            pltpu.VMEM((width, rows), BF16),
            pltpu.VMEM((rows, D), BF16),
            pltpu.VMEM((sections, width, rows), BF16),
            dma((16,)),
            dma((SHARDS,)),
            dma((SHARDS,)),
            dma(()),
            dma((sections,)),
            dma(()),
            dma((len(LOANS),)),
            dma((len(LOANS),)),
            dma((len(LOANS),)),
            dma((len(LOANS),)),
            dma((3, slots)),
            dma((3, slots)),
            dma((total,)),
            dma((total,)),
        ],
        compiler_params=pltpu.CompilerParams(
            collective_id=1, has_side_effects=True, vmem_limit_bytes=60 * MIB
        ),
        name="sum",
    )(gains, fin, inp, *factors)


def write_kernel(count, share, gains, *refs):
    gain_one, gain_two = refs[count], refs[count + 1]
    gain_one[...] = gains[0:2, 0:share]
    gain_two[...] = gains[2:4, 0:share]
    sources, results, held, wide = (
        refs[:count],
        refs[count + 2 : 2 * count + 2],
        refs[2 * count + 2 : 3 * count + 2],
        refs[3 * count + 2 : 4 * count + 2],
    )
    load_sem, store_sem = refs[4 * count + 2 :]
    loads = [pltpu.make_async_copy(sources[k], held[k], load_sem.at[k]) for k in range(count)]
    stores = [pltpu.make_async_copy(wide[k], results[k], store_sem.at[k]) for k in range(count)]
    for load in loads:
        load.start()
    for k in range(count):
        loads[k].wait()
        wide[k][...] = held[k][...].astype(wide[k].dtype)
        stores[k].start()
    for store in stores:
        store.wait()


def written(gains, share, arrays, types):
    count = len(arrays)
    anywhere = pl.BlockSpec(memory_space=pl.ANY)
    vmem = pl.BlockSpec(memory_space=pltpu.VMEM)
    return pl.pallas_call(
        functools.partial(write_kernel, count, share),
        out_shape=(jax.ShapeDtypeStruct((2, share), F32),) * 2
        + tuple(jax.ShapeDtypeStruct(a.shape, t) for a, t in zip(arrays, types)),
        in_specs=[vmem] + [anywhere] * count,
        out_specs=(vmem, vmem) + (anywhere,) * count,
        scratch_shapes=[pltpu.VMEM(a.shape, a.dtype) for a in arrays]
        + [pltpu.VMEM(a.shape, t) for a, t in zip(arrays, types)]
        + [pltpu.SemaphoreType.DMA((count,)), pltpu.SemaphoreType.DMA((count,))],
        compiler_params=pltpu.CompilerParams(vmem_limit_bytes=60 * MIB),
        name="write",
    )(gains, *arrays)


def body(
    tokens,
    gain_one,
    qkv_weight,
    out_weight,
    gain_two,
    up_weight,
    down_weight,
    cotangent,
    flags,
    groups,
):
    micros = tokens.shape[0] // SEQ
    fin, inp, gains, u, dqkv, o, da, u2, dz, act, dm, u2_other, dm_other, _ = relay(
        tokens,
        cotangent,
        flags.reshape(micros, SEQ),
        groups,
        gain_one,
        gain_two,
        qkv_weight,
        out_weight,
        up_weight,
        down_weight,
    )

    replicas = lax.axis_size("dp")
    share = D // replicas
    if replicas == SHARDS and share == ROWS:
        gains, fin, inp, g_qkv, g_out, g_up, g_down = summed(
            gains, fin, inp, u, dqkv, o, da, u2, dz, act, dm, u2_other, dm_other, up_weight, down_weight
        )
    else:

        def grad(a, g):
            total = jnp.einsum("lsa,lsb->lab", a, g, preferred_element_type=F32).astype(BF16)
            return lax.psum_scatter(total, "dp", scatter_dimension=1, tiled=True)

        gains = lax.psum_scatter(gains, "dp", scatter_dimension=0)
        sections = lax.axis_size("pipe")
        width = D // sections
        first_lanes = jnp.array([j * width - window_start(j, width) for j in range(sections)])
        fin = lax.dynamic_slice_in_dim(fin, first_lanes[lax.axis_index("pipe")], width, 1).T
        inp = jnp.where(lax.axis_index("pipe") == 0, inp.T, jnp.zeros_like(inp.T))
        inp = lax.psum_scatter(inp, "pipe", scatter_dimension=0, tiled=True)
        g_qkv, g_out, g_up, g_down = grad(u, dqkv), grad(o, da), grad(u2, dz), grad(act, dm)
    gain_one_grad, gain_two_grad, fin, inp, g_qkv, g_out, g_up, g_down = written(
        gains, share, (fin, inp, g_qkv, g_out, g_up, g_down), (BF16,) + (F32,) * 5
    )
    return (fin.T, inp.T, gain_one_grad, g_qkv, g_out, gain_two_grad, g_up, g_down)


def solution(mesh):
    return jax.shard_map(
        body,
        mesh=mesh,
        in_specs=(
            P("dp", None),
            P("pipe", None),
            P("pipe", None, None),
            P("pipe", None, None),
            P("pipe", None),
            P("pipe", None, None),
            P("pipe", None, None),
            P("dp", None),
            P("dp"),
            P("dp"),
        ),
        out_specs=(
            P("dp", "pipe"),
            P("dp", "pipe"),
            P("pipe", "dp"),
            P("pipe", "dp", None),
            P("pipe", "dp", None),
            P("pipe", "dp"),
            P("pipe", "dp", None),
            P("pipe", "dp", None),
        ),
        check_vma=False,
    )
```

```python
import functools

import jax
import jax.numpy as jnp
from jax import lax
from jax.experimental import pallas as pl
from jax.experimental.pallas import tpu as pltpu
from jax.sharding import PartitionSpec as P

D = 768
HEADS = 16
HEAD_DIM = 48
FF = 3072
SEQ = 128
EPS = 1e-06
MESH = pl.DeviceIdType.MESH
F32 = jnp.float32
BF16 = jnp.bfloat16
LOG2E = 1.4426950408889634
SCALE = HEAD_DIM ** (-0.5)
MIB = 2**20
CHUNK = 768
TILE = 256

KINDS = ((0, 3), (3, 1), (4, 4), (8, 4))

TURNED = (8, 11, 4, 0)
BLOCKS = 12

FIN_WINDOW = 256


def window_start(section, width):
    return min(section * width // 128 * 128, D - FIN_WINDOW)


SHARDS = 8

WINDOWS = tuple(
    (96 * j // 128, -(-(96 * j % 128 + 96) // 128), 96 * j % 128) for j in range(HEADS // 2)
)


def nn(a, b):
    return jnp.dot(a, b, preferred_element_type=F32)


def nt(a, b):
    return lax.dot_general(a, b, (((1,), (1,)), ((), ())), preferred_element_type=F32)


def tn(a, b):
    return lax.dot_general(a, b, (((0,), (0,)), ((), ())), preferred_element_type=F32)


def lanes_of_head(first, width):
    lane = lax.broadcasted_iota(jnp.int32, (SEQ, width), 1)
    return ((lane >= first) & (lane < first + HEAD_DIM)).astype(F32).astype(BF16)


def two_heads(window, first):
    width = window.shape[1]
    return jnp.concatenate(
        [window * lanes_of_head(first, width), window * lanes_of_head(first + HEAD_DIM, width)], axis=0
    )


def add_window(tiles, first, part):
    for i in range(part.shape[1] // 128):
        piece = part[:, i * 128 : (i + 1) * 128]
        tiles[first + i] = piece if tiles[first + i] is None else tiles[first + i] + piece


def norm_parts(x):
    centre = x - jnp.mean(x, axis=-1, keepdims=True)
    spread = jnp.mean(centre * centre, axis=-1, keepdims=True)
    inverse = lax.rsqrt(spread + EPS)
    return centre * inverse, inverse


def gelu_parts(z):
    phi = 0.5 * (1.0 + lax.erf(z * 0.7071067811865476))
    density = jnp.exp2(z * z * (-0.5 * LOG2E)) * 0.3989422804014327
    return z * phi, phi + z * density


def relay_kernel(
    sections,
    replicas,
    micros,
    paired,
    tokens,
    cotangent,
    flags,
    groups,
    gain_one,
    gain_two,
    wqkv_hbm,
    wout_hbm,
    wup_hbm,
    wdown_hbm,
    fin_out,
    inp_out,
    gains_out,
    u_out,
    dqkv_out,
    o_out,
    da_out,
    u2_out,
    dz_out,
    act_out,
    dm_out,
    u2_other,
    dm_other,
    turned_hbm,
    weights,
    fwd_in,
    fwd_out,
    bwd_in,
    bwd_out,
    u_s,
    qkv_s,
    p_s,
    u2_s,
    gp_s,
    stat_s,
    o_s,
    act_s,
    dm_s,
    da_s,
    state,
    acc,
    bias,
    w_sem,
    turn_sem,
    swap_sem,
    in_sem,
    fwd_send,
    fwd_recv,
    bwd_send,
    bwd_recv,
    fin_send,
    fin_recv,
    inp_send,
    out_sem,
    u2_send,
    u2_recv,
    dm_send,
    dm_recv,
):
    me = lax.axis_index("pipe")
    last = sections - 1
    width = D // sections

    barrier = pltpu.get_barrier_semaphore()
    for j in range(sections):

        @pl.when(me != j)
        def _():
            pl.semaphore_signal(barrier, inc=1, device_id={"pipe": j}, device_id_type=MESH)

    replica = lax.axis_index("dp")
    x, y = lax.rem(replica // 2, 2), replica // 4
    if paired:
        for j in (replica + 2 - 4 * x, replica + 4 - 8 * y):
            pl.semaphore_signal(barrier, inc=1, device_id={"dp": j}, device_id_type=MESH)

    def block_rows(b, count=1):
        start = b * D
        return pl.ds(start if isinstance(b, int) else pl.multiple_of(start, D), count * D)

    def weight_copy(l, k, j):
        first, _ = KINDS[k]
        if k == 1:
            src = wout_hbm.at[l]
        elif k == 3:
            src = wdown_hbm.at[l, block_rows(j)]
        else:
            src = (wqkv_hbm, None, wup_hbm)[k].at[l, :, block_rows(j)]
        return pltpu.make_async_copy(src, weights.at[l, block_rows(first + j)], w_sem.at[l, first + j])

    def turned_copy(l, b):
        return pltpu.make_async_copy(
            weights.at[l, block_rows(b)], turned_hbm.at[l, block_rows(b)], turn_sem.at[l, b]
        )

    def swap_copy(l, k):
        first, count = KINDS[k]
        to = block_rows(TURNED[k], count)
        return pltpu.make_async_copy(
            turned_hbm.at[l, block_rows(first, count)], weights.at[1 - l, to], swap_sem.at[l, k]
        )

    def swap_in(l, m, *kinds):
        @pl.when((m == micros - 1) & (me == last))
        def _():
            for k in kinds:
                swap_copy(1 - l, k).start()

    def turn(l, b):
        def tile(r, c):
            return l, pl.ds(pl.multiple_of(b * D + r * TILE, TILE), TILE), pl.ds(c * TILE, TILE)

        for r in range(D // TILE):
            weights[tile(r, r)] = weights[tile(r, r)].T
            for c in range(r):
                lower = weights[tile(r, c)].T
                upper = weights[tile(c, r)].T
                weights[tile(c, r)] = lower
                weights[tile(r, c)] = upper

    def each_block(l, action):
        for k, (_, count) in enumerate(KINDS):

            def one(j, c):
                action(l, k, j)
                return c

            lax.fori_loop(0, count, one, 0)

    def token_copy(m):
        return pltpu.make_async_copy(tokens.at[pl.ds(m * SEQ, SEQ)], fwd_in.at[m], in_sem.at[0, m])

    def cotangent_copy(m):
        return pltpu.make_async_copy(cotangent.at[pl.ds(m * SEQ, SEQ)], bwd_in.at[m], in_sem.at[1, m])

    @pl.when(me == 0)
    def _():
        for m in range(micros):
            token_copy(m).start()

    def weights_start(l):
        for k, (_, count) in enumerate(KINDS):
            for j in range(count):
                weight_copy(l, k, j).start()

    weights_start(0)

    @pl.when(me > 0)
    def _():
        weights_start(1)


    @pl.when(me == last)
    def _():
        for m in range(micros):
            cotangent_copy(m).start()

    def forward_copy(m):
        return pltpu.make_async_remote_copy(
            src_ref=fwd_out.at[m],
            dst_ref=fwd_in.at[m],
            send_sem=fwd_send.at[m],
            recv_sem=fwd_recv.at[m],
            device_id={"pipe": lax.rem(me + 1, sections)},
            device_id_type=MESH,
        )

    def backward_copy(m):
        return pltpu.make_async_remote_copy(
            src_ref=bwd_out.at[m],
            dst_ref=bwd_in.at[m],
            send_sem=bwd_send.at[m],
            recv_sem=bwd_recv.at[m],
            device_id={"pipe": lax.rem(me + sections - 1, sections)},
            device_id_type=MESH,
        )

    def slots_of(m):
        return pl.ds(pl.multiple_of(m * SEQ, SEQ), SEQ)

    def fin_source(m, j):
        return fwd_out.at[m, :, pl.ds(window_start(j, width), FIN_WINDOW)]

    def fin_copy(m, j):
        return pltpu.make_async_remote_copy(
            src_ref=fin_source(m, j),
            dst_ref=fin_out.at[slots_of(m)],
            send_sem=fin_send.at[m, j],
            recv_sem=fin_recv.at[m],
            device_id={"pipe": j},
            device_id_type=MESH,
        )

    def own_fin_copy(m):
        return pltpu.make_async_copy(fin_source(m, last), fin_out.at[slots_of(m)], fin_send.at[m, last])

    def inp_copy(m):
        return pltpu.make_async_copy(bwd_out.at[m], inp_out.at[slots_of(m)], inp_send.at[m])


    outs = (u_out, dqkv_out, o_out, da_out, u2_out, dz_out, act_out, dm_out)

    def out_copy(kind, l, m):
        slot = l
        src = (
            u_s.at[l, m],
            qkv_s.at[l, m],
            o_s.at[slot],
            da_s.at[slot],
            u2_s.at[l, m],
            gp_s.at[l, m],
            act_s.at[slot],
            dm_s.at[l, m],
        )[kind]
        return pltpu.make_async_copy(src, outs[kind].at[l, pl.ds(m * SEQ, SEQ)], out_sem.at[kind, l, m])

    def partner(l):
        return {"dp": lax.select(l == 1, replica + 2 - 4 * x, replica + 4 - 8 * y)}

    def u2_copy(l, m):
        return pltpu.make_async_remote_copy(
            src_ref=u2_s.at[l, m],
            dst_ref=u2_other.at[l, slots_of(m)],
            send_sem=u2_send.at[l, m],
            recv_sem=u2_recv.at[l, m],
            device_id=partner(l),
            device_id_type=MESH,
        )

    def dm_copy(l, m):
        return pltpu.make_async_remote_copy(
            src_ref=dm_s.at[l, m],
            dst_ref=dm_other.at[l, slots_of(m)],
            send_sem=dm_send.at[l, m],
            recv_sem=dm_recv.at[l, m],
            device_id=partner(l),
            device_id_type=MESH,
        )

    def free_slot(kind, l, m):
        @pl.when(m > 0)
        def _():
            out_copy(kind, l, m - 1).wait()

    row = lax.broadcasted_iota(jnp.int32, (SEQ, SEQ), 0) // (SEQ // 4)
    column = lax.broadcasted_iota(jnp.int32, (SEQ, SEQ), 1) // (SEQ // 4)
    same = (row == column).astype(F32)
    for m in range(micros):
        parted = (jnp.full((1, SEQ), groups[m], jnp.int32) == 1).astype(F32)
        valid = jnp.broadcast_to((flags[m : m + 1, :] == 1).astype(F32), (SEQ, SEQ)).T
        keep = jnp.maximum(same, 1.0 - parted) * valid
        bias[m] = (keep - 1.0) * 1e30

    def forward_layer(l, m):
        def weight_wait(k):
            @pl.when((m == 0) & (me < last))
            def _():
                for j in range(KINDS[k][1]):
                    weight_copy(l, k, j).wait()

        x = state[...]
        xhat, inverse = norm_parts(x)
        stat_s[l, m, :, 0:1] = inverse
        u = (xhat * gain_one[pl.ds(l, 1), :]).astype(BF16)
        u_s[l, m] = u
        out_copy(0, l, m).start()
        weight_wait(0)
        for j in range(3):
            qkv_s[l, m, :, j * D : (j + 1) * D] = nn(u_s[l, m], weights[l, block_rows(j)]).astype(BF16)
        free_slot(2, l, m)
        slot = l
        added = bias[m]
        scores, tiles = [], [None] * 6
        for tile, count, inside in WINDOWS:
            lo, hi = tile * 128, (tile + count) * 128
            keys = two_heads(qkv_s[l, m, :, D + lo : D + hi], inside)
            scores.append(nt(keys, qkv_s[l, m, :, lo:hi]) * (SCALE * LOG2E))
        for j in range(len(WINDOWS)):
            for h in range(2):
                s = scores[j][h * SEQ : (h + 1) * SEQ] + added
                e = jnp.exp2(s - jnp.max(s, axis=0, keepdims=True))
                p = e * (1.0 / jnp.sum(e, axis=0, keepdims=True))
                p_s[l, m, 2 * j + h] = p.astype(BF16)
        for j, (tile, count, inside) in enumerate(WINDOWS):
            lo, hi = tile * 128, (tile + count) * 128
            values = two_heads(qkv_s[l, m, :, 2 * D + lo : 2 * D + hi], inside)
            p = jnp.concatenate([p_s[l, m, 2 * j], p_s[l, m, 2 * j + 1]], axis=0)
            add_window(tiles, tile, tn(p, values))
        for i in range(6):
            o_s[slot, :, i * 128 : (i + 1) * 128] = tiles[i].astype(BF16)
        out_copy(2, l, m).start()
        weight_wait(1)

        @pl.when((m == 0) & (me == 0) & (l == 0))
        def _():
            weights_start(1)

        h = state[...] + nn(o_s[slot], weights[l, block_rows(3)])
        state[...] = h
        swap_in(l, m, 3)
        hhat, inverse = norm_parts(h)
        stat_s[l, m, :, 1:2] = inverse
        u2_s[l, m] = (hhat * gain_two[pl.ds(l, 1), :]).astype(BF16)
        out_copy(4, l, m).start()

        @pl.when((m == 0) & (l == 0))
        def _():
            pl.semaphore_wait(barrier, sections - 1 + 2 * paired)

        if paired:
            u2_copy(l, m).start()
        weight_wait(2)
        free_slot(6, l, m)
        weight_wait(3)
        for j in range(4):
            act, slope = gelu_parts(nn(u2_s[l, m], weights[l, block_rows(4 + j)]))
            act_s[slot, :, j * D : (j + 1) * D] = act.astype(BF16)
            gp_s[l, m, :, j * D : (j + 1) * D] = slope.astype(BF16)
        swap_in(l, m, 2)
        state[...] = state[...] + nn(act_s[slot], weights[l, block_rows(8, 4)])
        swap_in(l, m, 1, 0)
        out_copy(6, l, m).start()

    def norm_back(du, hat_scaled, gain, inverse):
        t = du * gain
        hat = hat_scaled * (1.0 / gain)
        weighted = du * hat_scaled
        return inverse * (
            t - jnp.mean(t, axis=-1, keepdims=True) - hat * jnp.mean(weighted, axis=-1, keepdims=True)
        ), weighted

    def add_rows(at, weighted):
        part = weighted[0:8]
        for r in range(8, SEQ, 8):
            part = part + weighted[r : r + 8]
        acc[at] = acc[at] + part

    def backward_layer(l, m):
        slot = l
        held = lax.select(me == last, 1 - l, l)

        def turned(k, j=0, count=1):
            return held, block_rows(lax.select(me == last, TURNED[k], KINDS[k][0]) + j, count)

        def turned_wait(k):
            @pl.when((m == 0) & (me == last))
            def _():
                swap_copy(l, k).wait()

        dy = state[...]
        turned_wait(3)
        turned_wait(2)
        dm_s[l, m] = dy.astype(BF16)
        out_copy(7, l, m).start()
        if paired:
            dm_copy(l, m).start()
        for j in range(4):
            da = nn(dm_s[l, m], weights[turned(3, j)])
            dz = gp_s[l, m, :, j * D : (j + 1) * D].astype(F32) * da
            gp_s[l, m, :, j * D : (j + 1) * D] = dz.astype(BF16)
        out_copy(5, l, m).start()
        dh, weighted = norm_back(
            nn(gp_s[l, m], weights[turned(2, 0, 4)]), u2_s[l, m].astype(F32), gain_two[pl.ds(l, 1), :], stat_s[l, m, :, 1:2]
        )
        add_rows(2 + l, weighted)
        dh = state[...] + dh
        state[...] = dh
        free_slot(3, l, m)
        da_s[slot] = dh.astype(BF16)
        out_copy(3, l, m).start()
        turned_wait(1)
        turned_wait(0)
        do = nn(da_s[slot], weights[turned(1)]).astype(BF16)
        slopes, products = [], []
        q_tiles, k_tiles, v_tiles = [None] * 6, [None] * 6, [None] * 6
        for tile, count, inside in WINDOWS:
            lo, hi = tile * 128, (tile + count) * 128
            values = two_heads(qkv_s[l, m, :, 2 * D + lo : 2 * D + hi], inside)
            products.append(nt(values, do[:, lo:hi]))
        for j in range(len(WINDOWS)):
            for h in range(2):
                p = p_s[l, m, 2 * j + h].astype(F32)
                dp = products[j][h * SEQ : (h + 1) * SEQ]
                slopes.append((p * (dp - jnp.sum(p * dp, axis=0, keepdims=True))).astype(BF16))
        for j, (tile, count, inside) in enumerate(WINDOWS):
            lo, hi = tile * 128, (tile + count) * 128
            pair = slopes[2 * j : 2 * j + 2]
            keys = two_heads(qkv_s[l, m, :, D + lo : D + hi], inside)
            query = two_heads(qkv_s[l, m, :, lo:hi], inside)
            add_window(q_tiles, tile, tn(jnp.concatenate(pair, axis=0), keys))
            add_window(k_tiles, tile, nn(jnp.concatenate(pair, axis=1), query))
        for j, (tile, count, inside) in enumerate(WINDOWS):
            given = two_heads(do[:, tile * 128 : (tile + count) * 128], inside)
            p = jnp.concatenate([p_s[l, m, 2 * j], p_s[l, m, 2 * j + 1]], axis=1)
            add_window(v_tiles, tile, nn(p, given))
        for i in range(6):
            at = i * 128
            qkv_s[l, m, :, at : at + 128] = (q_tiles[i] * SCALE).astype(BF16)
            qkv_s[l, m, :, D + at : D + at + 128] = (k_tiles[i] * SCALE).astype(BF16)
            qkv_s[l, m, :, 2 * D + at : 2 * D + at + 128] = v_tiles[i].astype(BF16)
        out_copy(1, l, m).start()
        du = nn(qkv_s[l, m], weights[turned(0, 0, 3)])
        dx, weighted = norm_back(
            du, u_s[l, m].astype(F32), gain_one[pl.ds(l, 1), :], stat_s[l, m, :, 0:1]
        )
        add_rows(l, weighted)
        state[...] = state[...] + dx

    @pl.when(me == last)
    def _():
        def make(l, k, j):
            b = KINDS[k][0] + j
            weight_copy(l, k, j).wait()
            turn(l, b)
            turned_copy(l, b).start()

        def again(l, k, j):
            turned_copy(l, KINDS[k][0] + j).wait()
            weight_copy(l, k, j).start()

        def ready(l, k, j):
            weight_copy(l, k, j).wait()

        for action in (make, again, ready):

            def one(l, c):
                each_block(l, action)
                return c

            lax.fori_loop(0, 2, one, 0)

    def forward_micro(m, carry):
        @pl.when(me == 0)
        def _():
            token_copy(m).wait()

        @pl.when(me > 0)
        def _():
            forward_copy(m).wait_recv()

        state[...] = fwd_in[m].astype(F32)

        def one(l, c):
            forward_layer(l, m)
            return c

        lax.fori_loop(0, 2, one, 0)

        fwd_out[m] = state[...].astype(BF16)

        @pl.when(me < last)
        def _():
            forward_copy(m).start()

        @pl.when(me == last)
        def _():
            own_fin_copy(m).start()
            for j in range(last):
                fin_copy(m, j).start()

        return carry

    lax.fori_loop(0, micros, forward_micro, 0)
    @pl.when(me < last)
    def _():
        def one(i, c):
            turn(1 - i // BLOCKS, lax.rem(i, BLOCKS))
            return c

        lax.fori_loop(0, 2 * BLOCKS, one, 0)

    acc[...] = jnp.zeros_like(acc)

    def backward_micro(m, carry):
        @pl.when(me == last)
        def _():
            cotangent_copy(m).wait()

        @pl.when(me < last)
        def _():
            backward_copy(m).wait_recv()

        state[...] = bwd_in[m].astype(F32)

        def one(i, c):
            backward_layer(1 - i, m)
            return c

        lax.fori_loop(0, 2, one, 0)

        bwd_out[m] = state[...].astype(BF16)

        @pl.when(me > 0)
        def _():
            backward_copy(m).start()

        @pl.when(me == 0)
        def _():
            inp_copy(m).start()

        return carry

    lax.fori_loop(0, micros, backward_micro, 0)

    share = D // replicas
    for k in range(4):
        gain = (gain_one, gain_two)[k // 2][k % 2 : k % 2 + 1, :]
        total = jnp.sum(acc[k], axis=0, keepdims=True) / gain
        for r in range(replicas):
            gains_out[r, k : k + 1, 0:share] = total[:, r * share : (r + 1) * share]

    for l in range(2):
        for kind in (2, 3, 6):
            out_copy(kind, l, micros - 1).wait()
        for m in range(micros):
            for kind in (0, 1, 4, 5, 7):
                out_copy(kind, l, m).wait()
            if paired:
                u2_copy(l, m).wait()
                dm_copy(l, m).wait()
    for m in range(micros):

        @pl.when(me < last)
        def _():
            forward_copy(m).wait_send()

        @pl.when(me > 0)
        def _():
            backward_copy(m).wait_send()

        @pl.when(me == last)
        def _():
            for j in range(last):
                fin_copy(m, j).wait_send()
            own_fin_copy(m).wait()

        @pl.when(me < last)
        def _():
            fin_copy(m, last).wait_recv()

        @pl.when(me == 0)
        def _():
            inp_copy(m).wait()


def relay(tokens, cotangent, flags, groups, gain_one, gain_two, wqkv, wout, wup, wdown):
    sections = lax.axis_size("pipe")
    replicas = lax.axis_size("dp")
    rows = tokens.shape[0]
    micros = rows // SEQ
    width = D // sections
    paired = replicas == SHARDS
    anywhere = pl.BlockSpec(memory_space=pl.ANY)
    vmem = pl.BlockSpec(memory_space=pltpu.VMEM)
    smem = pl.BlockSpec(memory_space=pltpu.SMEM)
    dma = pltpu.SemaphoreType.DMA

    def factor(columns):
        return jax.ShapeDtypeStruct((2, rows, columns), BF16)

    def saved(columns):
        return pltpu.VMEM((2, micros, SEQ, columns), BF16)

    def two(columns):
        return pltpu.VMEM((2, SEQ, columns), BF16)

    def per_micro(columns):
        return pltpu.VMEM((micros, SEQ, columns), BF16)

    return pl.pallas_call(
        functools.partial(relay_kernel, sections, replicas, micros, paired),
        out_shape=(
            jax.ShapeDtypeStruct((rows, FIN_WINDOW), BF16),
            jax.ShapeDtypeStruct((rows, D), BF16),
            jax.ShapeDtypeStruct((replicas, 8, 128), F32),
            factor(D),
            factor(3 * D),
            factor(D),
            factor(D),
            factor(D),
            factor(FF),
            factor(FF),
            factor(D),
            factor(D),
            factor(D),
            jax.ShapeDtypeStruct((2, BLOCKS * D, D), BF16),
        ),
        in_specs=[anywhere, anywhere, vmem, smem, vmem, vmem] + [anywhere] * 4,
        out_specs=(anywhere, anywhere, vmem) + (anywhere,) * 11,
        scratch_shapes=[
            pltpu.VMEM((2, BLOCKS * D, D), BF16),
            per_micro(D),
            per_micro(D),
            per_micro(D),
            per_micro(D),
            saved(D),
            saved(3 * D),
            pltpu.VMEM((2, micros, HEADS, SEQ, SEQ), BF16),
            saved(D),
            saved(FF),
            pltpu.VMEM((2, micros, SEQ, 128), F32),
            two(D),
            two(FF),
            saved(D),
            two(D),
            pltpu.VMEM((SEQ, D), F32),
            pltpu.VMEM((4, 8, D), F32),
            pltpu.VMEM((micros, SEQ, SEQ), F32),
            dma((2, BLOCKS)),
            dma((2, BLOCKS)),
            dma((2, len(KINDS))),
            dma((2, micros)),
            dma((micros,)),
            dma((micros,)),
            dma((micros,)),
            dma((micros,)),
            dma((micros, sections)),
            dma((micros,)),
            dma((micros,)),
            dma((8, 2, micros)),
            dma((2, micros)),
            dma((2, micros)),
            dma((2, micros)),
            dma((2, micros)),
        ],
        compiler_params=pltpu.CompilerParams(
            collective_id=0, has_side_effects=True, vmem_limit_bytes=60 * MIB
        ),
        name="relay",
    )(tokens, cotangent, flags, groups, gain_one, gain_two, wqkv, wout, wup, wdown)


ROWS = 96
CHUNKS = 10
UP, DOWN = 4, 6
AGAIN = 256
ORDER = (3, 0, 1, 2) + tuple(range(4, CHUNKS))

LOANS = ((0, 1, 1, 0), (0, 1, 2, 1))
GUESTS = 2


def sum_kernel(
    sections,
    gains_in,
    fin_in,
    inp_in,
    u_in,
    dqkv_in,
    o_in,
    da_in,
    u2_in,
    dz_in,
    act_in,
    dm_in,
    u2_other,
    dm_other,
    wup_hbm,
    wdown_hbm,
    gains_out,
    fin_out,
    inp_out,
    qkv_out,
    out_out,
    up_out,
    down_out,
    u_v,
    dqkv_v,
    o_v,
    da_v,
    u2_v,
    dz_v,
    act_v,
    dm_v,
    wup_v,
    wdown_v,
    own,
    first,
    second,
    third,
    gains_v,
    fin_v,
    fin_t,
    inp_v,
    inp_stage,
    load_sem,
    gain_send,
    gain_recv,
    fin_sem,
    inp_send,
    inp_recv,
    lend_send,
    lend_recv,
    back_send,
    back_recv,
    send,
    recv,
    up_sem,
    out_sem,
):
    me = lax.axis_index("dp")
    section = lax.axis_index("pipe")
    core = lax.rem(me, 2)
    x = lax.rem(me // 2, 2)
    y = me // 4
    other_core = me + 1 - 2 * core
    other_x = me + 2 - 4 * x
    other_y = me + 4 - 8 * y

    barrier = pltpu.get_barrier_semaphore()
    for j in range(SHARDS):

        @pl.when(me != j)
        def _():
            pl.semaphore_signal(barrier, inc=1, device_id={"dp": j}, device_id_type=MESH)

    loans = LOANS if sections > 3 else ()
    for j in range(1, sections):
        for to in sorted({0} | {lender for lender, k, _, _ in loans if sections - k == j}):

            @pl.when(section == j)
            def _():
                pl.semaphore_signal(barrier, inc=1, device_id={"pipe": to}, device_id_type=MESH)

    sources = (u_in, dqkv_in, o_in, da_in)
    held = (u_v, dqkv_v, o_v, da_v)
    rows = dm_in.shape[1]

    def load(k, l):
        return pltpu.make_async_copy(sources[k].at[l], held[k], load_sem.at[k])

    def hidden(l, b, other=False):
        px, py = (1 - x, 1 - y) if other else (x, y)
        block = l * (2 * b + px) + (1 - l) * (2 * py + b)
        return pl.ds(pl.multiple_of(block * CHUNK, CHUNK), CHUNK)

    def mlp_loads(l):
        own_rows, other_rows = pl.ds(0, rows), pl.ds(rows, rows)
        copies = [
            (u2_other.at[l], u2_v.at[other_rows]),
            (dm_other.at[l], dm_v.at[other_rows]),
            (u2_in.at[l], u2_v.at[own_rows]),
            (dm_in.at[l], dm_v.at[own_rows]),
        ]
        for b in range(2):
            units = hidden(l, b)
            copies.append((wup_hbm.at[l, :, units], wup_v.at[b]))
            copies.append((wdown_hbm.at[l, units], wdown_v.at[b]))
            copies.append((dz_in.at[l, :, units], dz_v.at[b, own_rows]))
            copies.append((act_in.at[l, :, units], act_v.at[b, own_rows]))
        return [pltpu.make_async_copy(src, dst, load_sem.at[4 + k]) for k, (src, dst) in enumerate(copies)]

    for k in (2, 3, 0, 1):
        load(k, 1).start()
    for copy in mlp_loads(1):
        copy.start()

    def gain_copy(j, source):
        return pltpu.make_async_remote_copy(
            src_ref=gains_in.at[j],
            dst_ref=gains_v.at[source],
            send_sem=gain_send.at[j],
            recv_sem=gain_recv.at[source],
            device_id={"dp": j},
            device_id_type=MESH,
        )

    def inp_copy(j):
        return pltpu.make_async_remote_copy(
            src_ref=inp_stage.at[j],
            dst_ref=inp_out,
            send_sem=inp_send.at[j],
            recv_sem=inp_recv,
            device_id={"pipe": j},
            device_id_type=MESH,
        )

    def own_inp_copy():
        return pltpu.make_async_copy(inp_stage.at[0], inp_out, inp_send.at[0])

    def inp_load():
        return pltpu.make_async_copy(inp_in, inp_v, inp_send.at[0])

    def meet():
        others = lax.select(section == 0, sections - 1, 0)
        for lender in {lender for lender, _, _, _ in loans} - {0}:
            hosts = {k for other, k, _, _ in loans if other == lender}
            others = others + lax.select(section == lender, len(hosts), 0)
        pl.semaphore_wait(barrier, SHARDS - 1 + others)
        for j in range(SHARDS):

            @pl.when(me != j)
            def _():
                gain_copy(j, me).start()


    def remote(src, dst, step, n, to):
        return pltpu.make_async_remote_copy(
            src_ref=src,
            dst_ref=dst,
            send_sem=send.at[step, n],
            recv_sem=recv.at[step, n],
            device_id={"dp": to},
            device_id_type=MESH,
        )

    def give_copy(n, i):
        if i >= DOWN:
            return remote(own.at[i, 1 - core, 0], first.at[n, 0], 0, n, other_core)
        return remote(own.at[i, 1 - core], first.at[n], 0, n, other_core)

    def down_copy(n, l):
        mine, to = lax.select(l == 1, y, x), lax.select(l == 1, other_y, other_x)
        return remote(first.at[n, 0, 1 - mine], third.at[n], 2, n, to)

    def first_copy(n, i, l=None):
        if i >= UP:
            mine = lax.select(l == 1, y, x)
            to = lax.select(l == 1, other_y, other_x)
            return remote(first.at[n, 1 - mine], second.at[n], 1, n, to)
        if i % 2 == 0:
            return remote(first.at[n, :, 1 - x], second.at[n], 1, n, other_x)
        return remote(first.at[n, 1 - y], second.at[n], 1, n, other_y)

    def second_copy(n, i, l=None):
        if i >= UP:
            mine = lax.select(l == 1, x, y)
            to = lax.select(l == 1, other_x, other_y)
            return remote(second.at[n, 1 - mine], third.at[n], 2, n, to)
        if i % 2 == 0:
            return remote(second.at[n, 1 - y], third.at[n], 2, n, other_y)
        return remote(second.at[n, 1 - x], third.at[n], 2, n, other_x)

    def lend_copy(g):
        lender, k, i, slot = loans[g]
        return pltpu.make_async_remote_copy(
            src_ref=first.at[i],
            dst_ref=first.at[2 * CHUNKS + slot],
            send_sem=lend_send.at[g],
            recv_sem=lend_recv.at[g],
            device_id={"pipe": sections - k},
            device_id_type=MESH,
        )

    def back_copy(g):
        lender, k, i, slot = loans[g]
        return pltpu.make_async_remote_copy(
            src_ref=third.at[2 * CHUNKS + slot],
            dst_ref=third.at[i],
            send_sem=back_send.at[g],
            recv_sem=back_recv.at[g],
            device_id={"pipe": lender},
            device_id_type=MESH,
        )

    def lent_or(step, i, lent, kept):
        away = None
        for g, (lender, _, chunk, _) in enumerate(loans):
            if chunk == i:
                here = (step == 0) & (section == lender)
                pl.when(here)(functools.partial(lent, g))
                away = here if away is None else away | here
        if away is None:
            kept()
        else:
            pl.when(jnp.logical_not(away))(kept)

    def as_host(action):
        for g, (_, k, i, slot) in enumerate(loans):
            pl.when(section == sections - k)(functools.partial(action, g, 2 * CHUNKS + slot, i))

    lent_chunks = sorted({i for _, _, i, _ in loans})

    def result_copy(n, l, i):
        if i < 3:
            dst = qkv_out.at[l, :, pl.ds(i * CHUNK, CHUNK)]
        elif i < 4:
            dst = out_out.at[l]
        elif i < DOWN:
            dst = up_out.at[l, :, hidden(l, i - UP, other=True)]
        else:
            dst = down_out.at[l, pl.ds((i - DOWN) * ROWS, ROWS)]
        return pltpu.make_async_copy(third.at[n], dst, out_sem.at[n])

    def own_up_copy(n, l, i):
        mine = lax.select(l == 1, x, y)
        return pltpu.make_async_copy(second.at[n, mine], up_out.at[l, :, hidden(l, i - UP)], up_sem.at[n])

    def add_core(n, l, i):
        give_copy(n, i).wait_recv()
        if i >= DOWN:
            first[n, 0] = first[n, 0] + own[i, core, 0]
            down_copy(n, l).start()
        else:
            first[n] = first[n] + own[i, core]
            lent_or(1 - l, i, lambda g: lend_copy(g).start(), lambda: first_copy(n, i, l).start())

    def free(step, i):
        @pl.when(step > 0)
        def _():
            give_copy(i, i).wait_send()

    def second_sum(n, i, l=None):
        first_copy(n, i, l).wait_recv()
        if i >= UP:
            kept = first[n, lax.select(l == 1, y, x)]
        else:
            kept = first[n, :, x] if i % 2 == 0 else first[n, y]
        second[n] = second[n] + kept
        second_copy(n, i, l).start()
        if i >= UP:
            own_up_copy(n, l, i).start()

    def plain_products(step, carry):
        l = 1 - step
        base = step * CHUNKS

        def products(k, a, g, slots):
            load(k, l).wait()
            load(k + 1, l).wait()
            for i, columns in slots:
                free(step, i)
                part = tn(a[...], g[:, columns * CHUNK : (columns + 1) * CHUNK]).astype(BF16)
                for r in range(SHARDS):
                    own[i, r % 2, r // 4, (r // 2) % 2] = part[r * ROWS : (r + 1) * ROWS]
                if i == ORDER[0]:
                    pl.when(step == 0)(meet)
                give_copy(base + i, i).start()
                if i != ORDER[0]:
                    before = ORDER[ORDER.index(i) - 1]
                    add_core(base + before, l, before)
                else:

                    @pl.when(step > 0)
                    def _():
                        add_core(base - CHUNKS + ORDER[UP - 1], l + 1, ORDER[UP - 1])

        def reload(k):
            @pl.when(step == 0)
            def _():
                load(k, 0).start()
                load(k + 1, 0).start()

        products(2, o_v, da_v, ((3, 0),))
        reload(2)
        products(0, u_v, dqkv_v, ((0, 0), (1, 1), (2, 2)))
        reload(0)
        return carry

    lax.fori_loop(0, 2, plain_products, 0)
    add_core(CHUNKS + ORDER[UP - 1], 0, ORDER[UP - 1])

    def plain_sums(step):
        for i in ORDER[:UP]:
            lent_or(step, i, lambda g: None, functools.partial(second_sum, step * CHUNKS + i, i))

    def mlp_products(step, carry):
        l = 1 - step
        base = step * CHUNKS
        copies = mlp_loads(l)

        def next_loads(*which):
            @pl.when(step == 0)
            def _():
                later = mlp_loads(0)
                for k in which:
                    later[k].start()

        for k in (0, 1, 4, 5, 8, 9):
            copies[k].wait()

        def again(k, c):
            at = pl.ds(pl.multiple_of(rows + k * AGAIN, AGAIN), AGAIN)
            for b in range(2):
                act, slope = gelu_parts(nn(u2_v[at], wup_v[b]))
                act_v[b, at] = act.astype(BF16)
                dz_v[b, at] = (slope * nt(dm_v[at], wdown_v[b])).astype(BF16)
            return c

        lax.fori_loop(0, rows // AGAIN, again, 0)
        next_loads(4, 5, 8, 9)
        pl.when(step == 0)(functools.partial(plain_sums, 0))
        for k in (2, 3, 6, 7, 10, 11):
            copies[k].wait()
        for b in range(2):
            i = UP + b
            free(step, i)
            part = tn(u2_v[...], dz_v[b]).astype(BF16)
            for r in range(SHARDS):
                ry, rx = r // 4, (r // 2) % 2
                across, along = l * ry + (1 - l) * rx, l * rx + (1 - l) * ry
                own[i, r % 2, across, along] = part[r * ROWS : (r + 1) * ROWS]
            give_copy(base + i, i).start()
            if b == 1:
                add_core(base + UP, l, UP)
        next_loads(0, 2, 6, 10)
        for i in range(DOWN, CHUNKS):
            free(step, i)
        for b in range(2):
            part = tn(act_v[b], dm_v[...]).astype(BF16)
            for r in range(8):
                own[DOWN + r % 4, r // 4, 0, b] = part[r * ROWS : (r + 1) * ROWS]
        next_loads(1, 3, 7, 11)
        for i in range(DOWN, CHUNKS):
            give_copy(base + i, i).start()
        for i in range(UP + 1, CHUNKS):
            add_core(base + i, l, i)
        pl.when(step == 0)(functools.partial(plain_sums, 1))
        return carry

    lax.fori_loop(0, 2, mlp_products, 0)

    def up_sums(step, carry):
        for i in range(UP, DOWN):
            second_sum(step * CHUNKS + i, i, 1 - step)
        return carry

    lax.fori_loop(0, 2, up_sums, 0)

    def take_in(g, n, i):
        lend_copy(g).wait_recv()
        first_copy(n, i).start()

    as_host(take_in)
    as_host(lambda g, n, i: second_sum(n, i))

    fin_load = pltpu.make_async_copy(fin_in, fin_v, fin_sem)
    fin_load.start()
    fin_load.wait()
    width = D // sections
    for j in range(sections):
        first_lane = j * width - window_start(j, width)

        @pl.when(section == j)
        def _():
            for r in range(0, rows, SEQ):
                part = fin_v[r : r + SEQ, :].astype(F32)[:, first_lane : first_lane + width]
                fin_t[:, r : r + SEQ] = part.T.astype(BF16)

    fin_store = pltpu.make_async_copy(fin_t, fin_out, fin_sem)
    fin_store.start()

    @pl.when(section == 0)
    def _():
        inp_load().start()
        inp_load().wait()
        for j in range(sections):
            for r in range(0, rows, SEQ):
                part = inp_v[r : r + SEQ, :].astype(F32)[:, j * width : (j + 1) * width]
                inp_stage[j, :, r : r + SEQ] = part.T.astype(BF16)
        own_inp_copy().start()
        for j in range(1, sections):
            inp_copy(j).start()

    def take_in(g, n, i):
        lend_copy(g).wait_recv()
        first_copy(n, i).start()

    gains_v[me] = gains_in[me]
    for j in range(SHARDS):

        @pl.when(me != j)
        def _():
            gain_copy(j, j).wait_recv()

    total = gains_v[0]
    for j in range(1, SHARDS):
        total = total + gains_v[j]
    gains_out[...] = total

    def last_sum(n, i):
        second_copy(n, i).wait_recv()
        third[n] = third[n] + second[n, y if i % 2 == 0 else x]

    def last_sums(step, carry):
        for i in ORDER:
            n = step * CHUNKS + i
            if i >= DOWN:
                down_copy(n, 1 - step).wait_recv()
                third[n] = third[n] + first[n, 0, lax.select(step == 0, y, x)]
            elif i >= UP:
                second_copy(n, i, 1 - step).wait_recv()
            else:
                lent_or(step, i, lambda g: None, functools.partial(last_sum, n, i))
            if i not in lent_chunks:
                result_copy(n, 1 - step, i).start()
        return carry

    lax.fori_loop(0, 2, last_sums, 0)

    def give_back(g, n, i):
        last_sum(n, i)
        back_copy(g).start()

    as_host(give_back)
    for g, (lender, _, _, _) in enumerate(loans):

        @pl.when(section == lender)
        def _():
            back_copy(g).wait_recv()

    for i in lent_chunks:
        for step in range(2):
            result_copy(step * CHUNKS + i, 1 - step, i).start()

    def finish(step, carry):
        for i in range(CHUNKS):
            n = step * CHUNKS + i
            if i >= DOWN:
                down_copy(n, 1 - step).wait_send()
            else:

                def sent():
                    first_copy(n, i, 1 - step).wait_send()
                    second_copy(n, i, 1 - step).wait_send()
                    if i >= UP:
                        own_up_copy(n, 1 - step, i).wait()

                lent_or(step, i, lambda g: lend_copy(g).wait_send(), sent)
            result_copy(n, 1 - step, i).wait()
        return carry

    lax.fori_loop(0, 2, finish, 0)
    def guest_sent(g, n, i):
        first_copy(n, i).wait_send()
        second_copy(n, i).wait_send()
        back_copy(g).wait_send()

    as_host(guest_sent)

    for i in range(CHUNKS):
        give_copy(CHUNKS + i, i).wait_send()
    for j in range(SHARDS):

        @pl.when(me != j)
        def _():
            gain_copy(j, me).wait_send()

    fin_store.wait()

    @pl.when(section == 0)
    def _():
        own_inp_copy().wait()
        for j in range(1, sections):
            inp_copy(j).wait_send()

    @pl.when(section > 0)
    def _():
        inp_copy(0).wait_recv()


def summed(gains, fin, inp, *factors):
    sections = lax.axis_size("pipe")
    rows, width = inp.shape[0], D // sections
    anywhere = pl.BlockSpec(memory_space=pl.ANY)
    vmem = pl.BlockSpec(memory_space=pltpu.VMEM)
    dma = pltpu.SemaphoreType.DMA
    total = 2 * CHUNKS
    slots = total + GUESTS

    def shard(height, columns):
        return jax.ShapeDtypeStruct((2, height, columns), BF16)

    return pl.pallas_call(
        functools.partial(sum_kernel, sections),
        out_shape=(
            jax.ShapeDtypeStruct((8, 128), F32),
            jax.ShapeDtypeStruct((width, rows), BF16),
            jax.ShapeDtypeStruct((width, rows), BF16),
            shard(ROWS, 3 * D),
            shard(ROWS, D),
            shard(ROWS, FF),
            shard(4 * ROWS, D),
        ),
        in_specs=[vmem] + [anywhere] * 14,
        out_specs=(vmem,) + (anywhere,) * 6,
        scratch_shapes=[pltpu.VMEM((rows, f.shape[2]), BF16) for f in factors[:4]]
        + [
            pltpu.VMEM((2 * rows, D), BF16),
            pltpu.VMEM((2, 2 * rows, CHUNK), BF16),
            pltpu.VMEM((2, 2 * rows, CHUNK), BF16),
            pltpu.VMEM((2 * rows, D), BF16),
            pltpu.VMEM((2, D, CHUNK), BF16),
            pltpu.VMEM((2, CHUNK, D), BF16),
            pltpu.VMEM((CHUNKS, 2, 2, 2, ROWS, CHUNK), BF16),
            pltpu.VMEM((slots, 2, 2, ROWS, CHUNK), BF16),
            pltpu.VMEM((slots, 2, ROWS, CHUNK), BF16),
            pltpu.VMEM((slots, ROWS, CHUNK), BF16),
            pltpu.VMEM((SHARDS, 8, 128), F32),
            pltpu.VMEM((rows, FIN_WINDOW), BF16),
            pltpu.VMEM((width, rows), BF16),
            pltpu.VMEM((rows, D), BF16),
            pltpu.VMEM((sections, width, rows), BF16),
            dma((16,)),
            dma((SHARDS,)),
            dma((SHARDS,)),
            dma(()),
            dma((sections,)),
            dma(()),
            dma((len(LOANS),)),
            dma((len(LOANS),)),
            dma((len(LOANS),)),
            dma((len(LOANS),)),
            dma((3, slots)),
            dma((3, slots)),
            dma((total,)),
            dma((total,)),
        ],
        compiler_params=pltpu.CompilerParams(
            collective_id=1, has_side_effects=True, vmem_limit_bytes=60 * MIB
        ),
        name="sum",
    )(gains, fin, inp, *factors)


def write_kernel(count, share, gains, *refs):
    gain_one, gain_two = refs[count], refs[count + 1]
    gain_one[...] = gains[0:2, 0:share]
    gain_two[...] = gains[2:4, 0:share]
    sources, results, held, wide = (
        refs[:count],
        refs[count + 2 : 2 * count + 2],
        refs[2 * count + 2 : 3 * count + 2],
        refs[3 * count + 2 : 4 * count + 2],
    )
    load_sem, store_sem = refs[4 * count + 2 :]
    loads = [pltpu.make_async_copy(sources[k], held[k], load_sem.at[k]) for k in range(count)]
    stores = [pltpu.make_async_copy(wide[k], results[k], store_sem.at[k]) for k in range(count)]
    for load in loads:
        load.start()
    for k in range(count):
        loads[k].wait()
        wide[k][...] = held[k][...].astype(wide[k].dtype)
        stores[k].start()
    for store in stores:
        store.wait()


def written(gains, share, arrays, types):
    count = len(arrays)
    anywhere = pl.BlockSpec(memory_space=pl.ANY)
    vmem = pl.BlockSpec(memory_space=pltpu.VMEM)
    return pl.pallas_call(
        functools.partial(write_kernel, count, share),
        out_shape=(jax.ShapeDtypeStruct((2, share), F32),) * 2
        + tuple(jax.ShapeDtypeStruct(a.shape, t) for a, t in zip(arrays, types)),
        in_specs=[vmem] + [anywhere] * count,
        out_specs=(vmem, vmem) + (anywhere,) * count,
        scratch_shapes=[pltpu.VMEM(a.shape, a.dtype) for a in arrays]
        + [pltpu.VMEM(a.shape, t) for a, t in zip(arrays, types)]
        + [pltpu.SemaphoreType.DMA((count,)), pltpu.SemaphoreType.DMA((count,))],
        compiler_params=pltpu.CompilerParams(vmem_limit_bytes=60 * MIB),
        name="write",
    )(gains, *arrays)


def body(
    tokens,
    gain_one,
    qkv_weight,
    out_weight,
    gain_two,
    up_weight,
    down_weight,
    cotangent,
    flags,
    groups,
):
    micros = tokens.shape[0] // SEQ
    fin, inp, gains, u, dqkv, o, da, u2, dz, act, dm, u2_other, dm_other, _ = relay(
        tokens,
        cotangent,
        flags.reshape(micros, SEQ),
        groups,
        gain_one,
        gain_two,
        qkv_weight,
        out_weight,
        up_weight,
        down_weight,
    )

    replicas = lax.axis_size("dp")
    share = D // replicas
    if replicas == SHARDS and share == ROWS:
        gains, fin, inp, g_qkv, g_out, g_up, g_down = summed(
            gains, fin, inp, u, dqkv, o, da, u2, dz, act, dm, u2_other, dm_other, up_weight, down_weight
        )
    else:

        def grad(a, g):
            total = jnp.einsum("lsa,lsb->lab", a, g, preferred_element_type=F32).astype(BF16)
            return lax.psum_scatter(total, "dp", scatter_dimension=1, tiled=True)

        gains = lax.psum_scatter(gains, "dp", scatter_dimension=0)
        sections = lax.axis_size("pipe")
        width = D // sections
        first_lanes = jnp.array([j * width - window_start(j, width) for j in range(sections)])
        fin = lax.dynamic_slice_in_dim(fin, first_lanes[lax.axis_index("pipe")], width, 1).T
        inp = jnp.where(lax.axis_index("pipe") == 0, inp.T, jnp.zeros_like(inp.T))
        inp = lax.psum_scatter(inp, "pipe", scatter_dimension=0, tiled=True)
        g_qkv, g_out, g_up, g_down = grad(u, dqkv), grad(o, da), grad(u2, dz), grad(act, dm)
    gain_one_grad, gain_two_grad, fin, inp, g_qkv, g_out, g_up, g_down = written(
        gains, share, (fin, inp, g_qkv, g_out, g_up, g_down), (BF16,) + (F32,) * 5
    )
    return (fin.T, inp.T, gain_one_grad, g_qkv, g_out, gain_two_grad, g_up, g_down)


def solution(mesh):
    return jax.shard_map(
        body,
        mesh=mesh,
        in_specs=(
            P("dp", None),
            P("pipe", None),
            P("pipe", None, None),
            P("pipe", None, None),
            P("pipe", None),
            P("pipe", None, None),
            P("pipe", None, None),
            P("dp", None),
            P("dp"),
            P("dp"),
        ),
        out_specs=(
            P("dp", "pipe"),
            P("dp", "pipe"),
            P("pipe", "dp"),
            P("pipe", "dp", None),
            P("pipe", "dp", None),
            P("pipe", "dp"),
            P("pipe", "dp", None),
            P("pipe", "dp", None),
        ),
        check_vma=False,
    )
```

```python
import functools

import jax
import jax.numpy as jnp
from jax import lax
from jax.experimental import pallas as pl
from jax.experimental.pallas import tpu as pltpu
from jax.sharding import PartitionSpec as P

D = 768
HEADS = 16
HEAD_DIM = 48
FF = 3072
SEQ = 128
EPS = 1e-06
MESH = pl.DeviceIdType.MESH
F32 = jnp.float32
BF16 = jnp.bfloat16
LOG2E = 1.4426950408889634
SCALE = HEAD_DIM ** (-0.5)
MIB = 2**20
CHUNK = 768
TILE = 256

KINDS = ((0, 3), (3, 1), (4, 4), (8, 4))

TURNED = (8, 11, 4, 0)
BLOCKS = 12

FIN_WINDOW = 256


def window_start(section, width):
    return min(section * width // 128 * 128, D - FIN_WINDOW)


SHARDS = 8

WINDOWS = tuple(
    (96 * j // 128, -(-(96 * j % 128 + 96) // 128), 96 * j % 128) for j in range(HEADS // 2)
)


def nn(a, b):
    return jnp.dot(a, b, preferred_element_type=F32)


def nt(a, b):
    return lax.dot_general(a, b, (((1,), (1,)), ((), ())), preferred_element_type=F32)


def tn(a, b):
    return lax.dot_general(a, b, (((0,), (0,)), ((), ())), preferred_element_type=F32)


def lanes_of_head(first, width):
    lane = lax.broadcasted_iota(jnp.int32, (SEQ, width), 1)
    return ((lane >= first) & (lane < first + HEAD_DIM)).astype(F32).astype(BF16)


def two_heads(window, first):
    width = window.shape[1]
    return jnp.concatenate(
        [window * lanes_of_head(first, width), window * lanes_of_head(first + HEAD_DIM, width)], axis=0
    )


def add_window(tiles, first, part):
    for i in range(part.shape[1] // 128):
        piece = part[:, i * 128 : (i + 1) * 128]
        tiles[first + i] = piece if tiles[first + i] is None else tiles[first + i] + piece


def norm_parts(x):
    centre = x - jnp.mean(x, axis=-1, keepdims=True)
    spread = jnp.mean(centre * centre, axis=-1, keepdims=True)
    inverse = lax.rsqrt(spread + EPS)
    return centre * inverse, inverse


def gelu_parts(z):
    phi = 0.5 * (1.0 + lax.erf(z * 0.7071067811865476))
    density = jnp.exp2(z * z * (-0.5 * LOG2E)) * 0.3989422804014327
    return z * phi, phi + z * density


def relay_kernel(
    sections,
    replicas,
    micros,
    paired,
    tokens,
    cotangent,
    flags,
    groups,
    gain_one,
    gain_two,
    wqkv_hbm,
    wout_hbm,
    wup_hbm,
    wdown_hbm,
    fin_out,
    inp_out,
    gains_out,
    u_out,
    dqkv_out,
    o_out,
    da_out,
    u2_out,
    dz_out,
    act_out,
    dm_out,
    u2_other,
    dm_other,
    turned_hbm,
    weights,
    fwd_in,
    fwd_out,
    bwd_in,
    bwd_out,
    u_s,
    qkv_s,
    p_s,
    u2_s,
    gp_s,
    stat_s,
    o_s,
    act_s,
    dm_s,
    da_s,
    state,
    acc,
    bias,
    w_sem,
    turn_sem,
    swap_sem,
    in_sem,
    fwd_send,
    fwd_recv,
    bwd_send,
    bwd_recv,
    fin_send,
    fin_recv,
    inp_send,
    out_sem,
    u2_send,
    u2_recv,
    dm_send,
    dm_recv,
):
    me = lax.axis_index("pipe")
    last = sections - 1
    width = D // sections

    barrier = pltpu.get_barrier_semaphore()
    for j in range(sections):

        @pl.when(me != j)
        def _():
            pl.semaphore_signal(barrier, inc=1, device_id={"pipe": j}, device_id_type=MESH)

    replica = lax.axis_index("dp")
    x, y = lax.rem(replica // 2, 2), replica // 4
    if paired:
        for j in (replica + 2 - 4 * x, replica + 4 - 8 * y):
            pl.semaphore_signal(barrier, inc=1, device_id={"dp": j}, device_id_type=MESH)

    def block_rows(b, count=1):
        start = b * D
        return pl.ds(start if isinstance(b, int) else pl.multiple_of(start, D), count * D)

    def weight_copy(l, k, j):
        first, _ = KINDS[k]
        if k == 1:
            src = wout_hbm.at[l]
        elif k == 3:
            src = wdown_hbm.at[l, block_rows(j)]
        else:
            src = (wqkv_hbm, None, wup_hbm)[k].at[l, :, block_rows(j)]
        return pltpu.make_async_copy(src, weights.at[l, block_rows(first + j)], w_sem.at[l, first + j])

    def turned_copy(l, b):
        return pltpu.make_async_copy(
            weights.at[l, block_rows(b)], turned_hbm.at[l, block_rows(b)], turn_sem.at[l, b]
        )

    def swap_copy(l, k):
        first, count = KINDS[k]
        to = block_rows(TURNED[k], count)
        return pltpu.make_async_copy(
            turned_hbm.at[l, block_rows(first, count)], weights.at[1 - l, to], swap_sem.at[l, k]
        )

    def swap_in(l, m, *kinds):
        @pl.when((m == micros - 1) & (me == last))
        def _():
            for k in kinds:
                swap_copy(1 - l, k).start()

    def turn(l, b):
        def tile(r, c):
            return l, pl.ds(pl.multiple_of(b * D + r * TILE, TILE), TILE), pl.ds(c * TILE, TILE)

        for r in range(D // TILE):
            weights[tile(r, r)] = weights[tile(r, r)].T
            for c in range(r):
                lower = weights[tile(r, c)].T
                upper = weights[tile(c, r)].T
                weights[tile(c, r)] = lower
                weights[tile(r, c)] = upper

    def each_block(l, action):
        for k, (_, count) in enumerate(KINDS):

            def one(j, c):
                action(l, k, j)
                return c

            lax.fori_loop(0, count, one, 0)

    def token_copy(m):
        return pltpu.make_async_copy(tokens.at[pl.ds(m * SEQ, SEQ)], fwd_in.at[m], in_sem.at[0, m])

    def cotangent_copy(m):
        return pltpu.make_async_copy(cotangent.at[pl.ds(m * SEQ, SEQ)], bwd_in.at[m], in_sem.at[1, m])

    @pl.when(me == 0)
    def _():
        for m in range(micros):
            token_copy(m).start()

    def weights_start(l):
        for k, (_, count) in enumerate(KINDS):
            for j in range(count):
                weight_copy(l, k, j).start()

    weights_start(0)

    @pl.when(me > 0)
    def _():
        weights_start(1)


    @pl.when(me == last)
    def _():
        for m in range(micros):
            cotangent_copy(m).start()

    def forward_copy(m):
        return pltpu.make_async_remote_copy(
            src_ref=fwd_out.at[m],
            dst_ref=fwd_in.at[m],
            send_sem=fwd_send.at[m],
            recv_sem=fwd_recv.at[m],
            device_id={"pipe": lax.rem(me + 1, sections)},
            device_id_type=MESH,
        )

    def backward_copy(m):
        return pltpu.make_async_remote_copy(
            src_ref=bwd_out.at[m],
            dst_ref=bwd_in.at[m],
            send_sem=bwd_send.at[m],
            recv_sem=bwd_recv.at[m],
            device_id={"pipe": lax.rem(me + sections - 1, sections)},
            device_id_type=MESH,
        )

    def slots_of(m):
        return pl.ds(pl.multiple_of(m * SEQ, SEQ), SEQ)

    def fin_source(m, j):
        return fwd_out.at[m, :, pl.ds(window_start(j, width), FIN_WINDOW)]

    def fin_copy(m, j):
        return pltpu.make_async_remote_copy(
            src_ref=fin_source(m, j),
            dst_ref=fin_out.at[slots_of(m)],
            send_sem=fin_send.at[m, j],
            recv_sem=fin_recv.at[m],
            device_id={"pipe": j},
            device_id_type=MESH,
        )

    def own_fin_copy(m):
        return pltpu.make_async_copy(fin_source(m, last), fin_out.at[slots_of(m)], fin_send.at[m, last])

    def inp_copy(m):
        return pltpu.make_async_copy(bwd_out.at[m], inp_out.at[slots_of(m)], inp_send.at[m])


    outs = (u_out, dqkv_out, o_out, da_out, u2_out, dz_out, act_out, dm_out)

    def out_copies(kind, l, m):
        src = (
            u_s.at[l, m],
            qkv_s.at[l, m],
            o_s.at[l],
            da_s.at[l],
            u2_s.at[l, m],
            gp_s.at[l, m],
            act_s.at[l],
            dm_s.at[l, m],
        )[kind]
        out = outs[kind].at[l, pl.ds(m * SEQ, SEQ)]
        if kind not in (5, 6) or not paired:
            return [pltpu.make_async_copy(src, out, out_sem.at[kind, l, m])]
        copies = []
        for b in range(2):
            units = block_rows(l * (2 * b + x) + (1 - l) * (2 * y + b))
            sem = out_sem.at[kind + 3 * b, l, m]
            copies.append(pltpu.make_async_copy(src.at[:, units], out.at[:, pl.ds(b * D, D)], sem))
        return copies

    def out_start(kind, l, m):
        for copy in out_copies(kind, l, m):
            copy.start()

    def out_wait(kind, l, m):
        for copy in out_copies(kind, l, m):
            copy.wait()

    def partner(l):
        return {"dp": lax.select(l == 1, replica + 2 - 4 * x, replica + 4 - 8 * y)}

    def u2_copy(l, m):
        return pltpu.make_async_remote_copy(
            src_ref=u2_s.at[l, m],
            dst_ref=u2_other.at[l, slots_of(m)],
            send_sem=u2_send.at[l, m],
            recv_sem=u2_recv.at[l, m],
            device_id=partner(l),
            device_id_type=MESH,
        )

    def dm_copy(l, m):
        return pltpu.make_async_remote_copy(
            src_ref=dm_s.at[l, m],
            dst_ref=dm_other.at[l, slots_of(m)],
            send_sem=dm_send.at[l, m],
            recv_sem=dm_recv.at[l, m],
            device_id=partner(l),
            device_id_type=MESH,
        )

    def free_slot(kind, l, m):
        @pl.when(m > 0)
        def _():
            out_wait(kind, l, m - 1)

    row = lax.broadcasted_iota(jnp.int32, (SEQ, SEQ), 0) // (SEQ // 4)
    column = lax.broadcasted_iota(jnp.int32, (SEQ, SEQ), 1) // (SEQ // 4)
    same = (row == column).astype(F32)
    for m in range(micros):
        parted = (jnp.full((1, SEQ), groups[m], jnp.int32) == 1).astype(F32)
        valid = jnp.broadcast_to((flags[m : m + 1, :] == 1).astype(F32), (SEQ, SEQ)).T
        keep = jnp.maximum(same, 1.0 - parted) * valid
        bias[m] = (keep - 1.0) * 1e30

    def forward_layer(l, m):
        def weight_wait(k):
            @pl.when((m == 0) & (me < last))
            def _():
                for j in range(KINDS[k][1]):
                    weight_copy(l, k, j).wait()

        x = state[...]
        xhat, inverse = norm_parts(x)
        stat_s[l, m, :, 0:1] = inverse
        u = (xhat * gain_one[pl.ds(l, 1), :]).astype(BF16)
        u_s[l, m] = u
        out_start(0, l, m)
        weight_wait(0)
        for j in range(3):
            qkv_s[l, m, :, j * D : (j + 1) * D] = nn(u_s[l, m], weights[l, block_rows(j)]).astype(BF16)
        free_slot(2, l, m)
        slot = l
        added = bias[m]
        scores, tiles = [], [None] * 6
        for tile, count, inside in WINDOWS:
            lo, hi = tile * 128, (tile + count) * 128
            keys = two_heads(qkv_s[l, m, :, D + lo : D + hi], inside)
            scores.append(nt(keys, qkv_s[l, m, :, lo:hi]) * (SCALE * LOG2E))
        for j in range(len(WINDOWS)):
            for h in range(2):
                s = scores[j][h * SEQ : (h + 1) * SEQ] + added
                e = jnp.exp2(s - jnp.max(s, axis=0, keepdims=True))
                p = e * (1.0 / jnp.sum(e, axis=0, keepdims=True))
                p_s[l, m, 2 * j + h] = p.astype(BF16)
        for j, (tile, count, inside) in enumerate(WINDOWS):
            lo, hi = tile * 128, (tile + count) * 128
            values = two_heads(qkv_s[l, m, :, 2 * D + lo : 2 * D + hi], inside)
            p = jnp.concatenate([p_s[l, m, 2 * j], p_s[l, m, 2 * j + 1]], axis=0)
            add_window(tiles, tile, tn(p, values))
        for i in range(6):
            o_s[slot, :, i * 128 : (i + 1) * 128] = tiles[i].astype(BF16)
        out_start(2, l, m)
        weight_wait(1)

        @pl.when((m == 0) & (me == 0) & (l == 0))
        def _():
            weights_start(1)

        h = state[...] + nn(o_s[slot], weights[l, block_rows(3)])
        state[...] = h
        swap_in(l, m, 3)
        hhat, inverse = norm_parts(h)
        stat_s[l, m, :, 1:2] = inverse
        u2_s[l, m] = (hhat * gain_two[pl.ds(l, 1), :]).astype(BF16)
        out_start(4, l, m)

        @pl.when((m == 0) & (l == 0))
        def _():
            pl.semaphore_wait(barrier, sections - 1 + 2 * paired)

        if paired:
            u2_copy(l, m).start()
        weight_wait(2)
        free_slot(6, l, m)
        weight_wait(3)
        for j in range(4):
            act, slope = gelu_parts(nn(u2_s[l, m], weights[l, block_rows(4 + j)]))
            act_s[slot, :, j * D : (j + 1) * D] = act.astype(BF16)
            gp_s[l, m, :, j * D : (j + 1) * D] = slope.astype(BF16)
        swap_in(l, m, 2)
        state[...] = state[...] + nn(act_s[slot], weights[l, block_rows(8, 4)])
        swap_in(l, m, 1, 0)
        out_start(6, l, m)

    def norm_back(du, hat_scaled, gain, inverse):
        t = du * gain
        hat = hat_scaled * (1.0 / gain)
        weighted = du * hat_scaled
        return inverse * (
            t - jnp.mean(t, axis=-1, keepdims=True) - hat * jnp.mean(weighted, axis=-1, keepdims=True)
        ), weighted

    def add_rows(at, weighted):
        part = weighted[0:8]
        for r in range(8, SEQ, 8):
            part = part + weighted[r : r + 8]
        acc[at] = acc[at] + part

    def backward_layer(l, m):
        slot = l
        held = lax.select(me == last, 1 - l, l)

        def turned(k, j=0, count=1):
            return held, block_rows(lax.select(me == last, TURNED[k], KINDS[k][0]) + j, count)

        def turned_wait(k):
            @pl.when((m == 0) & (me == last))
            def _():
                swap_copy(l, k).wait()

        dy = state[...]
        turned_wait(3)
        turned_wait(2)
        dm_s[l, m] = dy.astype(BF16)
        out_start(7, l, m)
        if paired:
            dm_copy(l, m).start()
        for j in range(4):
            da = nn(dm_s[l, m], weights[turned(3, j)])
            dz = gp_s[l, m, :, j * D : (j + 1) * D].astype(F32) * da
            gp_s[l, m, :, j * D : (j + 1) * D] = dz.astype(BF16)
        out_start(5, l, m)
        dh, weighted = norm_back(
            nn(gp_s[l, m], weights[turned(2, 0, 4)]), u2_s[l, m].astype(F32), gain_two[pl.ds(l, 1), :], stat_s[l, m, :, 1:2]
        )
        add_rows(2 + l, weighted)
        dh = state[...] + dh
        state[...] = dh
        free_slot(3, l, m)
        da_s[slot] = dh.astype(BF16)
        out_start(3, l, m)
        turned_wait(1)
        turned_wait(0)
        do = nn(da_s[slot], weights[turned(1)]).astype(BF16)
        slopes, products = [], []
        q_tiles, k_tiles, v_tiles = [None] * 6, [None] * 6, [None] * 6
        for tile, count, inside in WINDOWS:
            lo, hi = tile * 128, (tile + count) * 128
            values = two_heads(qkv_s[l, m, :, 2 * D + lo : 2 * D + hi], inside)
            products.append(nt(values, do[:, lo:hi]))
        for j in range(len(WINDOWS)):
            for h in range(2):
                p = p_s[l, m, 2 * j + h].astype(F32)
                dp = products[j][h * SEQ : (h + 1) * SEQ]
                slopes.append((p * (dp - jnp.sum(p * dp, axis=0, keepdims=True))).astype(BF16))
        for j, (tile, count, inside) in enumerate(WINDOWS):
            lo, hi = tile * 128, (tile + count) * 128
            pair = slopes[2 * j : 2 * j + 2]
            keys = two_heads(qkv_s[l, m, :, D + lo : D + hi], inside)
            query = two_heads(qkv_s[l, m, :, lo:hi], inside)
            add_window(q_tiles, tile, tn(jnp.concatenate(pair, axis=0), keys))
            add_window(k_tiles, tile, nn(jnp.concatenate(pair, axis=1), query))
        for j, (tile, count, inside) in enumerate(WINDOWS):
            given = two_heads(do[:, tile * 128 : (tile + count) * 128], inside)
            p = jnp.concatenate([p_s[l, m, 2 * j], p_s[l, m, 2 * j + 1]], axis=1)
            add_window(v_tiles, tile, nn(p, given))
        for i in range(6):
            at = i * 128
            qkv_s[l, m, :, at : at + 128] = (q_tiles[i] * SCALE).astype(BF16)
            qkv_s[l, m, :, D + at : D + at + 128] = (k_tiles[i] * SCALE).astype(BF16)
            qkv_s[l, m, :, 2 * D + at : 2 * D + at + 128] = v_tiles[i].astype(BF16)
        out_start(1, l, m)
        du = nn(qkv_s[l, m], weights[turned(0, 0, 3)])
        dx, weighted = norm_back(
            du, u_s[l, m].astype(F32), gain_one[pl.ds(l, 1), :], stat_s[l, m, :, 0:1]
        )
        add_rows(l, weighted)
        state[...] = state[...] + dx

    @pl.when(me == last)
    def _():
        def make(l, k, j):
            b = KINDS[k][0] + j
            weight_copy(l, k, j).wait()
            turn(l, b)
            turned_copy(l, b).start()

        def again(l, k, j):
            turned_copy(l, KINDS[k][0] + j).wait()
            weight_copy(l, k, j).start()

        def ready(l, k, j):
            weight_copy(l, k, j).wait()

        for action in (make, again, ready):

            def one(l, c):
                each_block(l, action)
                return c

            lax.fori_loop(0, 2, one, 0)

    def forward_micro(m, carry):
        @pl.when(me == 0)
        def _():
            token_copy(m).wait()

        @pl.when(me > 0)
        def _():
            forward_copy(m).wait_recv()

        state[...] = fwd_in[m].astype(F32)

        def one(l, c):
            forward_layer(l, m)
            return c

        lax.fori_loop(0, 2, one, 0)

        fwd_out[m] = state[...].astype(BF16)

        @pl.when(me < last)
        def _():
            forward_copy(m).start()

        @pl.when(me == last)
        def _():
            own_fin_copy(m).start()
            for j in range(last):
                fin_copy(m, j).start()

        return carry

    lax.fori_loop(0, micros, forward_micro, 0)
    @pl.when(me < last)
    def _():
        def one(i, c):
            turn(1 - i // BLOCKS, lax.rem(i, BLOCKS))
            return c

        lax.fori_loop(0, 2 * BLOCKS, one, 0)

    acc[...] = jnp.zeros_like(acc)

    def backward_micro(m, carry):
        @pl.when(me == last)
        def _():
            cotangent_copy(m).wait()

        @pl.when(me < last)
        def _():
            backward_copy(m).wait_recv()

        state[...] = bwd_in[m].astype(F32)

        def one(i, c):
            backward_layer(1 - i, m)
            return c

        lax.fori_loop(0, 2, one, 0)

        bwd_out[m] = state[...].astype(BF16)

        @pl.when(me > 0)
        def _():
            backward_copy(m).start()

        @pl.when(me == 0)
        def _():
            inp_copy(m).start()

        return carry

    lax.fori_loop(0, micros, backward_micro, 0)

    share = D // replicas
    for k in range(4):
        gain = (gain_one, gain_two)[k // 2][k % 2 : k % 2 + 1, :]
        total = jnp.sum(acc[k], axis=0, keepdims=True) / gain
        for r in range(replicas):
            gains_out[r, k : k + 1, 0:share] = total[:, r * share : (r + 1) * share]

    for l in range(2):
        for kind in (2, 3, 6):
            out_wait(kind, l, micros - 1)
        for m in range(micros):
            for kind in (0, 1, 4, 5, 7):
                out_wait(kind, l, m)
            if paired:
                u2_copy(l, m).wait()
                dm_copy(l, m).wait()
    for m in range(micros):

        @pl.when(me < last)
        def _():
            forward_copy(m).wait_send()

        @pl.when(me > 0)
        def _():
            backward_copy(m).wait_send()

        @pl.when(me == last)
        def _():
            for j in range(last):
                fin_copy(m, j).wait_send()
            own_fin_copy(m).wait()

        @pl.when(me < last)
        def _():
            fin_copy(m, last).wait_recv()

        @pl.when(me == 0)
        def _():
            inp_copy(m).wait()


def relay(tokens, cotangent, flags, groups, gain_one, gain_two, wqkv, wout, wup, wdown):
    sections = lax.axis_size("pipe")
    replicas = lax.axis_size("dp")
    rows = tokens.shape[0]
    micros = rows // SEQ
    width = D // sections
    paired = replicas == SHARDS
    hidden = FF // 2 if paired else FF
    anywhere = pl.BlockSpec(memory_space=pl.ANY)
    vmem = pl.BlockSpec(memory_space=pltpu.VMEM)
    smem = pl.BlockSpec(memory_space=pltpu.SMEM)
    dma = pltpu.SemaphoreType.DMA

    def factor(columns):
        return jax.ShapeDtypeStruct((2, rows, columns), BF16)

    def saved(columns):
        return pltpu.VMEM((2, micros, SEQ, columns), BF16)

    def two(columns):
        return pltpu.VMEM((2, SEQ, columns), BF16)

    def per_micro(columns):
        return pltpu.VMEM((micros, SEQ, columns), BF16)

    return pl.pallas_call(
        functools.partial(relay_kernel, sections, replicas, micros, paired),
        out_shape=(
            jax.ShapeDtypeStruct((rows, FIN_WINDOW), BF16),
            jax.ShapeDtypeStruct((rows, D), BF16),
            jax.ShapeDtypeStruct((replicas, 8, 128), F32),
            factor(D),
            factor(3 * D),
            factor(D),
            factor(D),
            factor(D),
            factor(hidden),
            factor(hidden),
            factor(D),
            factor(D),
            factor(D),
            jax.ShapeDtypeStruct((2, BLOCKS * D, D), BF16),
        ),
        in_specs=[anywhere, anywhere, vmem, smem, vmem, vmem] + [anywhere] * 4,
        out_specs=(anywhere, anywhere, vmem) + (anywhere,) * 11,
        scratch_shapes=[
            pltpu.VMEM((2, BLOCKS * D, D), BF16),
            per_micro(D),
            per_micro(D),
            per_micro(D),
            per_micro(D),
            saved(D),
            saved(3 * D),
            pltpu.VMEM((2, micros, HEADS, SEQ, SEQ), BF16),
            saved(D),
            saved(FF),
            pltpu.VMEM((2, micros, SEQ, 128), F32),
            two(D),
            two(FF),
            saved(D),
            two(D),
            pltpu.VMEM((SEQ, D), F32),
            pltpu.VMEM((4, 8, D), F32),
            pltpu.VMEM((micros, SEQ, SEQ), F32),
            dma((2, BLOCKS)),
            dma((2, BLOCKS)),
            dma((2, len(KINDS))),
            dma((2, micros)),
            dma((micros,)),
            dma((micros,)),
            dma((micros,)),
            dma((micros,)),
            dma((micros, sections)),
            dma((micros,)),
            dma((micros,)),
            dma((10, 2, micros)),
            dma((2, micros)),
            dma((2, micros)),
            dma((2, micros)),
            dma((2, micros)),
        ],
        compiler_params=pltpu.CompilerParams(
            collective_id=0, has_side_effects=True, vmem_limit_bytes=60 * MIB
        ),
        name="relay",
    )(tokens, cotangent, flags, groups, gain_one, gain_two, wqkv, wout, wup, wdown)


ROWS = 96
CHUNKS = 10
UP, DOWN = 4, 6
AGAIN = 512
ORDER = (3, 0, 1, 2) + tuple(range(4, CHUNKS))

LOANS = ((0, 1, 1, 0), (0, 1, 2, 1))
GUESTS = 2


def sum_kernel(
    sections,
    gains_in,
    fin_in,
    inp_in,
    u_in,
    dqkv_in,
    o_in,
    da_in,
    u2_in,
    dz_in,
    act_in,
    dm_in,
    u2_other,
    dm_other,
    wup_hbm,
    wdown_hbm,
    gains_out,
    fin_out,
    inp_out,
    qkv_out,
    out_out,
    up_out,
    down_out,
    u_v,
    dqkv_v,
    o_v,
    da_v,
    u2_v,
    dz_v,
    act_v,
    dm_v,
    wup_v,
    wdown_v,
    own,
    first,
    second,
    third,
    gains_v,
    fin_v,
    fin_t,
    inp_v,
    inp_stage,
    load_sem,
    gain_send,
    gain_recv,
    fin_sem,
    inp_send,
    inp_recv,
    lend_send,
    lend_recv,
    back_send,
    back_recv,
    send,
    recv,
    up_sem,
    out_sem,
):
    me = lax.axis_index("dp")
    section = lax.axis_index("pipe")
    core = lax.rem(me, 2)
    x = lax.rem(me // 2, 2)
    y = me // 4
    other_core = me + 1 - 2 * core
    other_x = me + 2 - 4 * x
    other_y = me + 4 - 8 * y

    barrier = pltpu.get_barrier_semaphore()
    for j in range(SHARDS):

        @pl.when(me != j)
        def _():
            pl.semaphore_signal(barrier, inc=1, device_id={"dp": j}, device_id_type=MESH)

    loans = LOANS if sections > 3 else ()
    for j in range(1, sections):
        for to in sorted({0} | {lender for lender, k, _, _ in loans if sections - k == j}):

            @pl.when(section == j)
            def _():
                pl.semaphore_signal(barrier, inc=1, device_id={"pipe": to}, device_id_type=MESH)

    sources = (u_in, dqkv_in, o_in, da_in)
    held = (u_v, dqkv_v, o_v, da_v)
    rows = dm_in.shape[1]

    def load(k, l):
        return pltpu.make_async_copy(sources[k].at[l], held[k], load_sem.at[k])

    def hidden(l, b, other=False):
        px, py = (1 - x, 1 - y) if other else (x, y)
        block = l * (2 * b + px) + (1 - l) * (2 * py + b)
        return pl.ds(pl.multiple_of(block * CHUNK, CHUNK), CHUNK)

    def mlp_loads(l):
        own_rows, other_rows = pl.ds(0, rows), pl.ds(rows, rows)
        copies = [
            (u2_other.at[l], u2_v.at[other_rows]),
            (dm_other.at[l], dm_v.at[other_rows]),
            (u2_in.at[l], u2_v.at[own_rows]),
            (dm_in.at[l], dm_v.at[own_rows]),
        ]
        for b in range(2):
            units = hidden(l, b)
            copies.append((wup_hbm.at[l, :, units], wup_v.at[b]))
            copies.append((wdown_hbm.at[l, units], wdown_v.at[b]))
            copies.append((dz_in.at[l, :, pl.ds(b * CHUNK, CHUNK)], dz_v.at[b, own_rows]))
            copies.append((act_in.at[l, :, pl.ds(b * CHUNK, CHUNK)], act_v.at[b, own_rows]))
        return [pltpu.make_async_copy(src, dst, load_sem.at[4 + k]) for k, (src, dst) in enumerate(copies)]

    for k in (2, 3, 0, 1):
        load(k, 1).start()
    for copy in mlp_loads(1):
        copy.start()

    def gain_copy(j, source):
        return pltpu.make_async_remote_copy(
            src_ref=gains_in.at[j],
            dst_ref=gains_v.at[source],
            send_sem=gain_send.at[j],
            recv_sem=gain_recv.at[source],
            device_id={"dp": j},
            device_id_type=MESH,
        )

    def inp_copy(j):
        return pltpu.make_async_remote_copy(
            src_ref=inp_stage.at[j],
            dst_ref=inp_out,
            send_sem=inp_send.at[j],
            recv_sem=inp_recv,
            device_id={"pipe": j},
            device_id_type=MESH,
        )

    def own_inp_copy():
        return pltpu.make_async_copy(inp_stage.at[0], inp_out, inp_send.at[0])

    def inp_load():
        return pltpu.make_async_copy(inp_in, inp_v, inp_send.at[0])

    def meet():
        others = lax.select(section == 0, sections - 1, 0)
        for lender in {lender for lender, _, _, _ in loans} - {0}:
            hosts = {k for other, k, _, _ in loans if other == lender}
            others = others + lax.select(section == lender, len(hosts), 0)
        pl.semaphore_wait(barrier, SHARDS - 1 + others)
        for j in range(SHARDS):

            @pl.when(me != j)
            def _():
                gain_copy(j, me).start()


    def remote(src, dst, step, n, to):
        return pltpu.make_async_remote_copy(
            src_ref=src,
            dst_ref=dst,
            send_sem=send.at[step, n],
            recv_sem=recv.at[step, n],
            device_id={"dp": to},
            device_id_type=MESH,
        )

    def give_copy(n, i):
        if i >= DOWN:
            return remote(own.at[i, 1 - core, 0], first.at[n, 0], 0, n, other_core)
        return remote(own.at[i, 1 - core], first.at[n], 0, n, other_core)

    def down_copy(n, l):
        mine, to = lax.select(l == 1, y, x), lax.select(l == 1, other_y, other_x)
        return remote(first.at[n, 0, 1 - mine], third.at[n], 2, n, to)

    def first_copy(n, i, l=None):
        if i >= UP:
            mine = lax.select(l == 1, y, x)
            to = lax.select(l == 1, other_y, other_x)
            return remote(first.at[n, 1 - mine], second.at[n], 1, n, to)
        if i % 2 == 1:
            return remote(first.at[n, :, 1 - x], second.at[n], 1, n, other_x)
        return remote(first.at[n, 1 - y], second.at[n], 1, n, other_y)

    def second_copy(n, i, l=None):
        if i >= UP:
            mine = lax.select(l == 1, x, y)
            to = lax.select(l == 1, other_x, other_y)
            return remote(second.at[n, 1 - mine], third.at[n], 2, n, to)
        if i % 2 == 1:
            return remote(second.at[n, 1 - y], third.at[n], 2, n, other_y)
        return remote(second.at[n, 1 - x], third.at[n], 2, n, other_x)

    def lend_copy(g):
        lender, k, i, slot = loans[g]
        return pltpu.make_async_remote_copy(
            src_ref=first.at[i],
            dst_ref=first.at[2 * CHUNKS + slot],
            send_sem=lend_send.at[g],
            recv_sem=lend_recv.at[g],
            device_id={"pipe": sections - k},
            device_id_type=MESH,
        )

    def back_copy(g):
        lender, k, i, slot = loans[g]
        return pltpu.make_async_remote_copy(
            src_ref=third.at[2 * CHUNKS + slot],
            dst_ref=third.at[i],
            send_sem=back_send.at[g],
            recv_sem=back_recv.at[g],
            device_id={"pipe": lender},
            device_id_type=MESH,
        )

    def lent_or(step, i, lent, kept):
        away = None
        for g, (lender, _, chunk, _) in enumerate(loans):
            if chunk == i:
                here = (step == 0) & (section == lender)
                pl.when(here)(functools.partial(lent, g))
                away = here if away is None else away | here
        if away is None:
            kept()
        else:
            pl.when(jnp.logical_not(away))(kept)

    def as_host(action):
        for g, (_, k, i, slot) in enumerate(loans):
            pl.when(section == sections - k)(functools.partial(action, g, 2 * CHUNKS + slot, i))

    lent_chunks = sorted({i for _, _, i, _ in loans})

    def result_copy(n, l, i):
        if i < 3:
            dst = qkv_out.at[l, :, pl.ds(i * CHUNK, CHUNK)]
        elif i < 4:
            dst = out_out.at[l]
        elif i < DOWN:
            dst = up_out.at[l, :, hidden(l, i - UP, other=True)]
        else:
            dst = down_out.at[l, pl.ds((i - DOWN) * ROWS, ROWS)]
        return pltpu.make_async_copy(third.at[n], dst, out_sem.at[n])

    def own_up_copy(n, l, i):
        mine = lax.select(l == 1, x, y)
        return pltpu.make_async_copy(second.at[n, mine], up_out.at[l, :, hidden(l, i - UP)], up_sem.at[n])

    def add_core(n, l, i):
        give_copy(n, i).wait_recv()
        if i >= DOWN:
            first[n, 0] = first[n, 0] + own[i, core, 0]
            down_copy(n, l).start()
        else:
            first[n] = first[n] + own[i, core]
            lent_or(1 - l, i, lambda g: lend_copy(g).start(), lambda: first_copy(n, i, l).start())

    def free(step, i):
        @pl.when(step > 0)
        def _():
            give_copy(i, i).wait_send()

    def second_sum(n, i, l=None):
        first_copy(n, i, l).wait_recv()
        if i >= UP:
            kept = first[n, lax.select(l == 1, y, x)]
        else:
            kept = first[n, :, x] if i % 2 == 1 else first[n, y]
        second[n] = second[n] + kept
        second_copy(n, i, l).start()
        if i >= UP:
            own_up_copy(n, l, i).start()

    def plain_products(step, carry):
        l = 1 - step
        base = step * CHUNKS

        def products(k, a, g, slots):
            load(k, l).wait()
            load(k + 1, l).wait()
            for i, columns in slots:
                free(step, i)
                part = tn(a[...], g[:, columns * CHUNK : (columns + 1) * CHUNK]).astype(BF16)
                for r in range(SHARDS):
                    own[i, r % 2, r // 4, (r // 2) % 2] = part[r * ROWS : (r + 1) * ROWS]
                if i == ORDER[0]:
                    pl.when(step == 0)(meet)
                give_copy(base + i, i).start()
                if i != ORDER[0]:
                    before = ORDER[ORDER.index(i) - 1]
                    add_core(base + before, l, before)
                else:

                    @pl.when(step > 0)
                    def _():
                        add_core(base - CHUNKS + ORDER[UP - 1], l + 1, ORDER[UP - 1])

        def reload(k):
            @pl.when(step == 0)
            def _():
                load(k, 0).start()
                load(k + 1, 0).start()

        products(2, o_v, da_v, ((3, 0),))
        reload(2)
        products(0, u_v, dqkv_v, ((0, 0), (1, 1), (2, 2)))
        reload(0)
        return carry

    lax.fori_loop(0, 2, plain_products, 0)
    add_core(CHUNKS + ORDER[UP - 1], 0, ORDER[UP - 1])

    def plain_sums(step):
        for i in ORDER[:UP]:
            lent_or(step, i, lambda g: None, functools.partial(second_sum, step * CHUNKS + i, i))

    def mlp_products(step, carry):
        l = 1 - step
        base = step * CHUNKS
        copies = mlp_loads(l)

        def next_loads(*which):
            @pl.when(step == 0)
            def _():
                later = mlp_loads(0)
                for k in which:
                    later[k].start()

        for k in (0, 1, 4, 5, 8, 9):
            copies[k].wait()

        def again(k, c):
            at = pl.ds(pl.multiple_of(rows + k * AGAIN, AGAIN), AGAIN)
            for b in range(2):
                act, slope = gelu_parts(nn(u2_v[at], wup_v[b]))
                act_v[b, at] = act.astype(BF16)
                dz_v[b, at] = (slope * nt(dm_v[at], wdown_v[b])).astype(BF16)
            return c

        lax.fori_loop(0, rows // AGAIN, again, 0)
        next_loads(4, 5, 8, 9)
        pl.when(step == 0)(functools.partial(plain_sums, 0))
        for k in (2, 3, 6, 7, 10, 11):
            copies[k].wait()
        for b in range(2):
            i = UP + b
            free(step, i)
            part = tn(u2_v[...], dz_v[b]).astype(BF16)
            for r in range(SHARDS):
                ry, rx = r // 4, (r // 2) % 2
                across, along = l * ry + (1 - l) * rx, l * rx + (1 - l) * ry
                own[i, r % 2, across, along] = part[r * ROWS : (r + 1) * ROWS]
            give_copy(base + i, i).start()
            if b == 1:
                add_core(base + UP, l, UP)
        next_loads(0, 2, 6, 10)
        for i in range(DOWN, CHUNKS):
            free(step, i)
        for b in range(2):
            part = tn(act_v[b], dm_v[...]).astype(BF16)
            for r in range(8):
                own[DOWN + r % 4, r // 4, 0, b] = part[r * ROWS : (r + 1) * ROWS]
        next_loads(1, 3, 7, 11)
        for i in range(DOWN, CHUNKS):
            give_copy(base + i, i).start()
        for i in range(UP + 1, CHUNKS):
            add_core(base + i, l, i)
        pl.when(step == 0)(functools.partial(plain_sums, 1))
        return carry

    lax.fori_loop(0, 2, mlp_products, 0)

    def up_sums(step, carry):
        for i in range(UP, DOWN):
            second_sum(step * CHUNKS + i, i, 1 - step)
        return carry

    lax.fori_loop(0, 2, up_sums, 0)

    def take_in(g, n, i):
        lend_copy(g).wait_recv()
        first_copy(n, i).start()

    as_host(take_in)
    as_host(lambda g, n, i: second_sum(n, i))

    fin_load = pltpu.make_async_copy(fin_in, fin_v, fin_sem)
    fin_load.start()
    fin_load.wait()
    width = D // sections
    for j in range(sections):
        first_lane = j * width - window_start(j, width)

        @pl.when(section == j)
        def _():
            for r in range(0, rows, SEQ):
                part = fin_v[r : r + SEQ, :].astype(F32)[:, first_lane : first_lane + width]
                fin_t[:, r : r + SEQ] = part.T.astype(BF16)

    fin_store = pltpu.make_async_copy(fin_t, fin_out, fin_sem)
    fin_store.start()

    @pl.when(section == 0)
    def _():
        inp_load().start()
        inp_load().wait()
        for j in range(sections):
            for r in range(0, rows, SEQ):
                part = inp_v[r : r + SEQ, :].astype(F32)[:, j * width : (j + 1) * width]
                inp_stage[j, :, r : r + SEQ] = part.T.astype(BF16)
        own_inp_copy().start()
        for j in range(1, sections):
            inp_copy(j).start()

    def take_in(g, n, i):
        lend_copy(g).wait_recv()
        first_copy(n, i).start()

    gains_v[me] = gains_in[me]
    for j in range(SHARDS):

        @pl.when(me != j)
        def _():
            gain_copy(j, j).wait_recv()

    total = gains_v[0]
    for j in range(1, SHARDS):
        total = total + gains_v[j]
    gains_out[...] = total

    def last_sum(n, i):
        second_copy(n, i).wait_recv()
        third[n] = third[n] + second[n, y if i % 2 == 1 else x]

    def last_sums(step, carry):
        for i in ORDER:
            n = step * CHUNKS + i
            if i >= DOWN:
                down_copy(n, 1 - step).wait_recv()
                third[n] = third[n] + first[n, 0, lax.select(step == 0, y, x)]
            elif i >= UP:
                second_copy(n, i, 1 - step).wait_recv()
            else:
                lent_or(step, i, lambda g: None, functools.partial(last_sum, n, i))
            if i not in lent_chunks:
                result_copy(n, 1 - step, i).start()
        return carry

    lax.fori_loop(0, 2, last_sums, 0)

    def give_back(g, n, i):
        last_sum(n, i)
        back_copy(g).start()

    as_host(give_back)
    for g, (lender, _, _, _) in enumerate(loans):

        @pl.when(section == lender)
        def _():
            back_copy(g).wait_recv()

    for i in lent_chunks:
        for step in range(2):
            result_copy(step * CHUNKS + i, 1 - step, i).start()

    def finish(step, carry):
        for i in range(CHUNKS):
            n = step * CHUNKS + i
            if i >= DOWN:
                down_copy(n, 1 - step).wait_send()
            else:

                def sent():
                    first_copy(n, i, 1 - step).wait_send()
                    second_copy(n, i, 1 - step).wait_send()
                    if i >= UP:
                        own_up_copy(n, 1 - step, i).wait()

                lent_or(step, i, lambda g: lend_copy(g).wait_send(), sent)
            result_copy(n, 1 - step, i).wait()
        return carry

    lax.fori_loop(0, 2, finish, 0)
    def guest_sent(g, n, i):
        first_copy(n, i).wait_send()
        second_copy(n, i).wait_send()
        back_copy(g).wait_send()

    as_host(guest_sent)

    for i in range(CHUNKS):
        give_copy(CHUNKS + i, i).wait_send()
    for j in range(SHARDS):

        @pl.when(me != j)
        def _():
            gain_copy(j, me).wait_send()

    fin_store.wait()

    @pl.when(section == 0)
    def _():
        own_inp_copy().wait()
        for j in range(1, sections):
            inp_copy(j).wait_send()

    @pl.when(section > 0)
    def _():
        inp_copy(0).wait_recv()


def summed(gains, fin, inp, *factors):
    sections = lax.axis_size("pipe")
    rows, width = inp.shape[0], D // sections
    anywhere = pl.BlockSpec(memory_space=pl.ANY)
    vmem = pl.BlockSpec(memory_space=pltpu.VMEM)
    dma = pltpu.SemaphoreType.DMA
    total = 2 * CHUNKS
    slots = total + GUESTS

    def shard(height, columns):
        return jax.ShapeDtypeStruct((2, height, columns), BF16)

    return pl.pallas_call(
        functools.partial(sum_kernel, sections),
        out_shape=(
            jax.ShapeDtypeStruct((8, 128), F32),
            jax.ShapeDtypeStruct((width, rows), BF16),
            jax.ShapeDtypeStruct((width, rows), BF16),
            shard(ROWS, 3 * D),
            shard(ROWS, D),
            shard(ROWS, FF),
            shard(4 * ROWS, D),
        ),
        in_specs=[vmem] + [anywhere] * 14,
        out_specs=(vmem,) + (anywhere,) * 6,
        scratch_shapes=[pltpu.VMEM((rows, f.shape[2]), BF16) for f in factors[:4]]
        + [
            pltpu.VMEM((2 * rows, D), BF16),
            pltpu.VMEM((2, 2 * rows, CHUNK), BF16),
            pltpu.VMEM((2, 2 * rows, CHUNK), BF16),
            pltpu.VMEM((2 * rows, D), BF16),
            pltpu.VMEM((2, D, CHUNK), BF16),
            pltpu.VMEM((2, CHUNK, D), BF16),
            pltpu.VMEM((CHUNKS, 2, 2, 2, ROWS, CHUNK), BF16),
            pltpu.VMEM((slots, 2, 2, ROWS, CHUNK), BF16),
            pltpu.VMEM((slots, 2, ROWS, CHUNK), BF16),
            pltpu.VMEM((slots, ROWS, CHUNK), BF16),
            pltpu.VMEM((SHARDS, 8, 128), F32),
            pltpu.VMEM((rows, FIN_WINDOW), BF16),
            pltpu.VMEM((width, rows), BF16),
            pltpu.VMEM((rows, D), BF16),
            pltpu.VMEM((sections, width, rows), BF16),
            dma((16,)),
            dma((SHARDS,)),
            dma((SHARDS,)),
            dma(()),
            dma((sections,)),
            dma(()),
            dma((len(LOANS),)),
            dma((len(LOANS),)),
            dma((len(LOANS),)),
            dma((len(LOANS),)),
            dma((3, slots)),
            dma((3, slots)),
            dma((total,)),
            dma((total,)),
        ],
        compiler_params=pltpu.CompilerParams(
            collective_id=1, has_side_effects=True, vmem_limit_bytes=60 * MIB
        ),
        name="sum",
    )(gains, fin, inp, *factors)


def write_kernel(count, share, gains, *refs):
    gain_one, gain_two = refs[count], refs[count + 1]
    gain_one[...] = gains[0:2, 0:share]
    gain_two[...] = gains[2:4, 0:share]
    sources, results, held, wide = (
        refs[:count],
        refs[count + 2 : 2 * count + 2],
        refs[2 * count + 2 : 3 * count + 2],
        refs[3 * count + 2 : 4 * count + 2],
    )
    load_sem, store_sem = refs[4 * count + 2 :]
    pieces = []
    for k in reversed(range(count)):
        if len(sources[k].shape) == 3:
            pieces += [tuple(r.at[l] for r in (sources[k], held[k], wide[k], results[k])) for l in range(2)]
        else:
            pieces.append((sources[k], held[k], wide[k], results[k]))
    loads = [pltpu.make_async_copy(p[0], p[1], load_sem.at[i]) for i, p in enumerate(pieces)]
    stores = [pltpu.make_async_copy(p[2], p[3], store_sem.at[i]) for i, p in enumerate(pieces)]
    for load in loads:
        load.start()
    for load, store, piece in zip(loads, stores, pieces):
        load.wait()
        piece[2][...] = piece[1][...].astype(piece[2].dtype)
        store.start()
    for store in stores:
        store.wait()


def written(gains, share, arrays, types):
    count = len(arrays)
    anywhere = pl.BlockSpec(memory_space=pl.ANY)
    vmem = pl.BlockSpec(memory_space=pltpu.VMEM)
    return pl.pallas_call(
        functools.partial(write_kernel, count, share),
        out_shape=(jax.ShapeDtypeStruct((2, share), F32),) * 2
        + tuple(jax.ShapeDtypeStruct(a.shape, t) for a, t in zip(arrays, types)),
        in_specs=[vmem] + [anywhere] * count,
        out_specs=(vmem, vmem) + (anywhere,) * count,
        scratch_shapes=[pltpu.VMEM(a.shape, a.dtype) for a in arrays]
        + [pltpu.VMEM(a.shape, t) for a, t in zip(arrays, types)]
        + [pltpu.SemaphoreType.DMA((2 * count,)), pltpu.SemaphoreType.DMA((2 * count,))],
        compiler_params=pltpu.CompilerParams(vmem_limit_bytes=60 * MIB),
        name="write",
    )(gains, *arrays)


def body(
    tokens,
    gain_one,
    qkv_weight,
    out_weight,
    gain_two,
    up_weight,
    down_weight,
    cotangent,
    flags,
    groups,
):
    micros = tokens.shape[0] // SEQ
    fin, inp, gains, u, dqkv, o, da, u2, dz, act, dm, u2_other, dm_other, _ = relay(
        tokens,
        cotangent,
        flags.reshape(micros, SEQ),
        groups,
        gain_one,
        gain_two,
        qkv_weight,
        out_weight,
        up_weight,
        down_weight,
    )

    replicas = lax.axis_size("dp")
    share = D // replicas
    if replicas == SHARDS and share == ROWS:
        gains, fin, inp, g_qkv, g_out, g_up, g_down = summed(
            gains, fin, inp, u, dqkv, o, da, u2, dz, act, dm, u2_other, dm_other, up_weight, down_weight
        )
    else:

        def grad(a, g):
            total = jnp.einsum("lsa,lsb->lab", a, g, preferred_element_type=F32).astype(BF16)
            return lax.psum_scatter(total, "dp", scatter_dimension=1, tiled=True)

        gains = lax.psum_scatter(gains, "dp", scatter_dimension=0)
        sections = lax.axis_size("pipe")
        width = D // sections
        first_lanes = jnp.array([j * width - window_start(j, width) for j in range(sections)])
        fin = lax.dynamic_slice_in_dim(fin, first_lanes[lax.axis_index("pipe")], width, 1).T
        inp = jnp.where(lax.axis_index("pipe") == 0, inp.T, jnp.zeros_like(inp.T))
        inp = lax.psum_scatter(inp, "pipe", scatter_dimension=0, tiled=True)
        g_qkv, g_out, g_up, g_down = grad(u, dqkv), grad(o, da), grad(u2, dz), grad(act, dm)
    gain_one_grad, gain_two_grad, fin, inp, g_qkv, g_out, g_up, g_down = written(
        gains, share, (fin, inp, g_qkv, g_out, g_up, g_down), (BF16,) + (F32,) * 5
    )
    return (fin.T, inp.T, gain_one_grad, g_qkv, g_out, gain_two_grad, g_up, g_down)


def solution(mesh):
    return jax.shard_map(
        body,
        mesh=mesh,
        in_specs=(
            P("dp", None),
            P("pipe", None),
            P("pipe", None, None),
            P("pipe", None, None),
            P("pipe", None),
            P("pipe", None, None),
            P("pipe", None, None),
            P("dp", None),
            P("dp"),
            P("dp"),
        ),
        out_specs=(
            P("dp", "pipe"),
            P("dp", "pipe"),
            P("pipe", "dp"),
            P("pipe", "dp", None),
            P("pipe", "dp", None),
            P("pipe", "dp"),
            P("pipe", "dp", None),
            P("pipe", "dp", None),
        ),
        check_vma=False,
    )
```

```python
import functools

import jax
import jax.numpy as jnp
from jax import lax
from jax.experimental import pallas as pl
from jax.experimental.pallas import tpu as pltpu
from jax.sharding import PartitionSpec as P

D = 768
HEADS = 16
HEAD_DIM = 48
FF = 3072
SEQ = 128
EPS = 1e-06
MESH = pl.DeviceIdType.MESH
F32 = jnp.float32
BF16 = jnp.bfloat16
LOG2E = 1.4426950408889634
SCALE = HEAD_DIM ** (-0.5)
MIB = 2**20
CHUNK = 768
TILE = 256

KINDS = ((0, 3), (3, 1), (4, 4), (8, 4))

TURNED = (8, 11, 4, 0)
BLOCKS = 12

FIN_WINDOW = 256


def window_start(section, width):
    return min(section * width // 128 * 128, D - FIN_WINDOW)


SHARDS = 8

WINDOWS = tuple(
    (96 * j // 128, -(-(96 * j % 128 + 96) // 128), 96 * j % 128) for j in range(HEADS // 2)
)


def nn(a, b):
    return jnp.dot(a, b, preferred_element_type=F32)


def nt(a, b):
    return lax.dot_general(a, b, (((1,), (1,)), ((), ())), preferred_element_type=F32)


def tn(a, b):
    return lax.dot_general(a, b, (((0,), (0,)), ((), ())), preferred_element_type=F32)


def lanes_of_head(first, width):
    lane = lax.broadcasted_iota(jnp.int32, (SEQ, width), 1)
    return ((lane >= first) & (lane < first + HEAD_DIM)).astype(F32).astype(BF16)


def two_heads(window, first):
    width = window.shape[1]
    return jnp.concatenate(
        [window * lanes_of_head(first, width), window * lanes_of_head(first + HEAD_DIM, width)], axis=0
    )


def add_window(tiles, first, part):
    for i in range(part.shape[1] // 128):
        piece = part[:, i * 128 : (i + 1) * 128]
        tiles[first + i] = piece if tiles[first + i] is None else tiles[first + i] + piece


def norm_parts(x):
    centre = x - jnp.mean(x, axis=-1, keepdims=True)
    spread = jnp.mean(centre * centre, axis=-1, keepdims=True)
    inverse = lax.rsqrt(spread + EPS)
    return centre * inverse, inverse


def gelu_parts(z):
    phi = 0.5 * (1.0 + lax.erf(z * 0.7071067811865476))
    density = jnp.exp2(z * z * (-0.5 * LOG2E)) * 0.3989422804014327
    return z * phi, phi + z * density


def relay_kernel(
    sections,
    replicas,
    micros,
    paired,
    tokens,
    cotangent,
    flags,
    groups,
    gain_one,
    gain_two,
    wqkv_hbm,
    wout_hbm,
    wup_hbm,
    wdown_hbm,
    fin_out,
    inp_out,
    gains_out,
    u_out,
    dqkv_out,
    o_out,
    da_out,
    u2_out,
    dz_out,
    act_out,
    dm_out,
    u2_other,
    dm_other,
    turned_hbm,
    weights,
    fwd_in,
    fwd_out,
    bwd_in,
    bwd_out,
    u_s,
    qkv_s,
    p_s,
    u2_s,
    gp_s,
    stat_s,
    o_s,
    act_s,
    dm_s,
    da_s,
    state,
    acc,
    bias,
    w_sem,
    turn_sem,
    swap_sem,
    in_sem,
    fwd_send,
    fwd_recv,
    bwd_send,
    bwd_recv,
    fin_send,
    fin_recv,
    inp_send,
    out_sem,
    u2_send,
    u2_recv,
    dm_send,
    dm_recv,
):
    me = lax.axis_index("pipe")
    last = sections - 1
    width = D // sections

    barrier = pltpu.get_barrier_semaphore()
    for j in range(sections):

        @pl.when(me != j)
        def _():
            pl.semaphore_signal(barrier, inc=1, device_id={"pipe": j}, device_id_type=MESH)

    replica = lax.axis_index("dp")
    x, y = lax.rem(replica // 2, 2), replica // 4
    if paired:
        for j in (replica + 2 - 4 * x, replica + 4 - 8 * y):
            pl.semaphore_signal(barrier, inc=1, device_id={"dp": j}, device_id_type=MESH)

    def block_rows(b, count=1):
        start = b * D
        return pl.ds(start if isinstance(b, int) else pl.multiple_of(start, D), count * D)

    def weight_copy(l, k, j):
        first, _ = KINDS[k]
        if k == 1:
            src = wout_hbm.at[l]
        elif k == 3:
            src = wdown_hbm.at[l, block_rows(j)]
        else:
            src = (wqkv_hbm, None, wup_hbm)[k].at[l, :, block_rows(j)]
        return pltpu.make_async_copy(src, weights.at[l, block_rows(first + j)], w_sem.at[l, first + j])

    def turned_copy(l, b):
        return pltpu.make_async_copy(
            weights.at[l, block_rows(b)], turned_hbm.at[l, block_rows(b)], turn_sem.at[l, b]
        )

    def swap_copy(l, k):
        first, count = KINDS[k]
        to = block_rows(TURNED[k], count)
        return pltpu.make_async_copy(
            turned_hbm.at[l, block_rows(first, count)], weights.at[1 - l, to], swap_sem.at[l, k]
        )

    def swap_in(l, m, *kinds):
        @pl.when((m == micros - 1) & (me == last))
        def _():
            for k in kinds:
                swap_copy(1 - l, k).start()

    def turn(l, b):
        def tile(r, c):
            return l, pl.ds(pl.multiple_of(b * D + r * TILE, TILE), TILE), pl.ds(c * TILE, TILE)

        for r in range(D // TILE):
            weights[tile(r, r)] = weights[tile(r, r)].T
            for c in range(r):
                lower = weights[tile(r, c)].T
                upper = weights[tile(c, r)].T
                weights[tile(c, r)] = lower
                weights[tile(r, c)] = upper

    def each_block(l, action):
        for k, (_, count) in enumerate(KINDS):

            def one(j, c):
                action(l, k, j)
                return c

            lax.fori_loop(0, count, one, 0)

    def token_copy(m):
        return pltpu.make_async_copy(tokens.at[pl.ds(m * SEQ, SEQ)], fwd_in.at[m], in_sem.at[0, m])

    def cotangent_copy(m):
        return pltpu.make_async_copy(cotangent.at[pl.ds(m * SEQ, SEQ)], bwd_in.at[m], in_sem.at[1, m])

    @pl.when(me == 0)
    def _():
        for m in range(micros):
            token_copy(m).start()

    def weights_start(l):
        for k, (_, count) in enumerate(KINDS):
            for j in range(count):
                weight_copy(l, k, j).start()

    weights_start(0)

    @pl.when(me > 0)
    def _():
        weights_start(1)


    @pl.when(me == last)
    def _():
        for m in range(micros):
            cotangent_copy(m).start()

    def forward_copy(m):
        return pltpu.make_async_remote_copy(
            src_ref=fwd_out.at[m],
            dst_ref=fwd_in.at[m],
            send_sem=fwd_send.at[m],
            recv_sem=fwd_recv.at[m],
            device_id={"pipe": lax.rem(me + 1, sections)},
            device_id_type=MESH,
        )

    def backward_copy(m):
        return pltpu.make_async_remote_copy(
            src_ref=bwd_out.at[m],
            dst_ref=bwd_in.at[m],
            send_sem=bwd_send.at[m],
            recv_sem=bwd_recv.at[m],
            device_id={"pipe": lax.rem(me + sections - 1, sections)},
            device_id_type=MESH,
        )

    def slots_of(m):
        return pl.ds(pl.multiple_of(m * SEQ, SEQ), SEQ)

    def fin_source(m, j):
        return fwd_out.at[m, :, pl.ds(window_start(j, width), FIN_WINDOW)]

    def fin_copy(m, j):
        return pltpu.make_async_remote_copy(
            src_ref=fin_source(m, j),
            dst_ref=fin_out.at[slots_of(m)],
            send_sem=fin_send.at[j],
            recv_sem=fin_recv,
            device_id={"pipe": j},
            device_id_type=MESH,
        )

    def own_fin_copy(m):
        return pltpu.make_async_copy(fin_source(m, last), fin_out.at[slots_of(m)], fin_send.at[last])

    def inp_copy(m):
        return pltpu.make_async_copy(bwd_out.at[m], inp_out.at[slots_of(m)], inp_send.at[m])


    outs = (u_out, dqkv_out, o_out, da_out, u2_out, dz_out, act_out, dm_out)

    def out_copies(kind, l, m):
        src = (
            u_s.at[l, m],
            qkv_s.at[l, m],
            o_s.at[l],
            da_s.at[l],
            u2_s.at[l, m],
            gp_s.at[l, m],
            act_s.at[l],
            dm_s.at[l, m],
        )[kind]
        out = outs[kind].at[l, pl.ds(m * SEQ, SEQ)]
        if kind not in (5, 6) or not paired:
            return [pltpu.make_async_copy(src, out, out_sem.at[kind, l])]
        copies = []
        for b in range(2):
            units = block_rows(l * (2 * b + x) + (1 - l) * (2 * y + b))
            sem = out_sem.at[kind + 3 * b, l]
            copies.append(pltpu.make_async_copy(src.at[:, units], out.at[:, pl.ds(b * D, D)], sem))
        return copies

    def out_start(kind, l, m):
        for copy in out_copies(kind, l, m):
            copy.start()

    def out_wait(kind, l, m):
        for copy in out_copies(kind, l, m):
            copy.wait()

    def whole_wait(ref, sem):
        pltpu.make_async_copy(ref, ref, sem).wait()

    def out_wait_all(kind, l):
        if kind == 5 and paired:
            for b in range(2):
                whole_wait(outs[kind].at[l, :, pl.ds(b * D, D)], out_sem.at[kind + 3 * b, l])
        else:
            whole_wait(outs[kind].at[l], out_sem.at[kind, l])

    def partner(l):
        return {"dp": lax.select(l == 1, replica + 2 - 4 * x, replica + 4 - 8 * y)}

    def u2_copy(l, m):
        return pltpu.make_async_remote_copy(
            src_ref=u2_s.at[l, m],
            dst_ref=u2_other.at[l, slots_of(m)],
            send_sem=u2_send.at[l],
            recv_sem=u2_recv.at[l],
            device_id=partner(l),
            device_id_type=MESH,
        )

    def dm_copy(l, m):
        return pltpu.make_async_remote_copy(
            src_ref=dm_s.at[l, m],
            dst_ref=dm_other.at[l, slots_of(m)],
            send_sem=dm_send.at[l],
            recv_sem=dm_recv.at[l],
            device_id=partner(l),
            device_id_type=MESH,
        )

    def free_slot(kind, l, m):
        @pl.when(m > 0)
        def _():
            out_wait(kind, l, m - 1)

    row = lax.broadcasted_iota(jnp.int32, (SEQ, SEQ), 0) // (SEQ // 4)
    column = lax.broadcasted_iota(jnp.int32, (SEQ, SEQ), 1) // (SEQ // 4)
    same = (row == column).astype(F32)
    for m in range(micros):
        parted = (jnp.full((1, SEQ), groups[m], jnp.int32) == 1).astype(F32)
        valid = jnp.broadcast_to((flags[m : m + 1, :] == 1).astype(F32), (SEQ, SEQ)).T
        keep = jnp.maximum(same, 1.0 - parted) * valid
        bias[m] = (keep - 1.0) * 1e30

    def forward_layer(l, m):
        def weight_wait(k):
            @pl.when((m == 0) & (me < last))
            def _():
                for j in range(KINDS[k][1]):
                    weight_copy(l, k, j).wait()

        x = state[...]
        xhat, inverse = norm_parts(x)
        stat_s[l, m, :, 0:1] = inverse
        u = (xhat * gain_one[pl.ds(l, 1), :]).astype(BF16)
        u_s[l, m] = u
        out_start(0, l, m)
        weight_wait(0)
        for j in range(3):
            qkv_s[l, m, :, j * D : (j + 1) * D] = nn(u_s[l, m], weights[l, block_rows(j)]).astype(BF16)
        free_slot(2, l, m)
        slot = l
        added = bias[m]
        scores, tiles = [], [None] * 6
        for tile, count, inside in WINDOWS:
            lo, hi = tile * 128, (tile + count) * 128
            keys = two_heads(qkv_s[l, m, :, D + lo : D + hi], inside)
            scores.append(nt(keys, qkv_s[l, m, :, lo:hi]) * (SCALE * LOG2E))
        for j in range(len(WINDOWS)):
            for h in range(2):
                s = scores[j][h * SEQ : (h + 1) * SEQ] + added
                e = jnp.exp2(s - jnp.max(s, axis=0, keepdims=True))
                p = e * (1.0 / jnp.sum(e, axis=0, keepdims=True))
                p_s[l, m, 2 * j + h] = p.astype(BF16)
        for j, (tile, count, inside) in enumerate(WINDOWS):
            lo, hi = tile * 128, (tile + count) * 128
            values = two_heads(qkv_s[l, m, :, 2 * D + lo : 2 * D + hi], inside)
            p = jnp.concatenate([p_s[l, m, 2 * j], p_s[l, m, 2 * j + 1]], axis=0)
            add_window(tiles, tile, tn(p, values))
        for i in range(6):
            o_s[slot, :, i * 128 : (i + 1) * 128] = tiles[i].astype(BF16)
        out_start(2, l, m)
        weight_wait(1)

        @pl.when((m == 0) & (me == 0) & (l == 0))
        def _():
            weights_start(1)

        h = state[...] + nn(o_s[slot], weights[l, block_rows(3)])
        state[...] = h
        swap_in(l, m, 3)
        hhat, inverse = norm_parts(h)
        stat_s[l, m, :, 1:2] = inverse
        u2_s[l, m] = (hhat * gain_two[pl.ds(l, 1), :]).astype(BF16)
        out_start(4, l, m)

        @pl.when((m == 0) & (l == 0))
        def _():
            pl.semaphore_wait(barrier, sections - 1 + 2 * paired)

        if paired:
            u2_copy(l, m).start()
        weight_wait(2)
        free_slot(6, l, m)
        weight_wait(3)
        for j in range(4):
            act, slope = gelu_parts(nn(u2_s[l, m], weights[l, block_rows(4 + j)]))
            act_s[slot, :, j * D : (j + 1) * D] = act.astype(BF16)
            gp_s[l, m, :, j * D : (j + 1) * D] = slope.astype(BF16)
        swap_in(l, m, 2)
        state[...] = state[...] + nn(act_s[slot], weights[l, block_rows(8, 4)])
        swap_in(l, m, 1, 0)
        out_start(6, l, m)

    def norm_back(du, hat_scaled, gain, inverse):
        t = du * gain
        hat = hat_scaled * (1.0 / gain)
        weighted = du * hat_scaled
        return inverse * (
            t - jnp.mean(t, axis=-1, keepdims=True) - hat * jnp.mean(weighted, axis=-1, keepdims=True)
        ), weighted

    def add_rows(at, weighted):
        part = weighted[0:8]
        for r in range(8, SEQ, 8):
            part = part + weighted[r : r + 8]
        acc[at] = acc[at] + part

    def backward_layer(l, m):
        slot = l
        held = lax.select(me == last, 1 - l, l)

        def turned(k, j=0, count=1):
            return held, block_rows(lax.select(me == last, TURNED[k], KINDS[k][0]) + j, count)

        def turned_wait(k):
            @pl.when((m == 0) & (me == last))
            def _():
                swap_copy(l, k).wait()

        dy = state[...]
        turned_wait(3)
        turned_wait(2)
        dm_s[l, m] = dy.astype(BF16)
        out_start(7, l, m)
        if paired:
            dm_copy(l, m).start()
        for j in range(4):
            da = nn(dm_s[l, m], weights[turned(3, j)])
            dz = gp_s[l, m, :, j * D : (j + 1) * D].astype(F32) * da
            gp_s[l, m, :, j * D : (j + 1) * D] = dz.astype(BF16)
        out_start(5, l, m)
        dh, weighted = norm_back(
            nn(gp_s[l, m], weights[turned(2, 0, 4)]), u2_s[l, m].astype(F32), gain_two[pl.ds(l, 1), :], stat_s[l, m, :, 1:2]
        )
        add_rows(2 + l, weighted)
        dh = state[...] + dh
        state[...] = dh
        free_slot(3, l, m)
        da_s[slot] = dh.astype(BF16)
        out_start(3, l, m)
        turned_wait(1)
        turned_wait(0)
        do = nn(da_s[slot], weights[turned(1)]).astype(BF16)
        slopes, products = [], []
        q_tiles, k_tiles, v_tiles = [None] * 6, [None] * 6, [None] * 6
        for tile, count, inside in WINDOWS:
            lo, hi = tile * 128, (tile + count) * 128
            values = two_heads(qkv_s[l, m, :, 2 * D + lo : 2 * D + hi], inside)
            products.append(nt(values, do[:, lo:hi]))
        for j in range(len(WINDOWS)):
            for h in range(2):
                p = p_s[l, m, 2 * j + h].astype(F32)
                dp = products[j][h * SEQ : (h + 1) * SEQ]
                slopes.append((p * (dp - jnp.sum(p * dp, axis=0, keepdims=True))).astype(BF16))
        for j, (tile, count, inside) in enumerate(WINDOWS):
            lo, hi = tile * 128, (tile + count) * 128
            pair = slopes[2 * j : 2 * j + 2]
            keys = two_heads(qkv_s[l, m, :, D + lo : D + hi], inside)
            query = two_heads(qkv_s[l, m, :, lo:hi], inside)
            add_window(q_tiles, tile, tn(jnp.concatenate(pair, axis=0), keys))
            add_window(k_tiles, tile, nn(jnp.concatenate(pair, axis=1), query))
        for j, (tile, count, inside) in enumerate(WINDOWS):
            given = two_heads(do[:, tile * 128 : (tile + count) * 128], inside)
            p = jnp.concatenate([p_s[l, m, 2 * j], p_s[l, m, 2 * j + 1]], axis=1)
            add_window(v_tiles, tile, nn(p, given))
        for i in range(6):
            at = i * 128
            qkv_s[l, m, :, at : at + 128] = (q_tiles[i] * SCALE).astype(BF16)
            qkv_s[l, m, :, D + at : D + at + 128] = (k_tiles[i] * SCALE).astype(BF16)
            qkv_s[l, m, :, 2 * D + at : 2 * D + at + 128] = v_tiles[i].astype(BF16)
        out_start(1, l, m)
        du = nn(qkv_s[l, m], weights[turned(0, 0, 3)])
        dx, weighted = norm_back(
            du, u_s[l, m].astype(F32), gain_one[pl.ds(l, 1), :], stat_s[l, m, :, 0:1]
        )
        add_rows(l, weighted)
        state[...] = state[...] + dx

    @pl.when(me == last)
    def _():
        def make(l, k, j):
            b = KINDS[k][0] + j
            weight_copy(l, k, j).wait()
            turn(l, b)
            turned_copy(l, b).start()

        def again(l, k, j):
            turned_copy(l, KINDS[k][0] + j).wait()
            weight_copy(l, k, j).start()

        def ready(l, k, j):
            weight_copy(l, k, j).wait()

        for action in (make, again, ready):

            def one(l, c):
                each_block(l, action)
                return c

            lax.fori_loop(0, 2, one, 0)

    def forward_micro(m, carry):
        @pl.when(me == 0)
        def _():
            token_copy(m).wait()

        @pl.when(me > 0)
        def _():
            forward_copy(m).wait_recv()

        state[...] = fwd_in[m].astype(F32)

        def one(l, c):
            forward_layer(l, m)
            return c

        lax.fori_loop(0, 2, one, 0)

        fwd_out[m] = state[...].astype(BF16)

        @pl.when(me < last)
        def _():
            forward_copy(m).start()

        @pl.when(me == last)
        def _():
            own_fin_copy(m).start()
            for j in range(last):
                fin_copy(m, j).start()

        return carry

    lax.fori_loop(0, micros, forward_micro, 0)
    @pl.when(me < last)
    def _():
        def one(i, c):
            turn(1 - i // BLOCKS, lax.rem(i, BLOCKS))
            return c

        lax.fori_loop(0, 2 * BLOCKS, one, 0)

    acc[...] = jnp.zeros_like(acc)

    def backward_micro(m, carry):
        @pl.when(me == last)
        def _():
            cotangent_copy(m).wait()

        @pl.when(me < last)
        def _():
            backward_copy(m).wait_recv()

        state[...] = bwd_in[m].astype(F32)

        def one(i, c):
            backward_layer(1 - i, m)
            return c

        lax.fori_loop(0, 2, one, 0)

        bwd_out[m] = state[...].astype(BF16)

        @pl.when(me > 0)
        def _():
            backward_copy(m).start()

        @pl.when(me == 0)
        def _():
            inp_copy(m).start()

        return carry

    lax.fori_loop(0, micros, backward_micro, 0)

    share = D // replicas
    for k in range(4):
        gain = (gain_one, gain_two)[k // 2][k % 2 : k % 2 + 1, :]
        total = jnp.sum(acc[k], axis=0, keepdims=True) / gain
        for r in range(replicas):
            gains_out[r, k : k + 1, 0:share] = total[:, r * share : (r + 1) * share]

    for l in range(2):
        for kind in (2, 3, 6):
            out_wait(kind, l, micros - 1)
        for kind in (0, 1, 4, 5, 7):
            out_wait_all(kind, l)
        if paired:
            for sem in (u2_send, u2_recv, dm_send, dm_recv):
                whole_wait(dm_other.at[l], sem.at[l])

    @pl.when(me == last)
    def _():
        for j in range(sections):
            whole_wait(fin_out, fin_send.at[j])

    @pl.when(me < last)
    def _():
        whole_wait(fin_out, fin_recv)

    for m in range(micros):

        @pl.when(me < last)
        def _():
            forward_copy(m).wait_send()

        @pl.when(me > 0)
        def _():
            backward_copy(m).wait_send()

        @pl.when(me == 0)
        def _():
            inp_copy(m).wait()


def relay(tokens, cotangent, flags, groups, gain_one, gain_two, wqkv, wout, wup, wdown):
    sections = lax.axis_size("pipe")
    replicas = lax.axis_size("dp")
    rows = tokens.shape[0]
    micros = rows // SEQ
    width = D // sections
    paired = replicas == SHARDS
    hidden = FF // 2 if paired else FF
    anywhere = pl.BlockSpec(memory_space=pl.ANY)
    vmem = pl.BlockSpec(memory_space=pltpu.VMEM)
    smem = pl.BlockSpec(memory_space=pltpu.SMEM)
    dma = pltpu.SemaphoreType.DMA

    def factor(columns):
        return jax.ShapeDtypeStruct((2, rows, columns), BF16)

    def saved(columns):
        return pltpu.VMEM((2, micros, SEQ, columns), BF16)

    def two(columns):
        return pltpu.VMEM((2, SEQ, columns), BF16)

    def per_micro(columns):
        return pltpu.VMEM((micros, SEQ, columns), BF16)

    return pl.pallas_call(
        functools.partial(relay_kernel, sections, replicas, micros, paired),
        out_shape=(
            jax.ShapeDtypeStruct((rows, FIN_WINDOW), BF16),
            jax.ShapeDtypeStruct((rows, D), BF16),
            jax.ShapeDtypeStruct((replicas, 8, 128), F32),
            factor(D),
            factor(3 * D),
            factor(D),
            factor(D),
            factor(D),
            factor(hidden),
            factor(hidden),
            factor(D),
            factor(D),
            factor(D),
            jax.ShapeDtypeStruct((2, BLOCKS * D, D), BF16),
        ),
        in_specs=[anywhere, anywhere, vmem, smem, vmem, vmem] + [anywhere] * 4,
        out_specs=(anywhere, anywhere, vmem) + (anywhere,) * 11,
        scratch_shapes=[
            pltpu.VMEM((2, BLOCKS * D, D), BF16),
            per_micro(D),
            per_micro(D),
            per_micro(D),
            per_micro(D),
            saved(D),
            saved(3 * D),
            pltpu.VMEM((2, micros, HEADS, SEQ, SEQ), BF16),
            saved(D),
            saved(FF),
            pltpu.VMEM((2, micros, SEQ, 128), F32),
            two(D),
            two(FF),
            saved(D),
            two(D),
            pltpu.VMEM((SEQ, D), F32),
            pltpu.VMEM((4, 8, D), F32),
            pltpu.VMEM((micros, SEQ, SEQ), F32),
            dma((2, BLOCKS)),
            dma((2, BLOCKS)),
            dma((2, len(KINDS))),
            dma((2, micros)),
            dma((micros,)),
            dma((micros,)),
            dma((micros,)),
            dma((micros,)),
            dma((sections,)),
            dma(()),
            dma((micros,)),
            dma((10, 2)),
            dma((2,)),
            dma((2,)),
            dma((2,)),
            dma((2,)),
        ],
        compiler_params=pltpu.CompilerParams(
            collective_id=0, has_side_effects=True, vmem_limit_bytes=60 * MIB
        ),
        name="relay",
    )(tokens, cotangent, flags, groups, gain_one, gain_two, wqkv, wout, wup, wdown)


ROWS = 96
CHUNKS = 10
UP, DOWN = 4, 6
AGAIN = 512
ORDER = (3, 0, 1, 2) + tuple(range(4, CHUNKS))

LOANS = ((0, 1, 1, 0), (0, 1, 2, 1))
GUESTS = 2


def sum_kernel(
    sections,
    gains_in,
    fin_in,
    inp_in,
    u_in,
    dqkv_in,
    o_in,
    da_in,
    u2_in,
    dz_in,
    act_in,
    dm_in,
    u2_other,
    dm_other,
    wup_hbm,
    wdown_hbm,
    gains_out,
    fin_out,
    inp_out,
    qkv_out,
    out_out,
    up_out,
    down_out,
    u_v,
    dqkv_v,
    o_v,
    da_v,
    u2_v,
    dz_v,
    act_v,
    dm_v,
    wup_v,
    wdown_v,
    own,
    first,
    second,
    third,
    gains_v,
    fin_v,
    fin_t,
    inp_v,
    inp_stage,
    load_sem,
    gain_send,
    gain_recv,
    fin_sem,
    inp_send,
    inp_recv,
    lend_send,
    lend_recv,
    back_send,
    back_recv,
    give_send,
    send,
    recv,
    up_sem,
    out_sem,
):
    me = lax.axis_index("dp")
    section = lax.axis_index("pipe")
    core = lax.rem(me, 2)
    x = lax.rem(me // 2, 2)
    y = me // 4
    other_core = me + 1 - 2 * core
    other_x = me + 2 - 4 * x
    other_y = me + 4 - 8 * y

    barrier = pltpu.get_barrier_semaphore()
    for j in range(SHARDS):

        @pl.when(me != j)
        def _():
            pl.semaphore_signal(barrier, inc=1, device_id={"dp": j}, device_id_type=MESH)

    loans = LOANS if sections > 3 else ()
    for j in range(1, sections):
        for to in sorted({0} | {lender for lender, k, _, _ in loans if sections - k == j}):

            @pl.when(section == j)
            def _():
                pl.semaphore_signal(barrier, inc=1, device_id={"pipe": to}, device_id_type=MESH)

    sources = (u_in, dqkv_in, o_in, da_in)
    held = (u_v, dqkv_v, o_v, da_v)
    rows = dm_in.shape[1]

    def load(k, l):
        return pltpu.make_async_copy(sources[k].at[l], held[k], load_sem.at[k])

    def hidden(l, b, other=False):
        px, py = (1 - x, 1 - y) if other else (x, y)
        block = l * (2 * b + px) + (1 - l) * (2 * py + b)
        return pl.ds(pl.multiple_of(block * CHUNK, CHUNK), CHUNK)

    def mlp_loads(l):
        own_rows, other_rows = pl.ds(0, rows), pl.ds(rows, rows)
        copies = [
            (u2_other.at[l], u2_v.at[other_rows]),
            (dm_other.at[l], dm_v.at[other_rows]),
            (u2_in.at[l], u2_v.at[own_rows]),
            (dm_in.at[l], dm_v.at[own_rows]),
        ]
        for b in range(2):
            units = hidden(l, b)
            copies.append((wup_hbm.at[l, :, units], wup_v.at[b]))
            copies.append((wdown_hbm.at[l, units], wdown_v.at[b]))
            copies.append((dz_in.at[l, :, pl.ds(b * CHUNK, CHUNK)], dz_v.at[b, own_rows]))
            copies.append((act_in.at[l, :, pl.ds(b * CHUNK, CHUNK)], act_v.at[b, own_rows]))
        return [pltpu.make_async_copy(src, dst, load_sem.at[4 + k]) for k, (src, dst) in enumerate(copies)]

    for k in (2, 3, 0, 1):
        load(k, 1).start()
    for copy in mlp_loads(1):
        copy.start()

    def gain_copy(j, source):
        return pltpu.make_async_remote_copy(
            src_ref=gains_in.at[j],
            dst_ref=gains_v.at[source],
            send_sem=gain_send,
            recv_sem=gain_recv,
            device_id={"dp": j},
            device_id_type=MESH,
        )

    def inp_copy(j):
        return pltpu.make_async_remote_copy(
            src_ref=inp_stage.at[j],
            dst_ref=inp_out,
            send_sem=inp_send.at[j],
            recv_sem=inp_recv,
            device_id={"pipe": j},
            device_id_type=MESH,
        )

    def own_inp_copy():
        return pltpu.make_async_copy(inp_stage.at[0], inp_out, inp_send.at[0])

    def inp_load():
        return pltpu.make_async_copy(inp_in, inp_v, inp_send.at[0])

    def meet():
        others = lax.select(section == 0, sections - 1, 0)
        for lender in {lender for lender, _, _, _ in loans} - {0}:
            hosts = {k for other, k, _, _ in loans if other == lender}
            others = others + lax.select(section == lender, len(hosts), 0)
        pl.semaphore_wait(barrier, SHARDS - 1 + others)
        for j in range(SHARDS):

            @pl.when(me != j)
            def _():
                gain_copy(j, me).start()


    def whole_wait(ref, sem):
        pltpu.make_async_copy(ref, ref, sem).wait()

    def remote(src, dst, step, n, to, sent=None):
        return pltpu.make_async_remote_copy(
            src_ref=src,
            dst_ref=dst,
            send_sem=send.at[step - 1, n] if sent is None else sent,
            recv_sem=recv.at[step, n],
            device_id={"dp": to},
            device_id_type=MESH,
        )

    def give_copy(n, i):
        if i >= DOWN:
            return remote(own.at[i, 1 - core, 0], first.at[n, 0], 0, n, other_core, give_send.at[i])
        return remote(own.at[i, 1 - core], first.at[n], 0, n, other_core, give_send.at[i])

    def down_copy(n, l):
        mine, to = lax.select(l == 1, y, x), lax.select(l == 1, other_y, other_x)
        return remote(first.at[n, 0, 1 - mine], third.at[n], 2, n, to)

    def first_copy(n, i, l=None):
        if i >= UP:
            mine = lax.select(l == 1, y, x)
            to = lax.select(l == 1, other_y, other_x)
            return remote(first.at[n, 1 - mine], second.at[n], 1, n, to)
        if i % 2 == 1:
            return remote(first.at[n, :, 1 - x], second.at[n], 1, n, other_x)
        return remote(first.at[n, 1 - y], second.at[n], 1, n, other_y)

    def second_copy(n, i, l=None):
        if i >= UP:
            mine = lax.select(l == 1, x, y)
            to = lax.select(l == 1, other_x, other_y)
            return remote(second.at[n, 1 - mine], third.at[n], 2, n, to)
        if i % 2 == 1:
            return remote(second.at[n, 1 - y], third.at[n], 2, n, other_y)
        return remote(second.at[n, 1 - x], third.at[n], 2, n, other_x)

    def lend_copy(g):
        lender, k, i, slot = loans[g]
        return pltpu.make_async_remote_copy(
            src_ref=first.at[i],
            dst_ref=first.at[2 * CHUNKS + slot],
            send_sem=lend_send.at[g],
            recv_sem=lend_recv.at[g],
            device_id={"pipe": sections - k},
            device_id_type=MESH,
        )

    def back_copy(g):
        lender, k, i, slot = loans[g]
        return pltpu.make_async_remote_copy(
            src_ref=third.at[2 * CHUNKS + slot],
            dst_ref=third.at[i],
            send_sem=back_send.at[g],
            recv_sem=back_recv.at[g],
            device_id={"pipe": lender},
            device_id_type=MESH,
        )

    def lent_or(step, i, lent, kept):
        away = None
        for g, (lender, _, chunk, _) in enumerate(loans):
            if chunk == i:
                here = (step == 0) & (section == lender)
                pl.when(here)(functools.partial(lent, g))
                away = here if away is None else away | here
        if away is None:
            kept()
        else:
            pl.when(jnp.logical_not(away))(kept)

    def as_host(action):
        for g, (_, k, i, slot) in enumerate(loans):
            pl.when(section == sections - k)(functools.partial(action, g, 2 * CHUNKS + slot, i))

    lent_chunks = sorted({i for _, _, i, _ in loans})

    def result_copy(n, l, i):
        if i < 3:
            dst = qkv_out.at[l, :, pl.ds(i * CHUNK, CHUNK)]
        elif i < 4:
            dst = out_out.at[l]
        elif i < DOWN:
            dst = up_out.at[l, :, hidden(l, i - UP, other=True)]
        else:
            dst = down_out.at[l, pl.ds((i - DOWN) * ROWS, ROWS)]
        return pltpu.make_async_copy(third.at[n], dst, out_sem.at[1 - l])

    def own_up_copy(n, l, i):
        mine = lax.select(l == 1, x, y)
        return pltpu.make_async_copy(second.at[n, mine], up_out.at[l, :, hidden(l, i - UP)], up_sem.at[1 - l])

    def add_core(n, l, i):
        give_copy(n, i).wait_recv()
        if i >= DOWN:
            first[n, 0] = first[n, 0] + own[i, core, 0]
            down_copy(n, l).start()
        else:
            first[n] = first[n] + own[i, core]
            lent_or(1 - l, i, lambda g: lend_copy(g).start(), lambda: first_copy(n, i, l).start())

    def free(step, i):
        @pl.when(step > 0)
        def _():
            give_copy(i, i).wait_send()

    def second_sum(n, i, l=None):
        first_copy(n, i, l).wait_recv()
        if i >= UP:
            kept = first[n, lax.select(l == 1, y, x)]
        else:
            kept = first[n, :, x] if i % 2 == 1 else first[n, y]
        second[n] = second[n] + kept
        second_copy(n, i, l).start()
        if i >= UP:
            own_up_copy(n, l, i).start()

    def plain_products(step, carry):
        l = 1 - step
        base = step * CHUNKS

        def products(k, a, g, slots):
            load(k, l).wait()
            load(k + 1, l).wait()
            for i, columns in slots:
                free(step, i)
                part = tn(a[...], g[:, columns * CHUNK : (columns + 1) * CHUNK]).astype(BF16)
                for r in range(SHARDS):
                    own[i, r % 2, r // 4, (r // 2) % 2] = part[r * ROWS : (r + 1) * ROWS]
                if i == ORDER[0]:
                    pl.when(step == 0)(meet)
                give_copy(base + i, i).start()
                if i != ORDER[0]:
                    before = ORDER[ORDER.index(i) - 1]
                    add_core(base + before, l, before)
                else:

                    @pl.when(step > 0)
                    def _():
                        add_core(base - CHUNKS + ORDER[UP - 1], l + 1, ORDER[UP - 1])

        def reload(k):
            @pl.when(step == 0)
            def _():
                load(k, 0).start()
                load(k + 1, 0).start()

        products(2, o_v, da_v, ((3, 0),))
        reload(2)
        products(0, u_v, dqkv_v, ((0, 0), (1, 1), (2, 2)))
        reload(0)
        return carry

    lax.fori_loop(0, 2, plain_products, 0)
    add_core(CHUNKS + ORDER[UP - 1], 0, ORDER[UP - 1])

    def plain_sums(step):
        for i in ORDER[:UP]:
            lent_or(step, i, lambda g: None, functools.partial(second_sum, step * CHUNKS + i, i))

    def mlp_products(step, carry):
        l = 1 - step
        base = step * CHUNKS
        copies = mlp_loads(l)

        def next_loads(*which):
            @pl.when(step == 0)
            def _():
                later = mlp_loads(0)
                for k in which:
                    later[k].start()

        for k in (0, 1, 4, 5, 8, 9):
            copies[k].wait()

        def again(k, c):
            at = pl.ds(pl.multiple_of(rows + k * AGAIN, AGAIN), AGAIN)
            for b in range(2):
                act, slope = gelu_parts(nn(u2_v[at], wup_v[b]))
                act_v[b, at] = act.astype(BF16)
                dz_v[b, at] = (slope * nt(dm_v[at], wdown_v[b])).astype(BF16)
            return c

        lax.fori_loop(0, rows // AGAIN, again, 0)
        next_loads(4, 5, 8, 9)
        pl.when(step == 0)(functools.partial(plain_sums, 0))
        for k in (2, 3, 6, 7, 10, 11):
            copies[k].wait()
        for b in range(2):
            i = UP + b
            free(step, i)
            part = tn(u2_v[...], dz_v[b]).astype(BF16)
            for r in range(SHARDS):
                ry, rx = r // 4, (r // 2) % 2
                across, along = l * ry + (1 - l) * rx, l * rx + (1 - l) * ry
                own[i, r % 2, across, along] = part[r * ROWS : (r + 1) * ROWS]
            give_copy(base + i, i).start()
            if b == 1:
                add_core(base + UP, l, UP)
        next_loads(0, 2, 6, 10)
        for i in range(DOWN, CHUNKS):
            free(step, i)
        for b in range(2):
            part = tn(act_v[b], dm_v[...]).astype(BF16)
            for r in range(8):
                own[DOWN + r % 4, r // 4, 0, b] = part[r * ROWS : (r + 1) * ROWS]
        next_loads(1, 3, 7, 11)
        for i in range(DOWN, CHUNKS):
            give_copy(base + i, i).start()
        for i in range(UP + 1, CHUNKS):
            add_core(base + i, l, i)
        pl.when(step == 0)(functools.partial(plain_sums, 1))
        return carry

    lax.fori_loop(0, 2, mlp_products, 0)

    def up_sums(step, carry):
        for i in range(UP, DOWN):
            second_sum(step * CHUNKS + i, i, 1 - step)
        return carry

    lax.fori_loop(0, 2, up_sums, 0)

    def take_in(g, n, i):
        lend_copy(g).wait_recv()
        first_copy(n, i).start()

    as_host(take_in)
    as_host(lambda g, n, i: second_sum(n, i))

    fin_load = pltpu.make_async_copy(fin_in, fin_v, fin_sem)
    fin_load.start()
    fin_load.wait()
    width = D // sections
    for j in range(sections):
        first_lane = j * width - window_start(j, width)

        @pl.when(section == j)
        def _():
            for r in range(0, rows, SEQ):
                part = fin_v[r : r + SEQ, :].astype(F32)[:, first_lane : first_lane + width]
                fin_t[:, r : r + SEQ] = part.T.astype(BF16)

    fin_store = pltpu.make_async_copy(fin_t, fin_out, fin_sem)
    fin_store.start()

    @pl.when(section == 0)
    def _():
        inp_load().start()
        inp_load().wait()
        for j in range(sections):
            for r in range(0, rows, SEQ):
                part = inp_v[r : r + SEQ, :].astype(F32)[:, j * width : (j + 1) * width]
                inp_stage[j, :, r : r + SEQ] = part.T.astype(BF16)
        own_inp_copy().start()
        for j in range(1, sections):
            inp_copy(j).start()

    def take_in(g, n, i):
        lend_copy(g).wait_recv()
        first_copy(n, i).start()

    gains_v[me] = gains_in[me]
    whole_wait(gains_v.at[0 : SHARDS - 1], gain_recv)
    total = gains_v[0]
    for j in range(1, SHARDS):
        total = total + gains_v[j]
    gains_out[...] = total

    def last_sum(n, i):
        second_copy(n, i).wait_recv()
        third[n] = third[n] + second[n, y if i % 2 == 1 else x]

    def last_sums(step, carry):
        for i in ORDER:
            n = step * CHUNKS + i
            if i >= DOWN:
                down_copy(n, 1 - step).wait_recv()
                third[n] = third[n] + first[n, 0, lax.select(step == 0, y, x)]
            elif i >= UP:
                second_copy(n, i, 1 - step).wait_recv()
            else:
                lent_or(step, i, lambda g: None, functools.partial(last_sum, n, i))
            if i not in lent_chunks:
                result_copy(n, 1 - step, i).start()
        return carry

    lax.fori_loop(0, 2, last_sums, 0)

    def give_back(g, n, i):
        last_sum(n, i)
        back_copy(g).start()

    as_host(give_back)
    for g, (lender, _, _, _) in enumerate(loans):

        @pl.when(section == lender)
        def _():
            back_copy(g).wait_recv()

    for i in lent_chunks:
        for step in range(2):
            result_copy(step * CHUNKS + i, 1 - step, i).start()

    def finish(step, carry):
        for i in range(CHUNKS):
            n = step * CHUNKS + i
            if i >= DOWN:
                down_copy(n, 1 - step).wait_send()
            else:

                def sent():
                    first_copy(n, i, 1 - step).wait_send()
                    second_copy(n, i, 1 - step).wait_send()

                lent_or(step, i, lambda g: lend_copy(g).wait_send(), sent)
        whole_wait(third.at[0:CHUNKS], out_sem.at[step])
        whole_wait(third.at[0 : DOWN - UP], up_sem.at[step])
        return carry

    lax.fori_loop(0, 2, finish, 0)
    def guest_sent(g, n, i):
        first_copy(n, i).wait_send()
        second_copy(n, i).wait_send()
        back_copy(g).wait_send()

    as_host(guest_sent)

    for i in range(CHUNKS):
        give_copy(CHUNKS + i, i).wait_send()
    whole_wait(gains_v.at[0 : SHARDS - 1], gain_send)
    fin_store.wait()

    @pl.when(section == 0)
    def _():
        own_inp_copy().wait()
        for j in range(1, sections):
            inp_copy(j).wait_send()

    @pl.when(section > 0)
    def _():
        inp_copy(0).wait_recv()


def summed(gains, fin, inp, *factors):
    sections = lax.axis_size("pipe")
    rows, width = inp.shape[0], D // sections
    anywhere = pl.BlockSpec(memory_space=pl.ANY)
    vmem = pl.BlockSpec(memory_space=pltpu.VMEM)
    dma = pltpu.SemaphoreType.DMA
    total = 2 * CHUNKS
    slots = total + GUESTS

    def shard(height, columns):
        return jax.ShapeDtypeStruct((2, height, columns), BF16)

    return pl.pallas_call(
        functools.partial(sum_kernel, sections),
        out_shape=(
            jax.ShapeDtypeStruct((8, 128), F32),
            jax.ShapeDtypeStruct((width, rows), BF16),
            jax.ShapeDtypeStruct((width, rows), BF16),
            shard(ROWS, 3 * D),
            shard(ROWS, D),
            shard(ROWS, FF),
            shard(4 * ROWS, D),
        ),
        in_specs=[vmem] + [anywhere] * 14,
        out_specs=(vmem,) + (anywhere,) * 6,
        scratch_shapes=[pltpu.VMEM((rows, f.shape[2]), BF16) for f in factors[:4]]
        + [
            pltpu.VMEM((2 * rows, D), BF16),
            pltpu.VMEM((2, 2 * rows, CHUNK), BF16),
            pltpu.VMEM((2, 2 * rows, CHUNK), BF16),
            pltpu.VMEM((2 * rows, D), BF16),
            pltpu.VMEM((2, D, CHUNK), BF16),
            pltpu.VMEM((2, CHUNK, D), BF16),
            pltpu.VMEM((CHUNKS, 2, 2, 2, ROWS, CHUNK), BF16),
            pltpu.VMEM((slots, 2, 2, ROWS, CHUNK), BF16),
            pltpu.VMEM((slots, 2, ROWS, CHUNK), BF16),
            pltpu.VMEM((slots, ROWS, CHUNK), BF16),
            pltpu.VMEM((SHARDS, 8, 128), F32),
            pltpu.VMEM((rows, FIN_WINDOW), BF16),
            pltpu.VMEM((width, rows), BF16),
            pltpu.VMEM((rows, D), BF16),
            pltpu.VMEM((sections, width, rows), BF16),
            dma((16,)),
            dma(()),
            dma(()),
            dma(()),
            dma((sections,)),
            dma(()),
            dma((len(LOANS),)),
            dma((len(LOANS),)),
            dma((len(LOANS),)),
            dma((len(LOANS),)),
            dma((CHUNKS,)),
            dma((2, slots)),
            dma((3, slots)),
            dma((2,)),
            dma((2,)),
        ],
        compiler_params=pltpu.CompilerParams(
            collective_id=1, has_side_effects=True, vmem_limit_bytes=60 * MIB
        ),
        name="sum",
    )(gains, fin, inp, *factors)


def write_kernel(count, share, gains, *refs):
    gain_one, gain_two = refs[count], refs[count + 1]
    gain_one[...] = gains[0:2, 0:share]
    gain_two[...] = gains[2:4, 0:share]
    sources, results, held, wide = (
        refs[:count],
        refs[count + 2 : 2 * count + 2],
        refs[2 * count + 2 : 3 * count + 2],
        refs[3 * count + 2 : 4 * count + 2],
    )
    load_sem, store_sem = refs[4 * count + 2 :]
    pieces = []
    for k in reversed(range(count)):
        if len(sources[k].shape) == 3:
            pieces += [tuple(r.at[l] for r in (sources[k], held[k], wide[k], results[k])) for l in range(2)]
        else:
            pieces.append((sources[k], held[k], wide[k], results[k]))
    loads = [pltpu.make_async_copy(p[0], p[1], load_sem.at[i]) for i, p in enumerate(pieces)]
    stores = [pltpu.make_async_copy(p[2], p[3], store_sem.at[i]) for i, p in enumerate(pieces)]
    for load in loads:
        load.start()
    for load, store, piece in zip(loads, stores, pieces):
        load.wait()
        piece[2][...] = piece[1][...].astype(piece[2].dtype)
        store.start()
    for store in stores:
        store.wait()


def written(gains, share, arrays, types):
    count = len(arrays)
    anywhere = pl.BlockSpec(memory_space=pl.ANY)
    vmem = pl.BlockSpec(memory_space=pltpu.VMEM)
    return pl.pallas_call(
        functools.partial(write_kernel, count, share),
        out_shape=(jax.ShapeDtypeStruct((2, share), F32),) * 2
        + tuple(jax.ShapeDtypeStruct(a.shape, t) for a, t in zip(arrays, types)),
        in_specs=[vmem] + [anywhere] * count,
        out_specs=(vmem, vmem) + (anywhere,) * count,
        scratch_shapes=[pltpu.VMEM(a.shape, a.dtype) for a in arrays]
        + [pltpu.VMEM(a.shape, t) for a, t in zip(arrays, types)]
        + [pltpu.SemaphoreType.DMA((2 * count,)), pltpu.SemaphoreType.DMA((2 * count,))],
        compiler_params=pltpu.CompilerParams(vmem_limit_bytes=60 * MIB),
        name="write",
    )(gains, *arrays)


def body(
    tokens,
    gain_one,
    qkv_weight,
    out_weight,
    gain_two,
    up_weight,
    down_weight,
    cotangent,
    flags,
    groups,
):
    micros = tokens.shape[0] // SEQ
    fin, inp, gains, u, dqkv, o, da, u2, dz, act, dm, u2_other, dm_other, _ = relay(
        tokens,
        cotangent,
        flags.reshape(micros, SEQ),
        groups,
        gain_one,
        gain_two,
        qkv_weight,
        out_weight,
        up_weight,
        down_weight,
    )

    replicas = lax.axis_size("dp")
    share = D // replicas
    if replicas == SHARDS and share == ROWS:
        gains, fin, inp, g_qkv, g_out, g_up, g_down = summed(
            gains, fin, inp, u, dqkv, o, da, u2, dz, act, dm, u2_other, dm_other, up_weight, down_weight
        )
    else:

        def grad(a, g):
            total = jnp.einsum("lsa,lsb->lab", a, g, preferred_element_type=F32).astype(BF16)
            return lax.psum_scatter(total, "dp", scatter_dimension=1, tiled=True)

        gains = lax.psum_scatter(gains, "dp", scatter_dimension=0)
        sections = lax.axis_size("pipe")
        width = D // sections
        first_lanes = jnp.array([j * width - window_start(j, width) for j in range(sections)])
        fin = lax.dynamic_slice_in_dim(fin, first_lanes[lax.axis_index("pipe")], width, 1).T
        inp = jnp.where(lax.axis_index("pipe") == 0, inp.T, jnp.zeros_like(inp.T))
        inp = lax.psum_scatter(inp, "pipe", scatter_dimension=0, tiled=True)
        g_qkv, g_out, g_up, g_down = grad(u, dqkv), grad(o, da), grad(u2, dz), grad(act, dm)
    gain_one_grad, gain_two_grad, fin, inp, g_qkv, g_out, g_up, g_down = written(
        gains, share, (fin, inp, g_qkv, g_out, g_up, g_down), (BF16,) + (F32,) * 5
    )
    return (fin.T, inp.T, gain_one_grad, g_qkv, g_out, gain_two_grad, g_up, g_down)


def solution(mesh):
    return jax.shard_map(
        body,
        mesh=mesh,
        in_specs=(
            P("dp", None),
            P("pipe", None),
            P("pipe", None, None),
            P("pipe", None, None),
            P("pipe", None),
            P("pipe", None, None),
            P("pipe", None, None),
            P("dp", None),
            P("dp"),
            P("dp"),
        ),
        out_specs=(
            P("dp", "pipe"),
            P("dp", "pipe"),
            P("pipe", "dp"),
            P("pipe", "dp", None),
            P("pipe", "dp", None),
            P("pipe", "dp"),
            P("pipe", "dp", None),
            P("pipe", "dp", None),
        ),
        check_vma=False,
    )
```

```python
import functools

import jax
import jax.numpy as jnp
from jax import lax
from jax.experimental import pallas as pl
from jax.experimental.pallas import tpu as pltpu
from jax.sharding import PartitionSpec as P

D = 768
HEADS = 16
HEAD_DIM = 48
FF = 3072
SEQ = 128
EPS = 1e-06
MESH = pl.DeviceIdType.MESH
F32 = jnp.float32
BF16 = jnp.bfloat16
LOG2E = 1.4426950408889634
SCALE = HEAD_DIM ** (-0.5)
MIB = 2**20
CHUNK = 768
TILE = 256

KINDS = ((0, 3), (3, 1), (4, 4), (8, 4))

TURNED = (8, 11, 4, 0)
BLOCKS = 12

FIN_WINDOW = 256


def window_start(section, width):
    return min(section * width // 128 * 128, D - FIN_WINDOW)


SHARDS = 8

WINDOWS = tuple(
    (96 * j // 128, -(-(96 * j % 128 + 96) // 128), 96 * j % 128) for j in range(HEADS // 2)
)


def nn(a, b):
    return jnp.dot(a, b, preferred_element_type=F32)


def nt(a, b):
    return lax.dot_general(a, b, (((1,), (1,)), ((), ())), preferred_element_type=F32)


def tn(a, b):
    return lax.dot_general(a, b, (((0,), (0,)), ((), ())), preferred_element_type=F32)


def lanes_of_head(first, width):
    lane = lax.broadcasted_iota(jnp.int32, (SEQ, width), 1)
    return ((lane >= first) & (lane < first + HEAD_DIM)).astype(F32).astype(BF16)


def two_heads(window, first):
    width = window.shape[1]
    return jnp.concatenate(
        [window * lanes_of_head(first, width), window * lanes_of_head(first + HEAD_DIM, width)], axis=0
    )


def add_window(tiles, first, part):
    for i in range(part.shape[1] // 128):
        piece = part[:, i * 128 : (i + 1) * 128]
        tiles[first + i] = piece if tiles[first + i] is None else tiles[first + i] + piece


def norm_parts(x):
    centre = x - jnp.mean(x, axis=-1, keepdims=True)
    spread = jnp.mean(centre * centre, axis=-1, keepdims=True)
    inverse = lax.rsqrt(spread + EPS)
    return centre * inverse, inverse


def gelu_parts(z):
    phi = 0.5 * (1.0 + lax.erf(z * 0.7071067811865476))
    density = jnp.exp2(z * z * (-0.5 * LOG2E)) * 0.3989422804014327
    return z * phi, phi + z * density


def relay_kernel(
    sections,
    replicas,
    micros,
    paired,
    tokens,
    cotangent,
    flags,
    groups,
    gain_one,
    gain_two,
    wqkv_hbm,
    wout_hbm,
    wup_hbm,
    wdown_hbm,
    fin_out,
    inp_out,
    gains_out,
    u_out,
    dqkv_out,
    o_out,
    da_out,
    u2_out,
    dz_out,
    act_out,
    dm_out,
    u2_other,
    dm_other,
    turned_hbm,
    weights,
    fwd_in,
    fwd_out,
    bwd_in,
    bwd_out,
    u_s,
    qkv_s,
    p_s,
    u2_s,
    gp_s,
    stat_s,
    o_s,
    act_s,
    dm_s,
    da_s,
    state,
    acc,
    bias,
    w_sem,
    turn_sem,
    swap_sem,
    in_sem,
    fwd_send,
    fwd_recv,
    bwd_send,
    bwd_recv,
    fin_send,
    fin_recv,
    inp_send,
    out_sem,
    u2_send,
    u2_recv,
    dm_send,
    dm_recv,
):
    me = lax.axis_index("pipe")
    last = sections - 1
    width = D // sections

    replica = lax.axis_index("dp")
    x, y = lax.rem(replica // 2, 2), replica // 4

    def block_rows(b, count=1):
        start = b * D
        return pl.ds(start if isinstance(b, int) else pl.multiple_of(start, D), count * D)

    def weight_copy(l, k, j):
        first, _ = KINDS[k]
        if k == 1:
            src = wout_hbm.at[l]
        elif k == 3:
            src = wdown_hbm.at[l, block_rows(j)]
        else:
            src = (wqkv_hbm, None, wup_hbm)[k].at[l, :, block_rows(j)]
        return pltpu.make_async_copy(src, weights.at[l, block_rows(first + j)], w_sem.at[l, k])

    def turned_copy(l, k, b):
        return pltpu.make_async_copy(
            weights.at[l, block_rows(b)], turned_hbm.at[l, block_rows(b)], turn_sem.at[l, k]
        )

    def whole_wait(ref, sem):
        pltpu.make_async_copy(ref, ref, sem).wait()

    def kind_wait(l, k, sem):
        whole_wait(weights.at[l, block_rows(*KINDS[k])], sem.at[l, k])

    def swap_copy(l, k):
        first, count = KINDS[k]
        to = block_rows(TURNED[k], count)
        return pltpu.make_async_copy(
            turned_hbm.at[l, block_rows(first, count)], weights.at[1 - l, to], swap_sem.at[l, k]
        )

    def swap_in(l, m, *kinds):
        @pl.when((m == micros - 1) & (me == last))
        def _():
            for k in kinds:
                swap_copy(1 - l, k).start()

    def turn(l, b):
        def tile(r, c):
            return l, pl.ds(pl.multiple_of(b * D + r * TILE, TILE), TILE), pl.ds(c * TILE, TILE)

        for r in range(D // TILE):
            weights[tile(r, r)] = weights[tile(r, r)].T
            for c in range(r):
                lower = weights[tile(r, c)].T
                upper = weights[tile(c, r)].T
                weights[tile(c, r)] = lower
                weights[tile(r, c)] = upper

    def token_copy(m):
        return pltpu.make_async_copy(tokens.at[pl.ds(m * SEQ, SEQ)], fwd_in.at[m], in_sem.at[0, m])

    def cotangent_copy(m):
        return pltpu.make_async_copy(cotangent.at[pl.ds(m * SEQ, SEQ)], bwd_in.at[m], in_sem.at[1, m])

    @pl.when(me == 0)
    def _():
        for m in range(micros):
            token_copy(m).start()

    def weights_start(l):
        for k, (_, count) in enumerate(KINDS):
            for j in range(count):
                weight_copy(l, k, j).start()

    weights_start(0)

    @pl.when(me > 0)
    def _():
        weights_start(1)


    barrier = pltpu.get_barrier_semaphore()
    for j in range(sections):

        @pl.when(me != j)
        def _():
            pl.semaphore_signal(barrier, inc=1, device_id={"pipe": j}, device_id_type=MESH)

    if paired:
        for j in (replica + 2 - 4 * x, replica + 4 - 8 * y):
            pl.semaphore_signal(barrier, inc=1, device_id={"dp": j}, device_id_type=MESH)

    @pl.when(me == last)
    def _():
        for m in range(micros):
            cotangent_copy(m).start()

    def forward_copy(m):
        return pltpu.make_async_remote_copy(
            src_ref=fwd_out.at[m],
            dst_ref=fwd_in.at[m],
            send_sem=fwd_send.at[m],
            recv_sem=fwd_recv.at[m],
            device_id={"pipe": lax.rem(me + 1, sections)},
            device_id_type=MESH,
        )

    def backward_copy(m):
        return pltpu.make_async_remote_copy(
            src_ref=bwd_out.at[m],
            dst_ref=bwd_in.at[m],
            send_sem=bwd_send.at[m],
            recv_sem=bwd_recv.at[m],
            device_id={"pipe": lax.rem(me + sections - 1, sections)},
            device_id_type=MESH,
        )

    def slots_of(m):
        return pl.ds(pl.multiple_of(m * SEQ, SEQ), SEQ)

    def fin_source(m, j):
        return fwd_out.at[m, :, pl.ds(window_start(j, width), FIN_WINDOW)]

    def fin_copy(m, j):
        return pltpu.make_async_remote_copy(
            src_ref=fin_source(m, j),
            dst_ref=fin_out.at[slots_of(m)],
            send_sem=fin_send.at[j],
            recv_sem=fin_recv,
            device_id={"pipe": j},
            device_id_type=MESH,
        )

    def own_fin_copy(m):
        return pltpu.make_async_copy(fin_source(m, last), fin_out.at[slots_of(m)], fin_send.at[last])

    def inp_copy(m):
        return pltpu.make_async_copy(bwd_out.at[m], inp_out.at[slots_of(m)], inp_send.at[m])


    outs = (u_out, dqkv_out, o_out, da_out, u2_out, dz_out, act_out, dm_out)

    def out_copies(kind, l, m):
        src = (
            u_s.at[l, m],
            qkv_s.at[l, m],
            o_s.at[l],
            da_s.at[l],
            u2_s.at[l, m],
            gp_s.at[l, m],
            act_s.at[l],
            dm_s.at[l, m],
        )[kind]
        out = outs[kind].at[l, pl.ds(m * SEQ, SEQ)]
        if kind not in (5, 6) or not paired:
            return [pltpu.make_async_copy(src, out, out_sem.at[kind, l])]
        copies = []
        for b in range(2):
            units = block_rows(l * (2 * b + x) + (1 - l) * (2 * y + b))
            sem = out_sem.at[kind + 3 * b, l]
            copies.append(pltpu.make_async_copy(src.at[:, units], out.at[:, pl.ds(b * D, D)], sem))
        return copies

    def out_start(kind, l, m):
        for copy in out_copies(kind, l, m):
            copy.start()

    def out_wait(kind, l, m):
        for copy in out_copies(kind, l, m):
            copy.wait()

    def out_wait_all(kind, l):
        if kind == 5 and paired:
            for b in range(2):
                whole_wait(outs[kind].at[l, :, pl.ds(b * D, D)], out_sem.at[kind + 3 * b, l])
        else:
            whole_wait(outs[kind].at[l], out_sem.at[kind, l])

    def partner(l):
        return {"dp": lax.select(l == 1, replica + 2 - 4 * x, replica + 4 - 8 * y)}

    def u2_copy(l, m):
        return pltpu.make_async_remote_copy(
            src_ref=u2_s.at[l, m],
            dst_ref=u2_other.at[l, slots_of(m)],
            send_sem=u2_send.at[l],
            recv_sem=u2_recv.at[l],
            device_id=partner(l),
            device_id_type=MESH,
        )

    def dm_copy(l, m):
        return pltpu.make_async_remote_copy(
            src_ref=dm_s.at[l, m],
            dst_ref=dm_other.at[l, slots_of(m)],
            send_sem=dm_send.at[l],
            recv_sem=dm_recv.at[l],
            device_id=partner(l),
            device_id_type=MESH,
        )

    def free_slot(kind, l, m):
        @pl.when(m > 0)
        def _():
            out_wait(kind, l, m - 1)

    row = lax.broadcasted_iota(jnp.int32, (SEQ, SEQ), 0) // (SEQ // 4)
    column = lax.broadcasted_iota(jnp.int32, (SEQ, SEQ), 1) // (SEQ // 4)
    same = (row == column).astype(F32)
    for m in range(micros):
        parted = (jnp.full((1, SEQ), groups[m], jnp.int32) == 1).astype(F32)
        valid = jnp.broadcast_to((flags[m : m + 1, :] == 1).astype(F32), (SEQ, SEQ)).T
        keep = jnp.maximum(same, 1.0 - parted) * valid
        bias[m] = (keep - 1.0) * 1e30

    def forward_layer(l, m):
        def weight_wait(k):
            @pl.when((m == 0) & (me < last))
            def _():
                kind_wait(l, k, w_sem)

        x = state[...]
        xhat, inverse = norm_parts(x)
        stat_s[l, m, :, 0:1] = inverse
        u = (xhat * gain_one[pl.ds(l, 1), :]).astype(BF16)
        u_s[l, m] = u
        out_start(0, l, m)
        weight_wait(0)
        for j in range(3):
            qkv_s[l, m, :, j * D : (j + 1) * D] = nn(u_s[l, m], weights[l, block_rows(j)]).astype(BF16)
        free_slot(2, l, m)
        slot = l
        added = bias[m]
        scores, tiles = [], [None] * 6
        for tile, count, inside in WINDOWS:
            lo, hi = tile * 128, (tile + count) * 128
            keys = two_heads(qkv_s[l, m, :, D + lo : D + hi], inside)
            scores.append(nt(keys, qkv_s[l, m, :, lo:hi]) * (SCALE * LOG2E))
        for j in range(len(WINDOWS)):
            for h in range(2):
                s = scores[j][h * SEQ : (h + 1) * SEQ] + added
                e = jnp.exp2(s - jnp.max(s, axis=0, keepdims=True))
                p = e * (1.0 / jnp.sum(e, axis=0, keepdims=True))
                p_s[l, m, 2 * j + h] = p.astype(BF16)
        for j, (tile, count, inside) in enumerate(WINDOWS):
            lo, hi = tile * 128, (tile + count) * 128
            values = two_heads(qkv_s[l, m, :, 2 * D + lo : 2 * D + hi], inside)
            p = jnp.concatenate([p_s[l, m, 2 * j], p_s[l, m, 2 * j + 1]], axis=0)
            add_window(tiles, tile, tn(p, values))
        for i in range(6):
            o_s[slot, :, i * 128 : (i + 1) * 128] = tiles[i].astype(BF16)
        out_start(2, l, m)
        weight_wait(1)

        @pl.when((m == 0) & (me == 0) & (l == 0))
        def _():
            weights_start(1)

        h = state[...] + nn(o_s[slot], weights[l, block_rows(3)])
        state[...] = h
        swap_in(l, m, 3)
        hhat, inverse = norm_parts(h)
        stat_s[l, m, :, 1:2] = inverse
        u2_s[l, m] = (hhat * gain_two[pl.ds(l, 1), :]).astype(BF16)
        out_start(4, l, m)

        @pl.when((m == 0) & (l == 0))
        def _():
            pl.semaphore_wait(barrier, sections - 1 + 2 * paired)

        if paired:
            u2_copy(l, m).start()
        weight_wait(2)
        free_slot(6, l, m)
        weight_wait(3)
        for j in range(4):
            act, slope = gelu_parts(nn(u2_s[l, m], weights[l, block_rows(4 + j)]))
            act_s[slot, :, j * D : (j + 1) * D] = act.astype(BF16)
            gp_s[l, m, :, j * D : (j + 1) * D] = slope.astype(BF16)
        swap_in(l, m, 2)
        state[...] = state[...] + nn(act_s[slot], weights[l, block_rows(8, 4)])
        swap_in(l, m, 1, 0)
        out_start(6, l, m)

    def norm_back(du, hat_scaled, gain, inverse):
        t = du * gain
        hat = hat_scaled * (1.0 / gain)
        weighted = du * hat_scaled
        return inverse * (
            t - jnp.mean(t, axis=-1, keepdims=True) - hat * jnp.mean(weighted, axis=-1, keepdims=True)
        ), weighted

    def add_rows(at, weighted):
        part = weighted[0:8]
        for r in range(8, SEQ, 8):
            part = part + weighted[r : r + 8]
        acc[at] = acc[at] + part

    def backward_layer(l, m):
        slot = l
        held = lax.select(me == last, 1 - l, l)

        def turned(k, j=0, count=1):
            return held, block_rows(lax.select(me == last, TURNED[k], KINDS[k][0]) + j, count)

        def turned_wait(k):
            @pl.when((m == 0) & (me == last))
            def _():
                swap_copy(l, k).wait()

        dy = state[...]
        turned_wait(3)
        turned_wait(2)
        dm_s[l, m] = dy.astype(BF16)
        out_start(7, l, m)
        if paired:
            dm_copy(l, m).start()
        for j in range(4):
            da = nn(dm_s[l, m], weights[turned(3, j)])
            dz = gp_s[l, m, :, j * D : (j + 1) * D].astype(F32) * da
            gp_s[l, m, :, j * D : (j + 1) * D] = dz.astype(BF16)
        out_start(5, l, m)
        dh, weighted = norm_back(
            nn(gp_s[l, m], weights[turned(2, 0, 4)]), u2_s[l, m].astype(F32), gain_two[pl.ds(l, 1), :], stat_s[l, m, :, 1:2]
        )
        add_rows(2 + l, weighted)
        dh = state[...] + dh
        state[...] = dh
        free_slot(3, l, m)
        da_s[slot] = dh.astype(BF16)
        out_start(3, l, m)
        turned_wait(1)
        turned_wait(0)
        do = nn(da_s[slot], weights[turned(1)]).astype(BF16)
        slopes, products = [], []
        q_tiles, k_tiles, v_tiles = [None] * 6, [None] * 6, [None] * 6
        for tile, count, inside in WINDOWS:
            lo, hi = tile * 128, (tile + count) * 128
            values = two_heads(qkv_s[l, m, :, 2 * D + lo : 2 * D + hi], inside)
            products.append(nt(values, do[:, lo:hi]))
        for j in range(len(WINDOWS)):
            for h in range(2):
                p = p_s[l, m, 2 * j + h].astype(F32)
                dp = products[j][h * SEQ : (h + 1) * SEQ]
                slopes.append((p * (dp - jnp.sum(p * dp, axis=0, keepdims=True))).astype(BF16))
        for j, (tile, count, inside) in enumerate(WINDOWS):
            lo, hi = tile * 128, (tile + count) * 128
            pair = slopes[2 * j : 2 * j + 2]
            keys = two_heads(qkv_s[l, m, :, D + lo : D + hi], inside)
            query = two_heads(qkv_s[l, m, :, lo:hi], inside)
            add_window(q_tiles, tile, tn(jnp.concatenate(pair, axis=0), keys))
            add_window(k_tiles, tile, nn(jnp.concatenate(pair, axis=1), query))
        for j, (tile, count, inside) in enumerate(WINDOWS):
            given = two_heads(do[:, tile * 128 : (tile + count) * 128], inside)
            p = jnp.concatenate([p_s[l, m, 2 * j], p_s[l, m, 2 * j + 1]], axis=1)
            add_window(v_tiles, tile, nn(p, given))
        for i in range(6):
            at = i * 128
            qkv_s[l, m, :, at : at + 128] = (q_tiles[i] * SCALE).astype(BF16)
            qkv_s[l, m, :, D + at : D + at + 128] = (k_tiles[i] * SCALE).astype(BF16)
            qkv_s[l, m, :, 2 * D + at : 2 * D + at + 128] = v_tiles[i].astype(BF16)
        out_start(1, l, m)
        du = nn(qkv_s[l, m], weights[turned(0, 0, 3)])
        dx, weighted = norm_back(
            du, u_s[l, m].astype(F32), gain_one[pl.ds(l, 1), :], stat_s[l, m, :, 0:1]
        )
        add_rows(l, weighted)
        state[...] = state[...] + dx

    @pl.when(me == last)
    def _():
        def make(l, c):
            for k, (first, count) in enumerate(KINDS):
                kind_wait(l, k, w_sem)

                def one(j, c):
                    turn(l, first + j)
                    turned_copy(l, k, first + j).start()
                    return c

                lax.fori_loop(0, count, one, 0)
            return c

        def again(l, c):
            for k, (_, count) in enumerate(KINDS):
                kind_wait(l, k, turn_sem)
                for j in range(count):
                    weight_copy(l, k, j).start()
            return c

        def ready(l, c):
            for k in range(len(KINDS)):
                kind_wait(l, k, w_sem)
            return c

        for action in (make, again, ready):
            lax.fori_loop(0, 2, action, 0)

    def forward_micro(m, carry):
        @pl.when(me == 0)
        def _():
            token_copy(m).wait()

        @pl.when(me > 0)
        def _():
            forward_copy(m).wait_recv()

        state[...] = fwd_in[m].astype(F32)

        def one(l, c):
            forward_layer(l, m)
            return c

        lax.fori_loop(0, 2, one, 0)

        fwd_out[m] = state[...].astype(BF16)

        @pl.when(me < last)
        def _():
            forward_copy(m).start()

        @pl.when(me == last)
        def _():
            own_fin_copy(m).start()
            for j in range(last):
                fin_copy(m, j).start()

        return carry

    lax.fori_loop(0, micros, forward_micro, 0)
    @pl.when(me < last)
    def _():
        def one(i, c):
            turn(1 - i // BLOCKS, lax.rem(i, BLOCKS))
            return c

        lax.fori_loop(0, 2 * BLOCKS, one, 0)

    acc[...] = jnp.zeros_like(acc)

    def backward_micro(m, carry):
        @pl.when(me == last)
        def _():
            cotangent_copy(m).wait()

        @pl.when(me < last)
        def _():
            backward_copy(m).wait_recv()

        state[...] = bwd_in[m].astype(F32)

        def one(i, c):
            backward_layer(1 - i, m)
            return c

        lax.fori_loop(0, 2, one, 0)

        bwd_out[m] = state[...].astype(BF16)

        @pl.when(me > 0)
        def _():
            backward_copy(m).start()

        @pl.when(me == 0)
        def _():
            inp_copy(m).start()

        return carry

    lax.fori_loop(0, micros, backward_micro, 0)

    share = D // replicas
    for k in range(4):
        gain = (gain_one, gain_two)[k // 2][k % 2 : k % 2 + 1, :]
        total = jnp.sum(acc[k], axis=0, keepdims=True) / gain
        for r in range(replicas):
            gains_out[r, k : k + 1, 0:share] = total[:, r * share : (r + 1) * share]

    for l in range(2):
        for kind in (2, 3, 6):
            out_wait(kind, l, micros - 1)
        for kind in (0, 1, 4, 5, 7):
            out_wait_all(kind, l)
        if paired:
            for sem in (u2_send, u2_recv, dm_send, dm_recv):
                whole_wait(dm_other.at[l], sem.at[l])

    @pl.when(me == last)
    def _():
        for j in range(sections):
            whole_wait(fin_out, fin_send.at[j])

    @pl.when(me < last)
    def _():
        whole_wait(fin_out, fin_recv)

    for m in range(micros):

        @pl.when(me < last)
        def _():
            forward_copy(m).wait_send()

        @pl.when(me > 0)
        def _():
            backward_copy(m).wait_send()

        @pl.when(me == 0)
        def _():
            inp_copy(m).wait()


def relay(tokens, cotangent, flags, groups, gain_one, gain_two, wqkv, wout, wup, wdown):
    sections = lax.axis_size("pipe")
    replicas = lax.axis_size("dp")
    rows = tokens.shape[0]
    micros = rows // SEQ
    width = D // sections
    paired = replicas == SHARDS
    hidden = FF // 2 if paired else FF
    anywhere = pl.BlockSpec(memory_space=pl.ANY)
    vmem = pl.BlockSpec(memory_space=pltpu.VMEM)
    smem = pl.BlockSpec(memory_space=pltpu.SMEM)
    dma = pltpu.SemaphoreType.DMA

    def factor(columns):
        return jax.ShapeDtypeStruct((2, rows, columns), BF16)

    def saved(columns):
        return pltpu.VMEM((2, micros, SEQ, columns), BF16)

    def two(columns):
        return pltpu.VMEM((2, SEQ, columns), BF16)

    def per_micro(columns):
        return pltpu.VMEM((micros, SEQ, columns), BF16)

    return pl.pallas_call(
        functools.partial(relay_kernel, sections, replicas, micros, paired),
        out_shape=(
            jax.ShapeDtypeStruct((rows, FIN_WINDOW), BF16),
            jax.ShapeDtypeStruct((rows, D), BF16),
            jax.ShapeDtypeStruct((replicas, 8, 128), F32),
            factor(D),
            factor(3 * D),
            factor(D),
            factor(D),
            factor(D),
            factor(hidden),
            factor(hidden),
            factor(D),
            factor(D),
            factor(D),
            jax.ShapeDtypeStruct((2, BLOCKS * D, D), BF16),
        ),
        in_specs=[anywhere, anywhere, vmem, smem, vmem, vmem] + [anywhere] * 4,
        out_specs=(anywhere, anywhere, vmem) + (anywhere,) * 11,
        scratch_shapes=[
            pltpu.VMEM((2, BLOCKS * D, D), BF16),
            per_micro(D),
            per_micro(D),
            per_micro(D),
            per_micro(D),
            saved(D),
            saved(3 * D),
            pltpu.VMEM((2, micros, HEADS, SEQ, SEQ), BF16),
            saved(D),
            saved(FF),
            pltpu.VMEM((2, micros, SEQ, 128), F32),
            two(D),
            two(FF),
            saved(D),
            two(D),
            pltpu.VMEM((SEQ, D), F32),
            pltpu.VMEM((4, 8, D), F32),
            pltpu.VMEM((micros, SEQ, SEQ), F32),
            dma((2, len(KINDS))),
            dma((2, len(KINDS))),
            dma((2, len(KINDS))),
            dma((2, micros)),
            dma((micros,)),
            dma((micros,)),
            dma((micros,)),
            dma((micros,)),
            dma((sections,)),
            dma(()),
            dma((micros,)),
            dma((10, 2)),
            dma((2,)),
            dma((2,)),
            dma((2,)),
            dma((2,)),
        ],
        compiler_params=pltpu.CompilerParams(
            collective_id=0, has_side_effects=True, vmem_limit_bytes=60 * MIB
        ),
        name="relay",
    )(tokens, cotangent, flags, groups, gain_one, gain_two, wqkv, wout, wup, wdown)


ROWS = 96
CHUNKS = 10
UP, DOWN = 4, 6
AGAIN = 512
ORDER = (3, 0, 1, 2) + tuple(range(4, CHUNKS))

LOANS = ((0, 1, 1, 0), (0, 1, 2, 1))
GUESTS = 2


def sum_kernel(
    sections,
    gains_in,
    fin_in,
    inp_in,
    u_in,
    dqkv_in,
    o_in,
    da_in,
    u2_in,
    dz_in,
    act_in,
    dm_in,
    u2_other,
    dm_other,
    wup_hbm,
    wdown_hbm,
    gains_out,
    fin_out,
    inp_out,
    qkv_out,
    out_out,
    up_out,
    down_out,
    u_v,
    dqkv_v,
    o_v,
    da_v,
    u2_v,
    dz_v,
    act_v,
    dm_v,
    wup_v,
    wdown_v,
    own,
    first,
    second,
    third,
    gains_v,
    fin_v,
    fin_t,
    inp_v,
    inp_stage,
    load_sem,
    gain_send,
    gain_recv,
    fin_sem,
    inp_send,
    inp_recv,
    lend_send,
    lend_recv,
    back_send,
    back_recv,
    give_send,
    send,
    recv,
    up_sem,
    out_sem,
):
    me = lax.axis_index("dp")
    section = lax.axis_index("pipe")
    core = lax.rem(me, 2)
    x = lax.rem(me // 2, 2)
    y = me // 4
    other_core = me + 1 - 2 * core
    other_x = me + 2 - 4 * x
    other_y = me + 4 - 8 * y

    loans = LOANS if sections > 3 else ()
    sources = (u_in, dqkv_in, o_in, da_in)
    held = (u_v, dqkv_v, o_v, da_v)
    rows = dm_in.shape[1]

    def load(k, l):
        return pltpu.make_async_copy(sources[k].at[l], held[k], load_sem.at[k])

    def hidden(l, b, other=False):
        px, py = (1 - x, 1 - y) if other else (x, y)
        block = l * (2 * b + px) + (1 - l) * (2 * py + b)
        return pl.ds(pl.multiple_of(block * CHUNK, CHUNK), CHUNK)

    def mlp_loads(l):
        own_rows, other_rows = pl.ds(0, rows), pl.ds(rows, rows)
        copies = [
            (u2_other.at[l], u2_v.at[other_rows]),
            (dm_other.at[l], dm_v.at[other_rows]),
            (u2_in.at[l], u2_v.at[own_rows]),
            (dm_in.at[l], dm_v.at[own_rows]),
        ]
        for b in range(2):
            units = hidden(l, b)
            copies.append((wup_hbm.at[l, :, units], wup_v.at[b]))
            copies.append((wdown_hbm.at[l, units], wdown_v.at[b]))
            copies.append((dz_in.at[l, :, pl.ds(b * CHUNK, CHUNK)], dz_v.at[b, own_rows]))
            copies.append((act_in.at[l, :, pl.ds(b * CHUNK, CHUNK)], act_v.at[b, own_rows]))
        return [pltpu.make_async_copy(src, dst, load_sem.at[4 + k]) for k, (src, dst) in enumerate(copies)]

    for k in (2, 3, 0, 1):
        load(k, 1).start()

    barrier = pltpu.get_barrier_semaphore()
    for j in range(SHARDS):

        @pl.when(me != j)
        def _():
            pl.semaphore_signal(barrier, inc=1, device_id={"dp": j}, device_id_type=MESH)

    for j in range(1, sections):
        for to in sorted({0} | {lender for lender, k, _, _ in loans if sections - k == j}):

            @pl.when(section == j)
            def _():
                pl.semaphore_signal(barrier, inc=1, device_id={"pipe": to}, device_id_type=MESH)

    for copy in mlp_loads(1):
        copy.start()

    def gain_copy(j, source):
        return pltpu.make_async_remote_copy(
            src_ref=gains_in.at[j],
            dst_ref=gains_v.at[source],
            send_sem=gain_send,
            recv_sem=gain_recv,
            device_id={"dp": j},
            device_id_type=MESH,
        )

    def inp_copy(j):
        return pltpu.make_async_remote_copy(
            src_ref=inp_stage.at[j],
            dst_ref=inp_out,
            send_sem=inp_send.at[j],
            recv_sem=inp_recv,
            device_id={"pipe": j},
            device_id_type=MESH,
        )

    def own_inp_copy():
        return pltpu.make_async_copy(inp_stage.at[0], inp_out, inp_send.at[0])

    def inp_load():
        return pltpu.make_async_copy(inp_in, inp_v, inp_send.at[0])

    def meet():
        others = lax.select(section == 0, sections - 1, 0)
        for lender in {lender for lender, _, _, _ in loans} - {0}:
            hosts = {k for other, k, _, _ in loans if other == lender}
            others = others + lax.select(section == lender, len(hosts), 0)
        pl.semaphore_wait(barrier, SHARDS - 1 + others)
        for j in range(SHARDS):

            @pl.when(me != j)
            def _():
                gain_copy(j, me).start()


    def whole_wait(ref, sem):
        pltpu.make_async_copy(ref, ref, sem).wait()

    def sender(n):
        return 2 + n - 2 * CHUNKS if isinstance(n, int) and n >= 2 * CHUNKS else n // CHUNKS

    def remote(src, dst, step, n, to, sent=None):
        return pltpu.make_async_remote_copy(
            src_ref=src,
            dst_ref=dst,
            send_sem=send.at[step - 1, sender(n)] if sent is None else sent,
            recv_sem=recv.at[step, n],
            device_id={"dp": to},
            device_id_type=MESH,
        )

    def give_copy(n, i):
        if i >= DOWN:
            return remote(own.at[i, 1 - core, 0], first.at[n, 0], 0, n, other_core, give_send.at[i])
        return remote(own.at[i, 1 - core], first.at[n], 0, n, other_core, give_send.at[i])

    def down_copy(n, l):
        mine, to = lax.select(l == 1, y, x), lax.select(l == 1, other_y, other_x)
        return remote(first.at[n, 0, 1 - mine], third.at[n], 2, n, to)

    def first_copy(n, i, l=None):
        if i >= UP:
            mine = lax.select(l == 1, y, x)
            to = lax.select(l == 1, other_y, other_x)
            return remote(first.at[n, 1 - mine], second.at[n], 1, n, to)
        if i % 2 == 1:
            return remote(first.at[n, :, 1 - x], second.at[n], 1, n, other_x)
        return remote(first.at[n, 1 - y], second.at[n], 1, n, other_y)

    def second_copy(n, i, l=None):
        if i >= UP:
            mine = lax.select(l == 1, x, y)
            to = lax.select(l == 1, other_x, other_y)
            return remote(second.at[n, 1 - mine], third.at[n], 2, n, to)
        if i % 2 == 1:
            return remote(second.at[n, 1 - y], third.at[n], 2, n, other_y)
        return remote(second.at[n, 1 - x], third.at[n], 2, n, other_x)

    def lend_copy(g):
        lender, k, i, slot = loans[g]
        return pltpu.make_async_remote_copy(
            src_ref=first.at[i],
            dst_ref=first.at[2 * CHUNKS + slot],
            send_sem=lend_send.at[g],
            recv_sem=lend_recv.at[g],
            device_id={"pipe": sections - k},
            device_id_type=MESH,
        )

    def back_copy(g):
        lender, k, i, slot = loans[g]
        return pltpu.make_async_remote_copy(
            src_ref=third.at[2 * CHUNKS + slot],
            dst_ref=third.at[i],
            send_sem=back_send.at[g],
            recv_sem=back_recv.at[g],
            device_id={"pipe": lender},
            device_id_type=MESH,
        )

    def lent_or(step, i, lent, kept):
        away = None
        for g, (lender, _, chunk, _) in enumerate(loans):
            if chunk == i:
                here = (step == 0) & (section == lender)
                pl.when(here)(functools.partial(lent, g))
                away = here if away is None else away | here
        if away is None:
            kept()
        else:
            pl.when(jnp.logical_not(away))(kept)

    def as_host(action):
        for g, (_, k, i, slot) in enumerate(loans):
            pl.when(section == sections - k)(functools.partial(action, g, 2 * CHUNKS + slot, i))

    lent_chunks = sorted({i for _, _, i, _ in loans})

    def result_copy(n, l, i):
        if i < 3:
            dst = qkv_out.at[l, :, pl.ds(i * CHUNK, CHUNK)]
        elif i < 4:
            dst = out_out.at[l]
        elif i < DOWN:
            dst = up_out.at[l, :, hidden(l, i - UP, other=True)]
        else:
            dst = down_out.at[l, pl.ds((i - DOWN) * ROWS, ROWS)]
        return pltpu.make_async_copy(third.at[n], dst, out_sem.at[1 - l])

    def own_up_copy(n, l, i):
        mine = lax.select(l == 1, x, y)
        return pltpu.make_async_copy(second.at[n, mine], up_out.at[l, :, hidden(l, i - UP)], up_sem.at[1 - l])

    def add_core(n, l, i):
        give_copy(n, i).wait_recv()
        if i >= DOWN:
            first[n, 0] = first[n, 0] + own[i, core, 0]
            down_copy(n, l).start()
        else:
            first[n] = first[n] + own[i, core]
            lent_or(1 - l, i, lambda g: lend_copy(g).start(), lambda: first_copy(n, i, l).start())

    def free(step, i):
        @pl.when(step > 0)
        def _():
            give_copy(i, i).wait_send()

    def second_sum(n, i, l=None):
        first_copy(n, i, l).wait_recv()
        if i >= UP:
            kept = first[n, lax.select(l == 1, y, x)]
        else:
            kept = first[n, :, x] if i % 2 == 1 else first[n, y]
        second[n] = second[n] + kept
        second_copy(n, i, l).start()
        if i >= UP:
            own_up_copy(n, l, i).start()

    def plain_products(step, carry):
        l = 1 - step
        base = step * CHUNKS

        def products(k, a, g, slots):
            load(k, l).wait()
            load(k + 1, l).wait()
            for i, columns in slots:
                free(step, i)
                part = tn(a[...], g[:, columns * CHUNK : (columns + 1) * CHUNK]).astype(BF16)
                for r in range(SHARDS):
                    own[i, r % 2, r // 4, (r // 2) % 2] = part[r * ROWS : (r + 1) * ROWS]
                if i == ORDER[0]:
                    pl.when(step == 0)(meet)
                give_copy(base + i, i).start()
                if i != ORDER[0]:
                    before = ORDER[ORDER.index(i) - 1]
                    add_core(base + before, l, before)
                else:

                    @pl.when(step > 0)
                    def _():
                        add_core(base - CHUNKS + ORDER[UP - 1], l + 1, ORDER[UP - 1])

        def reload(k):
            @pl.when(step == 0)
            def _():
                load(k, 0).start()
                load(k + 1, 0).start()

        products(2, o_v, da_v, ((3, 0),))
        reload(2)
        products(0, u_v, dqkv_v, ((0, 0), (1, 1), (2, 2)))
        reload(0)
        return carry

    lax.fori_loop(0, 2, plain_products, 0)
    add_core(CHUNKS + ORDER[UP - 1], 0, ORDER[UP - 1])

    def plain_sums(step):
        for i in ORDER[:UP]:
            lent_or(step, i, lambda g: None, functools.partial(second_sum, step * CHUNKS + i, i))

    def mlp_products(step, carry):
        l = 1 - step
        base = step * CHUNKS
        copies = mlp_loads(l)

        def next_loads(*which):
            @pl.when(step == 0)
            def _():
                later = mlp_loads(0)
                for k in which:
                    later[k].start()

        for k in (0, 1, 4, 5, 8, 9):
            copies[k].wait()

        def again(k, c):
            at = pl.ds(pl.multiple_of(rows + k * AGAIN, AGAIN), AGAIN)
            for b in range(2):
                act, slope = gelu_parts(nn(u2_v[at], wup_v[b]))
                act_v[b, at] = act.astype(BF16)
                dz_v[b, at] = (slope * nt(dm_v[at], wdown_v[b])).astype(BF16)
            return c

        lax.fori_loop(0, rows // AGAIN, again, 0)
        next_loads(4, 5, 8, 9)
        pl.when(step == 0)(functools.partial(plain_sums, 0))
        for k in (2, 3, 6, 7, 10, 11):
            copies[k].wait()
        for b in range(2):
            i = UP + b
            free(step, i)
            part = tn(u2_v[...], dz_v[b]).astype(BF16)
            for r in range(SHARDS):
                ry, rx = r // 4, (r // 2) % 2
                across, along = l * ry + (1 - l) * rx, l * rx + (1 - l) * ry
                own[i, r % 2, across, along] = part[r * ROWS : (r + 1) * ROWS]
            give_copy(base + i, i).start()
            if b == 1:
                add_core(base + UP, l, UP)
        next_loads(0, 2, 6, 10)
        for i in range(DOWN, CHUNKS):
            free(step, i)
        for b in range(2):
            part = tn(act_v[b], dm_v[...]).astype(BF16)
            for r in range(8):
                own[DOWN + r % 4, r // 4, 0, b] = part[r * ROWS : (r + 1) * ROWS]
        next_loads(1, 3, 7, 11)
        for i in range(DOWN, CHUNKS):
            give_copy(base + i, i).start()
        for i in range(UP + 1, CHUNKS):
            add_core(base + i, l, i)
        pl.when(step == 0)(functools.partial(plain_sums, 1))
        return carry

    lax.fori_loop(0, 2, mlp_products, 0)

    def up_sums(step, carry):
        for i in range(UP, DOWN):
            second_sum(step * CHUNKS + i, i, 1 - step)
        return carry

    lax.fori_loop(0, 2, up_sums, 0)

    def take_in(g, n, i):
        lend_copy(g).wait_recv()
        first_copy(n, i).start()

    as_host(take_in)
    as_host(lambda g, n, i: second_sum(n, i))

    fin_load = pltpu.make_async_copy(fin_in, fin_v, fin_sem)
    fin_load.start()
    fin_load.wait()
    width = D // sections
    for j in range(sections):
        first_lane = j * width - window_start(j, width)

        @pl.when(section == j)
        def _():
            for r in range(0, rows, SEQ):
                part = fin_v[r : r + SEQ, :].astype(F32)[:, first_lane : first_lane + width]
                fin_t[:, r : r + SEQ] = part.T.astype(BF16)

    fin_store = pltpu.make_async_copy(fin_t, fin_out, fin_sem)
    fin_store.start()

    @pl.when(section == 0)
    def _():
        inp_load().start()
        inp_load().wait()
        for j in range(sections):
            for r in range(0, rows, SEQ):
                part = inp_v[r : r + SEQ, :].astype(F32)[:, j * width : (j + 1) * width]
                inp_stage[j, :, r : r + SEQ] = part.T.astype(BF16)
        own_inp_copy().start()
        for j in range(1, sections):
            inp_copy(j).start()

    def take_in(g, n, i):
        lend_copy(g).wait_recv()
        first_copy(n, i).start()

    gains_v[me] = gains_in[me]
    whole_wait(gains_v.at[0 : SHARDS - 1], gain_recv)
    total = gains_v[0]
    for j in range(1, SHARDS):
        total = total + gains_v[j]
    gains_out[...] = total

    def last_sum(n, i):
        second_copy(n, i).wait_recv()
        third[n] = third[n] + second[n, y if i % 2 == 1 else x]

    def last_sums(step, carry):
        for i in ORDER:
            n = step * CHUNKS + i
            if i >= DOWN:
                down_copy(n, 1 - step).wait_recv()
                third[n] = third[n] + first[n, 0, lax.select(step == 0, y, x)]
            elif i >= UP:
                second_copy(n, i, 1 - step).wait_recv()
            else:
                lent_or(step, i, lambda g: None, functools.partial(last_sum, n, i))
            if i not in lent_chunks:
                result_copy(n, 1 - step, i).start()
        return carry

    lax.fori_loop(0, 2, last_sums, 0)

    def give_back(g, n, i):
        last_sum(n, i)
        back_copy(g).start()

    as_host(give_back)
    for g, (lender, _, _, _) in enumerate(loans):

        @pl.when(section == lender)
        def _():
            back_copy(g).wait_recv()

    for i in lent_chunks:
        for step in range(2):
            result_copy(step * CHUNKS + i, 1 - step, i).start()

    def sent(step, lent):
        whole_wait(second.at[0 : DOWN - lent], send.at[0, step])
        whole_wait(third.at[0 : CHUNKS - lent], send.at[1, step])

    for step in range(2):
        whole_wait(third.at[0:CHUNKS], out_sem.at[step])
        whole_wait(third.at[0 : DOWN - UP], up_sem.at[step])
    sent(1, 0)
    lenders = sorted({lender for lender, _, _, _ in loans})
    keeps = section >= 0
    for lender in lenders:
        keeps = keeps & (section != lender)

        @pl.when(section == lender)
        def _():
            lent = [g for g, loan in enumerate(loans) if loan[0] == lender]
            sent(0, len(lent))
            for g in lent:
                lend_copy(g).wait_send()

    pl.when(keeps)(functools.partial(sent, 0, 0))

    def guest_sent(g, n, i):
        first_copy(n, i).wait_send()
        second_copy(n, i).wait_send()
        back_copy(g).wait_send()

    as_host(guest_sent)

    for i in range(CHUNKS):
        give_copy(CHUNKS + i, i).wait_send()
    whole_wait(gains_v.at[0 : SHARDS - 1], gain_send)
    fin_store.wait()

    @pl.when(section == 0)
    def _():
        own_inp_copy().wait()
        for j in range(1, sections):
            inp_copy(j).wait_send()

    @pl.when(section > 0)
    def _():
        inp_copy(0).wait_recv()


def summed(gains, fin, inp, *factors):
    sections = lax.axis_size("pipe")
    rows, width = inp.shape[0], D // sections
    anywhere = pl.BlockSpec(memory_space=pl.ANY)
    vmem = pl.BlockSpec(memory_space=pltpu.VMEM)
    dma = pltpu.SemaphoreType.DMA
    total = 2 * CHUNKS
    slots = total + GUESTS

    def shard(height, columns):
        return jax.ShapeDtypeStruct((2, height, columns), BF16)

    return pl.pallas_call(
        functools.partial(sum_kernel, sections),
        out_shape=(
            jax.ShapeDtypeStruct((8, 128), F32),
            jax.ShapeDtypeStruct((width, rows), BF16),
            jax.ShapeDtypeStruct((width, rows), BF16),
            shard(ROWS, 3 * D),
            shard(ROWS, D),
            shard(ROWS, FF),
            shard(4 * ROWS, D),
        ),
        in_specs=[vmem] + [anywhere] * 14,
        out_specs=(vmem,) + (anywhere,) * 6,
        scratch_shapes=[pltpu.VMEM((rows, f.shape[2]), BF16) for f in factors[:4]]
        + [
            pltpu.VMEM((2 * rows, D), BF16),
            pltpu.VMEM((2, 2 * rows, CHUNK), BF16),
            pltpu.VMEM((2, 2 * rows, CHUNK), BF16),
            pltpu.VMEM((2 * rows, D), BF16),
            pltpu.VMEM((2, D, CHUNK), BF16),
            pltpu.VMEM((2, CHUNK, D), BF16),
            pltpu.VMEM((CHUNKS, 2, 2, 2, ROWS, CHUNK), BF16),
            pltpu.VMEM((slots, 2, 2, ROWS, CHUNK), BF16),
            pltpu.VMEM((slots, 2, ROWS, CHUNK), BF16),
            pltpu.VMEM((slots, ROWS, CHUNK), BF16),
            pltpu.VMEM((SHARDS, 8, 128), F32),
            pltpu.VMEM((rows, FIN_WINDOW), BF16),
            pltpu.VMEM((width, rows), BF16),
            pltpu.VMEM((rows, D), BF16),
            pltpu.VMEM((sections, width, rows), BF16),
            dma((16,)),
            dma(()),
            dma(()),
            dma(()),
            dma((sections,)),
            dma(()),
            dma((len(LOANS),)),
            dma((len(LOANS),)),
            dma((len(LOANS),)),
            dma((len(LOANS),)),
            dma((CHUNKS,)),
            dma((2, 2 + GUESTS)),
            dma((3, slots)),
            dma((2,)),
            dma((2,)),
        ],
        compiler_params=pltpu.CompilerParams(
            collective_id=1, has_side_effects=True, vmem_limit_bytes=60 * MIB
        ),
        name="sum",
    )(gains, fin, inp, *factors)


def write_kernel(count, share, gains, *refs):
    gain_one, gain_two = refs[count], refs[count + 1]
    gain_one[...] = gains[0:2, 0:share]
    gain_two[...] = gains[2:4, 0:share]
    sources, results, held, wide = (
        refs[:count],
        refs[count + 2 : 2 * count + 2],
        refs[2 * count + 2 : 3 * count + 2],
        refs[3 * count + 2 : 4 * count + 2],
    )
    load_sem, store_sem = refs[4 * count + 2 :]
    pieces = []
    for k in reversed(range(count)):
        if len(sources[k].shape) == 3:
            pieces += [tuple(r.at[l] for r in (sources[k], held[k], wide[k], results[k])) for l in range(2)]
        else:
            pieces.append((sources[k], held[k], wide[k], results[k]))
    loads = [pltpu.make_async_copy(p[0], p[1], load_sem.at[i]) for i, p in enumerate(pieces)]
    stores = [pltpu.make_async_copy(p[2], p[3], store_sem.at[i]) for i, p in enumerate(pieces)]
    for load in loads:
        load.start()
    for load, store, piece in zip(loads, stores, pieces):
        load.wait()
        piece[2][...] = piece[1][...].astype(piece[2].dtype)
        store.start()
    for store in stores:
        store.wait()


def written(gains, share, arrays, types):
    count = len(arrays)
    anywhere = pl.BlockSpec(memory_space=pl.ANY)
    vmem = pl.BlockSpec(memory_space=pltpu.VMEM)
    return pl.pallas_call(
        functools.partial(write_kernel, count, share),
        out_shape=(jax.ShapeDtypeStruct((2, share), F32),) * 2
        + tuple(jax.ShapeDtypeStruct(a.shape, t) for a, t in zip(arrays, types)),
        in_specs=[vmem] + [anywhere] * count,
        out_specs=(vmem, vmem) + (anywhere,) * count,
        scratch_shapes=[pltpu.VMEM(a.shape, a.dtype) for a in arrays]
        + [pltpu.VMEM(a.shape, t) for a, t in zip(arrays, types)]
        + [pltpu.SemaphoreType.DMA((2 * count,)), pltpu.SemaphoreType.DMA((2 * count,))],
        compiler_params=pltpu.CompilerParams(vmem_limit_bytes=60 * MIB),
        name="write",
    )(gains, *arrays)


def body(
    tokens,
    gain_one,
    qkv_weight,
    out_weight,
    gain_two,
    up_weight,
    down_weight,
    cotangent,
    flags,
    groups,
):
    micros = tokens.shape[0] // SEQ
    fin, inp, gains, u, dqkv, o, da, u2, dz, act, dm, u2_other, dm_other, _ = relay(
        tokens,
        cotangent,
        flags.reshape(micros, SEQ),
        groups,
        gain_one,
        gain_two,
        qkv_weight,
        out_weight,
        up_weight,
        down_weight,
    )

    replicas = lax.axis_size("dp")
    share = D // replicas
    if replicas == SHARDS and share == ROWS:
        gains, fin, inp, g_qkv, g_out, g_up, g_down = summed(
            gains, fin, inp, u, dqkv, o, da, u2, dz, act, dm, u2_other, dm_other, up_weight, down_weight
        )
    else:

        def grad(a, g):
            total = jnp.einsum("lsa,lsb->lab", a, g, preferred_element_type=F32).astype(BF16)
            return lax.psum_scatter(total, "dp", scatter_dimension=1, tiled=True)

        gains = lax.psum_scatter(gains, "dp", scatter_dimension=0)
        sections = lax.axis_size("pipe")
        width = D // sections
        first_lanes = jnp.array([j * width - window_start(j, width) for j in range(sections)])
        fin = lax.dynamic_slice_in_dim(fin, first_lanes[lax.axis_index("pipe")], width, 1).T
        inp = jnp.where(lax.axis_index("pipe") == 0, inp.T, jnp.zeros_like(inp.T))
        inp = lax.psum_scatter(inp, "pipe", scatter_dimension=0, tiled=True)
        g_qkv, g_out, g_up, g_down = grad(u, dqkv), grad(o, da), grad(u2, dz), grad(act, dm)
    gain_one_grad, gain_two_grad, fin, inp, g_qkv, g_out, g_up, g_down = written(
        gains, share, (fin, inp, g_qkv, g_out, g_up, g_down), (BF16,) + (F32,) * 5
    )
    return (fin.T, inp.T, gain_one_grad, g_qkv, g_out, gain_two_grad, g_up, g_down)


def solution(mesh):
    return jax.shard_map(
        body,
        mesh=mesh,
        in_specs=(
            P("dp", None),
            P("pipe", None),
            P("pipe", None, None),
            P("pipe", None, None),
            P("pipe", None),
            P("pipe", None, None),
            P("pipe", None, None),
            P("dp", None),
            P("dp"),
            P("dp"),
        ),
        out_specs=(
            P("dp", "pipe"),
            P("dp", "pipe"),
            P("pipe", "dp"),
            P("pipe", "dp", None),
            P("pipe", "dp", None),
            P("pipe", "dp"),
            P("pipe", "dp", None),
            P("pipe", "dp", None),
        ),
        check_vma=False,
    )
```

```python
import functools

import jax
import jax.numpy as jnp
from jax import lax
from jax.experimental import pallas as pl
from jax.experimental.pallas import tpu as pltpu
from jax.sharding import PartitionSpec as P

D = 768
HEADS = 16
HEAD_DIM = 48
FF = 3072
SEQ = 128
EPS = 1e-06
MESH = pl.DeviceIdType.MESH
F32 = jnp.float32
BF16 = jnp.bfloat16
LOG2E = 1.4426950408889634
SCALE = HEAD_DIM ** (-0.5)
MIB = 2**20
CHUNK = 768
TILE = 256

KINDS = ((0, 3), (3, 1), (4, 4), (8, 4))

TURNED = (8, 11, 4, 0)
BLOCKS = 12

FIN_WINDOW = 256


def window_start(section, width):
    return min(section * width // 128 * 128, D - FIN_WINDOW)


SHARDS = 8

WINDOWS = tuple(
    (96 * j // 128, -(-(96 * j % 128 + 96) // 128), 96 * j % 128) for j in range(HEADS // 2)
)


def nn(a, b):
    return jnp.dot(a, b, preferred_element_type=F32)


def nt(a, b):
    return lax.dot_general(a, b, (((1,), (1,)), ((), ())), preferred_element_type=F32)


def tn(a, b):
    return lax.dot_general(a, b, (((0,), (0,)), ((), ())), preferred_element_type=F32)


def lanes_of_head(first, width):
    lane = lax.broadcasted_iota(jnp.int32, (SEQ, width), 1)
    return ((lane >= first) & (lane < first + HEAD_DIM)).astype(F32).astype(BF16)


def two_heads(window, first):
    width = window.shape[1]
    return jnp.concatenate(
        [window * lanes_of_head(first, width), window * lanes_of_head(first + HEAD_DIM, width)], axis=0
    )


def add_window(tiles, first, part):
    for i in range(part.shape[1] // 128):
        piece = part[:, i * 128 : (i + 1) * 128]
        tiles[first + i] = piece if tiles[first + i] is None else tiles[first + i] + piece


def norm_parts(x):
    centre = x - jnp.mean(x, axis=-1, keepdims=True)
    spread = jnp.mean(centre * centre, axis=-1, keepdims=True)
    inverse = lax.rsqrt(spread + EPS)
    return centre * inverse, inverse


def gelu_parts(z):
    phi = 0.5 * (1.0 + lax.erf(z * 0.7071067811865476))
    density = jnp.exp2(z * z * (-0.5 * LOG2E)) * 0.3989422804014327
    return z * phi, phi + z * density


def relay_kernel(
    sections,
    replicas,
    micros,
    paired,
    tokens,
    cotangent,
    flags,
    groups,
    gain_one,
    gain_two,
    wqkv_hbm,
    wout_hbm,
    wup_hbm,
    wdown_hbm,
    fin_out,
    inp_out,
    gains_out,
    u_out,
    dqkv_out,
    o_out,
    da_out,
    u2_out,
    dz_out,
    act_out,
    dm_out,
    u2_other,
    dm_other,
    turned_hbm,
    weights,
    fwd_in,
    fwd_out,
    bwd_in,
    bwd_out,
    u_s,
    qkv_s,
    p_s,
    u2_s,
    gp_s,
    stat_s,
    o_s,
    act_s,
    dm_s,
    da_s,
    state,
    acc,
    bias,
    w_sem,
    turn_sem,
    swap_sem,
    in_sem,
    fwd_send,
    fwd_recv,
    bwd_send,
    bwd_recv,
    fin_send,
    fin_recv,
    inp_send,
    out_sem,
    u2_send,
    u2_recv,
    dm_send,
    dm_recv,
):
    me = lax.axis_index("pipe")
    last = sections - 1
    width = D // sections

    replica = lax.axis_index("dp")
    x, y = lax.rem(replica // 2, 2), replica // 4

    def block_rows(b, count=1):
        start = b * D
        return pl.ds(start if isinstance(b, int) else pl.multiple_of(start, D), count * D)

    def weight_copy(l, k, j):
        first, _ = KINDS[k]
        if k == 1:
            src = wout_hbm.at[l]
        elif k == 3:
            src = wdown_hbm.at[l, block_rows(j)]
        else:
            src = (wqkv_hbm, None, wup_hbm)[k].at[l, :, block_rows(j)]
        return pltpu.make_async_copy(src, weights.at[l, block_rows(first + j)], w_sem.at[l, k])

    def turned_copy(l, k, b):
        return pltpu.make_async_copy(
            weights.at[l, block_rows(b)], turned_hbm.at[l, block_rows(b)], turn_sem.at[l, k]
        )

    def whole_wait(ref, sem):
        pltpu.make_async_copy(ref, ref, sem).wait()

    def kind_wait(l, k, sem):
        whole_wait(weights.at[l, block_rows(*KINDS[k])], sem.at[l, k])

    def swap_copy(l, k):
        first, count = KINDS[k]
        to = block_rows(TURNED[k], count)
        return pltpu.make_async_copy(
            turned_hbm.at[l, block_rows(first, count)], weights.at[1 - l, to], swap_sem.at[l, k]
        )

    def swap_in(l, m, *kinds):
        @pl.when((m == micros - 1) & (me == last))
        def _():
            for k in kinds:
                swap_copy(1 - l, k).start()

    def turn(l, b):
        def tile(r, c):
            return l, pl.ds(pl.multiple_of(b * D + r * TILE, TILE), TILE), pl.ds(c * TILE, TILE)

        for r in range(D // TILE):
            weights[tile(r, r)] = weights[tile(r, r)].T
            for c in range(r):
                lower = weights[tile(r, c)].T
                upper = weights[tile(c, r)].T
                weights[tile(c, r)] = lower
                weights[tile(r, c)] = upper

    def token_copy(m):
        return pltpu.make_async_copy(tokens.at[pl.ds(m * SEQ, SEQ)], fwd_in.at[m], in_sem.at[0, m])

    def cotangent_copy(m):
        return pltpu.make_async_copy(cotangent.at[pl.ds(m * SEQ, SEQ)], bwd_in.at[m], in_sem.at[1, m])

    @pl.when(me == 0)
    def _():
        for m in range(micros):
            token_copy(m).start()

    def weights_start(l):
        for k, (_, count) in enumerate(KINDS):
            for j in range(count):
                weight_copy(l, k, j).start()

    weights_start(0)

    @pl.when(me > 0)
    def _():
        weights_start(1)


    barrier = pltpu.get_barrier_semaphore()
    for j in range(sections):

        @pl.when(me != j)
        def _():
            pl.semaphore_signal(barrier, inc=1, device_id={"pipe": j}, device_id_type=MESH)

    if paired:
        for j in (replica + 2 - 4 * x, replica + 4 - 8 * y):
            pl.semaphore_signal(barrier, inc=1, device_id={"dp": j}, device_id_type=MESH)

    @pl.when(me == last)
    def _():
        for m in range(micros):
            cotangent_copy(m).start()

    def forward_copy(m):
        return pltpu.make_async_remote_copy(
            src_ref=fwd_out.at[m],
            dst_ref=fwd_in.at[m],
            send_sem=fwd_send.at[m],
            recv_sem=fwd_recv.at[m],
            device_id={"pipe": lax.rem(me + 1, sections)},
            device_id_type=MESH,
        )

    def backward_copy(m):
        return pltpu.make_async_remote_copy(
            src_ref=bwd_out.at[m],
            dst_ref=bwd_in.at[m],
            send_sem=bwd_send.at[m],
            recv_sem=bwd_recv.at[m],
            device_id={"pipe": lax.rem(me + sections - 1, sections)},
            device_id_type=MESH,
        )

    def slots_of(m):
        return pl.ds(pl.multiple_of(m * SEQ, SEQ), SEQ)

    def fin_source(m, j):
        return fwd_out.at[m, :, pl.ds(window_start(j, width), FIN_WINDOW)]

    def fin_copy(m, j):
        return pltpu.make_async_remote_copy(
            src_ref=fin_source(m, j),
            dst_ref=fin_out.at[slots_of(m)],
            send_sem=fin_send.at[j],
            recv_sem=fin_recv,
            device_id={"pipe": j},
            device_id_type=MESH,
        )

    def own_fin_copy(m):
        return pltpu.make_async_copy(fin_source(m, last), fin_out.at[slots_of(m)], fin_send.at[last])

    def inp_copy(m):
        return pltpu.make_async_copy(bwd_out.at[m], inp_out.at[slots_of(m)], inp_send.at[m])


    outs = (u_out, dqkv_out, o_out, da_out, u2_out, dz_out, act_out, dm_out)

    def out_copies(kind, l, m):
        src = (
            u_s.at[l, m],
            qkv_s.at[l, m],
            o_s.at[l],
            da_s.at[l],
            u2_s.at[l, m],
            gp_s.at[l, m],
            act_s.at[l],
            dm_s.at[l, m],
        )[kind]
        out = outs[kind].at[l, pl.ds(m * SEQ, SEQ)]
        if kind not in (5, 6) or not paired:
            return [pltpu.make_async_copy(src, out, out_sem.at[kind, l])]
        copies = []
        for b in range(2):
            units = block_rows(l * (2 * b + x) + (1 - l) * (2 * y + b))
            sem = out_sem.at[kind + 3 * b, l]
            copies.append(pltpu.make_async_copy(src.at[:, units], out.at[:, pl.ds(b * D, D)], sem))
        return copies

    def out_start(kind, l, m):
        for copy in out_copies(kind, l, m):
            copy.start()

    def out_wait(kind, l, m):
        for copy in out_copies(kind, l, m):
            copy.wait()

    def out_wait_all(kind, l):
        if kind == 5 and paired:
            for b in range(2):
                whole_wait(outs[kind].at[l, :, pl.ds(b * D, D)], out_sem.at[kind + 3 * b, l])
        else:
            whole_wait(outs[kind].at[l], out_sem.at[kind, l])

    def partner(l):
        return {"dp": lax.select(l == 1, replica + 2 - 4 * x, replica + 4 - 8 * y)}

    def u2_copy(l, m):
        return pltpu.make_async_remote_copy(
            src_ref=u2_s.at[l, m],
            dst_ref=u2_other.at[l, slots_of(m)],
            send_sem=u2_send.at[l],
            recv_sem=u2_recv.at[l],
            device_id=partner(l),
            device_id_type=MESH,
        )

    def dm_copy(l, m):
        return pltpu.make_async_remote_copy(
            src_ref=dm_s.at[l, m],
            dst_ref=dm_other.at[l, slots_of(m)],
            send_sem=dm_send.at[l],
            recv_sem=dm_recv.at[l],
            device_id=partner(l),
            device_id_type=MESH,
        )

    def free_slot(kind, l, m):
        @pl.when(m > 0)
        def _():
            out_wait(kind, l, m - 1)

    row = lax.broadcasted_iota(jnp.int32, (SEQ, SEQ), 0) // (SEQ // 4)
    column = lax.broadcasted_iota(jnp.int32, (SEQ, SEQ), 1) // (SEQ // 4)
    same = (row == column).astype(F32)
    for m in range(micros):
        parted = (jnp.full((1, SEQ), groups[m], jnp.int32) == 1).astype(F32)
        valid = jnp.broadcast_to((flags[m : m + 1, :] == 1).astype(F32), (SEQ, SEQ)).T
        keep = jnp.maximum(same, 1.0 - parted) * valid
        bias[m] = (keep - 1.0) * 1e30

    def forward_layer(l, m):
        def weight_wait(k):
            @pl.when((m == 0) & (me < last))
            def _():
                kind_wait(l, k, w_sem)

        x = state[...]
        xhat, inverse = norm_parts(x)
        stat_s[l, m, :, 0:1] = inverse
        u = (xhat * gain_one[pl.ds(l, 1), :]).astype(BF16)
        u_s[l, m] = u
        out_start(0, l, m)
        weight_wait(0)
        for j in range(3):
            qkv_s[l, m, :, j * D : (j + 1) * D] = nn(u_s[l, m], weights[l, block_rows(j)]).astype(BF16)
        free_slot(2, l, m)
        slot = l
        added = bias[m]
        scores, tiles = [], [None] * 6
        for tile, count, inside in WINDOWS:
            lo, hi = tile * 128, (tile + count) * 128
            keys = two_heads(qkv_s[l, m, :, D + lo : D + hi], inside)
            scores.append(nt(keys, qkv_s[l, m, :, lo:hi]) * (SCALE * LOG2E))
        for j in range(len(WINDOWS)):
            for h in range(2):
                s = scores[j][h * SEQ : (h + 1) * SEQ] + added
                e = jnp.exp2(s - jnp.max(s, axis=0, keepdims=True))
                p = e * (1.0 / jnp.sum(e, axis=0, keepdims=True))
                p_s[l, m, 2 * j + h] = p.astype(BF16)
        for j, (tile, count, inside) in enumerate(WINDOWS):
            lo, hi = tile * 128, (tile + count) * 128
            values = two_heads(qkv_s[l, m, :, 2 * D + lo : 2 * D + hi], inside)
            p = jnp.concatenate([p_s[l, m, 2 * j], p_s[l, m, 2 * j + 1]], axis=0)
            add_window(tiles, tile, tn(p, values))
        for i in range(6):
            o_s[slot, :, i * 128 : (i + 1) * 128] = tiles[i].astype(BF16)
        out_start(2, l, m)
        weight_wait(1)

        @pl.when((m == 0) & (me == 0) & (l == 0))
        def _():
            weights_start(1)

        h = state[...] + nn(o_s[slot], weights[l, block_rows(3)])
        state[...] = h
        swap_in(l, m, 3)
        hhat, inverse = norm_parts(h)
        stat_s[l, m, :, 1:2] = inverse
        u2_s[l, m] = (hhat * gain_two[pl.ds(l, 1), :]).astype(BF16)
        out_start(4, l, m)

        @pl.when((m == 0) & (l == 0))
        def _():
            pl.semaphore_wait(barrier, sections - 1 + 2 * paired)

        if paired:
            u2_copy(l, m).start()
        weight_wait(2)
        free_slot(6, l, m)
        for j in range(4):
            act, slope = gelu_parts(nn(u2_s[l, m], weights[l, block_rows(4 + j)]))
            act_s[slot, :, j * D : (j + 1) * D] = act.astype(BF16)
            gp_s[l, m, :, j * D : (j + 1) * D] = slope.astype(BF16)
        swap_in(l, m, 2)
        weight_wait(3)
        state[...] = state[...] + nn(act_s[slot], weights[l, block_rows(8, 4)])
        swap_in(l, m, 1, 0)
        out_start(6, l, m)

    def norm_back(du, hat_scaled, gain, inverse):
        t = du * gain
        hat = hat_scaled * (1.0 / gain)
        weighted = du * hat_scaled
        return inverse * (
            t - jnp.mean(t, axis=-1, keepdims=True) - hat * jnp.mean(weighted, axis=-1, keepdims=True)
        ), weighted

    def add_rows(at, weighted):
        part = weighted[0:8]
        for r in range(8, SEQ, 8):
            part = part + weighted[r : r + 8]
        acc[at] = acc[at] + part

    def backward_layer(l, m):
        slot = l
        held = lax.select(me == last, 1 - l, l)

        def turned(k, j=0, count=1):
            return held, block_rows(lax.select(me == last, TURNED[k], KINDS[k][0]) + j, count)

        def turned_wait(k):
            @pl.when((m == 0) & (me == last))
            def _():
                swap_copy(l, k).wait()

        dy = state[...]
        turned_wait(3)
        dm_s[l, m] = dy.astype(BF16)
        out_start(7, l, m)
        if paired:
            dm_copy(l, m).start()
        for j in range(4):
            da = nn(dm_s[l, m], weights[turned(3, j)])
            dz = gp_s[l, m, :, j * D : (j + 1) * D].astype(F32) * da
            gp_s[l, m, :, j * D : (j + 1) * D] = dz.astype(BF16)
        out_start(5, l, m)
        turned_wait(2)
        dh, weighted = norm_back(
            nn(gp_s[l, m], weights[turned(2, 0, 4)]), u2_s[l, m].astype(F32), gain_two[pl.ds(l, 1), :], stat_s[l, m, :, 1:2]
        )
        add_rows(2 + l, weighted)
        dh = state[...] + dh
        state[...] = dh
        free_slot(3, l, m)
        da_s[slot] = dh.astype(BF16)
        out_start(3, l, m)
        turned_wait(1)
        do = nn(da_s[slot], weights[turned(1)]).astype(BF16)
        slopes, products = [], []
        q_tiles, k_tiles, v_tiles = [None] * 6, [None] * 6, [None] * 6
        for tile, count, inside in WINDOWS:
            lo, hi = tile * 128, (tile + count) * 128
            values = two_heads(qkv_s[l, m, :, 2 * D + lo : 2 * D + hi], inside)
            products.append(nt(values, do[:, lo:hi]))
        for j in range(len(WINDOWS)):
            for h in range(2):
                p = p_s[l, m, 2 * j + h].astype(F32)
                dp = products[j][h * SEQ : (h + 1) * SEQ]
                slopes.append((p * (dp - jnp.sum(p * dp, axis=0, keepdims=True))).astype(BF16))
        for j, (tile, count, inside) in enumerate(WINDOWS):
            lo, hi = tile * 128, (tile + count) * 128
            pair = slopes[2 * j : 2 * j + 2]
            keys = two_heads(qkv_s[l, m, :, D + lo : D + hi], inside)
            query = two_heads(qkv_s[l, m, :, lo:hi], inside)
            add_window(q_tiles, tile, tn(jnp.concatenate(pair, axis=0), keys))
            add_window(k_tiles, tile, nn(jnp.concatenate(pair, axis=1), query))
        for j, (tile, count, inside) in enumerate(WINDOWS):
            given = two_heads(do[:, tile * 128 : (tile + count) * 128], inside)
            p = jnp.concatenate([p_s[l, m, 2 * j], p_s[l, m, 2 * j + 1]], axis=1)
            add_window(v_tiles, tile, nn(p, given))
        for i in range(6):
            at = i * 128
            qkv_s[l, m, :, at : at + 128] = (q_tiles[i] * SCALE).astype(BF16)
            qkv_s[l, m, :, D + at : D + at + 128] = (k_tiles[i] * SCALE).astype(BF16)
            qkv_s[l, m, :, 2 * D + at : 2 * D + at + 128] = v_tiles[i].astype(BF16)
        out_start(1, l, m)
        turned_wait(0)
        du = nn(qkv_s[l, m], weights[turned(0, 0, 3)])
        dx, weighted = norm_back(
            du, u_s[l, m].astype(F32), gain_one[pl.ds(l, 1), :], stat_s[l, m, :, 0:1]
        )
        add_rows(l, weighted)
        state[...] = state[...] + dx

    @pl.when(me == last)
    def _():
        def make(l, c):
            for k, (first, count) in enumerate(KINDS):
                kind_wait(l, k, w_sem)

                def one(j, c):
                    turn(l, first + j)
                    turned_copy(l, k, first + j).start()
                    return c

                lax.fori_loop(0, count, one, 0)
            return c

        def again(l, c):
            for k, (_, count) in enumerate(KINDS):
                kind_wait(l, k, turn_sem)
                for j in range(count):
                    weight_copy(l, k, j).start()
            return c

        def ready(l, c):
            for k in range(len(KINDS)):
                kind_wait(l, k, w_sem)
            return c

        for action in (make, again, ready):
            lax.fori_loop(0, 2, action, 0)

    def forward_micro(m, carry):
        @pl.when(me == 0)
        def _():
            token_copy(m).wait()

        @pl.when(me > 0)
        def _():
            forward_copy(m).wait_recv()

        state[...] = fwd_in[m].astype(F32)

        def one(l, c):
            forward_layer(l, m)
            return c

        lax.fori_loop(0, 2, one, 0)

        fwd_out[m] = state[...].astype(BF16)

        @pl.when(me < last)
        def _():
            forward_copy(m).start()

        @pl.when(me == last)
        def _():
            own_fin_copy(m).start()
            for j in range(last):
                fin_copy(m, j).start()

        return carry

    lax.fori_loop(0, micros, forward_micro, 0)
    @pl.when(me < last)
    def _():
        def one(i, c):
            turn(1 - i // BLOCKS, lax.rem(i, BLOCKS))
            return c

        lax.fori_loop(0, 2 * BLOCKS, one, 0)

    acc[...] = jnp.zeros_like(acc)

    def backward_micro(m, carry):
        @pl.when(me == last)
        def _():
            cotangent_copy(m).wait()

        @pl.when(me < last)
        def _():
            backward_copy(m).wait_recv()

        state[...] = bwd_in[m].astype(F32)

        def one(i, c):
            backward_layer(1 - i, m)
            return c

        lax.fori_loop(0, 2, one, 0)

        bwd_out[m] = state[...].astype(BF16)

        @pl.when(me > 0)
        def _():
            backward_copy(m).start()

        @pl.when(me == 0)
        def _():
            inp_copy(m).start()

        return carry

    lax.fori_loop(0, micros, backward_micro, 0)

    share = D // replicas
    for k in range(4):
        gain = (gain_one, gain_two)[k // 2][k % 2 : k % 2 + 1, :]
        total = jnp.sum(acc[k], axis=0, keepdims=True) / gain
        for r in range(replicas):
            gains_out[r, k : k + 1, 0:share] = total[:, r * share : (r + 1) * share]

    for l in range(2):
        for kind in (2, 3, 6):
            out_wait(kind, l, micros - 1)
        for kind in (0, 1, 4, 5, 7):
            out_wait_all(kind, l)
        if paired:
            for sem in (u2_send, u2_recv, dm_send, dm_recv):
                whole_wait(dm_other.at[l], sem.at[l])

    @pl.when(me == last)
    def _():
        for j in range(sections):
            whole_wait(fin_out, fin_send.at[j])

    @pl.when(me < last)
    def _():
        whole_wait(fin_out, fin_recv)

    for m in range(micros):

        @pl.when(me < last)
        def _():
            forward_copy(m).wait_send()

        @pl.when(me > 0)
        def _():
            backward_copy(m).wait_send()

        @pl.when(me == 0)
        def _():
            inp_copy(m).wait()


def relay(tokens, cotangent, flags, groups, gain_one, gain_two, wqkv, wout, wup, wdown):
    sections = lax.axis_size("pipe")
    replicas = lax.axis_size("dp")
    rows = tokens.shape[0]
    micros = rows // SEQ
    width = D // sections
    paired = replicas == SHARDS
    hidden = FF // 2 if paired else FF
    anywhere = pl.BlockSpec(memory_space=pl.ANY)
    vmem = pl.BlockSpec(memory_space=pltpu.VMEM)
    smem = pl.BlockSpec(memory_space=pltpu.SMEM)
    dma = pltpu.SemaphoreType.DMA

    def factor(columns):
        return jax.ShapeDtypeStruct((2, rows, columns), BF16)

    def saved(columns):
        return pltpu.VMEM((2, micros, SEQ, columns), BF16)

    def two(columns):
        return pltpu.VMEM((2, SEQ, columns), BF16)

    def per_micro(columns):
        return pltpu.VMEM((micros, SEQ, columns), BF16)

    return pl.pallas_call(
        functools.partial(relay_kernel, sections, replicas, micros, paired),
        out_shape=(
            jax.ShapeDtypeStruct((rows, FIN_WINDOW), BF16),
            jax.ShapeDtypeStruct((rows, D), BF16),
            jax.ShapeDtypeStruct((replicas, 8, 128), F32),
            factor(D),
            factor(3 * D),
            factor(D),
            factor(D),
            factor(D),
            factor(hidden),
            factor(hidden),
            factor(D),
            factor(D),
            factor(D),
            jax.ShapeDtypeStruct((2, BLOCKS * D, D), BF16),
        ),
        in_specs=[anywhere, anywhere, vmem, smem, vmem, vmem] + [anywhere] * 4,
        out_specs=(anywhere, anywhere, vmem) + (anywhere,) * 11,
        scratch_shapes=[
            pltpu.VMEM((2, BLOCKS * D, D), BF16),
            per_micro(D),
            per_micro(D),
            per_micro(D),
            per_micro(D),
            saved(D),
            saved(3 * D),
            pltpu.VMEM((2, micros, HEADS, SEQ, SEQ), BF16),
            saved(D),
            saved(FF),
            pltpu.VMEM((2, micros, SEQ, 128), F32),
            two(D),
            two(FF),
            saved(D),
            two(D),
            pltpu.VMEM((SEQ, D), F32),
            pltpu.VMEM((4, 8, D), F32),
            pltpu.VMEM((micros, SEQ, SEQ), F32),
            dma((2, len(KINDS))),
            dma((2, len(KINDS))),
            dma((2, len(KINDS))),
            dma((2, micros)),
            dma((micros,)),
            dma((micros,)),
            dma((micros,)),
            dma((micros,)),
            dma((sections,)),
            dma(()),
            dma((micros,)),
            dma((10, 2)),
            dma((2,)),
            dma((2,)),
            dma((2,)),
            dma((2,)),
        ],
        compiler_params=pltpu.CompilerParams(
            collective_id=0, has_side_effects=True, vmem_limit_bytes=60 * MIB
        ),
        name="relay",
    )(tokens, cotangent, flags, groups, gain_one, gain_two, wqkv, wout, wup, wdown)


ROWS = 96
CHUNKS = 10
UP, DOWN = 4, 6
AGAIN = 512
ORDER = (3, 0, 1, 2) + tuple(range(4, CHUNKS))

LOANS = ((0, 1, 1, 0), (0, 1, 2, 1))
GUESTS = 2


def sum_kernel(
    sections,
    gains_in,
    fin_in,
    inp_in,
    u_in,
    dqkv_in,
    o_in,
    da_in,
    u2_in,
    dz_in,
    act_in,
    dm_in,
    u2_other,
    dm_other,
    wup_hbm,
    wdown_hbm,
    gains_out,
    fin_out,
    inp_out,
    qkv_out,
    out_out,
    up_out,
    down_out,
    u_v,
    dqkv_v,
    o_v,
    da_v,
    u2_v,
    dz_v,
    act_v,
    dm_v,
    wup_v,
    wdown_v,
    own,
    first,
    second,
    third,
    gains_v,
    fin_v,
    fin_t,
    inp_v,
    inp_stage,
    load_sem,
    gain_send,
    gain_recv,
    fin_sem,
    inp_send,
    inp_recv,
    lend_send,
    lend_recv,
    back_send,
    back_recv,
    give_send,
    send,
    recv,
    up_sem,
    out_sem,
):
    me = lax.axis_index("dp")
    section = lax.axis_index("pipe")
    core = lax.rem(me, 2)
    x = lax.rem(me // 2, 2)
    y = me // 4
    other_core = me + 1 - 2 * core
    other_x = me + 2 - 4 * x
    other_y = me + 4 - 8 * y

    loans = LOANS if sections > 3 else ()
    sources = (u_in, dqkv_in, o_in, da_in)
    held = (u_v, dqkv_v, o_v, da_v)
    rows = dm_in.shape[1]

    def load(k, l):
        return pltpu.make_async_copy(sources[k].at[l], held[k], load_sem.at[k])

    def hidden(l, b, other=False):
        px, py = (1 - x, 1 - y) if other else (x, y)
        block = l * (2 * b + px) + (1 - l) * (2 * py + b)
        return pl.ds(pl.multiple_of(block * CHUNK, CHUNK), CHUNK)

    def mlp_loads(l):
        own_rows, other_rows = pl.ds(0, rows), pl.ds(rows, rows)
        copies = [
            (u2_other.at[l], u2_v.at[other_rows]),
            (dm_other.at[l], dm_v.at[other_rows]),
            (u2_in.at[l], u2_v.at[own_rows]),
            (dm_in.at[l], dm_v.at[own_rows]),
        ]
        for b in range(2):
            units = hidden(l, b)
            copies.append((wup_hbm.at[l, :, units], wup_v.at[b]))
            copies.append((wdown_hbm.at[l, units], wdown_v.at[b]))
            copies.append((dz_in.at[l, :, pl.ds(b * CHUNK, CHUNK)], dz_v.at[b, own_rows]))
            copies.append((act_in.at[l, :, pl.ds(b * CHUNK, CHUNK)], act_v.at[b, own_rows]))
        return [pltpu.make_async_copy(src, dst, load_sem.at[4 + k]) for k, (src, dst) in enumerate(copies)]

    for k in (2, 3, 0, 1):
        load(k, 1).start()

    barrier = pltpu.get_barrier_semaphore()
    for j in range(SHARDS):

        @pl.when(me != j)
        def _():
            pl.semaphore_signal(barrier, inc=1, device_id={"dp": j}, device_id_type=MESH)

    for j in range(1, sections):
        for to in sorted({0} | {lender for lender, k, _, _ in loans if sections - k == j}):

            @pl.when(section == j)
            def _():
                pl.semaphore_signal(barrier, inc=1, device_id={"pipe": to}, device_id_type=MESH)

    for copy in mlp_loads(1):
        copy.start()

    def gain_copy(j, source):
        return pltpu.make_async_remote_copy(
            src_ref=gains_in.at[j],
            dst_ref=gains_v.at[source],
            send_sem=gain_send,
            recv_sem=gain_recv,
            device_id={"dp": j},
            device_id_type=MESH,
        )

    def inp_copy(j):
        return pltpu.make_async_remote_copy(
            src_ref=inp_stage.at[j],
            dst_ref=inp_out,
            send_sem=inp_send.at[j],
            recv_sem=inp_recv,
            device_id={"pipe": j},
            device_id_type=MESH,
        )

    def own_inp_copy():
        return pltpu.make_async_copy(inp_stage.at[0], inp_out, inp_send.at[0])

    def inp_load():
        return pltpu.make_async_copy(inp_in, inp_v, inp_send.at[0])

    def meet():
        others = lax.select(section == 0, sections - 1, 0)
        for lender in {lender for lender, _, _, _ in loans} - {0}:
            hosts = {k for other, k, _, _ in loans if other == lender}
            others = others + lax.select(section == lender, len(hosts), 0)
        pl.semaphore_wait(barrier, SHARDS - 1 + others)
        for j in range(SHARDS):

            @pl.when(me != j)
            def _():
                gain_copy(j, me).start()


    def whole_wait(ref, sem):
        pltpu.make_async_copy(ref, ref, sem).wait()

    def sender(n):
        return 2 + n - 2 * CHUNKS if isinstance(n, int) and n >= 2 * CHUNKS else n // CHUNKS

    def remote(src, dst, step, n, to, sent=None):
        return pltpu.make_async_remote_copy(
            src_ref=src,
            dst_ref=dst,
            send_sem=send.at[step - 1, sender(n)] if sent is None else sent,
            recv_sem=recv.at[step, n],
            device_id={"dp": to},
            device_id_type=MESH,
        )

    def give_copy(n, i):
        if i >= DOWN:
            return remote(own.at[i, 1 - core, 0], first.at[n, 0], 0, n, other_core, give_send.at[i])
        return remote(own.at[i, 1 - core], first.at[n], 0, n, other_core, give_send.at[i])

    def down_copy(n, l):
        mine, to = lax.select(l == 1, y, x), lax.select(l == 1, other_y, other_x)
        return remote(first.at[n, 0, 1 - mine], third.at[n], 2, n, to)

    def first_copy(n, i, l=None):
        if i >= UP:
            mine = lax.select(l == 1, y, x)
            to = lax.select(l == 1, other_y, other_x)
            return remote(first.at[n, 1 - mine], second.at[n], 1, n, to)
        if i % 2 == 1:
            return remote(first.at[n, :, 1 - x], second.at[n], 1, n, other_x)
        return remote(first.at[n, 1 - y], second.at[n], 1, n, other_y)

    def second_copy(n, i, l=None):
        if i >= UP:
            mine = lax.select(l == 1, x, y)
            to = lax.select(l == 1, other_x, other_y)
            return remote(second.at[n, 1 - mine], third.at[n], 2, n, to)
        if i % 2 == 1:
            return remote(second.at[n, 1 - y], third.at[n], 2, n, other_y)
        return remote(second.at[n, 1 - x], third.at[n], 2, n, other_x)

    def lend_copy(g):
        lender, k, i, slot = loans[g]
        return pltpu.make_async_remote_copy(
            src_ref=first.at[i],
            dst_ref=first.at[2 * CHUNKS + slot],
            send_sem=lend_send.at[g],
            recv_sem=lend_recv.at[g],
            device_id={"pipe": sections - k},
            device_id_type=MESH,
        )

    def back_copy(g):
        lender, k, i, slot = loans[g]
        return pltpu.make_async_remote_copy(
            src_ref=third.at[2 * CHUNKS + slot],
            dst_ref=third.at[i],
            send_sem=back_send.at[g],
            recv_sem=back_recv.at[g],
            device_id={"pipe": lender},
            device_id_type=MESH,
        )

    def lent_or(step, i, lent, kept):
        away = None
        for g, (lender, _, chunk, _) in enumerate(loans):
            if chunk == i:
                here = (step == 0) & (section == lender)
                pl.when(here)(functools.partial(lent, g))
                away = here if away is None else away | here
        if away is None:
            kept()
        else:
            pl.when(jnp.logical_not(away))(kept)

    def as_host(action):
        for g, (_, k, i, slot) in enumerate(loans):
            pl.when(section == sections - k)(functools.partial(action, g, 2 * CHUNKS + slot, i))

    lent_chunks = sorted({i for _, _, i, _ in loans})

    def result_copy(n, l, i):
        if i < 3:
            dst = qkv_out.at[l, :, pl.ds(i * CHUNK, CHUNK)]
        elif i < 4:
            dst = out_out.at[l]
        elif i < DOWN:
            dst = up_out.at[l, :, hidden(l, i - UP, other=True)]
        else:
            dst = down_out.at[l, pl.ds((i - DOWN) * ROWS, ROWS)]
        return pltpu.make_async_copy(third.at[n], dst, out_sem.at[1 - l])

    def own_up_copy(n, l, i):
        mine = lax.select(l == 1, x, y)
        return pltpu.make_async_copy(second.at[n, mine], up_out.at[l, :, hidden(l, i - UP)], up_sem.at[1 - l])

    def add_core(n, l, i):
        give_copy(n, i).wait_recv()
        if i >= DOWN:
            first[n, 0] = first[n, 0] + own[i, core, 0]
            down_copy(n, l).start()
        else:
            first[n] = first[n] + own[i, core]
            lent_or(1 - l, i, lambda g: lend_copy(g).start(), lambda: first_copy(n, i, l).start())

    def free(step, i):
        @pl.when(step > 0)
        def _():
            give_copy(i, i).wait_send()

    def second_sum(n, i, l=None):
        first_copy(n, i, l).wait_recv()
        if i >= UP:
            kept = first[n, lax.select(l == 1, y, x)]
        else:
            kept = first[n, :, x] if i % 2 == 1 else first[n, y]
        second[n] = second[n] + kept
        second_copy(n, i, l).start()
        if i >= UP:
            own_up_copy(n, l, i).start()

    def plain_products(step, carry):
        l = 1 - step
        base = step * CHUNKS

        def products(k, a, g, slots):
            load(k, l).wait()
            load(k + 1, l).wait()
            for i, columns in slots:
                free(step, i)
                part = tn(a[...], g[:, columns * CHUNK : (columns + 1) * CHUNK]).astype(BF16)
                for r in range(SHARDS):
                    own[i, r % 2, r // 4, (r // 2) % 2] = part[r * ROWS : (r + 1) * ROWS]
                if i == ORDER[0]:
                    pl.when(step == 0)(meet)
                give_copy(base + i, i).start()
                if i != ORDER[0]:
                    before = ORDER[ORDER.index(i) - 1]
                    add_core(base + before, l, before)
                else:

                    @pl.when(step > 0)
                    def _():
                        add_core(base - CHUNKS + ORDER[UP - 1], l + 1, ORDER[UP - 1])

        def reload(k):
            @pl.when(step == 0)
            def _():
                load(k, 0).start()
                load(k + 1, 0).start()

        products(2, o_v, da_v, ((3, 0),))
        reload(2)
        products(0, u_v, dqkv_v, ((0, 0), (1, 1), (2, 2)))
        reload(0)
        return carry

    lax.fori_loop(0, 2, plain_products, 0)
    add_core(CHUNKS + ORDER[UP - 1], 0, ORDER[UP - 1])

    def plain_sums(step):
        for i in ORDER[:UP]:
            lent_or(step, i, lambda g: None, functools.partial(second_sum, step * CHUNKS + i, i))

    def mlp_products(step, carry):
        l = 1 - step
        base = step * CHUNKS
        copies = mlp_loads(l)

        def next_loads(*which):
            @pl.when(step == 0)
            def _():
                later = mlp_loads(0)
                for k in which:
                    later[k].start()

        for k in (0, 1, 4, 5, 8, 9):
            copies[k].wait()

        def again(k, c):
            at = pl.ds(pl.multiple_of(rows + k * AGAIN, AGAIN), AGAIN)
            for b in range(2):
                act, slope = gelu_parts(nn(u2_v[at], wup_v[b]))
                act_v[b, at] = act.astype(BF16)
                dz_v[b, at] = (slope * nt(dm_v[at], wdown_v[b])).astype(BF16)
            return c

        lax.fori_loop(0, rows // AGAIN, again, 0)
        next_loads(4, 5, 8, 9)
        pl.when(step == 0)(functools.partial(plain_sums, 0))
        for k in (2, 3, 6, 7, 10, 11):
            copies[k].wait()
        for b in range(2):
            i = UP + b
            free(step, i)
            part = tn(u2_v[...], dz_v[b]).astype(BF16)
            for r in range(SHARDS):
                ry, rx = r // 4, (r // 2) % 2
                across, along = l * ry + (1 - l) * rx, l * rx + (1 - l) * ry
                own[i, r % 2, across, along] = part[r * ROWS : (r + 1) * ROWS]
            give_copy(base + i, i).start()
            if b == 1:
                add_core(base + UP, l, UP)
        next_loads(0, 2, 6, 10)
        for i in range(DOWN, CHUNKS):
            free(step, i)
        for b in range(2):
            part = tn(act_v[b], dm_v[...]).astype(BF16)
            for r in range(8):
                own[DOWN + r % 4, r // 4, 0, b] = part[r * ROWS : (r + 1) * ROWS]
        next_loads(1, 3, 7, 11)
        for i in range(DOWN, CHUNKS):
            give_copy(base + i, i).start()
        for i in range(UP + 1, CHUNKS):
            add_core(base + i, l, i)
        pl.when(step == 0)(functools.partial(plain_sums, 1))
        return carry

    lax.fori_loop(0, 2, mlp_products, 0)

    def up_sums(step, carry):
        for i in range(UP, DOWN):
            second_sum(step * CHUNKS + i, i, 1 - step)
        return carry

    lax.fori_loop(0, 2, up_sums, 0)

    def take_in(g, n, i):
        lend_copy(g).wait_recv()
        first_copy(n, i).start()

    as_host(take_in)
    as_host(lambda g, n, i: second_sum(n, i))

    fin_load = pltpu.make_async_copy(fin_in, fin_v, fin_sem)
    fin_load.start()
    fin_load.wait()
    width = D // sections
    for j in range(sections):
        first_lane = j * width - window_start(j, width)

        @pl.when(section == j)
        def _():
            for r in range(0, rows, SEQ):
                part = fin_v[r : r + SEQ, :].astype(F32)[:, first_lane : first_lane + width]
                fin_t[:, r : r + SEQ] = part.T.astype(BF16)

    fin_store = pltpu.make_async_copy(fin_t, fin_out, fin_sem)
    fin_store.start()

    @pl.when(section == 0)
    def _():
        inp_load().start()
        inp_load().wait()
        for j in range(sections):
            for r in range(0, rows, SEQ):
                part = inp_v[r : r + SEQ, :].astype(F32)[:, j * width : (j + 1) * width]
                inp_stage[j, :, r : r + SEQ] = part.T.astype(BF16)
        own_inp_copy().start()
        for j in range(1, sections):
            inp_copy(j).start()

    def take_in(g, n, i):
        lend_copy(g).wait_recv()
        first_copy(n, i).start()

    gains_v[me] = gains_in[me]
    whole_wait(gains_v.at[0 : SHARDS - 1], gain_recv)
    total = gains_v[0]
    for j in range(1, SHARDS):
        total = total + gains_v[j]
    gains_out[...] = total

    def last_sum(n, i):
        second_copy(n, i).wait_recv()
        third[n] = third[n] + second[n, y if i % 2 == 1 else x]

    def last_sums(step, carry):
        for i in ORDER:
            n = step * CHUNKS + i
            if i >= DOWN:
                down_copy(n, 1 - step).wait_recv()
                third[n] = third[n] + first[n, 0, lax.select(step == 0, y, x)]
            elif i >= UP:
                second_copy(n, i, 1 - step).wait_recv()
            else:
                lent_or(step, i, lambda g: None, functools.partial(last_sum, n, i))
            if i not in lent_chunks:
                result_copy(n, 1 - step, i).start()
        return carry

    lax.fori_loop(0, 2, last_sums, 0)

    def give_back(g, n, i):
        last_sum(n, i)
        back_copy(g).start()

    as_host(give_back)
    for g, (lender, _, _, _) in enumerate(loans):

        @pl.when(section == lender)
        def _():
            back_copy(g).wait_recv()

    for i in lent_chunks:
        for step in range(2):
            result_copy(step * CHUNKS + i, 1 - step, i).start()

    def sent(step, lent):
        whole_wait(second.at[0 : DOWN - lent], send.at[0, step])
        whole_wait(third.at[0 : CHUNKS - lent], send.at[1, step])

    for step in range(2):
        whole_wait(third.at[0:CHUNKS], out_sem.at[step])
        whole_wait(third.at[0 : DOWN - UP], up_sem.at[step])
    sent(1, 0)
    lenders = sorted({lender for lender, _, _, _ in loans})
    keeps = section >= 0
    for lender in lenders:
        keeps = keeps & (section != lender)

        @pl.when(section == lender)
        def _():
            lent = [g for g, loan in enumerate(loans) if loan[0] == lender]
            sent(0, len(lent))
            for g in lent:
                lend_copy(g).wait_send()

    pl.when(keeps)(functools.partial(sent, 0, 0))

    def guest_sent(g, n, i):
        first_copy(n, i).wait_send()
        second_copy(n, i).wait_send()
        back_copy(g).wait_send()

    as_host(guest_sent)

    for i in range(CHUNKS):
        give_copy(CHUNKS + i, i).wait_send()
    whole_wait(gains_v.at[0 : SHARDS - 1], gain_send)
    fin_store.wait()

    @pl.when(section == 0)
    def _():
        own_inp_copy().wait()
        for j in range(1, sections):
            inp_copy(j).wait_send()

    @pl.when(section > 0)
    def _():
        inp_copy(0).wait_recv()


def summed(gains, fin, inp, *factors):
    sections = lax.axis_size("pipe")
    rows, width = inp.shape[0], D // sections
    anywhere = pl.BlockSpec(memory_space=pl.ANY)
    vmem = pl.BlockSpec(memory_space=pltpu.VMEM)
    dma = pltpu.SemaphoreType.DMA
    total = 2 * CHUNKS
    slots = total + GUESTS

    def shard(height, columns):
        return jax.ShapeDtypeStruct((2, height, columns), BF16)

    return pl.pallas_call(
        functools.partial(sum_kernel, sections),
        out_shape=(
            jax.ShapeDtypeStruct((8, 128), F32),
            jax.ShapeDtypeStruct((width, rows), BF16),
            jax.ShapeDtypeStruct((width, rows), BF16),
            shard(ROWS, 3 * D),
            shard(ROWS, D),
            shard(ROWS, FF),
            shard(4 * ROWS, D),
        ),
        in_specs=[vmem] + [anywhere] * 14,
        out_specs=(vmem,) + (anywhere,) * 6,
        scratch_shapes=[pltpu.VMEM((rows, f.shape[2]), BF16) for f in factors[:4]]
        + [
            pltpu.VMEM((2 * rows, D), BF16),
            pltpu.VMEM((2, 2 * rows, CHUNK), BF16),
            pltpu.VMEM((2, 2 * rows, CHUNK), BF16),
            pltpu.VMEM((2 * rows, D), BF16),
            pltpu.VMEM((2, D, CHUNK), BF16),
            pltpu.VMEM((2, CHUNK, D), BF16),
            pltpu.VMEM((CHUNKS, 2, 2, 2, ROWS, CHUNK), BF16),
            pltpu.VMEM((slots, 2, 2, ROWS, CHUNK), BF16),
            pltpu.VMEM((slots, 2, ROWS, CHUNK), BF16),
            pltpu.VMEM((slots, ROWS, CHUNK), BF16),
            pltpu.VMEM((SHARDS, 8, 128), F32),
            pltpu.VMEM((rows, FIN_WINDOW), BF16),
            pltpu.VMEM((width, rows), BF16),
            pltpu.VMEM((rows, D), BF16),
            pltpu.VMEM((sections, width, rows), BF16),
            dma((16,)),
            dma(()),
            dma(()),
            dma(()),
            dma((sections,)),
            dma(()),
            dma((len(LOANS),)),
            dma((len(LOANS),)),
            dma((len(LOANS),)),
            dma((len(LOANS),)),
            dma((CHUNKS,)),
            dma((2, 2 + GUESTS)),
            dma((3, slots)),
            dma((2,)),
            dma((2,)),
        ],
        compiler_params=pltpu.CompilerParams(
            collective_id=1, has_side_effects=True, vmem_limit_bytes=60 * MIB
        ),
        name="sum",
    )(gains, fin, inp, *factors)


def write_kernel(count, share, gains, *refs):
    gain_one, gain_two = refs[count], refs[count + 1]
    gain_one[...] = gains[0:2, 0:share]
    gain_two[...] = gains[2:4, 0:share]
    sources, results, held, wide = (
        refs[:count],
        refs[count + 2 : 2 * count + 2],
        refs[2 * count + 2 : 3 * count + 2],
        refs[3 * count + 2 : 4 * count + 2],
    )
    load_sem, store_sem = refs[4 * count + 2 :]
    pieces = []
    for k in reversed(range(count)):
        if len(sources[k].shape) == 3:
            pieces += [tuple(r.at[l] for r in (sources[k], held[k], wide[k], results[k])) for l in range(2)]
        else:
            pieces.append((sources[k], held[k], wide[k], results[k]))
    loads = [pltpu.make_async_copy(p[0], p[1], load_sem.at[i]) for i, p in enumerate(pieces)]
    stores = [pltpu.make_async_copy(p[2], p[3], store_sem.at[i]) for i, p in enumerate(pieces)]
    for load in loads:
        load.start()
    for load, store, piece in zip(loads, stores, pieces):
        load.wait()
        piece[2][...] = piece[1][...].astype(piece[2].dtype)
        store.start()
    for store in stores:
        store.wait()


def written(gains, share, arrays, types):
    count = len(arrays)
    anywhere = pl.BlockSpec(memory_space=pl.ANY)
    vmem = pl.BlockSpec(memory_space=pltpu.VMEM)
    return pl.pallas_call(
        functools.partial(write_kernel, count, share),
        out_shape=(jax.ShapeDtypeStruct((2, share), F32),) * 2
        + tuple(jax.ShapeDtypeStruct(a.shape, t) for a, t in zip(arrays, types)),
        in_specs=[vmem] + [anywhere] * count,
        out_specs=(vmem, vmem) + (anywhere,) * count,
        scratch_shapes=[pltpu.VMEM(a.shape, a.dtype) for a in arrays]
        + [pltpu.VMEM(a.shape, t) for a, t in zip(arrays, types)]
        + [pltpu.SemaphoreType.DMA((2 * count,)), pltpu.SemaphoreType.DMA((2 * count,))],
        compiler_params=pltpu.CompilerParams(vmem_limit_bytes=60 * MIB),
        name="write",
    )(gains, *arrays)


def body(
    tokens,
    gain_one,
    qkv_weight,
    out_weight,
    gain_two,
    up_weight,
    down_weight,
    cotangent,
    flags,
    groups,
):
    micros = tokens.shape[0] // SEQ
    fin, inp, gains, u, dqkv, o, da, u2, dz, act, dm, u2_other, dm_other, _ = relay(
        tokens,
        cotangent,
        flags.reshape(micros, SEQ),
        groups,
        gain_one,
        gain_two,
        qkv_weight,
        out_weight,
        up_weight,
        down_weight,
    )

    replicas = lax.axis_size("dp")
    share = D // replicas
    if replicas == SHARDS and share == ROWS:
        gains, fin, inp, g_qkv, g_out, g_up, g_down = summed(
            gains, fin, inp, u, dqkv, o, da, u2, dz, act, dm, u2_other, dm_other, up_weight, down_weight
        )
    else:

        def grad(a, g):
            total = jnp.einsum("lsa,lsb->lab", a, g, preferred_element_type=F32).astype(BF16)
            return lax.psum_scatter(total, "dp", scatter_dimension=1, tiled=True)

        gains = lax.psum_scatter(gains, "dp", scatter_dimension=0)
        sections = lax.axis_size("pipe")
        width = D // sections
        first_lanes = jnp.array([j * width - window_start(j, width) for j in range(sections)])
        fin = lax.dynamic_slice_in_dim(fin, first_lanes[lax.axis_index("pipe")], width, 1).T
        inp = jnp.where(lax.axis_index("pipe") == 0, inp.T, jnp.zeros_like(inp.T))
        inp = lax.psum_scatter(inp, "pipe", scatter_dimension=0, tiled=True)
        g_qkv, g_out, g_up, g_down = grad(u, dqkv), grad(o, da), grad(u2, dz), grad(act, dm)
    gain_one_grad, gain_two_grad, fin, inp, g_qkv, g_out, g_up, g_down = written(
        gains, share, (fin, inp, g_qkv, g_out, g_up, g_down), (BF16,) + (F32,) * 5
    )
    return (fin.T, inp.T, gain_one_grad, g_qkv, g_out, gain_two_grad, g_up, g_down)


def solution(mesh):
    return jax.shard_map(
        body,
        mesh=mesh,
        in_specs=(
            P("dp", None),
            P("pipe", None),
            P("pipe", None, None),
            P("pipe", None, None),
            P("pipe", None),
            P("pipe", None, None),
            P("pipe", None, None),
            P("dp", None),
            P("dp"),
            P("dp"),
        ),
        out_specs=(
            P("dp", "pipe"),
            P("dp", "pipe"),
            P("pipe", "dp"),
            P("pipe", "dp", None),
            P("pipe", "dp", None),
            P("pipe", "dp"),
            P("pipe", "dp", None),
            P("pipe", "dp", None),
        ),
        check_vma=False,
    )
```
